32 devices in a mesh: track: 2 (over y), pix: 16 (over z, x, core).
Axes of the slice: x: 2, y: 2, z: 4, core: 2. Of those that a mesh axis runs over, the one named last changes fastest.
Arguments:
- phases: bfloat16 [2, 256, 131072], P('track', 'pix'), may hold values from -15 to 15
- coherent: int32 [2, 256, 1024], P('track', 'pix'), may hold values 0 or 1
- pairs: int32 [2, 256, 2], P('track'), may hold values from 0 to 199, as said below
- res_index: int32 [2, 4, 131072], P('track', None, 'pix'), may hold values from -128 to 128, as said below
- res_weight: float32 [2, 4, 131072], P('track', None, 'pix'), may hold values from 0.05 to 1
- coverage: int32 [2, 128, 8], P('track', 'pix'), may hold values 0 or 1
- los: float32 [2, 3], replicated
- north: float32 [128, 1024], P('pix'), may hold values from -6 to 6
Outputs:
- east_up: float32 [2, 128, 1024], P(None, 'pix', 'track')
- strain: float32 [3, 128, 1024], P(None, 'pix', 'track')
The draws below stay inside these ranges and needn't reach their ends.
Inputs may be any that keep to these rules, and one draw needn't show every extreme that they name: `pairs`: each row holds an earlier epoch and a strictly later one. `res_index`: cell index plus offset lies within 0 to 131071.
All inputs are finite; a program needn't handle non-finite values. No bound on the sum of `coherent` or of `coverage` on one device may be relied on, other than what follows from the above.
Results may differ from the reference program's by a relative error of at most 0.0031.
Values may be sent and summed in bfloat16 or wider, within the bound.
No kernel may reach another device: no remote copies, remote signals or barrier semaphores. Data moves between devices by JAX's collectives and lax.ppermute only.
A program may use at most 128 MiB of HBM per device.

```python
import jax
import jax.numpy as jnp
from jax import lax

IFGS = 256
EPOCHS = 200
GRD = 8
GCOLS = 1024
HALO = 128
CTILE = 128
MBLK = 128
TRACKS = 2
GROWS = 128
NCELLS = 131072


def draw_pairs(key, part):
    first_key, gap_key = jax.random.split(jax.random.fold_in(key, 11))
    first = jax.random.randint(first_key, (TRACKS, IFGS), 0, EPOCHS - 1)
    spread = jax.random.randint(gap_key, (TRACKS, IFGS), 1, EPOCHS // 4 + 2)
    second = jnp.minimum(first + spread, EPOCHS - 1)
    first = first.at[:, 0].set(0)
    second = jnp.maximum(second, first + 1)
    second = second.at[:, IFGS - 1].set(EPOCHS - 1)
    return jnp.stack([first, second], axis=-1).astype(jnp.int32)


def draw_res_index(key, part):
    offset = jax.random.randint(jax.random.fold_in(key, 23), (TRACKS, 4, NCELLS), -HALO, HALO + 1)
    offset = offset.at[:, 0, HALO].set(-HALO)
    offset = offset.at[:, 1, NCELLS - 1 - HALO].set(HALO)
    cells = jnp.arange(NCELLS, dtype=jnp.int32)
    target = jnp.clip(cells[None, None, :] + offset, 0, NCELLS - 1)
    return (target - cells[None, None, :]).astype(jnp.int32)


def draw_los(key, part):
    keys = jax.random.split(jax.random.fold_in(key, 37), 3)
    signs = jnp.where(jnp.arange(TRACKS) % 2 == 0, 1.0, -1.0).astype(jnp.float32)
    east = signs * jax.random.uniform(keys[0], (TRACKS,), jnp.float32, 0.35, 0.7)
    north_c = jax.random.uniform(keys[1], (TRACKS,), jnp.float32, -0.2, 0.2)
    up_c = jax.random.uniform(keys[2], (TRACKS,), jnp.float32, 0.6, 0.9)
    return jnp.stack([east, north_c, up_c], axis=1).astype(jnp.float32)


def set_ends(entries, own_key, least, largest):
    longest = entries.shape.index(max(entries.shape))
    spots = []
    for shift in (0, 1):
        where = [jax.random.randint(jax.random.fold_in(own_key, axis), (), 0, length) for axis, length in enumerate(entries.shape)]
        where[longest] = (where[longest] + shift) % entries.shape[longest]
        spots.append(tuple(where))
    return entries.at[spots[0]].set(least).at[spots[1]].set(largest)


def levels(stream_key, shape, cuts, low, largest):
    gain, own = 1.0, jax.random.fold_in(stream_key, 6)
    for position, shards_of in cuts:
        steps = jnp.exp(jax.random.uniform(jax.random.fold_in(own, position), (shards_of,), jnp.float32, low / len(cuts), largest / len(cuts)))
        gain = gain * jnp.repeat(steps, shape[position] // shards_of).reshape([-1 if axis == position else 1 for axis in range(len(shape))])
    return gain


def scatter_about(stream_key, shape, scale, reach, cuts=(), kind=jnp.bfloat16):
    drawn = scale * jax.random.normal(stream_key, shape, jnp.float32)
    if cuts:
        drawn = drawn * levels(stream_key, shape, cuts, -0.22, 0.18)
    return jnp.clip(drawn, -reach, reach).astype(kind)


def setup_inputs(seed: int = 0) -> dict:
    seeds = jax.random.split(jax.random.key(seed), 9)
    phases = scatter_about(seeds[0], (TRACKS, IFGS, NCELLS), 3.0, 15.0, ((0, 2), (1, 16)))
    coherent = set_ends((jax.random.randint(seeds[1], (TRACKS, IFGS, NCELLS // MBLK), 0, 4) < 3).astype(jnp.int32), jax.random.fold_in(seeds[1], 1), 0, 1)
    pairs = draw_pairs(jax.random.fold_in(seeds[8], 71), 0)
    res_index = draw_res_index(jax.random.fold_in(seeds[8], 71), 0)
    res_weight = jnp.clip(0.05 + 0.95 * jax.random.uniform(seeds[4], (TRACKS, 4, NCELLS), jnp.float32) ** levels(seeds[4], (TRACKS, 4, NCELLS), ((0, 2), (2, 16)), -0.2, 0.2), 0.05, 1.0)
    coverage = set_ends((jax.random.randint(seeds[5], (TRACKS, GROWS, GCOLS // CTILE), 0, 8) < 5).astype(jnp.int32), jax.random.fold_in(seeds[5], 1), 0, 1)
    los = draw_los(jax.random.fold_in(seeds[8], 71), 0)
    north = scatter_about(seeds[7], (GROWS, GCOLS), 1.0, 6.0, ((0, 16),), jnp.float32)
    return dict(phases=phases, coherent=coherent, pairs=pairs, res_index=res_index, res_weight=res_weight, coverage=coverage, los=los, north=north)


prior_var = 0.1
ridge_term = 0.5

def setup_track(pair_rows):
    epochs = jnp.arange(EPOCHS, dtype=jnp.int32)
    design = (epochs[None, :] == pair_rows[:, 1:2]).astype(jnp.float32) - (epochs[None, :] == pair_rows[:, 0:1]).astype(jnp.float32)
    normal = jnp.dot(design.T.astype(jnp.float32), design.astype(jnp.float32), precision=lax.Precision.HIGHEST, preferred_element_type=jnp.float32) + jnp.eye(EPOCHS, dtype=jnp.float32)
    factor = jnp.linalg.cholesky(normal)
    pseudo = jax.scipy.linalg.cho_solve((factor, True), design.T)
    centred = jnp.arange(EPOCHS).astype(jnp.float32) - (EPOCHS - 1) / 2.0
    slope = centred * (EPOCHS - 1) / jnp.sum(centred * centred)
    return (design, pseudo.astype(jnp.bfloat16), slope)

def invert_block(stack, design, pseudo_bf, slope):
    series = jnp.dot(pseudo_bf.astype(jnp.float32), stack.astype(jnp.float32), preferred_element_type=jnp.float32)
    velocity = jnp.dot(slope.astype(jnp.float32), series.astype(jnp.float32), precision=lax.Precision.HIGHEST, preferred_element_type=jnp.float32)
    fitted = jnp.dot(design.astype(jnp.bfloat16).astype(jnp.float32), series.astype(jnp.bfloat16).astype(jnp.float32), preferred_element_type=jnp.float32)
    misfit = stack.astype(jnp.float32) - fitted
    variance = jnp.sum(misfit * misfit, axis=0) / IFGS
    return jnp.stack([velocity, variance])

def solve_cells(vals, cover, north_part, los):
    east_c = los[:, 0][:, None, None]
    north_c = los[:, 1][:, None, None]
    up_c = los[:, 2][:, None, None]
    weight = cover / (vals[1] + prior_var)
    target = vals[0] - north_c * north_part[None]
    a11 = jnp.sum(weight * east_c * east_c, axis=0) + ridge_term
    a12 = jnp.sum(weight * east_c * up_c, axis=0)
    a22 = jnp.sum(weight * up_c * up_c, axis=0) + ridge_term
    b1 = jnp.sum(weight * east_c * target, axis=0)
    b2 = jnp.sum(weight * up_c * target, axis=0)
    determ = a11 * a22 - a12 * a12
    return ((a22 * b1 - a12 * b2) / determ, (a11 * b2 - a12 * b1) / determ)

def stencil(padded):
    east_p = padded[0]
    north_p = padded[1]
    exx = (east_p[1:-1, 2:] - east_p[1:-1, :-2]) / 2.0
    eyy = (north_p[2:, 1:-1] - north_p[:-2, 1:-1]) / 2.0
    exy = (east_p[2:, 1:-1] - east_p[:-2, 1:-1] + north_p[1:-1, 2:] - north_p[1:-1, :-2]) / 4.0
    return jnp.stack([exx, eyy, exy])

def one_track(packed):
    phase_t, flag_t, pair_t, offset_t, weight_t, cover_t = packed
    design, pseudo_bf, slope = setup_track(pair_t)
    blocked = phase_t.reshape(IFGS, NCELLS // MBLK, MBLK)
    masked = jnp.where(flag_t[:, :, None] == 1, blocked, jnp.zeros((), jnp.bfloat16)).reshape(IFGS, NCELLS)
    width = GRD * GCOLS
    pieces = masked.reshape(IFGS, NCELLS // width, width).transpose(1, 0, 2)
    fields = lax.map(lambda piece: invert_block(piece, design, pseudo_bf, slope), pieces)
    fields = fields.transpose(1, 0, 2).reshape(2, NCELLS)
    padded = jnp.pad(fields, ((0, 0), (HALO, HALO)))
    cells = jnp.arange(NCELLS, dtype=jnp.int32)
    picked = padded[:, (cells[None, :] + offset_t + HALO).astype(jnp.int32)]
    grid = jnp.sum(picked * weight_t[None], axis=1) / jnp.sum(weight_t, axis=0)
    tiles = GCOLS // CTILE
    cover = jnp.broadcast_to(cover_t.astype(jnp.float32)[:, :, None], (GROWS, tiles, CTILE)).reshape(GROWS, GCOLS)
    return (grid.reshape(2, GROWS, GCOLS), cover)

def reference(phases, coherent, pairs, res_index, res_weight, coverage, los, north):
    grids, covers = lax.map(one_track, (phases, coherent, pairs, res_index, res_weight, coverage))
    vals = grids.transpose(1, 0, 2, 3)
    east, up = solve_cells(vals, covers, north, los)
    padded = jnp.pad(jnp.stack([east, north]), ((0, 0), (1, 1), (1, 1)))
    return (jnp.stack([east, up]), stencil(padded))
```

```python
import functools

import jax
import jax.numpy as jnp
from jax import lax
from jax.experimental import pallas as pl
from jax.experimental.pallas import tpu as pltpu
from jax.sharding import PartitionSpec as P

EPOCHS = 200
ROWS = 208
HALO = 128
CTILE = 128
MBLK = 128
LANES = 128


prior_var = 0.1
ridge_term = 0.5


def pack_kernel(span, flags_ref, before_ref, x_ref, after_ref, out_ref):
    step = pl.program_id(0)
    steps = pl.num_programs(0)
    each = span // MBLK

    def flags_at(block):
        start = pl.multiple_of(block * LANES, LANES)
        return (flags_ref[:, pl.ds(start, LANES)] == 1).astype(jnp.float32)

    def masked(values, flags, j):
        spread = jnp.broadcast_to(flags[:, j : j + 1], values.shape).astype(jnp.bfloat16)
        return values * spread

    flags = flags_at(step)
    parts = out_ref.shape[0]
    for j in range(parts * each):
        part, inner = divmod(j, each)
        block = masked(x_ref[:, j * MBLK : (j + 1) * MBLK], flags, j)
        out_ref[part, :, HALO + inner * MBLK : HALO + (inner + 1) * MBLK] = block
        if inner == 0 and part > 0:
            out_ref[part - 1, :, HALO + span :] = block
        if inner == each - 1 and part < parts - 1:
            out_ref[part + 1, :, :HALO] = block
    earlier = flags_at(jnp.maximum(step - 1, 0))
    later = flags_at(jnp.minimum(step + 1, steps - 1))
    out_ref[0, :, :HALO] = masked(before_ref[...], earlier, LANES - 1)
    out_ref[parts - 1, :, HALO + span :] = masked(after_ref[...], later, 0)


def pack(phases, flags, parts):
    ifgs, cells = phases.shape
    blocks = flags.shape[1]
    span = cells // parts
    steps = blocks // LANES
    each = parts // steps
    return pl.pallas_call(
        functools.partial(pack_kernel, span),
        grid=(steps,),
        in_specs=[
            pl.BlockSpec((ifgs, blocks), lambda i: (0, 0)),
            pl.BlockSpec((ifgs, MBLK), lambda i: (0, jnp.maximum(i * LANES - 1, 0))),
            pl.BlockSpec((ifgs, each * span), lambda i: (0, i)),
            pl.BlockSpec((ifgs, MBLK), lambda i: (0, jnp.minimum((i + 1) * LANES, blocks - 1))),
        ],
        out_specs=pl.BlockSpec((each, ifgs, span + 2 * HALO), lambda i: (i, 0, 0)),
        out_shape=jax.ShapeDtypeStruct((parts, ifgs, span + 2 * HALO), jnp.bfloat16),
        compiler_params=pltpu.CompilerParams(vmem_limit_bytes=32 * 1024 * 1024),
        name="mask_pack",
    )(flags, phases, phases, phases)


def extend_kernel(pseudo_ref, slope_ref, out_ref):
    pseudo = pseudo_ref[...].astype(jnp.bfloat16)
    row = jnp.sum(pseudo.astype(jnp.float32) * slope_ref[...], axis=0, keepdims=True)
    high = row.astype(jnp.bfloat16).astype(jnp.float32)
    rest = row - high
    middle = rest.astype(jnp.bfloat16).astype(jnp.float32)
    low = rest - middle
    place = lax.broadcasted_iota(jnp.int32, (ROWS - EPOCHS, row.shape[1]), 0)
    terms = jnp.where(place == 0, high, jnp.where(place == 1, middle, jnp.where(place == 2, low, 0.0)))
    whole = jnp.concatenate([pseudo.astype(jnp.float32), terms], axis=0)
    out_ref[...] = whole.astype(jnp.bfloat16)


def setup_track(pair_rows):
    epochs = jnp.arange(ROWS, dtype=jnp.int32)
    wide = (epochs[None, :] == pair_rows[:, 1:2]).astype(jnp.float32) - (
        epochs[None, :] == pair_rows[:, 0:1]
    ).astype(jnp.float32)
    design = wide[:, :EPOCHS]
    normal = jnp.dot(
        design.T, design, precision=lax.Precision.HIGHEST, preferred_element_type=jnp.float32
    ) + jnp.eye(EPOCHS, dtype=jnp.float32)
    factor = jnp.linalg.cholesky(normal)
    pseudo = jax.scipy.linalg.cho_solve((factor, True), design.T)
    centred = jnp.arange(EPOCHS).astype(jnp.float32) - (EPOCHS - 1) / 2.0
    slope = centred * (EPOCHS - 1) / jnp.sum(centred * centred)
    extended = pl.pallas_call(
        extend_kernel,
        out_shape=jax.ShapeDtypeStruct((ROWS, pair_rows.shape[0]), jnp.bfloat16),
        name="extend_pseudo",
    )(pseudo, slope[:, None])
    return wide.astype(jnp.bfloat16), extended


def pick(source, lane):
    return jnp.take_along_axis(source, lane, axis=1, mode="promise_in_bounds")


def invert_kernel(
    tile, stack_ref, pseudo_ref, design_ref, index_ref, weight_ref, cover_ref, north_ref, los_ref, out_ref, fields_ref
):
    step = pl.program_id(0)
    ifgs, width = stack_ref.shape
    chunk_rows = width // LANES
    base = step * chunk_rows
    for first in range(0, width, tile):
        stack = stack_ref[:, first : first + tile]
        series = jnp.dot(pseudo_ref[...], stack, preferred_element_type=jnp.float32)
        velocity = jnp.sum(series[EPOCHS:], axis=0, keepdims=True)
        fitted = jnp.dot(design_ref[...], series.astype(jnp.bfloat16), preferred_element_type=jnp.float32)
        misfit = stack.astype(jnp.float32) - fitted
        variance = jnp.sum(misfit * misfit, axis=0, keepdims=True) / ifgs
        for k in range(tile // LANES):
            row = pl.ds(base + first // LANES + k, 1)
            fields_ref[0, row, :] = velocity[:, k * LANES : (k + 1) * LANES]
            fields_ref[1, row, :] = variance[:, k * LANES : (k + 1) * LANES]

    @pl.when(step == pl.num_programs(0) - 1)
    def _():
        taps, rows, _ = index_ref.shape
        lanes = lax.broadcasted_iota(jnp.int32, (8, LANES), 1)
        for r in range(0, rows, 8):
            here = slice(r, r + 8)
            near = [[fields_ref[f, r + k : r + k + 8, :] for k in range(3)] for f in range(2)]
            sums = [jnp.zeros((8, LANES), jnp.float32)] * 2
            total = jnp.zeros((8, LANES), jnp.float32)
            for b in range(taps):
                weight = weight_ref[b, here, :]
                place = lanes + index_ref[b, here, :] + HALO
                lane = place & (LANES - 1)
                which = place >> 7
                total = total + weight
                for f in range(2):
                    low, mid, high = (pick(near[f][k], lane) for k in range(3))
                    taken = jnp.where(which == 0, low, jnp.where(which == 1, mid, high))
                    sums[f] = sums[f] + taken * weight
            velocity = sums[0] / total
            variance = sums[1] / total
            out_ref[0, here, :] = cover_ref[here, :] / (variance + prior_var)
            out_ref[1, here, :] = velocity - los_ref[1] * north_ref[here, :]


def invert(stack, pseudo, design, index, weight, cover, north, los):
    ifgs, width = stack.shape
    rows = index.shape[1]
    blocks = width // LANES
    chunk_blocks = max(n for n in range(2, blocks + 1, 2) if blocks % n == 0 and n <= 24)
    chunk = chunk_blocks * LANES
    tile = 2 * LANES

    def whole(a):
        return pl.BlockSpec(a.shape, lambda i: (0,) * a.ndim)

    return pl.pallas_call(
        functools.partial(invert_kernel, tile),
        grid=(width // chunk,),
        in_specs=[
            pl.BlockSpec((ifgs, chunk), lambda i: (0, i)),
            whole(pseudo),
            whole(design),
            whole(index),
            whole(weight),
            whole(cover),
            whole(north),
            pl.BlockSpec(memory_space=pltpu.SMEM),
        ],
        out_specs=pl.BlockSpec((2, rows, LANES), lambda i: (0, 0, 0)),
        out_shape=jax.ShapeDtypeStruct((2, rows, LANES), jnp.float32),
        scratch_shapes=[pltpu.VMEM((2, -(-blocks // 8) * 8, LANES), jnp.float32)],
        compiler_params=pltpu.CompilerParams(vmem_limit_bytes=40 * 1024 * 1024),
        name="invert_resample",
    )(stack, pseudo, design, index, weight, cover, north, los)


def solve_kernel(tiles, vals_ref, north_ref, los_ref, east_ref, up_ref, first_ref, last_ref):
    tracks, _, rows, _ = vals_ref.shape
    a11 = a12 = a22 = b1 = b2 = 0.0
    for t in range(tracks):
        weight, target = vals_ref[t, 0], vals_ref[t, 1]
        east_c, up_c = los_ref[t, 0], los_ref[t, 2]
        by_east, by_up = weight * east_c, weight * up_c
        a11 = a11 + by_east * east_c
        a12 = a12 + by_east * up_c
        a22 = a22 + by_up * up_c
        b1 = b1 + by_east * target
        b2 = b2 + by_up * target
    a11 = a11 + ridge_term
    a22 = a22 + ridge_term
    determ = a11 * a22 - a12 * a12
    east = (a22 * b1 - a12 * b2) / determ
    up = (a11 * b2 - a12 * b1) / determ
    east_ref[...] = east
    up_ref[...] = up
    first_ref[0] = east[:tiles]
    first_ref[1] = north_ref[:tiles, :]
    last_ref[0] = east[rows - tiles :]
    last_ref[1] = north_ref[rows - tiles :, :]


def solve(vals, north, los, tiles):
    rows = vals.shape[2]
    field = jax.ShapeDtypeStruct((rows, LANES), jnp.float32)
    edge = jax.ShapeDtypeStruct((2, tiles, LANES), jnp.float32)
    vmem = pl.BlockSpec(memory_space=pltpu.VMEM)
    return pl.pallas_call(
        functools.partial(solve_kernel, tiles),
        in_specs=[vmem, vmem, pl.BlockSpec(memory_space=pltpu.SMEM)],
        out_specs=[vmem] * 4,
        out_shape=[field, field, edge, edge],
        name="solve_cells",
    )(vals, north, los)


def strain_kernel(tiles, own, block_ref, east_ref, up_ref, north_ref, before_ref, after_ref, east_up_ref, strain_ref, work_ref):
    rows = east_ref.shape[0]
    lane = lax.broadcasted_iota(jnp.int32, (rows, LANES), 1)
    tile = lax.broadcasted_iota(jnp.int32, (rows, LANES), 0) % tiles

    def across(field):
        right = jnp.where(tile == tiles - 1, 0.0, pltpu.roll(field, rows - 1, 0))
        left = jnp.where(tile == 0, 0.0, pltpu.roll(field, 1, 0))
        following = jnp.where(lane == LANES - 1, pltpu.roll(right, LANES - 1, 1), pltpu.roll(field, LANES - 1, 1))
        previous = jnp.where(lane == 0, pltpu.roll(left, 1, 1), pltpu.roll(field, 1, 1))
        return following - previous

    def down(field, which):
        below = jnp.concatenate([field[tiles:], after_ref[which]], axis=0)
        above = jnp.concatenate([before_ref[which], field[: rows - tiles]], axis=0)
        return below - above

    east = east_ref[...]
    north = north_ref[...]
    work_ref[0] = east
    work_ref[1] = up_ref[...]
    work_ref[2] = across(east) / 2.0
    work_ref[3] = down(north, 1) / 2.0
    work_ref[4] = (down(east, 0) + across(north)) / 4.0
    start = block_ref[0] * own
    for field in range(5):
        target, at = (east_up_ref, field) if field < 2 else (strain_ref, field - 2)
        for i in range(rows // tiles):
            for j in range(own):
                target[at, i : i + 1, j * LANES : (j + 1) * LANES] = work_ref[field, pl.ds(i * tiles + start + j, 1), :]


def strain(block, east, up, north, before, after, tiles, own):
    rows = east.shape[0]
    shape = (rows // tiles, own * LANES)
    vmem = pl.BlockSpec(memory_space=pltpu.VMEM)
    return pl.pallas_call(
        functools.partial(strain_kernel, tiles, own),
        in_specs=[pl.BlockSpec(memory_space=pltpu.SMEM)] + [vmem] * 5,
        out_specs=[vmem] * 2,
        out_shape=[jax.ShapeDtypeStruct((2, *shape), jnp.float32), jax.ShapeDtypeStruct((3, *shape), jnp.float32)],
        scratch_shapes=[pltpu.VMEM((5, rows, LANES), jnp.float32)],
        name="strain_rates",
    )(block, east, up, north, before, after)


def per_device(phases, coherent, pairs, res_index, res_weight, coverage, los, north):
    parts = lax.axis_size("pix")
    tracks = lax.axis_size("track")
    here = lax.axis_index("track")
    grid_rows, columns = north.shape
    tiles = columns // CTILE
    rows = grid_rows * tiles
    packed = pack(phases[0], coherent[0], parts)
    stack = lax.all_to_all(packed, "pix", split_axis=0, concat_axis=0, tiled=True)
    design, pseudo = setup_track(pairs[0])
    cells = north.reshape(rows, LANES)
    vals = invert(
        stack.reshape(-1, stack.shape[2]),
        pseudo,
        design,
        res_index.reshape(-1, rows, LANES),
        res_weight.reshape(-1, rows, LANES),
        coverage.astype(jnp.float32).reshape(rows, 1),
        cells,
        lax.dynamic_index_in_dim(los, here, 0, keepdims=False),
    )
    vals = lax.all_gather(vals, "track", axis=0)
    east, up, first, last = solve(vals, cells, los, tiles)
    onward = [(i, i + 1) for i in range(parts - 1)]
    back = [(j, i) for i, j in onward]
    before = lax.ppermute(last, "pix", onward)
    after = lax.ppermute(first, "pix", back)
    return tuple(strain(here.astype(jnp.int32)[None], east, up, cells, before, after, tiles, tiles // tracks))


def solution(mesh):
    in_specs = (
        P("track", "pix", None),
        P("track", "pix", None),
        P("track", None, None),
        P("track", None, "pix"),
        P("track", None, "pix"),
        P("track", "pix", None),
        P(),
        P("pix", None),
    )
    out_specs = (P(None, "pix", "track"), P(None, "pix", "track"))
    return jax.shard_map(
        per_device, mesh=mesh, in_specs=in_specs, out_specs=out_specs, check_vma=False
    )
```

```python
import functools

import jax
import jax.numpy as jnp
from jax import lax
from jax.experimental import pallas as pl
from jax.experimental.pallas import tpu as pltpu
from jax.sharding import PartitionSpec as P

EPOCHS = 200
ROWS = 208
HALO = 128
CTILE = 128
MBLK = 128
LANES = 128
TILE = 256


prior_var = 0.1
ridge_term = 0.5
big = 56 * 1024 * 1024


def masked(values, flags, j):
    spread = jnp.broadcast_to(flags[:, j : j + 1], values.shape).astype(jnp.bfloat16)
    return values * spread


def flags_of(flags_ref, block):
    first = block // LANES * LANES
    return (flags_ref[:, first : first + LANES] == 1).astype(jnp.float32), block - first


def pack_edges_kernel(tiles, flags_ref, phases_ref, out_ref, near_ref, sem):
    parts = out_ref.shape[0]
    blocks = flags_ref.shape[1]
    span = blocks // parts
    reach = tiles + 1
    copies = []
    for b in range(parts + 1):
        low, high = max(span * b - reach, 0), min(span * b + reach, blocks)
        at = low - (span * b - reach)
        copies.append(
            pltpu.make_async_copy(
                phases_ref.at[:, pl.ds(low * MBLK, (high - low) * MBLK)],
                near_ref.at[b, :, pl.ds(at * MBLK, (high - low) * MBLK)],
                sem.at[b],
            )
        )
    for copy in copies:
        copy.start()
    empty = jnp.zeros((out_ref.shape[1], MBLK), jnp.bfloat16)
    out_ref[0, :, :MBLK] = empty
    out_ref[parts - 1, :, (2 * reach + 1) * MBLK :] = empty
    for b in range(parts + 1):
        copies[b].wait()
        for k in range(2 * reach):
            block = span * b - reach + k
            if not 0 <= block < blocks:
                continue
            flags, j = flags_of(flags_ref, block)
            value = masked(near_ref[b, :, k * MBLK : (k + 1) * MBLK], flags, j)
            if b > 0 and k <= reach:
                out_ref[b - 1, :, (reach + 1 + k) * MBLK : (reach + 2 + k) * MBLK] = value
            if b < parts and k >= reach - 1:
                out_ref[b, :, (k - reach + 1) * MBLK : (k - reach + 2) * MBLK] = value


def pack_edges(phases, flags, parts, tiles):
    ifgs = phases.shape[0]
    vmem = pl.BlockSpec(memory_space=pltpu.VMEM)
    return pl.pallas_call(
        functools.partial(pack_edges_kernel, tiles),
        in_specs=[vmem, pl.BlockSpec(memory_space=pltpu.HBM)],
        out_specs=vmem,
        out_shape=jax.ShapeDtypeStruct((parts, ifgs, 2 * (tiles + 2) * MBLK), jnp.bfloat16),
        scratch_shapes=[
            pltpu.VMEM((parts + 1, ifgs, 2 * (tiles + 1) * MBLK), jnp.bfloat16),
            pltpu.SemaphoreType.DMA((parts + 1,)),
        ],
        compiler_params=pltpu.CompilerParams(vmem_limit_bytes=big),
        name="pack_edges",
    )(flags, phases)


def pack_inner_kernel(reach, flags_ref, x_ref, out_ref):
    parts = out_ref.shape[0]
    each = LANES // parts
    start = pl.multiple_of(pl.program_id(0) * LANES, LANES)
    flags = (flags_ref[:, pl.ds(start, LANES)] == 1).astype(jnp.float32)
    for part in range(parts):
        for k in range(reach, each - reach):
            j = part * each + k
            value = masked(x_ref[:, j * MBLK : (j + 1) * MBLK], flags, j)
            out_ref[part, :, (k - reach) * MBLK : (k - reach + 1) * MBLK] = value


def pack_inner(phases, flags, parts, tiles):
    ifgs, cells = phases.shape
    blocks = flags.shape[1]
    steps = blocks // LANES
    each = parts // steps
    reach = tiles + 1
    width = (blocks // parts - 2 * reach) * MBLK
    return pl.pallas_call(
        functools.partial(pack_inner_kernel, reach),
        grid=(steps,),
        in_specs=[
            pl.BlockSpec((ifgs, blocks), lambda i: (0, 0)),
            pl.BlockSpec((ifgs, LANES * MBLK), lambda i: (0, i)),
        ],
        out_specs=pl.BlockSpec((each, ifgs, width), lambda i: (i, 0, 0)),
        out_shape=jax.ShapeDtypeStruct((parts, ifgs, width), jnp.bfloat16),
        compiler_params=pltpu.CompilerParams(vmem_limit_bytes=big),
        name="pack_inner",
    )(flags, phases)


def extend_kernel(pseudo_ref, slope_ref, out_ref):
    pseudo = pseudo_ref[...].astype(jnp.bfloat16)
    row = jnp.sum(pseudo.astype(jnp.float32) * slope_ref[...], axis=0, keepdims=True)
    high = row.astype(jnp.bfloat16).astype(jnp.float32)
    rest = row - high
    middle = rest.astype(jnp.bfloat16).astype(jnp.float32)
    low = rest - middle
    place = lax.broadcasted_iota(jnp.int32, (ROWS - EPOCHS, row.shape[1]), 0)
    terms = jnp.where(place == 0, high, jnp.where(place == 1, middle, jnp.where(place == 2, low, 0.0)))
    whole = jnp.concatenate([pseudo.astype(jnp.float32), terms], axis=0)
    out_ref[...] = whole.astype(jnp.bfloat16)


def setup_track(pair_rows):
    epochs = jnp.arange(ROWS, dtype=jnp.int32)
    wide = (epochs[None, :] == pair_rows[:, 1:2]).astype(jnp.float32) - (
        epochs[None, :] == pair_rows[:, 0:1]
    ).astype(jnp.float32)
    design = wide[:, :EPOCHS]
    normal = jnp.dot(
        design.T, design, precision=lax.Precision.HIGHEST, preferred_element_type=jnp.float32
    ) + jnp.eye(EPOCHS, dtype=jnp.float32)
    factor = jnp.linalg.cholesky(normal)
    pseudo = jax.scipy.linalg.cho_solve((factor, True), design.T)
    centred = jnp.arange(EPOCHS).astype(jnp.float32) - (EPOCHS - 1) / 2.0
    slope = centred * (EPOCHS - 1) / jnp.sum(centred * centred)
    extended = pl.pallas_call(
        extend_kernel,
        out_shape=jax.ShapeDtypeStruct((ROWS, pair_rows.shape[0]), jnp.bfloat16),
        name="extend_pseudo",
    )(pseudo, slope[:, None])
    return wide.astype(jnp.bfloat16), extended


def invert_tile(stack, pseudo_ref, design_ref, fields_ref, base):
    series = jnp.dot(pseudo_ref[...], stack, preferred_element_type=jnp.float32)
    velocity = jnp.sum(series[EPOCHS:], axis=0, keepdims=True)
    fitted = jnp.dot(design_ref[...], series.astype(jnp.bfloat16), preferred_element_type=jnp.float32)
    misfit = stack.astype(jnp.float32) - fitted
    variance = jnp.sum(misfit * misfit, axis=0, keepdims=True) / stack.shape[0]
    for k in range(stack.shape[1] // LANES):
        row = pl.ds(base + k, 1)
        fields_ref[0, row, :] = velocity[:, k * LANES : (k + 1) * LANES]
        fields_ref[1, row, :] = variance[:, k * LANES : (k + 1) * LANES]


def pick(source, lane):
    return jnp.take_along_axis(source, lane, axis=1, mode="promise_in_bounds")


def resample(fields_ref, base, first, count, index_ref, weight_ref, cover_ref, north_ref, los_ref, out_ref):
    lanes = lax.broadcasted_iota(jnp.int32, (8, LANES), 1)
    for r in range(0, count, 8):
        here = slice(first + r, first + r + 8)
        near = [[fields_ref[f, base + r + k : base + r + k + 8, :] for k in range(3)] for f in range(2)]
        sums = [jnp.zeros((8, LANES), jnp.float32)] * 2
        total = jnp.zeros((8, LANES), jnp.float32)
        for b in range(index_ref.shape[0]):
            weight = weight_ref[b, here, :]
            place = lanes + index_ref[b, here, :] + HALO
            lane = place & (LANES - 1)
            which = place >> 7
            total = total + weight
            for f in range(2):
                low, mid, high = (pick(near[f][k], lane) for k in range(3))
                taken = jnp.where(which == 0, low, jnp.where(which == 1, mid, high))
                sums[f] = sums[f] + taken * weight
        out_ref[0, here, :] = cover_ref[here, :] / (sums[1] / total + prior_var)
        out_ref[1, here, :] = sums[0] / total - los_ref[1] * north_ref[here, :]


def edges_kernel(
    tiles, stack_ref, pseudo_ref, design_ref, index_ref, weight_ref, cover_ref, north_ref, los_ref, out_ref, seam_ref, fields_ref
):
    for first in range(0, stack_ref.shape[1], TILE):
        invert_tile(stack_ref[:, first : first + TILE], pseudo_ref, design_ref, fields_ref, first // LANES)
    seam_ref[...] = fields_ref[:, tiles : tiles + 4, :]
    for half in range(2):
        resample(
            fields_ref, half * (tiles + 2), half * tiles, tiles,
            index_ref, weight_ref, cover_ref, north_ref, los_ref, out_ref,
        )


def edges(stack, pseudo, design, index, weight, cover, north, los, tiles):
    rows = 2 * (tiles + 2)
    vmem = pl.BlockSpec(memory_space=pltpu.VMEM)
    return pl.pallas_call(
        functools.partial(edges_kernel, tiles),
        in_specs=[vmem] * 7 + [pl.BlockSpec(memory_space=pltpu.SMEM)],
        out_specs=[vmem] * 2,
        out_shape=[
            jax.ShapeDtypeStruct((2, 2 * tiles, LANES), jnp.float32),
            jax.ShapeDtypeStruct((2, 4, LANES), jnp.float32),
        ],
        scratch_shapes=[pltpu.VMEM((2, -(-rows // 8) * 8, LANES), jnp.float32)],
        compiler_params=pltpu.CompilerParams(vmem_limit_bytes=big),
        name="edge_rows",
    )(stack, pseudo, design, index, weight, cover, north, los)


def inner_kernel(
    stack_ref, seam_ref, pseudo_ref, design_ref, index_ref, weight_ref, cover_ref, north_ref, los_ref, out_ref, fields_ref,
    held_ref, sem,
):
    ifgs, width = stack_ref.shape
    tiles = width // TILE
    cuts = [tiles * k // held_ref.shape[0] for k in range(held_ref.shape[0] + 1)]
    copies = []
    for k in range(held_ref.shape[0]):
        size = (cuts[k + 1] - cuts[k]) * TILE
        copies.append(
            pltpu.make_async_copy(
                stack_ref.at[:, pl.ds(cuts[k] * TILE, size)], held_ref.at[k, :, pl.ds(0, size)], sem.at[k]
            )
        )
        copies[k].start()
    pixel_rows = width // LANES
    fields_ref[:, 0:2, :] = seam_ref[:, 0:2, :]
    fields_ref[:, pixel_rows + 2 : pixel_rows + 4, :] = seam_ref[:, 2:4, :]
    for k in range(held_ref.shape[0]):
        copies[k].wait()
        for t in range(cuts[k + 1] - cuts[k]):
            invert_tile(
                held_ref[k, :, t * TILE : (t + 1) * TILE], pseudo_ref, design_ref, fields_ref,
                2 + (cuts[k] + t) * (TILE // LANES),
            )
    resample(
        fields_ref, 0, 0, index_ref.shape[1], index_ref, weight_ref, cover_ref, north_ref, los_ref, out_ref
    )


def inner(stack, seam, pseudo, design, index, weight, cover, north, los):
    ifgs, width = stack.shape
    rows = index.shape[1]
    pieces = 4
    largest = -(-(width // TILE) // pieces) * TILE
    vmem = pl.BlockSpec(memory_space=pltpu.VMEM)
    return pl.pallas_call(
        inner_kernel,
        in_specs=[pl.BlockSpec(memory_space=pltpu.HBM)] + [vmem] * 7 + [pl.BlockSpec(memory_space=pltpu.SMEM)],
        out_specs=vmem,
        out_shape=jax.ShapeDtypeStruct((2, rows, LANES), jnp.float32),
        scratch_shapes=[
            pltpu.VMEM((2, -(-(rows + 2) // 8) * 8, LANES), jnp.float32),
            pltpu.VMEM((pieces, ifgs, largest), jnp.bfloat16),
            pltpu.SemaphoreType.DMA((pieces,)),
        ],
        compiler_params=pltpu.CompilerParams(vmem_limit_bytes=big),
        name="inner_rows",
    )(stack, seam, pseudo, design, index, weight, cover, north, los)


def solve_cells(vals_ref, los_ref):
    a11 = a12 = a22 = b1 = b2 = 0.0
    for t in range(vals_ref.shape[0]):
        weight, target = vals_ref[t, 0], vals_ref[t, 1]
        east_c, up_c = los_ref[t, 0], los_ref[t, 2]
        by_east, by_up = weight * east_c, weight * up_c
        a11 = a11 + by_east * east_c
        a12 = a12 + by_east * up_c
        a22 = a22 + by_up * up_c
        b1 = b1 + by_east * target
        b2 = b2 + by_up * target
    a11 = a11 + ridge_term
    a22 = a22 + ridge_term
    determ = a11 * a22 - a12 * a12
    return (a22 * b1 - a12 * b2) / determ, (a11 * b2 - a12 * b1) / determ


def solve_kernel(tiles, vals_ref, north_ref, los_ref, solved_ref, first_ref, last_ref):
    east, up = solve_cells(vals_ref, los_ref)
    solved_ref[0] = east
    solved_ref[1] = up
    first_ref[0] = east[:tiles]
    first_ref[1] = north_ref[:tiles, :]
    last_ref[0] = east[tiles:]
    last_ref[1] = north_ref[tiles:, :]


def solve_edges(vals, north, los, tiles):
    edge = jax.ShapeDtypeStruct((2, tiles, LANES), jnp.float32)
    vmem = pl.BlockSpec(memory_space=pltpu.VMEM)
    return pl.pallas_call(
        functools.partial(solve_kernel, tiles),
        in_specs=[vmem, vmem, pl.BlockSpec(memory_space=pltpu.SMEM)],
        out_specs=[vmem] * 3,
        out_shape=[jax.ShapeDtypeStruct((2, 2 * tiles, LANES), jnp.float32), edge, edge],
        name="solve_edges",
    )(vals, north, los)


def final_kernel(
    tiles, own, block_ref, los_ref, vals_ref, solved_ref, north_ref, before_ref, after_ref, east_up_ref, strain_ref, work_ref
):
    rows = north_ref.shape[0]
    lane = lax.broadcasted_iota(jnp.int32, (rows, LANES), 1)
    tile = lax.broadcasted_iota(jnp.int32, (rows, LANES), 0) % tiles

    def across(field):
        right = jnp.where(tile == tiles - 1, 0.0, pltpu.roll(field, rows - 1, 0))
        left = jnp.where(tile == 0, 0.0, pltpu.roll(field, 1, 0))
        following = jnp.where(lane == LANES - 1, pltpu.roll(right, LANES - 1, 1), pltpu.roll(field, LANES - 1, 1))
        previous = jnp.where(lane == 0, pltpu.roll(left, 1, 1), pltpu.roll(field, 1, 1))
        return following - previous

    def down(field, which):
        below = jnp.concatenate([field[tiles:], after_ref[which]], axis=0)
        above = jnp.concatenate([before_ref[which], field[: rows - tiles]], axis=0)
        return below - above

    east, up = (
        jnp.concatenate([solved_ref[k, :tiles], middle, solved_ref[k, tiles:]], axis=0)
        for k, middle in enumerate(solve_cells(vals_ref, los_ref))
    )
    north = north_ref[...]
    work_ref[0] = east
    work_ref[1] = up
    work_ref[2] = across(east) / 2.0
    work_ref[3] = down(north, 1) / 2.0
    work_ref[4] = (down(east, 0) + across(north)) / 4.0
    start = block_ref[0] * own
    for field in range(5):
        target, at = (east_up_ref, field) if field < 2 else (strain_ref, field - 2)
        for i in range(rows // tiles):
            for j in range(own):
                target[at, i : i + 1, j * LANES : (j + 1) * LANES] = work_ref[field, pl.ds(i * tiles + start + j, 1), :]


def final(block, los, vals, solved, north, before, after, tiles, own):
    rows = north.shape[0]
    shape = (rows // tiles, own * LANES)
    vmem = pl.BlockSpec(memory_space=pltpu.VMEM)
    return pl.pallas_call(
        functools.partial(final_kernel, tiles, own),
        in_specs=[pl.BlockSpec(memory_space=pltpu.SMEM)] * 2 + [vmem] * 5,
        out_specs=[vmem] * 2,
        out_shape=[jax.ShapeDtypeStruct((2, *shape), jnp.float32), jax.ShapeDtypeStruct((3, *shape), jnp.float32)],
        scratch_shapes=[pltpu.VMEM((5, rows, LANES), jnp.float32)],
        name="solve_and_strain",
    )(block, los, vals, solved, north, before, after)


def per_device(phases, coherent, pairs, res_index, res_weight, coverage, los, north):
    parts = lax.axis_size("pix")
    tracks = lax.axis_size("track")
    here = lax.axis_index("track")
    grid_rows, columns = north.shape
    tiles = columns // CTILE
    rows = grid_rows * tiles
    edge_stack = lax.all_to_all(
        pack_edges(phases[0], coherent[0], parts, tiles), "pix", split_axis=0, concat_axis=0, tiled=True
    )
    inner_stack = lax.all_to_all(
        pack_inner(phases[0], coherent[0], parts, tiles), "pix", split_axis=0, concat_axis=0, tiled=True
    )
    design, pseudo = setup_track(pairs[0])
    cells = north.reshape(rows, LANES)
    own_los = lax.dynamic_index_in_dim(los, here, 0, keepdims=False)
    per_cell = (
        res_index.reshape(-1, rows, LANES),
        res_weight.reshape(-1, rows, LANES),
        coverage.astype(jnp.float32).reshape(rows, 1),
        cells,
    )
    at_edges = [jnp.concatenate([a[..., :tiles, :], a[..., rows - tiles :, :]], axis=-2) for a in per_cell]
    at_inner = [a[..., tiles : rows - tiles, :] for a in per_cell]

    def flat(stack):
        return stack.reshape(-1, stack.shape[2])

    edge_vals, seam = edges(flat(edge_stack), pseudo, design, *at_edges, own_los, tiles)
    edge_vals = lax.all_gather(edge_vals, "track", axis=0)
    solved, first, last = solve_edges(edge_vals, at_edges[3], los, tiles)
    onward = [(i, i + 1) for i in range(parts - 1)]
    back = [(j, i) for i, j in onward]
    before = lax.ppermute(last, "pix", onward)
    after = lax.ppermute(first, "pix", back)
    inner_vals = inner(flat(inner_stack), seam, pseudo, design, *at_inner, own_los)
    inner_vals = lax.all_gather(inner_vals, "track", axis=0)
    return tuple(
        final(
            here.astype(jnp.int32)[None], los, inner_vals, solved, cells, before, after, tiles, tiles // tracks
        )
    )


def solution(mesh):
    in_specs = (
        P("track", "pix", None),
        P("track", "pix", None),
        P("track", None, None),
        P("track", None, "pix"),
        P("track", None, "pix"),
        P("track", "pix", None),
        P(),
        P("pix", None),
    )
    out_specs = (P(None, "pix", "track"), P(None, "pix", "track"))
    return jax.shard_map(
        per_device, mesh=mesh, in_specs=in_specs, out_specs=out_specs, check_vma=False
    )
```

```python
import functools

import jax
import jax.numpy as jnp
from jax import lax
from jax.experimental import pallas as pl
from jax.experimental.pallas import tpu as pltpu
from jax.sharding import PartitionSpec as P

EPOCHS = 200
ROWS = 208
HALO = 128
CTILE = 128
MBLK = 128
LANES = 128
TILE = 256
PIECE = 1024


prior_var = 0.1
ridge_term = 0.5
medium = 24 * 1024 * 1024


def spread(flags, j, shape):
    return jnp.broadcast_to(flags[:, j : j + 1], shape).astype(jnp.bfloat16)


def part_flags(flags_ref, first):
    lead = pl.multiple_of(first // LANES * LANES, LANES)
    flags = (flags_ref[:, pl.ds(lead, LANES)] == 1).astype(jnp.float32)
    return pltpu.roll(flags, (LANES - (first - lead)) % LANES, 1)


def pack_edges_kernel(tiles, flags_ref, phases_ref, out_ref, near_ref, in_sem):
    parts, ifgs, _ = out_ref.shape
    blocks = flags_ref.shape[1]
    span = blocks // parts
    reach = tiles + 1
    bound = 2 * reach * MBLK
    ends = []
    for b, low, at in ((0, 0, reach), (parts, blocks - reach, 0)):
        ends.append(
            pltpu.make_async_copy(
                phases_ref.at[:, pl.ds(low * MBLK, reach * MBLK)], near_ref.at[b, :, pl.ds(at * MBLK, reach * MBLK)], in_sem.at[b]
            )
        )

    def between(b):
        low = pl.multiple_of((span * b - reach) * MBLK, MBLK)
        return pltpu.make_async_copy(phases_ref.at[:, pl.ds(low, bound)], near_ref.at[b], in_sem.at[b])

    ends[0].start()

    @pl.loop(1, parts)
    def _(b):
        between(b).start()

    ends[1].start()
    empty = jnp.zeros((ifgs, reach * MBLK), jnp.bfloat16)
    near_ref[0, :, : reach * MBLK] = empty
    near_ref[parts, :, reach * MBLK :] = empty
    ends[0].wait()

    @pl.loop(0, parts)
    def _(p):
        @pl.when(p < parts - 1)
        def _():
            between(p + 1).wait()

        @pl.when(p == parts - 1)
        def _():
            ends[1].wait()

        first = p * span
        flags = part_flags(flags_ref, first)
        earlier = part_flags(flags_ref, jnp.maximum(first - 1, 0))
        later = part_flags(flags_ref, jnp.minimum(first + span, blocks - 1))
        shape = (ifgs, MBLK)
        for half in range(2):
            for k in range(tiles + 2):
                block = k - 1 if half == 0 else span - reach + k
                if block < 0:
                    keep = spread(earlier, 0, shape)
                elif block == span:
                    keep = spread(later, 0, shape)
                else:
                    keep = spread(flags, block, shape)
                at = (reach - 1 + k if half == 0 else k) * MBLK
                to = (half * (tiles + 2) + k) * MBLK
                out_ref[p, :, to : to + MBLK] = near_ref[p + half, :, at : at + MBLK] * keep


def pack_edges(phases, flags, parts, tiles):
    ifgs = phases.shape[0]
    vmem = pl.BlockSpec(memory_space=pltpu.VMEM)
    return pl.pallas_call(
        functools.partial(pack_edges_kernel, tiles),
        in_specs=[vmem, pl.BlockSpec(memory_space=pltpu.HBM)],
        out_specs=vmem,
        out_shape=jax.ShapeDtypeStruct((parts, ifgs, 2 * (tiles + 2) * MBLK), jnp.bfloat16),
        scratch_shapes=[
            pltpu.VMEM((parts + 1, ifgs, 2 * (tiles + 1) * MBLK), jnp.bfloat16),
            pltpu.SemaphoreType.DMA((parts + 1,)),
        ],
        compiler_params=pltpu.CompilerParams(vmem_limit_bytes=medium),
        name="pack_edges",
    )(flags, phases)


def pack_inner_kernel(reach, flags_ref, phases_ref, out_ref, held_ref, ready_ref, in_sem, out_sem):
    parts, ifgs, width = out_ref.shape
    span = flags_ref.shape[1] // parts

    def inward(p):
        low = pl.multiple_of((p * span + reach) * MBLK, MBLK)
        return pltpu.make_async_copy(phases_ref.at[:, pl.ds(low, width)], held_ref.at[p], in_sem.at[p])

    def outward(p):
        return pltpu.make_async_copy(ready_ref.at[p], out_ref.at[p], out_sem.at[p])

    @pl.loop(0, parts)
    def _(p):
        inward(p).start()

    @pl.loop(0, parts)
    def _(p):
        inward(p).wait()
        flags = part_flags(flags_ref, p * span)
        for k in range(width // MBLK):
            at = slice(k * MBLK, (k + 1) * MBLK)
            ready_ref[p, :, at] = held_ref[p, :, at] * spread(flags, reach + k, (ifgs, MBLK))
        outward(p).start()

    @pl.loop(0, parts)
    def _(p):
        outward(p).wait()


def pack_inner(phases, flags, parts, tiles):
    ifgs = phases.shape[0]
    reach = tiles + 1
    width = (flags.shape[1] // parts - 2 * reach) * MBLK
    hbm = pl.BlockSpec(memory_space=pltpu.HBM)
    return pl.pallas_call(
        functools.partial(pack_inner_kernel, reach),
        in_specs=[pl.BlockSpec(memory_space=pltpu.VMEM), hbm],
        out_specs=hbm,
        out_shape=jax.ShapeDtypeStruct((parts, ifgs, width), jnp.bfloat16),
        scratch_shapes=[
            pltpu.VMEM((parts, ifgs, width), jnp.bfloat16),
            pltpu.VMEM((parts, ifgs, width), jnp.bfloat16),
            pltpu.SemaphoreType.DMA((parts,)),
            pltpu.SemaphoreType.DMA((parts,)),
        ],
        compiler_params=pltpu.CompilerParams(vmem_limit_bytes=medium),
        name="pack_inner",
    )(flags, phases)


def exact_dot(a, b):
    return jnp.dot(a, b, precision=lax.Precision.HIGHEST, preferred_element_type=jnp.float32)


def pseudo_kernel(pairs_ref, design_ref, out_ref, normal_ref, inverse_ref):
    ifgs = pairs_ref.shape[1]
    size = normal_ref.shape[0]
    epoch = lax.broadcasted_iota(jnp.int32, (size, ifgs), 0)
    across = (epoch == pairs_ref[1:2, :]).astype(jnp.float32) - (epoch == pairs_ref[0:1, :]).astype(jnp.float32)
    down = across.T
    design_ref[...] = down[:, :ROWS].astype(jnp.bfloat16)
    eye = (
        lax.broadcasted_iota(jnp.int32, (size, size), 0) == lax.broadcasted_iota(jnp.int32, (size, size), 1)
    ).astype(jnp.float32)
    normal = eye + jnp.dot(
        across.astype(jnp.bfloat16), down.astype(jnp.bfloat16), preferred_element_type=jnp.float32
    )
    normal_ref[...] = normal
    inverse_ref[...] = eye / jnp.where(eye == 1.0, normal, 1.0)

    def unfinished(state):
        step, gap = state
        return jnp.logical_and(step < 24, gap > 1e-5)

    def improve(state):
        step, _ = state
        inverse = inverse_ref[...]
        rest = eye - exact_dot(normal_ref[...], inverse)
        inverse_ref[...] = inverse + exact_dot(inverse, rest)
        return step + 1, jnp.max(jnp.abs(rest))

    lax.while_loop(unfinished, improve, (jnp.int32(0), jnp.float32(1.0)))
    pseudo = exact_dot(inverse_ref[...], across)[:ROWS].astype(jnp.bfloat16).astype(jnp.float32)
    place = lax.broadcasted_iota(jnp.int32, (ROWS, ifgs), 0)
    centred = place.astype(jnp.float32) - (EPOCHS - 1) / 2.0
    square = sum((e - (EPOCHS - 1) / 2.0) ** 2 for e in range(EPOCHS))
    slope = centred * (EPOCHS - 1) / square
    row = jnp.sum(pseudo * jnp.where(place < EPOCHS, slope, 0.0), axis=0, keepdims=True)
    high = row.astype(jnp.bfloat16).astype(jnp.float32)
    rest = row - high
    middle = rest.astype(jnp.bfloat16).astype(jnp.float32)
    low = rest - middle
    extra = place - EPOCHS
    terms = jnp.where(extra == 0, high, jnp.where(extra == 1, middle, jnp.where(extra == 2, low, 0.0)))
    out_ref[...] = jnp.where(extra < 0, pseudo, terms).astype(jnp.bfloat16)


def setup_track(pair_rows):
    ifgs = pair_rows.shape[0]
    size = 256
    vmem = pl.BlockSpec(memory_space=pltpu.VMEM)
    return pl.pallas_call(
        pseudo_kernel,
        in_specs=[vmem],
        out_specs=[vmem] * 2,
        out_shape=[jax.ShapeDtypeStruct((ifgs, ROWS), jnp.bfloat16), jax.ShapeDtypeStruct((ROWS, ifgs), jnp.bfloat16)],
        scratch_shapes=[pltpu.VMEM((size, size), jnp.float32), pltpu.VMEM((size, size), jnp.float32)],
        compiler_params=pltpu.CompilerParams(vmem_limit_bytes=medium),
        name="pseudo_inverse",
    )(pair_rows.T)


def invert_tiles(stack_ref, first, width, pseudo_ref, design_ref, fields_ref, base):
    for start in range(0, width, TILE):
        stack = stack_ref[:, pl.ds(pl.multiple_of(first + start, LANES), TILE)]
        series = jnp.dot(pseudo_ref[...], stack, preferred_element_type=jnp.float32)
        velocity = jnp.sum(series[EPOCHS:], axis=0, keepdims=True)
        fitted = jnp.dot(design_ref[...], series.astype(jnp.bfloat16), preferred_element_type=jnp.float32)
        misfit = stack.astype(jnp.float32) - fitted
        variance = jnp.sum(misfit * misfit, axis=0, keepdims=True) / stack.shape[0]
        for k in range(TILE // LANES):
            row = pl.ds(base + start // LANES + k, 1)
            fields_ref[0, row, :] = velocity[:, k * LANES : (k + 1) * LANES]
            fields_ref[1, row, :] = variance[:, k * LANES : (k + 1) * LANES]


def pick(source, lane):
    return jnp.take_along_axis(source, lane, axis=1, mode="promise_in_bounds")


def resample(fields_ref, base, cell, to, index_ref, weight_ref, cover_ref, north_ref, north_c, out_ref):
    lanes = lax.broadcasted_iota(jnp.int32, (8, LANES), 1)
    here = pl.ds(cell, 8)
    near = [[fields_ref[f, pl.ds(base + k, 8), :] for k in range(3)] for f in range(2)]
    sums = [jnp.zeros((8, LANES), jnp.float32)] * 2
    total = jnp.zeros((8, LANES), jnp.float32)
    for b in range(index_ref.shape[0]):
        weight = weight_ref[b, here, :]
        place = lanes + index_ref[b, here, :] + HALO
        lane = place & (LANES - 1)
        which = place >> 7
        total = total + weight
        for f in range(2):
            low, mid, high = (pick(near[f][k], lane) for k in range(3))
            taken = jnp.where(which == 0, low, jnp.where(which == 1, mid, high))
            sums[f] = sums[f] + taken * weight
    cover = cover_ref[here, :].astype(jnp.float32)
    out_ref[0, pl.ds(to, 8), :] = cover / (sums[1] / total + prior_var)
    out_ref[1, pl.ds(to, 8), :] = sums[0] / total - north_c * north_ref[here, :]


def edges_kernel(
    tiles, here_ref, los_ref, stack_ref, pseudo_ref, design_ref, index_ref, weight_ref, cover_ref, north_ref, out_ref, seam_ref, fields_ref
):
    rows = index_ref.shape[1]
    width = stack_ref.shape[1] // 2

    @pl.loop(0, 2)
    def _(half):
        invert_tiles(stack_ref, half * width, width, pseudo_ref, design_ref, fields_ref, half * (tiles + 2))

    seam_ref[...] = fields_ref[:, tiles : tiles + 4, :]
    north_c = los_ref[here_ref[0], 1]
    for half in range(2):
        for r in range(0, tiles, 8):
            resample(
                fields_ref, half * (tiles + 2) + r, half * (rows - tiles) + r, half * tiles + r,
                index_ref, weight_ref, cover_ref, north_ref, north_c, out_ref,
            )


def edges(here, los, stack, pseudo, design, cells, tiles):
    rows = 2 * (tiles + 2)
    vmem = pl.BlockSpec(memory_space=pltpu.VMEM)
    return pl.pallas_call(
        functools.partial(edges_kernel, tiles),
        in_specs=[pl.BlockSpec(memory_space=pltpu.SMEM)] * 2 + [vmem] * 7,
        out_specs=[vmem] * 2,
        out_shape=[
            jax.ShapeDtypeStruct((2, 2 * tiles, LANES), jnp.float32),
            jax.ShapeDtypeStruct((2, 4, LANES), jnp.float32),
        ],
        scratch_shapes=[pltpu.VMEM((2, -(-rows // 8) * 8, LANES), jnp.float32)],
        compiler_params=pltpu.CompilerParams(vmem_limit_bytes=medium),
        name="edge_rows",
    )(here, los, stack, pseudo, design, *cells)


def inner_kernel(
    tiles, here_ref, los_ref, stack_ref, seam_ref, pseudo_ref, design_ref, index_ref, weight_ref, cover_ref, north_ref, out_ref,
    fields_ref, held_ref, sem,
):
    ifgs, width = stack_ref.shape
    pieces = -(-width // PIECE)
    last = width - (pieces - 1) * PIECE

    def piece(k, size):
        part = pl.ds(pl.multiple_of(k * PIECE, LANES), size)
        return pltpu.make_async_copy(stack_ref.at[:, part], held_ref.at[:, part], sem.at[k])

    for k in range(pieces):
        piece(k, PIECE if k < pieces - 1 else last).start()
    pixel_rows = width // LANES
    fields_ref[:, 0:2, :] = seam_ref[:, 0:2, :]
    fields_ref[:, pixel_rows + 2 : pixel_rows + 4, :] = seam_ref[:, 2:4, :]

    @pl.loop(0, pieces)
    def _(k):
        @pl.when(k < pieces - 1)
        def _():
            piece(k, PIECE).wait()

        @pl.when(k == pieces - 1)
        def _():
            piece(pieces - 1, last).wait()

        first = jnp.minimum(k * PIECE, width - PIECE)
        invert_tiles(held_ref, first, PIECE, pseudo_ref, design_ref, fields_ref, 2 + first // LANES)

    north_c = los_ref[here_ref[0], 1]

    @pl.loop(0, out_ref.shape[1], step=8)
    def _(r):
        r = pl.multiple_of(r, 8)
        resample(fields_ref, r, tiles + r, r, index_ref, weight_ref, cover_ref, north_ref, north_c, out_ref)


def inner(here, los, stack, seam, pseudo, design, cells, tiles):
    ifgs, width = stack.shape
    rows = cells[0].shape[1] - 2 * tiles
    vmem = pl.BlockSpec(memory_space=pltpu.VMEM)
    return pl.pallas_call(
        functools.partial(inner_kernel, tiles),
        in_specs=[pl.BlockSpec(memory_space=pltpu.SMEM)] * 2 + [pl.BlockSpec(memory_space=pltpu.HBM)] + [vmem] * 7,
        out_specs=vmem,
        out_shape=jax.ShapeDtypeStruct((2, rows, LANES), jnp.float32),
        scratch_shapes=[
            pltpu.VMEM((2, -(-(rows + 2) // 8) * 8, LANES), jnp.float32),
            pltpu.VMEM((ifgs, width), jnp.bfloat16),
            pltpu.SemaphoreType.DMA((-(-width // PIECE),)),
        ],
        compiler_params=pltpu.CompilerParams(vmem_limit_bytes=medium),
        name="inner_rows",
    )(here, los, stack, seam, pseudo, design, *cells)


def solve_cells(vals_ref, los_ref):
    a11 = a12 = a22 = b1 = b2 = 0.0
    for t in range(vals_ref.shape[0]):
        weight, target = vals_ref[t, 0], vals_ref[t, 1]
        east_c, up_c = los_ref[t, 0], los_ref[t, 2]
        by_east, by_up = weight * east_c, weight * up_c
        a11 = a11 + by_east * east_c
        a12 = a12 + by_east * up_c
        a22 = a22 + by_up * up_c
        b1 = b1 + by_east * target
        b2 = b2 + by_up * target
    a11 = a11 + ridge_term
    a22 = a22 + ridge_term
    determ = a11 * a22 - a12 * a12
    return (a22 * b1 - a12 * b2) / determ, (a11 * b2 - a12 * b1) / determ


def solve_kernel(tiles, vals_ref, north_ref, los_ref, solved_ref, first_ref, last_ref):
    east, up = solve_cells(vals_ref, los_ref)
    solved_ref[0] = east
    solved_ref[1] = up
    first_ref[0] = east[:tiles]
    first_ref[1] = north_ref[:tiles, :]
    last_ref[0] = east[tiles:]
    last_ref[1] = north_ref[north_ref.shape[0] - tiles :, :]


def solve_edges(vals, north, los, tiles):
    edge = jax.ShapeDtypeStruct((2, tiles, LANES), jnp.float32)
    vmem = pl.BlockSpec(memory_space=pltpu.VMEM)
    return pl.pallas_call(
        functools.partial(solve_kernel, tiles),
        in_specs=[vmem, vmem, pl.BlockSpec(memory_space=pltpu.SMEM)],
        out_specs=[vmem] * 3,
        out_shape=[jax.ShapeDtypeStruct((2, 2 * tiles, LANES), jnp.float32), edge, edge],
        name="solve_edges",
    )(vals, north, los)


def final_kernel(
    tiles, own, block_ref, los_ref, vals_ref, solved_ref, north_ref, before_ref, after_ref, east_up_ref, strain_ref, work_ref
):
    rows = north_ref.shape[0]
    lane = lax.broadcasted_iota(jnp.int32, (rows, LANES), 1)
    tile = lax.broadcasted_iota(jnp.int32, (rows, LANES), 0) % tiles

    def across(field):
        right = jnp.where(tile == tiles - 1, 0.0, pltpu.roll(field, rows - 1, 0))
        left = jnp.where(tile == 0, 0.0, pltpu.roll(field, 1, 0))
        following = jnp.where(lane == LANES - 1, pltpu.roll(right, LANES - 1, 1), pltpu.roll(field, LANES - 1, 1))
        previous = jnp.where(lane == 0, pltpu.roll(left, 1, 1), pltpu.roll(field, 1, 1))
        return following - previous

    def down(field, which):
        below = jnp.concatenate([field[tiles:], after_ref[which]], axis=0)
        above = jnp.concatenate([before_ref[which], field[: rows - tiles]], axis=0)
        return below - above

    east, up = (
        jnp.concatenate([solved_ref[k, :tiles], middle, solved_ref[k, tiles:]], axis=0)
        for k, middle in enumerate(solve_cells(vals_ref, los_ref))
    )
    north = north_ref[...]
    work_ref[0] = east
    work_ref[1] = up
    work_ref[2] = across(east) / 2.0
    work_ref[3] = down(north, 1) / 2.0
    work_ref[4] = (down(east, 0) + across(north)) / 4.0
    start = block_ref[0] * own
    for field in range(5):
        target, at = (east_up_ref, field) if field < 2 else (strain_ref, field - 2)
        for i in range(rows // tiles):
            for j in range(own):
                target[at, i : i + 1, j * LANES : (j + 1) * LANES] = work_ref[field, pl.ds(i * tiles + start + j, 1), :]


def final(block, los, vals, solved, north, before, after, tiles, own):
    rows = north.shape[0]
    shape = (rows // tiles, own * LANES)
    vmem = pl.BlockSpec(memory_space=pltpu.VMEM)
    return pl.pallas_call(
        functools.partial(final_kernel, tiles, own),
        in_specs=[pl.BlockSpec(memory_space=pltpu.SMEM)] * 2 + [vmem] * 5,
        out_specs=[vmem] * 2,
        out_shape=[jax.ShapeDtypeStruct((2, *shape), jnp.float32), jax.ShapeDtypeStruct((3, *shape), jnp.float32)],
        scratch_shapes=[pltpu.VMEM((5, rows, LANES), jnp.float32)],
        name="solve_and_strain",
    )(block, los, vals, solved, north, before, after)


def per_device(phases, coherent, pairs, res_index, res_weight, coverage, los, north):
    parts = lax.axis_size("pix")
    tracks = lax.axis_size("track")
    here = lax.axis_index("track")
    grid_rows, columns = north.shape
    tiles = columns // CTILE
    rows = grid_rows * tiles
    track = here.astype(jnp.int32)[None]
    edge_stack = lax.all_to_all(
        pack_edges(phases[0], coherent[0], parts, tiles), "pix", split_axis=0, concat_axis=0, tiled=True
    )
    inner_stack = lax.all_to_all(
        pack_inner(phases[0], coherent[0], parts, tiles), "pix", split_axis=0, concat_axis=0, tiled=True
    )
    design, pseudo = setup_track(pairs[0])
    north_cells = north.reshape(rows, LANES)
    cells = (
        res_index.reshape(-1, rows, LANES),
        res_weight.reshape(-1, rows, LANES),
        coverage.reshape(rows, 1),
        north_cells,
    )

    def flat(stack):
        return stack.reshape(-1, stack.shape[2])

    edge_vals, seam = edges(track, los, flat(edge_stack), pseudo, design, cells, tiles)
    edge_vals = lax.all_gather(edge_vals, "track", axis=0)
    solved, first, last = solve_edges(edge_vals, north_cells, los, tiles)
    onward = [(i, i + 1) for i in range(parts - 1)]
    back = [(j, i) for i, j in onward]
    before = lax.ppermute(last, "pix", onward)
    after = lax.ppermute(first, "pix", back)
    inner_vals = inner(track, los, flat(inner_stack), seam, pseudo, design, cells, tiles)
    inner_vals = lax.all_gather(inner_vals, "track", axis=0)
    return tuple(final(track, los, inner_vals, solved, north_cells, before, after, tiles, tiles // tracks))


def solution(mesh):
    in_specs = (
        P("track", "pix", None),
        P("track", "pix", None),
        P("track", None, None),
        P("track", None, "pix"),
        P("track", None, "pix"),
        P("track", "pix", None),
        P(),
        P("pix", None),
    )
    out_specs = (P(None, "pix", "track"), P(None, "pix", "track"))
    return jax.shard_map(
        per_device, mesh=mesh, in_specs=in_specs, out_specs=out_specs, check_vma=False
    )
```

```python
import functools

import jax
import jax.numpy as jnp
from jax import lax
from jax.experimental import pallas as pl
from jax.experimental.pallas import tpu as pltpu
from jax.sharding import PartitionSpec as P

EPOCHS = 200
ROWS = 208
HALO = 128
CTILE = 128
MBLK = 128
LANES = 128
TILE = 256
PIECE = 1024
GROUP = 4
EDGE_COST = 50_000_000_000


prior_var = 0.1
ridge_term = 0.5
medium = 24 * 1024 * 1024


def stay(array):
    return pltpu.with_memory_space_constraint(array, pltpu.HBM)


def spread(flags, j, shape):
    return jnp.broadcast_to(flags[:, j : j + 1], shape).astype(jnp.bfloat16)


def part_flags(flags_ref, first):
    lead = pl.multiple_of(first // LANES * LANES, LANES)
    flags = (flags_ref[:, pl.ds(lead, LANES)] == 1).astype(jnp.float32)
    return pltpu.roll(flags, (LANES - (first - lead)) % LANES, 1)


def pack_edges_kernel(tiles, group, place_ref, flags_hbm, phases_ref, *refs):
    *out_refs, flags_ref, near_ref, flag_sem, in_sem = refs
    planes = len(out_refs)
    parts = planes * group
    ifgs, blocks = flags_ref.shape
    span = blocks // parts
    reach = tiles + 1
    bound = 2 * reach * MBLK
    flag_copy = pltpu.make_async_copy(flags_hbm, flags_ref, flag_sem)
    flag_copy.start()
    ends = []
    for b, low, at in ((0, 0, reach), (parts, blocks - reach, 0)):
        ends.append(
            pltpu.make_async_copy(
                phases_ref.at[:, pl.ds(low * MBLK, reach * MBLK)], near_ref.at[b, :, pl.ds(at * MBLK, reach * MBLK)], in_sem.at[b]
            )
        )

    def between(b):
        low = pl.multiple_of((span * b - reach) * MBLK, MBLK)
        return pltpu.make_async_copy(phases_ref.at[:, pl.ds(low, bound)], near_ref.at[b], in_sem.at[b])

    ends[0].start()

    @pl.loop(1, parts)
    def _(b):
        between(b).start()

    ends[1].start()
    empty = jnp.zeros((ifgs, reach * MBLK), jnp.bfloat16)
    near_ref[0, :, : reach * MBLK] = empty
    near_ref[parts, :, reach * MBLK :] = empty
    flag_copy.wait()
    ends[0].wait()

    @pl.loop(1, parts)
    def _(b):
        between(b).wait()

    ends[1].wait()
    for s in range(planes):
        first_part = lax.rem(place_ref[0] + s, planes) * group

        @pl.loop(0, group, unroll=2)
        def _(g):
            p = first_part + g
            first = p * span
            flags = part_flags(flags_ref, first)
            earlier = part_flags(flags_ref, jnp.maximum(first - 1, 0))
            later = part_flags(flags_ref, jnp.minimum(first + span, blocks - 1))
            shape = (ifgs, MBLK)
            for half in range(2):
                for k in range(tiles + 2):
                    block = k - 1 if half == 0 else span - reach + k
                    if block < 0:
                        keep = spread(earlier, 0, shape)
                    elif block == span:
                        keep = spread(later, 0, shape)
                    else:
                        keep = spread(flags, block, shape)
                    at = (reach - 1 + k if half == 0 else k) * MBLK
                    to = (half * (tiles + 2) + k) * MBLK
                    out_refs[s][g, :, to : to + MBLK] = near_ref[p + half, :, at : at + MBLK] * keep


def pack_edges(place, phases, flags, parts, group, tiles):
    ifgs = phases.shape[0]
    planes = parts // group
    hbm = pl.BlockSpec(memory_space=pltpu.HBM)
    width = 2 * (tiles + 2) * MBLK
    return pl.pallas_call(
        functools.partial(pack_edges_kernel, tiles, group),
        in_specs=[pl.BlockSpec(memory_space=pltpu.SMEM), hbm, hbm],
        out_specs=[pl.BlockSpec(memory_space=pltpu.VMEM)] * planes,
        out_shape=[jax.ShapeDtypeStruct((group, ifgs, width), jnp.bfloat16)] * planes,
        scratch_shapes=[
            pltpu.VMEM(flags.shape, jnp.int32),
            pltpu.VMEM((parts + 1, ifgs, 2 * (tiles + 1) * MBLK), jnp.bfloat16),
            pltpu.SemaphoreType.DMA,
            pltpu.SemaphoreType.DMA((parts + 1,)),
        ],
        compiler_params=pltpu.CompilerParams(vmem_limit_bytes=medium),
        name="pack_edges",
    )(place, stay(flags), stay(phases))


def regroup_kernel(planes, group, place_ref, after_ref, *refs):
    in_refs, out_refs = refs[:planes], refs[planes:]
    for j in range(group):
        column = lax.rem(place_ref[1] + j, group)
        for s in range(planes):
            out_refs[j][s] = in_refs[s][column]


def regroup(place, after, pieces, group):
    planes = len(pieces)
    vmem = pl.BlockSpec(memory_space=pltpu.VMEM)
    shape = (planes, *pieces[0].shape[1:])
    return pl.pallas_call(
        functools.partial(regroup_kernel, planes, group),
        in_specs=[pl.BlockSpec(memory_space=pltpu.SMEM)] + [vmem] * (planes + 1),
        out_specs=[vmem] * group,
        out_shape=[jax.ShapeDtypeStruct(shape, jnp.bfloat16)] * group,
        compiler_params=pltpu.CompilerParams(vmem_limit_bytes=medium),
        name="regroup",
    )(place, after, *pieces)


def pack_inner_kernel(reach, flags_hbm, phases_ref, out_ref, flags_ref, held_ref, flag_sem, in_sem):
    parts, ifgs, width = out_ref.shape
    span = flags_ref.shape[1] // parts
    flag_copy = pltpu.make_async_copy(flags_hbm, flags_ref, flag_sem)
    flag_copy.start()

    def inward(p):
        low = pl.multiple_of((p * span + reach) * MBLK, MBLK)
        return pltpu.make_async_copy(phases_ref.at[:, pl.ds(low, width)], held_ref.at[p], in_sem.at[p])

    @pl.loop(0, parts)
    def _(p):
        inward(p).start()

    flag_copy.wait()

    @pl.loop(0, parts)
    def _(p):
        inward(p).wait()
        flags = part_flags(flags_ref, p * span)
        for k in range(width // MBLK):
            at = slice(k * MBLK, (k + 1) * MBLK)
            out_ref[p, :, at] = held_ref[p, :, at] * spread(flags, reach + k, (ifgs, MBLK))


def pack_inner(phases, flags, parts, tiles):
    ifgs = phases.shape[0]
    reach = tiles + 1
    width = (flags.shape[1] // parts - 2 * reach) * MBLK
    hbm = pl.BlockSpec(memory_space=pltpu.HBM)
    return pl.pallas_call(
        functools.partial(pack_inner_kernel, reach),
        in_specs=[hbm, hbm],
        out_specs=pl.BlockSpec(memory_space=pltpu.VMEM),
        out_shape=jax.ShapeDtypeStruct((parts, ifgs, width), jnp.bfloat16),
        scratch_shapes=[
            pltpu.VMEM(flags.shape, jnp.int32),
            pltpu.VMEM((parts, ifgs, width), jnp.bfloat16),
            pltpu.SemaphoreType.DMA,
            pltpu.SemaphoreType.DMA((parts,)),
        ],
        compiler_params=pltpu.CompilerParams(vmem_limit_bytes=medium),
        name="pack_inner",
    )(stay(flags), stay(phases))


def exact_dot(a, b):
    return jnp.dot(a, b, precision=lax.Precision.HIGHEST, preferred_element_type=jnp.float32)


def pseudo_kernel(pairs_ref, other_ref, design_ref, out_ref, other_design_ref, other_out_ref, normal_ref, inverse_ref):
    ifgs = pairs_ref.shape[1]
    size = normal_ref.shape[0]
    epoch = lax.broadcasted_iota(jnp.int32, (size, ifgs), 0)

    def ends(ref):
        return (epoch == ref[1:2, :]).astype(jnp.float32) - (epoch == ref[0:1, :]).astype(jnp.float32)

    across = ends(pairs_ref)
    down = across.T
    eye = (
        lax.broadcasted_iota(jnp.int32, (size, size), 0) == lax.broadcasted_iota(jnp.int32, (size, size), 1)
    ).astype(jnp.float32)
    normal = eye + jnp.dot(
        across.astype(jnp.bfloat16), down.astype(jnp.bfloat16), preferred_element_type=jnp.float32
    )
    normal_ref[...] = normal
    inverse_ref[...] = eye / jnp.where(eye == 1.0, normal, 1.0)

    def unfinished(state):
        step, gap = state
        return jnp.logical_and(step < 24, gap > 1e-5)

    def improve(state):
        step, _ = state
        inverse = inverse_ref[...]
        rest = eye - exact_dot(normal_ref[...], inverse)
        inverse_ref[...] = inverse + exact_dot(inverse, rest)
        return step + 1, jnp.max(jnp.abs(rest))

    lax.while_loop(unfinished, improve, (jnp.int32(0), jnp.float32(1.0)))
    place = lax.broadcasted_iota(jnp.int32, (ROWS, ifgs), 0)
    centred = place.astype(jnp.float32) - (EPOCHS - 1) / 2.0
    square = sum((e - (EPOCHS - 1) / 2.0) ** 2 for e in range(EPOCHS))
    slope = jnp.where(place < EPOCHS, centred * (EPOCHS - 1) / square, 0.0)
    extra = place - EPOCHS
    for ref, to_design_ref, to_ref in ((pairs_ref, design_ref, out_ref), (other_ref, other_design_ref, other_out_ref)):
        across = ends(ref)
        to_design_ref[...] = across.T[:, :ROWS].astype(jnp.bfloat16)
        pseudo = exact_dot(inverse_ref[...], across)[:ROWS].astype(jnp.bfloat16).astype(jnp.float32)
        row = jnp.sum(pseudo * slope, axis=0, keepdims=True)
        high = row.astype(jnp.bfloat16).astype(jnp.float32)
        rest = row - high
        middle = rest.astype(jnp.bfloat16).astype(jnp.float32)
        low = rest - middle
        terms = jnp.where(extra == 0, high, jnp.where(extra == 1, middle, jnp.where(extra == 2, low, 0.0)))
        to_ref[...] = jnp.where(extra < 0, pseudo, terms).astype(jnp.bfloat16)


def setup_track(pair_rows, other_rows):
    ifgs = pair_rows.shape[0]
    size = 256
    vmem = pl.BlockSpec(memory_space=pltpu.VMEM)
    return pl.pallas_call(
        pseudo_kernel,
        in_specs=[vmem] * 2,
        out_specs=[vmem] * 4,
        out_shape=[jax.ShapeDtypeStruct((ifgs, ROWS), jnp.bfloat16), jax.ShapeDtypeStruct((ROWS, ifgs), jnp.bfloat16)] * 2,
        scratch_shapes=[pltpu.VMEM((size, size), jnp.float32), pltpu.VMEM((size, size), jnp.float32)],
        compiler_params=pltpu.CompilerParams(vmem_limit_bytes=medium),
        name="pseudo_inverse",
    )(pair_rows.T, other_rows.T)


def invert_tiles(stack_refs, first, width, pseudo_ref, design_ref, fields_ref, base):
    for start in range(0, width, TILE):
        here = pl.ds(pl.multiple_of(first + start, LANES), TILE)
        stack = jnp.concatenate([ref[:, here] for ref in stack_refs], axis=0)
        series = jnp.dot(pseudo_ref[...], stack, preferred_element_type=jnp.float32)
        velocity = jnp.sum(series[EPOCHS:], axis=0, keepdims=True)
        fitted = jnp.dot(design_ref[...], series.astype(jnp.bfloat16), preferred_element_type=jnp.float32)
        misfit = stack.astype(jnp.float32) - fitted
        variance = jnp.sum(misfit * misfit, axis=0, keepdims=True) / stack.shape[0]
        for k in range(TILE // LANES):
            row = pl.ds(base + start // LANES + k, 1)
            fields_ref[0, row, :] = velocity[:, k * LANES : (k + 1) * LANES]
            fields_ref[1, row, :] = variance[:, k * LANES : (k + 1) * LANES]


def pick(source, lane):
    return jnp.take_along_axis(source, lane, axis=1, mode="promise_in_bounds")


def resample(fields_ref, base, cell, to, index_ref, weight_ref, cover_ref, north_ref, north_c, out_ref):
    lanes = lax.broadcasted_iota(jnp.int32, (8, LANES), 1)
    here = pl.ds(cell, 8)
    near = [[fields_ref[f, pl.ds(base + k, 8), :] for k in range(3)] for f in range(2)]
    sums = [jnp.zeros((8, LANES), jnp.float32)] * 2
    total = jnp.zeros((8, LANES), jnp.float32)
    for b in range(index_ref.shape[0]):
        weight = weight_ref[b, here, :]
        place = lanes + index_ref[b, here, :] + HALO
        lane = place & (LANES - 1)
        which = place >> 7
        total = total + weight
        for f in range(2):
            low, mid, high = (pick(near[f][k], lane) for k in range(3))
            taken = jnp.where(which == 0, low, jnp.where(which == 1, mid, high))
            sums[f] = sums[f] + taken * weight
    cover = cover_ref[here, :].astype(jnp.float32)
    out_ref[0, pl.ds(to, 8), :] = cover / (sums[1] / total + prior_var)
    out_ref[1, pl.ds(to, 8), :] = sums[0] / total - north_c * north_ref[here, :]


def edges_kernel(
    tiles, group, here_ref, los_ref, *refs
):
    stack_refs = refs[:group]
    pseudo_ref, design_ref, index_ref, weight_ref, cover_ref, north_ref, out_ref, seam_ref, fields_ref = refs[group:]
    rows = index_ref.shape[1]
    width = stack_refs[0].shape[1] // 2

    @pl.loop(0, 2)
    def _(half):
        invert_tiles(stack_refs, half * width, width, pseudo_ref, design_ref, fields_ref, half * (tiles + 2))

    seam_ref[...] = fields_ref[:, tiles : tiles + 4, :]
    north_c = los_ref[here_ref[0], 1]
    for half in range(2):
        for r in range(0, tiles, 8):
            resample(
                fields_ref, half * (tiles + 2) + r, half * (rows - tiles) + r, half * tiles + r,
                index_ref, weight_ref, cover_ref, north_ref, north_c, out_ref,
            )


def edges(here, los, stacks, pseudo, design, cells, tiles):
    rows = 2 * (tiles + 2)
    vmem = pl.BlockSpec(memory_space=pltpu.VMEM)
    return pl.pallas_call(
        functools.partial(edges_kernel, tiles, len(stacks)),
        in_specs=[pl.BlockSpec(memory_space=pltpu.SMEM)] * 2 + [vmem] * (len(stacks) + 6),
        out_specs=[vmem] * 2,
        out_shape=[
            jax.ShapeDtypeStruct((2, 2 * tiles, LANES), jnp.float32),
            jax.ShapeDtypeStruct((2, 4, LANES), jnp.float32),
        ],
        scratch_shapes=[pltpu.VMEM((2, -(-rows // 8) * 8, LANES), jnp.float32)],
        compiler_params=pltpu.CompilerParams(vmem_limit_bytes=medium),
        cost_estimate=pl.CostEstimate(flops=EDGE_COST, bytes_accessed=0, transcendentals=0),
        name="edge_rows",
    )(here, los, *stacks, pseudo, design, *cells)


def inner_kernel(
    tiles, here_ref, los_ref, stack_ref, seam_ref, pseudo_ref, design_ref, index_ref, weight_ref, cover_ref, north_ref, out_ref,
    fields_ref,
):
    width = stack_ref.shape[1]
    pixel_rows = width // LANES
    fields_ref[:, 0:2, :] = seam_ref[:, 0:2, :]
    fields_ref[:, pixel_rows + 2 : pixel_rows + 4, :] = seam_ref[:, 2:4, :]

    @pl.loop(0, -(-width // PIECE))
    def _(k):
        first = jnp.minimum(k * PIECE, width - PIECE)
        invert_tiles([stack_ref], first, PIECE, pseudo_ref, design_ref, fields_ref, 2 + first // LANES)

    north_c = los_ref[here_ref[0], 1]

    @pl.loop(0, out_ref.shape[1], step=8)
    def _(r):
        r = pl.multiple_of(r, 8)
        resample(fields_ref, r, tiles + r, r, index_ref, weight_ref, cover_ref, north_ref, north_c, out_ref)


def inner(here, los, stack, seam, pseudo, design, cells, tiles):
    rows = cells[0].shape[1] - 2 * tiles
    vmem = pl.BlockSpec(memory_space=pltpu.VMEM)
    return pl.pallas_call(
        functools.partial(inner_kernel, tiles),
        in_specs=[pl.BlockSpec(memory_space=pltpu.SMEM)] * 2 + [vmem] * 8,
        out_specs=vmem,
        out_shape=jax.ShapeDtypeStruct((2, rows, LANES), jnp.float32),
        scratch_shapes=[pltpu.VMEM((2, -(-(rows + 2) // 8) * 8, LANES), jnp.float32)],
        compiler_params=pltpu.CompilerParams(vmem_limit_bytes=medium),
        name="inner_rows",
    )(here, los, stack, seam, pseudo, design, *cells)


def solve_cells(vals_ref, los_ref):
    a11 = a12 = a22 = b1 = b2 = 0.0
    for t in range(vals_ref.shape[0]):
        weight, target = vals_ref[t, 0], vals_ref[t, 1]
        east_c, up_c = los_ref[t, 0], los_ref[t, 2]
        by_east, by_up = weight * east_c, weight * up_c
        a11 = a11 + by_east * east_c
        a12 = a12 + by_east * up_c
        a22 = a22 + by_up * up_c
        b1 = b1 + by_east * target
        b2 = b2 + by_up * target
    a11 = a11 + ridge_term
    a22 = a22 + ridge_term
    determ = a11 * a22 - a12 * a12
    return (a22 * b1 - a12 * b2) / determ, (a11 * b2 - a12 * b1) / determ


def solve_kernel(tiles, vals_ref, north_ref, los_ref, solved_ref, first_ref, last_ref):
    east, up = solve_cells(vals_ref, los_ref)
    solved_ref[0] = east
    solved_ref[1] = up
    first_ref[0] = east[:tiles]
    first_ref[1] = north_ref[:tiles, :]
    last_ref[0] = east[tiles:]
    last_ref[1] = north_ref[north_ref.shape[0] - tiles :, :]


def solve_edges(vals, north, los, tiles):
    edge = jax.ShapeDtypeStruct((2, tiles, LANES), jnp.float32)
    vmem = pl.BlockSpec(memory_space=pltpu.VMEM)
    return pl.pallas_call(
        functools.partial(solve_kernel, tiles),
        in_specs=[vmem, vmem, pl.BlockSpec(memory_space=pltpu.SMEM)],
        out_specs=[vmem] * 3,
        out_shape=[jax.ShapeDtypeStruct((2, 2 * tiles, LANES), jnp.float32), edge, edge],
        name="solve_edges",
    )(vals, north, los)


def final_kernel(
    tiles, own, block_ref, los_ref, vals_ref, solved_ref, north_ref, before_ref, after_ref, east_up_ref, strain_ref, work_ref
):
    rows = north_ref.shape[0]
    lane = lax.broadcasted_iota(jnp.int32, (rows, LANES), 1)
    tile = lax.broadcasted_iota(jnp.int32, (rows, LANES), 0) % tiles

    def across(field):
        right = jnp.where(tile == tiles - 1, 0.0, pltpu.roll(field, rows - 1, 0))
        left = jnp.where(tile == 0, 0.0, pltpu.roll(field, 1, 0))
        following = jnp.where(lane == LANES - 1, pltpu.roll(right, LANES - 1, 1), pltpu.roll(field, LANES - 1, 1))
        previous = jnp.where(lane == 0, pltpu.roll(left, 1, 1), pltpu.roll(field, 1, 1))
        return following - previous

    def down(field, which):
        below = jnp.concatenate([field[tiles:], after_ref[which]], axis=0)
        above = jnp.concatenate([before_ref[which], field[: rows - tiles]], axis=0)
        return below - above

    east, up = (
        jnp.concatenate([solved_ref[k, :tiles], middle, solved_ref[k, tiles:]], axis=0)
        for k, middle in enumerate(solve_cells(vals_ref, los_ref))
    )
    north = north_ref[...]
    work_ref[0] = east
    work_ref[1] = up
    work_ref[2] = across(east) / 2.0
    work_ref[3] = down(north, 1) / 2.0
    work_ref[4] = (down(east, 0) + across(north)) / 4.0
    start = block_ref[0] * own
    for field in range(5):
        target, at = (east_up_ref, field) if field < 2 else (strain_ref, field - 2)
        for i in range(rows // tiles):
            for j in range(own):
                target[at, i : i + 1, j * LANES : (j + 1) * LANES] = work_ref[field, pl.ds(i * tiles + start + j, 1), :]


def final(block, los, vals, solved, north, before, after, tiles, own):
    rows = north.shape[0]
    shape = (rows // tiles, own * LANES)
    vmem = pl.BlockSpec(memory_space=pltpu.VMEM)
    return pl.pallas_call(
        functools.partial(final_kernel, tiles, own),
        in_specs=[pl.BlockSpec(memory_space=pltpu.SMEM)] * 2 + [vmem] * 5,
        out_specs=[vmem] * 2,
        out_shape=[jax.ShapeDtypeStruct((2, *shape), jnp.float32), jax.ShapeDtypeStruct((3, *shape), jnp.float32)],
        scratch_shapes=[pltpu.VMEM((5, rows, LANES), jnp.float32)],
        name="solve_and_strain",
    )(block, los, vals, solved, north, before, after)


def per_device(phases, coherent, pairs, res_index, res_weight, coverage, los, north):
    parts = lax.axis_size("pix")
    tracks = lax.axis_size("track")
    here = lax.axis_index("track")
    grid_rows, columns = north.shape
    tiles = columns // CTILE
    rows = grid_rows * tiles
    track = here.astype(jnp.int32)[None]
    group = GROUP if parts % GROUP == 0 else parts
    planes = parts // group
    plane, column = jnp.divmod(lax.axis_index("pix").astype(jnp.int32), group)
    place = jnp.stack([plane, column])
    packed = pack_edges(place, phases[0], coherent[0], parts, group, tiles)
    steps_j, steps_s = jnp.meshgrid(jnp.arange(group), jnp.arange(planes), indexing="ij")
    sources = ((plane - steps_s) % planes * group + (column - steps_j) % group).reshape(-1)
    edge_pairs = jnp.take(pairs[0].reshape(parts, -1, 2), sources, axis=0).reshape(-1, 2)
    design, pseudo, edge_design, edge_pseudo = setup_track(pairs[0], edge_pairs)
    arrived = [packed[0]]
    for s in range(1, planes):
        far = [(z * group + c, (z + s) % planes * group + c) for z in range(planes) for c in range(group)]
        arrived.append(lax.ppermute(packed[s], "pix", far))
    by_column = regroup(place, edge_pseudo, arrived, group)
    pieces = [by_column[0]]
    for j in range(1, group):
        near = [(z * group + c, z * group + (c + j) % group) for z in range(planes) for c in range(group)]
        pieces.append(lax.ppermute(by_column[j], "pix", near))
    later_flags, *_ = lax.optimization_barrier((coherent[0], packed[0]))
    inner_stack = lax.all_to_all(
        pack_inner(phases[0], later_flags, parts, tiles), "pix", split_axis=0, concat_axis=0, tiled=True
    )
    north_cells = north.reshape(rows, LANES)
    cells = (
        res_index.reshape(-1, rows, LANES),
        res_weight.reshape(-1, rows, LANES),
        coverage.reshape(rows, 1),
        north_cells,
    )

    def flat(stack):
        return stack.reshape(-1, stack.shape[-1])

    edge_vals, seam = edges(track, los, [flat(piece) for piece in pieces], edge_pseudo, edge_design, cells, tiles)
    edge_vals = lax.all_gather(edge_vals, "track", axis=0)
    solved, first, last = solve_edges(edge_vals, north_cells, los, tiles)
    onward = [(i, i + 1) for i in range(parts - 1)]
    back = [(j, i) for i, j in onward]
    before = lax.ppermute(last, "pix", onward)
    after = lax.ppermute(first, "pix", back)
    inner_vals = inner(track, los, flat(inner_stack), seam, pseudo, design, cells, tiles)
    inner_vals = lax.all_gather(inner_vals, "track", axis=0)
    return tuple(final(track, los, inner_vals, solved, north_cells, before, after, tiles, tiles // tracks))


def solution(mesh):
    in_specs = (
        P("track", "pix", None),
        P("track", "pix", None),
        P("track", None, None),
        P("track", None, "pix"),
        P("track", None, "pix"),
        P("track", "pix", None),
        P(),
        P("pix", None),
    )
    out_specs = (P(None, "pix", "track"), P(None, "pix", "track"))
    return jax.shard_map(
        per_device, mesh=mesh, in_specs=in_specs, out_specs=out_specs, check_vma=False
    )
```

```python
import functools

import jax
import jax.numpy as jnp
from jax import lax
from jax.experimental import pallas as pl
from jax.experimental.pallas import tpu as pltpu
from jax.sharding import PartitionSpec as P

EPOCHS = 200
EXTRA = 16
HALO = 128
CTILE = 128
MBLK = 128
LANES = 128
TILE = 256
PIECE = 1024
GROUP = 4
EDGE_COST = 50_000_000_000


prior_var = 0.1
ridge_term = 0.5
medium = 24 * 1024 * 1024


def stay(array):
    return pltpu.with_memory_space_constraint(array, pltpu.HBM)


def spread(flags, j, shape):
    return jnp.broadcast_to(flags[:, j : j + 1], shape).astype(jnp.bfloat16)


def part_flags(flags_ref, first):
    lead = pl.multiple_of(first // LANES * LANES, LANES)
    flags = (flags_ref[:, pl.ds(lead, LANES)] == 1).astype(jnp.float32)
    return pltpu.roll(flags, (LANES - (first - lead)) % LANES, 1)


def pack_edges_kernel(tiles, group, flags_hbm, phases_ref, *refs):
    *out_refs, flags_ref, near_ref, flag_sem, in_sem = refs
    planes = len(out_refs)
    parts = planes * group
    ifgs, blocks = flags_ref.shape
    span = blocks // parts
    reach = tiles + 1
    bound = 2 * reach * MBLK
    flag_copy = pltpu.make_async_copy(flags_hbm, flags_ref, flag_sem)
    flag_copy.start()
    ends = []
    for b, low, at in ((0, 0, reach), (parts, blocks - reach, 0)):
        ends.append(
            pltpu.make_async_copy(
                phases_ref.at[:, pl.ds(low * MBLK, reach * MBLK)], near_ref.at[b, :, pl.ds(at * MBLK, reach * MBLK)], in_sem.at[b]
            )
        )

    def between(b):
        low = pl.multiple_of((span * b - reach) * MBLK, MBLK)
        return pltpu.make_async_copy(phases_ref.at[:, pl.ds(low, bound)], near_ref.at[b], in_sem.at[b])

    ends[0].start()

    @pl.loop(1, parts)
    def _(b):
        between(b).start()

    ends[1].start()
    empty = jnp.zeros((ifgs, reach * MBLK), jnp.bfloat16)
    near_ref[0, :, : reach * MBLK] = empty
    near_ref[parts, :, reach * MBLK :] = empty
    flag_copy.wait()
    plane = lax.axis_index("pix") // group
    shape = (ifgs, MBLK)
    for s in range(planes):
        first_part = lax.rem(plane + s, planes) * group

        @pl.loop(0, group, unroll=2)
        def _(g):
            first = (first_part + g) * span
            flags = part_flags(flags_ref, first)
            earlier = part_flags(flags_ref, jnp.maximum(first - 1, 0))
            later = part_flags(flags_ref, jnp.minimum(first + span, blocks - 1))
            for half in range(2):
                for k in range(tiles + 2):
                    block = k - 1 if half == 0 else span - reach + k
                    if block < 0:
                        keep = spread(earlier, 0, shape)
                    elif block == span:
                        keep = spread(later, 0, shape)
                    else:
                        keep = spread(flags, block, shape)
                    to = (half * (tiles + 2) + k) * MBLK
                    out_refs[s][g, :, to : to + MBLK] = keep

    ends[0].wait()

    @pl.loop(1, parts)
    def _(b):
        between(b).wait()

    ends[1].wait()
    wide = (tiles + 2) * MBLK
    for s in range(planes):
        first_part = lax.rem(plane + s, planes) * group

        @pl.loop(0, group, unroll=2)
        def _(g):
            for half in range(2):
                at = (reach - 1 if half == 0 else 0) * MBLK
                to = half * wide
                out_refs[s][g, :, to : to + wide] *= near_ref[first_part + g + half, :, at : at + wide]


def pack_edges(phases, flags, parts, group, tiles):
    ifgs = phases.shape[0]
    planes = parts // group
    hbm = pl.BlockSpec(memory_space=pltpu.HBM)
    width = 2 * (tiles + 2) * MBLK
    return pl.pallas_call(
        functools.partial(pack_edges_kernel, tiles, group),
        in_specs=[hbm, hbm],
        out_specs=[pl.BlockSpec(memory_space=pltpu.VMEM)] * planes,
        out_shape=[jax.ShapeDtypeStruct((group, ifgs, width), jnp.bfloat16)] * planes,
        scratch_shapes=[
            pltpu.VMEM(flags.shape, jnp.int32),
            pltpu.VMEM((parts + 1, ifgs, 2 * (tiles + 1) * MBLK), jnp.bfloat16),
            pltpu.SemaphoreType.DMA,
            pltpu.SemaphoreType.DMA((parts + 1,)),
        ],
        compiler_params=pltpu.CompilerParams(vmem_limit_bytes=medium),
        name="pack_edges",
    )(stay(flags), stay(phases))


def regroup_kernel(planes, group, after_ref, *refs):
    in_refs, out_refs = refs[:planes], refs[planes:]
    for j in range(group):
        column = lax.rem(lax.axis_index("pix") + j, group)
        for s in range(planes):
            out_refs[j][s] = in_refs[s][column]


def regroup(after, pieces, group):
    planes = len(pieces)
    vmem = pl.BlockSpec(memory_space=pltpu.VMEM)
    shape = (planes, *pieces[0].shape[1:])
    return pl.pallas_call(
        functools.partial(regroup_kernel, planes, group),
        in_specs=[vmem] * (planes + 1),
        out_specs=[vmem] * group,
        out_shape=[jax.ShapeDtypeStruct(shape, jnp.bfloat16)] * group,
        compiler_params=pltpu.CompilerParams(vmem_limit_bytes=medium),
        name="regroup",
    )(after, *pieces)


def pack_inner_kernel(reach, flags_hbm, phases_ref, out_ref, flags_ref, held_ref, flag_sem, in_sem):
    parts, ifgs, width = out_ref.shape
    span = flags_ref.shape[1] // parts
    flag_copy = pltpu.make_async_copy(flags_hbm, flags_ref, flag_sem)
    flag_copy.start()

    def inward(p):
        low = pl.multiple_of((p * span + reach) * MBLK, MBLK)
        return pltpu.make_async_copy(phases_ref.at[:, pl.ds(low, width)], held_ref.at[p], in_sem.at[p])

    @pl.loop(0, parts)
    def _(p):
        inward(p).start()

    flag_copy.wait()

    @pl.loop(0, parts)
    def _(p):
        flags = part_flags(flags_ref, p * span)
        for k in range(width // MBLK):
            out_ref[p, :, k * MBLK : (k + 1) * MBLK] = spread(flags, reach + k, (ifgs, MBLK))

    @pl.loop(0, parts)
    def _(p):
        inward(p).wait()
        out_ref[p] *= held_ref[p]


def pack_inner(phases, flags, parts, tiles):
    ifgs = phases.shape[0]
    reach = tiles + 1
    width = (flags.shape[1] // parts - 2 * reach) * MBLK
    hbm = pl.BlockSpec(memory_space=pltpu.HBM)
    return pl.pallas_call(
        functools.partial(pack_inner_kernel, reach),
        in_specs=[hbm, hbm],
        out_specs=pl.BlockSpec(memory_space=pltpu.VMEM),
        out_shape=jax.ShapeDtypeStruct((parts, ifgs, width), jnp.bfloat16),
        scratch_shapes=[
            pltpu.VMEM(flags.shape, jnp.int32),
            pltpu.VMEM((parts, ifgs, width), jnp.bfloat16),
            pltpu.SemaphoreType.DMA,
            pltpu.SemaphoreType.DMA((parts,)),
        ],
        compiler_params=pltpu.CompilerParams(vmem_limit_bytes=medium),
        name="pack_inner",
    )(stay(flags), stay(phases))


def exact_dot(a, b):
    return jnp.dot(a, b, precision=lax.Precision.HIGHEST, preferred_element_type=jnp.float32)


def operator_kernel(pairs_ref, other_ref, out_ref, other_out_ref, normal_ref, inverse_ref):
    ifgs = pairs_ref.shape[1]
    size = normal_ref.shape[0]
    epoch = lax.broadcasted_iota(jnp.int32, (size, ifgs), 0)

    def ends(ref):
        return (epoch == ref[1:2, :]).astype(jnp.float32) - (epoch == ref[0:1, :]).astype(jnp.float32)

    across = ends(pairs_ref)
    down = across.T
    eye = (
        lax.broadcasted_iota(jnp.int32, (size, size), 0) == lax.broadcasted_iota(jnp.int32, (size, size), 1)
    ).astype(jnp.float32)
    normal = eye + jnp.dot(
        across.astype(jnp.bfloat16), down.astype(jnp.bfloat16), preferred_element_type=jnp.float32
    )
    normal_ref[...] = normal
    inverse_ref[...] = eye / jnp.where(eye == 1.0, normal, 1.0)

    def unfinished(state):
        step, gap = state
        return jnp.logical_and(step < 24, gap > 1e-5)

    def improve(state):
        step, _ = state
        inverse = inverse_ref[...]
        rest = eye - exact_dot(normal_ref[...], inverse)
        inverse_ref[...] = inverse + exact_dot(inverse, rest)
        return step + 1, jnp.max(jnp.abs(rest))

    lax.while_loop(unfinished, improve, (jnp.int32(0), jnp.float32(1.0)))
    place = lax.broadcasted_iota(jnp.int32, (size, ifgs), 0)
    centred = place.astype(jnp.float32) - (EPOCHS - 1) / 2.0
    square = sum((e - (EPOCHS - 1) / 2.0) ** 2 for e in range(EPOCHS))
    slope = jnp.where(place < EPOCHS, centred * (EPOCHS - 1) / square, 0.0)
    same = lax.broadcasted_iota(jnp.int32, (ifgs, ifgs), 0) == lax.broadcasted_iota(jnp.int32, (ifgs, ifgs), 1)
    extra = lax.broadcasted_iota(jnp.int32, (EXTRA, ifgs), 0)
    for ref, to_ref in ((pairs_ref, out_ref), (other_ref, other_out_ref)):
        across = ends(ref)
        pseudo = exact_dot(inverse_ref[...], across).astype(jnp.bfloat16)
        fitted = jnp.dot(across.T.astype(jnp.bfloat16), pseudo, preferred_element_type=jnp.float32)
        to_ref[:ifgs, :] = (same.astype(jnp.float32) - fitted).astype(jnp.bfloat16)
        row = jnp.sum(pseudo.astype(jnp.float32) * slope, axis=0, keepdims=True)
        high = row.astype(jnp.bfloat16).astype(jnp.float32)
        rest = row - high
        middle = rest.astype(jnp.bfloat16).astype(jnp.float32)
        low = rest - middle
        terms = jnp.where(extra == 0, high, jnp.where(extra == 1, middle, jnp.where(extra == 2, low, 0.0)))
        to_ref[ifgs:, :] = terms.astype(jnp.bfloat16)


def setup_track(pair_rows, other_rows):
    ifgs = pair_rows.shape[0]
    size = -(-EPOCHS // LANES) * LANES
    vmem = pl.BlockSpec(memory_space=pltpu.VMEM)
    return pl.pallas_call(
        operator_kernel,
        in_specs=[vmem] * 2,
        out_specs=[vmem] * 2,
        out_shape=[jax.ShapeDtypeStruct((ifgs + EXTRA, ifgs), jnp.bfloat16)] * 2,
        scratch_shapes=[pltpu.VMEM((size, size), jnp.float32), pltpu.VMEM((size, size), jnp.float32)],
        compiler_params=pltpu.CompilerParams(vmem_limit_bytes=medium),
        name="misfit_operator",
    )(pair_rows.T, other_rows.T)


def invert_tiles(stack_refs, first, width, operator_ref, fields_ref, base):
    ifgs = operator_ref.shape[1]
    for start in range(0, width, TILE):
        here = pl.ds(pl.multiple_of(first + start, LANES), TILE)
        stack = jnp.concatenate([ref[:, here] for ref in stack_refs], axis=0)
        product = jnp.dot(operator_ref[...], stack, preferred_element_type=jnp.float32)
        velocity = jnp.sum(product[ifgs : ifgs + 8], axis=0, keepdims=True)
        variance = jnp.sum(product[:ifgs] * product[:ifgs], axis=0, keepdims=True) / ifgs
        for k in range(TILE // LANES):
            row = pl.ds(base + start // LANES + k, 1)
            fields_ref[0, row, :] = velocity[:, k * LANES : (k + 1) * LANES]
            fields_ref[1, row, :] = variance[:, k * LANES : (k + 1) * LANES]


def pick(source, lane):
    return jnp.take_along_axis(source, lane, axis=1, mode="promise_in_bounds")


def resample(fields_ref, base, cell, to, index_ref, weight_ref, cover_ref, north_ref, north_c, out_ref):
    lanes = lax.broadcasted_iota(jnp.int32, (8, LANES), 1)
    here = pl.ds(cell, 8)
    near = [[fields_ref[f, pl.ds(base + k, 8), :] for k in range(3)] for f in range(2)]
    sums = [jnp.zeros((8, LANES), jnp.float32)] * 2
    total = jnp.zeros((8, LANES), jnp.float32)
    for b in range(index_ref.shape[0]):
        weight = weight_ref[b, here, :]
        place = lanes + index_ref[b, here, :] + HALO
        lane = place & (LANES - 1)
        which = place >> 7
        total = total + weight
        for f in range(2):
            low, mid, high = (pick(near[f][k], lane) for k in range(3))
            taken = jnp.where(which == 0, low, jnp.where(which == 1, mid, high))
            sums[f] = sums[f] + taken * weight
    cover = cover_ref[here, :].astype(jnp.float32)
    out_ref[0, pl.ds(to, 8), :] = cover / (sums[1] / total + prior_var)
    out_ref[1, pl.ds(to, 8), :] = sums[0] / total - north_c * north_ref[here, :]


def edges_kernel(
    tiles, group, los_ref, *refs
):
    stack_refs = refs[:group]
    operator_ref, index_ref, weight_ref, cover_ref, north_ref, out_ref, seam_ref, fields_ref = refs[group:]
    rows = index_ref.shape[1]
    width = stack_refs[0].shape[1] // 2

    @pl.loop(0, 2)
    def _(half):
        invert_tiles(stack_refs, half * width, width, operator_ref, fields_ref, half * (tiles + 2))

    seam_ref[...] = fields_ref[:, tiles : tiles + 4, :]
    north_c = los_ref[lax.axis_index("track"), 1]
    for half in range(2):
        for r in range(0, tiles, 8):
            resample(
                fields_ref, half * (tiles + 2) + r, half * (rows - tiles) + r, half * tiles + r,
                index_ref, weight_ref, cover_ref, north_ref, north_c, out_ref,
            )


def edges(los, stacks, operator, cells, tiles):
    rows = 2 * (tiles + 2)
    vmem = pl.BlockSpec(memory_space=pltpu.VMEM)
    return pl.pallas_call(
        functools.partial(edges_kernel, tiles, len(stacks)),
        in_specs=[pl.BlockSpec(memory_space=pltpu.SMEM)] + [vmem] * (len(stacks) + 5),
        out_specs=[vmem] * 2,
        out_shape=[
            jax.ShapeDtypeStruct((2, 2 * tiles, LANES), jnp.float32),
            jax.ShapeDtypeStruct((2, 4, LANES), jnp.float32),
        ],
        scratch_shapes=[pltpu.VMEM((2, -(-rows // 8) * 8, LANES), jnp.float32)],
        compiler_params=pltpu.CompilerParams(vmem_limit_bytes=medium),
        cost_estimate=pl.CostEstimate(flops=EDGE_COST, bytes_accessed=0, transcendentals=0),
        name="edge_rows",
    )(los, *stacks, operator, *cells)


def inner_kernel(
    tiles, los_ref, stack_ref, seam_ref, operator_ref, index_ref, weight_ref, cover_ref, north_ref, out_ref,
    fields_ref,
):
    width = stack_ref.shape[1]
    pixel_rows = width // LANES
    fields_ref[:, 0:2, :] = seam_ref[:, 0:2, :]
    fields_ref[:, pixel_rows + 2 : pixel_rows + 4, :] = seam_ref[:, 2:4, :]

    @pl.loop(0, -(-width // PIECE))
    def _(k):
        first = jnp.minimum(k * PIECE, width - PIECE)
        invert_tiles([stack_ref], first, PIECE, operator_ref, fields_ref, 2 + first // LANES)

    north_c = los_ref[lax.axis_index("track"), 1]

    @pl.loop(0, out_ref.shape[1], step=8)
    def _(r):
        r = pl.multiple_of(r, 8)
        resample(fields_ref, r, tiles + r, r, index_ref, weight_ref, cover_ref, north_ref, north_c, out_ref)


def inner(los, stack, seam, operator, cells, tiles):
    rows = cells[0].shape[1] - 2 * tiles
    vmem = pl.BlockSpec(memory_space=pltpu.VMEM)
    return pl.pallas_call(
        functools.partial(inner_kernel, tiles),
        in_specs=[pl.BlockSpec(memory_space=pltpu.SMEM)] + [vmem] * 7,
        out_specs=vmem,
        out_shape=jax.ShapeDtypeStruct((2, rows, LANES), jnp.float32),
        scratch_shapes=[pltpu.VMEM((2, -(-(rows + 2) // 8) * 8, LANES), jnp.float32)],
        compiler_params=pltpu.CompilerParams(vmem_limit_bytes=medium),
        name="inner_rows",
    )(los, stack, seam, operator, *cells)


def solve_cells(vals_ref, los_ref):
    a11 = a12 = a22 = b1 = b2 = 0.0
    for t in range(vals_ref.shape[0]):
        weight, target = vals_ref[t, 0], vals_ref[t, 1]
        east_c, up_c = los_ref[t, 0], los_ref[t, 2]
        by_east, by_up = weight * east_c, weight * up_c
        a11 = a11 + by_east * east_c
        a12 = a12 + by_east * up_c
        a22 = a22 + by_up * up_c
        b1 = b1 + by_east * target
        b2 = b2 + by_up * target
    a11 = a11 + ridge_term
    a22 = a22 + ridge_term
    determ = a11 * a22 - a12 * a12
    return (a22 * b1 - a12 * b2) / determ, (a11 * b2 - a12 * b1) / determ


def solve_kernel(tiles, vals_ref, north_ref, los_ref, solved_ref, first_ref, last_ref):
    east, up = solve_cells(vals_ref, los_ref)
    solved_ref[0] = east
    solved_ref[1] = up
    first_ref[0] = east[:tiles]
    first_ref[1] = north_ref[:tiles, :]
    last_ref[0] = east[tiles:]
    last_ref[1] = north_ref[north_ref.shape[0] - tiles :, :]


def solve_edges(vals, north, los, tiles):
    edge = jax.ShapeDtypeStruct((2, tiles, LANES), jnp.float32)
    vmem = pl.BlockSpec(memory_space=pltpu.VMEM)
    return pl.pallas_call(
        functools.partial(solve_kernel, tiles),
        in_specs=[vmem, vmem, pl.BlockSpec(memory_space=pltpu.SMEM)],
        out_specs=[vmem] * 3,
        out_shape=[jax.ShapeDtypeStruct((2, 2 * tiles, LANES), jnp.float32), edge, edge],
        compiler_params=pltpu.CompilerParams(vmem_limit_bytes=medium),
        name="solve_edges",
    )(vals, north, los)


def final_kernel(
    tiles, own, los_ref, vals_ref, solved_ref, north_ref, before_ref, after_ref, east_up_ref, strain_ref, work_ref
):
    rows = north_ref.shape[0]
    lane = lax.broadcasted_iota(jnp.int32, (rows, LANES), 1)
    tile = lax.broadcasted_iota(jnp.int32, (rows, LANES), 0) % tiles

    def across(field):
        right = jnp.where(tile == tiles - 1, 0.0, pltpu.roll(field, rows - 1, 0))
        left = jnp.where(tile == 0, 0.0, pltpu.roll(field, 1, 0))
        following = jnp.where(lane == LANES - 1, pltpu.roll(right, LANES - 1, 1), pltpu.roll(field, LANES - 1, 1))
        previous = jnp.where(lane == 0, pltpu.roll(left, 1, 1), pltpu.roll(field, 1, 1))
        return following - previous

    def down(field, which):
        below = jnp.concatenate([field[tiles:], after_ref[which]], axis=0)
        above = jnp.concatenate([before_ref[which], field[: rows - tiles]], axis=0)
        return below - above

    east, up = (
        jnp.concatenate([solved_ref[k, :tiles], middle, solved_ref[k, tiles:]], axis=0)
        for k, middle in enumerate(solve_cells(vals_ref, los_ref))
    )
    north = north_ref[...]
    work_ref[0] = east
    work_ref[1] = up
    work_ref[2] = across(east) / 2.0
    work_ref[3] = down(north, 1) / 2.0
    work_ref[4] = (down(east, 0) + across(north)) / 4.0
    start = lax.axis_index("track") * own
    for field in range(5):
        target, at = (east_up_ref, field) if field < 2 else (strain_ref, field - 2)
        for i in range(rows // tiles):
            for j in range(own):
                target[at, i : i + 1, j * LANES : (j + 1) * LANES] = work_ref[field, pl.ds(i * tiles + start + j, 1), :]


def final(los, vals, solved, north, before, after, tiles, own):
    rows = north.shape[0]
    shape = (rows // tiles, own * LANES)
    vmem = pl.BlockSpec(memory_space=pltpu.VMEM)
    return pl.pallas_call(
        functools.partial(final_kernel, tiles, own),
        in_specs=[pl.BlockSpec(memory_space=pltpu.SMEM)] + [vmem] * 5,
        out_specs=[vmem] * 2,
        out_shape=[jax.ShapeDtypeStruct((2, *shape), jnp.float32), jax.ShapeDtypeStruct((3, *shape), jnp.float32)],
        scratch_shapes=[pltpu.VMEM((5, rows, LANES), jnp.float32)],
        compiler_params=pltpu.CompilerParams(vmem_limit_bytes=medium),
        name="solve_and_strain",
    )(los, vals, solved, north, before, after)


def per_device(phases, coherent, pairs, res_index, res_weight, coverage, los, north):
    parts = lax.axis_size("pix")
    tracks = lax.axis_size("track")
    grid_rows, columns = north.shape
    tiles = columns // CTILE
    rows = grid_rows * tiles
    group = GROUP if parts % GROUP == 0 else parts
    planes = parts // group
    plane, column = jnp.divmod(lax.axis_index("pix").astype(jnp.int32), group)
    packed = pack_edges(phases[0], coherent[0], parts, group, tiles)
    steps_j, steps_s = jnp.meshgrid(jnp.arange(group), jnp.arange(planes), indexing="ij")
    sources = ((plane - steps_s) % planes * group + (column - steps_j) % group).reshape(-1)
    edge_pairs = jnp.take(pairs[0].reshape(parts, -1, 2), sources, axis=0).reshape(-1, 2)
    operator, edge_operator = setup_track(pairs[0], edge_pairs)
    arrived = [packed[0]]
    for s in range(1, planes):
        far = [(z * group + c, (z + s) % planes * group + c) for z in range(planes) for c in range(group)]
        arrived.append(lax.ppermute(packed[s], "pix", far))
    by_column = regroup(edge_operator, arrived, group)
    pieces = [by_column[0]]
    for j in range(1, group):
        near = [(z * group + c, z * group + (c + j) % group) for z in range(planes) for c in range(group)]
        pieces.append(lax.ppermute(by_column[j], "pix", near))
    later_flags, *_ = lax.optimization_barrier((coherent[0], packed[0]))
    inner_stack = lax.all_to_all(
        pack_inner(phases[0], later_flags, parts, tiles), "pix", split_axis=0, concat_axis=0, tiled=True
    )
    north_cells = north.reshape(rows, LANES)
    cells = (
        res_index.reshape(-1, rows, LANES),
        res_weight.reshape(-1, rows, LANES),
        coverage.reshape(rows, 1),
        north_cells,
    )

    def flat(stack):
        return stack.reshape(-1, stack.shape[-1])

    edge_vals, seam = edges(los, [flat(piece) for piece in pieces], edge_operator, cells, tiles)
    edge_vals = lax.all_gather(edge_vals, "track", axis=0)
    solved, first, last = solve_edges(edge_vals, north_cells, los, tiles)
    onward = [(i, i + 1) for i in range(parts - 1)]
    back = [(j, i) for i, j in onward]
    before = lax.ppermute(last, "pix", onward)
    after = lax.ppermute(first, "pix", back)
    inner_vals = inner(los, flat(inner_stack), seam, operator, cells, tiles)
    inner_vals = lax.all_gather(inner_vals, "track", axis=0)
    return tuple(final(los, inner_vals, solved, north_cells, before, after, tiles, tiles // tracks))


def solution(mesh):
    in_specs = (
        P("track", "pix", None),
        P("track", "pix", None),
        P("track", None, None),
        P("track", None, "pix"),
        P("track", None, "pix"),
        P("track", "pix", None),
        P(),
        P("pix", None),
    )
    out_specs = (P(None, "pix", "track"), P(None, "pix", "track"))
    return jax.shard_map(
        per_device, mesh=mesh, in_specs=in_specs, out_specs=out_specs, check_vma=False
    )
```

```python
import functools

import jax
import jax.numpy as jnp
from jax import lax
from jax.experimental import pallas as pl
from jax.experimental.pallas import tpu as pltpu
from jax.sharding import PartitionSpec as P

EPOCHS = 200
EXTRA = 16
HALO = 128
CTILE = 128
MBLK = 128
LANES = 128
TILE = 256
GROUP = 4
EDGE_COST = 54_000_000_000


prior_var = 0.1
ridge_term = 0.5
medium = 24 * 1024 * 1024


def stay(array):
    return pltpu.with_memory_space_constraint(array, pltpu.HBM)


def expand_masks(flags_ref, stacked_ref, firsts, wanted, tile_out):
    ifgs = flags_ref.shape[0]
    for n, first in enumerate(firsts):
        stacked_ref[n * ifgs : (n + 1) * ifgs, :] = part_flags(flags_ref, first)
    stacked = stacked_ref[...].astype(jnp.bfloat16)
    block = lax.broadcasted_iota(jnp.int32, (LANES, 2 * MBLK), 0)
    right = lax.broadcasted_iota(jnp.int32, (LANES, 2 * MBLK), 1) >= MBLK
    for start in range(0, len(wanted), 2):
        here = jnp.where(right, wanted[start + 1], wanted[start])
        ones = (block == here).astype(jnp.bfloat16)
        keep = jnp.dot(stacked, ones, preferred_element_type=jnp.float32).astype(jnp.bfloat16)
        for n in range(len(firsts)):
            tile_out(n, start * MBLK, keep[n * ifgs : (n + 1) * ifgs])


def part_flags(flags_ref, first):
    lead = pl.multiple_of(first // LANES * LANES, LANES)
    flags = (flags_ref[:, pl.ds(lead, LANES)] == 1).astype(jnp.float32)
    return pltpu.roll(flags, (LANES - (first - lead)) % LANES, 1)


def partner(index, step, size):
    return index ^ step if size & (size - 1) == 0 else (index + step) % size


def partner_back(index, step, size):
    return index ^ step if size & (size - 1) == 0 else (index - step + size) % size


def pack_edges_kernel(tiles, group, flags_hbm, phases_ref, *refs):
    *out_refs, flags_ref, stacked_ref, near_ref, flag_sem, in_sem = refs
    planes = len(out_refs)
    parts = planes * group
    ifgs, blocks = flags_ref.shape
    span = blocks // parts
    reach = tiles + 1
    half = reach * MBLK
    flag_copy = pltpu.make_async_copy(flags_hbm, flags_ref, flag_sem)
    flag_copy.start()
    ends = [
        pltpu.make_async_copy(phases_ref.at[:, pl.ds(0, half)], near_ref.at[0, :, pl.ds(half, half)], in_sem.at[0]),
        pltpu.make_async_copy(
            phases_ref.at[:, pl.ds(blocks * MBLK - half, half)], near_ref.at[parts, :, pl.ds(0, half)], in_sem.at[parts]
        ),
    ]

    def between(b):
        low = pl.multiple_of((span * b - reach) * MBLK, MBLK)
        return pltpu.make_async_copy(phases_ref.at[:, pl.ds(low, 2 * half)], near_ref.at[b], in_sem.at[b])

    ends[0].start()

    @pl.loop(1, parts)
    def _(b):
        between(b).start()

    ends[1].start()
    flag_copy.wait()
    plane = lax.axis_index("pix") // group
    firsts = [(partner(plane, s, planes) * group + g) * span for s in range(planes) for g in range(group)]

    def tile_out(n, start, keep):
        out_refs[n // group][n % group, :, start : start + 2 * MBLK] = keep

    wanted = [k if k < reach else span - 2 * reach + k for k in range(2 * reach)]
    expand_masks(flags_ref, stacked_ref, firsts, wanted, tile_out)
    ends[0].wait()

    @pl.loop(1, parts)
    def _(b):
        between(b).wait()

    ends[1].wait()
    for s in range(planes):
        first_part = partner(plane, s, planes) * group

        @pl.loop(0, group, unroll=2)
        def _(g):
            out_refs[s][g, :, :half] *= near_ref[first_part + g, :, half:]
            out_refs[s][g, :, half:] *= near_ref[first_part + g + 1, :, :half]


def pack_edges(phases, flags, parts, group, tiles):
    ifgs = phases.shape[0]
    planes = parts // group
    hbm = pl.BlockSpec(memory_space=pltpu.HBM)
    width = 2 * (tiles + 1) * MBLK
    return pl.pallas_call(
        functools.partial(pack_edges_kernel, tiles, group),
        in_specs=[hbm, hbm],
        out_specs=[pl.BlockSpec(memory_space=pltpu.VMEM)] * planes,
        out_shape=[jax.ShapeDtypeStruct((group, ifgs, width), jnp.bfloat16)] * planes,
        scratch_shapes=[
            pltpu.VMEM(flags.shape, jnp.int32),
            pltpu.VMEM((parts * ifgs, LANES), jnp.float32),
            pltpu.VMEM((parts + 1, ifgs, 2 * (tiles + 1) * MBLK), jnp.bfloat16),
            pltpu.SemaphoreType.DMA,
            pltpu.SemaphoreType.DMA((parts + 1,)),
        ],
        compiler_params=pltpu.CompilerParams(vmem_limit_bytes=medium),
        name="pack_edges",
    )(stay(flags), stay(phases))


def regroup_kernel(planes, group, after_ref, *refs):
    in_refs, out_refs = refs[:planes], refs[planes:]
    for j in range(group):
        column = partner(lax.rem(lax.axis_index("pix"), group), j, group)
        for s in range(planes):
            out_refs[j][s] = in_refs[s][column]


def regroup(after, pieces, group):
    planes = len(pieces)
    vmem = pl.BlockSpec(memory_space=pltpu.VMEM)
    shape = (planes, *pieces[0].shape[1:])
    return pl.pallas_call(
        functools.partial(regroup_kernel, planes, group),
        in_specs=[vmem] * (planes + 1),
        out_specs=[vmem] * group,
        out_shape=[jax.ShapeDtypeStruct(shape, jnp.bfloat16)] * group,
        compiler_params=pltpu.CompilerParams(vmem_limit_bytes=medium),
        name="regroup",
    )(after, *pieces)


def pack_inner_kernel(reach, flags_hbm, phases_ref, out_ref, flags_ref, stacked_ref, held_ref, flag_sem, in_sem):
    parts, ifgs, width = out_ref.shape
    span = flags_ref.shape[1] // parts
    flag_copy = pltpu.make_async_copy(flags_hbm, flags_ref, flag_sem)
    flag_copy.start()

    def inward(p):
        low = pl.multiple_of((p * span + reach) * MBLK, MBLK)
        return pltpu.make_async_copy(phases_ref.at[:, pl.ds(low, width)], held_ref.at[p], in_sem.at[p])

    @pl.loop(0, parts)
    def _(p):
        inward(p).start()

    flag_copy.wait()

    def tile_out(n, start, keep):
        out_ref[n, :, start : start + 2 * MBLK] = keep

    wanted = list(range(reach, span - reach))
    expand_masks(flags_ref, stacked_ref, [p * span for p in range(parts)], wanted, tile_out)

    @pl.loop(0, parts)
    def _(p):
        inward(p).wait()
        out_ref[p] *= held_ref[p]


def pack_inner(phases, flags, parts, tiles):
    ifgs = phases.shape[0]
    reach = tiles + 1
    width = (flags.shape[1] // parts - 2 * reach) * MBLK
    hbm = pl.BlockSpec(memory_space=pltpu.HBM)
    return pl.pallas_call(
        functools.partial(pack_inner_kernel, reach),
        in_specs=[hbm, hbm],
        out_specs=pl.BlockSpec(memory_space=pltpu.VMEM),
        out_shape=jax.ShapeDtypeStruct((parts, ifgs, width), jnp.bfloat16),
        scratch_shapes=[
            pltpu.VMEM(flags.shape, jnp.int32),
            pltpu.VMEM((parts * ifgs, LANES), jnp.float32),
            pltpu.VMEM((parts, ifgs, width), jnp.bfloat16),
            pltpu.SemaphoreType.DMA,
            pltpu.SemaphoreType.DMA((parts,)),
        ],
        compiler_params=pltpu.CompilerParams(vmem_limit_bytes=medium),
        name="pack_inner",
    )(stay(flags), stay(phases))


def exact_dot(a, b):
    return jnp.dot(a, b, precision=lax.Precision.HIGHEST, preferred_element_type=jnp.float32)


def operator_kernel(pairs_ref, other_ref, out_ref, other_out_ref, normal_ref, inverse_ref):
    ifgs = pairs_ref.shape[1]
    size = normal_ref.shape[0]
    epoch = lax.broadcasted_iota(jnp.int32, (size, ifgs), 0)

    def ends(ref):
        return (epoch == ref[1:2, :]).astype(jnp.float32) - (epoch == ref[0:1, :]).astype(jnp.float32)

    across = ends(pairs_ref)
    down = across.T
    eye = (
        lax.broadcasted_iota(jnp.int32, (size, size), 0) == lax.broadcasted_iota(jnp.int32, (size, size), 1)
    ).astype(jnp.float32)
    normal = eye + jnp.dot(
        across.astype(jnp.bfloat16), down.astype(jnp.bfloat16), preferred_element_type=jnp.float32
    )
    normal_ref[...] = normal
    inverse_ref[...] = eye / jnp.where(eye == 1.0, normal, 1.0)

    def unfinished(state):
        step, gap = state
        return jnp.logical_and(step < 24, gap > 1e-5)

    def improve(state):
        step, _ = state
        inverse = inverse_ref[...]
        rest = eye - exact_dot(normal_ref[...], inverse)
        inverse_ref[...] = inverse + exact_dot(inverse, rest)
        return step + 1, jnp.max(jnp.abs(rest))

    lax.while_loop(unfinished, improve, (jnp.int32(0), jnp.float32(1.0)))
    place = lax.broadcasted_iota(jnp.int32, (size, ifgs), 0)
    centred = place.astype(jnp.float32) - (EPOCHS - 1) / 2.0
    square = sum((e - (EPOCHS - 1) / 2.0) ** 2 for e in range(EPOCHS))
    slope = jnp.where(place < EPOCHS, centred * (EPOCHS - 1) / square, 0.0)
    same = lax.broadcasted_iota(jnp.int32, (ifgs, ifgs), 0) == lax.broadcasted_iota(jnp.int32, (ifgs, ifgs), 1)
    extra = lax.broadcasted_iota(jnp.int32, (EXTRA, ifgs), 0)
    for ref, to_ref in ((pairs_ref, out_ref), (other_ref, other_out_ref)):
        across = ends(ref)
        pseudo = exact_dot(inverse_ref[...], across).astype(jnp.bfloat16)
        fitted = jnp.dot(across.T.astype(jnp.bfloat16), pseudo, preferred_element_type=jnp.float32)
        to_ref[:ifgs, :] = (same.astype(jnp.float32) - fitted).astype(jnp.bfloat16)
        row = jnp.sum(pseudo.astype(jnp.float32) * slope, axis=0, keepdims=True)
        high = row.astype(jnp.bfloat16).astype(jnp.float32)
        rest = row - high
        middle = rest.astype(jnp.bfloat16).astype(jnp.float32)
        low = rest - middle
        terms = jnp.where(extra == 0, high, jnp.where(extra == 1, middle, jnp.where(extra == 2, low, 0.0)))
        to_ref[ifgs:, :] = terms.astype(jnp.bfloat16)


def setup_track(pair_rows, other_rows):
    ifgs = pair_rows.shape[0]
    size = -(-EPOCHS // LANES) * LANES
    vmem = pl.BlockSpec(memory_space=pltpu.VMEM)
    return pl.pallas_call(
        operator_kernel,
        in_specs=[vmem] * 2,
        out_specs=[vmem] * 2,
        out_shape=[jax.ShapeDtypeStruct((ifgs + EXTRA, ifgs), jnp.bfloat16)] * 2,
        scratch_shapes=[pltpu.VMEM((size, size), jnp.float32), pltpu.VMEM((size, size), jnp.float32)],
        compiler_params=pltpu.CompilerParams(vmem_limit_bytes=medium),
        name="misfit_operator",
    )(pair_rows.T, other_rows.T)


def invert_tiles(stack_refs, first, width, operator_ref, fields_ref, base):
    ifgs = operator_ref.shape[1]
    for start in range(0, width, TILE):
        here = pl.ds(pl.multiple_of(first + start, LANES), TILE)
        stack = jnp.concatenate([ref[:, here] for ref in stack_refs], axis=0)
        product = jnp.dot(operator_ref[...], stack, preferred_element_type=jnp.float32)
        velocity = jnp.sum(product[ifgs : ifgs + 8], axis=0, keepdims=True)
        variance = jnp.sum(product[:ifgs] * product[:ifgs], axis=0, keepdims=True) / ifgs
        for k in range(TILE // LANES):
            row = pl.ds(base + start // LANES + k, 1)
            fields_ref[0, row, :] = velocity[:, k * LANES : (k + 1) * LANES]
            fields_ref[1, row, :] = variance[:, k * LANES : (k + 1) * LANES]


def pick(source, lane):
    return jnp.take_along_axis(source, lane, axis=1, mode="promise_in_bounds")


def resample(near, cell, index_ref, weight_ref):
    lanes = lax.broadcasted_iota(jnp.int32, (8, LANES), 1)
    here = pl.ds(cell, 8)
    sums = [jnp.zeros((8, LANES), jnp.float32)] * 2
    total = jnp.zeros((8, LANES), jnp.float32)
    for b in range(index_ref.shape[0]):
        weight = weight_ref[b, here, :]
        place = lanes + index_ref[b, here, :] + HALO
        lane = place & (LANES - 1)
        which = place >> 7
        total = total + weight
        for f in range(2):
            low, mid, high = (pick(near[f][k], lane) for k in range(3))
            taken = jnp.where(which == 0, low, jnp.where(which == 1, mid, high))
            sums[f] = sums[f] + taken * weight
    return sums[0] / total, sums[1] / total, total


def boundary(row, offsets, weights, sources, wanted):
    lanes = lax.broadcasted_iota(jnp.int32, (8, LANES), 1)
    rows = lax.broadcasted_iota(jnp.int32, (8, LANES), 0)
    sums = [jnp.zeros((8, LANES), jnp.float32)] * 2
    for offset, weight in zip(offsets, weights):
        place = lanes + offset + HALO
        lane = place & (LANES - 1)
        keep = jnp.where(jnp.logical_and(place >> 7 == wanted, rows == row), weight, 0.0)
        for f in range(2):
            sums[f] = sums[f] + pick(jnp.broadcast_to(sources[f], (8, LANES)), lane) * keep
    return sums


def store_cells(out_ref, at, velocity, variance, cover, north, north_c):
    out_ref[0, at : at + 8, :] = cover / (variance + prior_var)
    out_ref[1, at : at + 8, :] = velocity - north_c * north


def edges_kernel(tiles, group, *refs):
    stack_refs = refs[:group]
    operator_ref, index_ref, weight_ref, cover_ref, north_ref, seam_ref, own_ref, ends_ref, back_ref, onward_ref, fields_ref = refs[group:]
    width = stack_refs[0].shape[1]
    count = width // LANES
    taps, rows, _ = index_ref.shape
    none = jnp.zeros((2, 1, LANES), jnp.float32)
    fields_ref[:, :1, :] = none
    fields_ref[:, count + 1 : count + 2, :] = none
    invert_tiles(stack_refs, 0, width, operator_ref, fields_ref, 1)
    seam_ref[...] = fields_ref[:, tiles : tiles + 4, :]
    ends_ref[:, :1, :] = fields_ref[:, 1:2, :]
    ends_ref[:, 1:, :] = fields_ref[:, count : count + 1, :]
    for half, to_ref in enumerate((back_ref, onward_ref)):
        first = half * (rows - tiles)
        to_ref[:tiles, :] = north_ref[first : first + tiles, :]
        to_ref[tiles : 2 * tiles, :] = jnp.broadcast_to(cover_ref[first : first + tiles, :].astype(jnp.float32), (tiles, LANES))
        for r in range(0, tiles, 8):
            base = half * (tiles + 2) + r
            near = [[fields_ref[f, base + k : base + k + 8, :] for k in range(3)] for f in range(2)]
            velocity, variance, total = resample(near, first + r, index_ref, weight_ref)
            for f, values in enumerate((velocity, variance)):
                own_ref[f, half * tiles + r : half * tiles + r + 8, :] = values
                to_ref[(2 + f) * tiles + r : (2 + f) * tiles + r + 8, :] = values
            if r == (tiles - 8 if half else 0):
                outer = total[7:] if half else total[:1]
        outermost = first + (tiles - 1 if half else 0)
        at = 4 * tiles
        for b in range(taps):
            to_ref[at + b : at + b + 1, :] = index_ref[b, outermost : outermost + 1, :].astype(jnp.float32)
            to_ref[at + taps + b : at + taps + b + 1, :] = weight_ref[b, outermost : outermost + 1, :] / outer
        at += 2 * taps
        for f in range(2):
            to_ref[at + f : at + f + 1, :] = ends_ref[f, half : half + 1, :]
        left = to_ref.shape[0] - at - 2
        to_ref[at + 2 :, :] = jnp.zeros((left, LANES), jnp.float32)


def edges(stacks, operator, cells, tiles):
    rows = 2 * (tiles + 1)
    payload = -(-(4 * tiles + 2 * cells[0].shape[0] + 2) // 8) * 8
    shapes = [(2, 4, LANES), (2, 2 * tiles, LANES), (2, 2, LANES), (payload, LANES), (payload, LANES)]
    vmem = pl.BlockSpec(memory_space=pltpu.VMEM)
    return pl.pallas_call(
        functools.partial(edges_kernel, tiles, len(stacks)),
        in_specs=[vmem] * (len(stacks) + 5),
        out_specs=[vmem] * 5,
        out_shape=[jax.ShapeDtypeStruct(shape, jnp.float32) for shape in shapes],
        scratch_shapes=[pltpu.VMEM((2, -(-(rows + 2) // 8) * 8, LANES), jnp.float32)],
        compiler_params=pltpu.CompilerParams(vmem_limit_bytes=medium),
        cost_estimate=pl.CostEstimate(flops=EDGE_COST, bytes_accessed=0, transcendentals=0),
        name="edge_rows",
    )(*stacks, operator, *cells)


def inner_kernel(
    tiles, los_ref, stack_ref, seam_ref, own_ref, ends_ref, before_ref, after_ref, operator_ref, index_ref, weight_ref, cover_ref,
    north_ref, out_ref, fields_ref,
):
    width = stack_ref.shape[1]
    taps, rows, _ = index_ref.shape
    north_c = los_ref[lax.axis_index("track"), 1]
    pixel_rows = width // LANES
    fields_ref[:, 0:2, :] = seam_ref[:, 0:2, :]
    fields_ref[:, pixel_rows + 2 : pixel_rows + 4, :] = seam_ref[:, 2:4, :]
    for half, from_ref in enumerate((before_ref, after_ref)):
        edge = half * (tiles - 8)
        row = 7 * half
        outermost = half * (rows - 1)
        total = sum(weight_ref[b, outermost : outermost + 1, :] for b in range(taps))
        at = 4 * tiles
        theirs = [from_ref[at + 2 * taps + f : at + 2 * taps + f + 1, :] for f in range(2)]
        mine = [ends_ref[f, half : half + 1, :] for f in range(2)]
        to_own = boundary(
            row,
            [index_ref[b, outermost : outermost + 1, :] for b in range(taps)],
            [weight_ref[b, outermost : outermost + 1, :] / total for b in range(taps)],
            theirs,
            2 * half,
        )
        to_other = boundary(
            7 - row,
            [from_ref[at + b : at + b + 1, :].astype(jnp.int32) for b in range(taps)],
            [from_ref[at + taps + b : at + taps + b + 1, :] for b in range(taps)],
            mine,
            2 - 2 * half,
        )
        for r in range(0, tiles, 8):
            first = half * (rows - tiles) + r
            values = [own_ref[f, half * tiles + r : half * tiles + r + 8, :] for f in range(2)]
            if r == edge:
                values = [value + more for value, more in zip(values, to_own)]
            cover = cover_ref[first : first + 8, :].astype(jnp.float32)
            store_cells(out_ref, tiles + first, *values, cover, north_ref[first : first + 8, :], north_c)
            values = [from_ref[(2 + f) * tiles + r : (2 + f) * tiles + r + 8, :] for f in range(2)]
            if r == tiles - 8 - edge:
                values = [value + more for value, more in zip(values, to_other)]
            cover = from_ref[tiles + r : tiles + r + 8, :]
            store_cells(out_ref, half * (rows + tiles) + r, *values, cover, from_ref[r : r + 8, :], north_c)
    invert_tiles([stack_ref], 0, width, operator_ref, fields_ref, 2)
    for r in range(0, rows - 2 * tiles, 8):
        near = [[fields_ref[f, r + k : r + k + 8, :] for k in range(3)] for f in range(2)]
        first = tiles + r
        velocity, variance, _ = resample(near, first, index_ref, weight_ref)
        cover = cover_ref[first : first + 8, :].astype(jnp.float32)
        store_cells(out_ref, tiles + first, velocity, variance, cover, north_ref[first : first + 8, :], north_c)


def inner(los, stack, seam, own, ends, before, after, operator, cells, tiles):
    rows = cells[0].shape[1]
    vmem = pl.BlockSpec(memory_space=pltpu.VMEM)
    return pl.pallas_call(
        functools.partial(inner_kernel, tiles),
        in_specs=[pl.BlockSpec(memory_space=pltpu.SMEM)] + [vmem] * 11,
        out_specs=vmem,
        out_shape=jax.ShapeDtypeStruct((2, rows + 2 * tiles, LANES), jnp.float32),
        scratch_shapes=[pltpu.VMEM((2, -(-(rows - 2 * tiles + 2) // 8) * 8, LANES), jnp.float32)],
        compiler_params=pltpu.CompilerParams(vmem_limit_bytes=medium),
        name="inner_rows",
    )(los, stack, seam, own, ends, before, after, operator, *cells)


def solve_cells(vals_ref, los_ref):
    a11 = a12 = a22 = b1 = b2 = 0.0
    for t in range(vals_ref.shape[0]):
        weight, target = vals_ref[t, 0], vals_ref[t, 1]
        east_c, up_c = los_ref[t, 0], los_ref[t, 2]
        by_east, by_up = weight * east_c, weight * up_c
        a11 = a11 + by_east * east_c
        a12 = a12 + by_east * up_c
        a22 = a22 + by_up * up_c
        b1 = b1 + by_east * target
        b2 = b2 + by_up * target
    a11 = a11 + ridge_term
    a22 = a22 + ridge_term
    determ = a11 * a22 - a12 * a12
    return (a22 * b1 - a12 * b2) / determ, (a11 * b2 - a12 * b1) / determ


def final_kernel(tiles, own, los_ref, vals_ref, north_ref, before_ref, after_ref, east_up_ref, strain_ref, work_ref):
    rows = north_ref.shape[0]
    lane = lax.broadcasted_iota(jnp.int32, (rows, LANES), 1)
    tile = lax.broadcasted_iota(jnp.int32, (rows, LANES), 0) % tiles

    def across(field):
        right = jnp.where(tile == tiles - 1, 0.0, pltpu.roll(field, rows - 1, 0))
        left = jnp.where(tile == 0, 0.0, pltpu.roll(field, 1, 0))
        following = jnp.where(lane == LANES - 1, pltpu.roll(right, LANES - 1, 1), pltpu.roll(field, LANES - 1, 1))
        previous = jnp.where(lane == 0, pltpu.roll(left, 1, 1), pltpu.roll(field, 1, 1))
        return following - previous

    wide_east, wide_up = solve_cells(vals_ref, los_ref)
    wide_north = jnp.concatenate([before_ref[:tiles, :], north_ref[...], after_ref[:tiles, :]], axis=0)
    east, north = (wide[tiles : tiles + rows] for wide in (wide_east, wide_north))
    work_ref[0] = east
    work_ref[1] = wide_up[tiles : tiles + rows]
    work_ref[2] = across(east) / 2.0
    work_ref[3] = (wide_north[2 * tiles :] - wide_north[:rows]) / 2.0
    work_ref[4] = (wide_east[2 * tiles :] - wide_east[:rows] + across(north)) / 4.0
    start = lax.axis_index("track") * own
    for field in range(5):
        target, at = (east_up_ref, field) if field < 2 else (strain_ref, field - 2)
        for i in range(rows // tiles):
            for j in range(own):
                target[at, i : i + 1, j * LANES : (j + 1) * LANES] = work_ref[field, pl.ds(i * tiles + start + j, 1), :]


def final(los, vals, north, before, after, tiles, own):
    rows = north.shape[0]
    shape = (rows // tiles, own * LANES)
    vmem = pl.BlockSpec(memory_space=pltpu.VMEM)
    return pl.pallas_call(
        functools.partial(final_kernel, tiles, own),
        in_specs=[pl.BlockSpec(memory_space=pltpu.SMEM)] + [vmem] * 4,
        out_specs=[vmem] * 2,
        out_shape=[jax.ShapeDtypeStruct((2, *shape), jnp.float32), jax.ShapeDtypeStruct((3, *shape), jnp.float32)],
        scratch_shapes=[pltpu.VMEM((5, rows, LANES), jnp.float32)],
        compiler_params=pltpu.CompilerParams(vmem_limit_bytes=medium),
        name="solve_and_strain",
    )(los, vals, north, before, after)


def per_device(phases, coherent, pairs, res_index, res_weight, coverage, los, north):
    parts = lax.axis_size("pix")
    tracks = lax.axis_size("track")
    grid_rows, columns = north.shape
    tiles = columns // CTILE
    rows = grid_rows * tiles
    group = GROUP if parts % GROUP == 0 else parts
    planes = parts // group
    plane, column = jnp.divmod(lax.axis_index("pix").astype(jnp.int32), group)
    packed = pack_edges(phases[0], coherent[0], parts, group, tiles)
    later_pairs, _ = lax.optimization_barrier((pairs[0], packed[0]))
    steps_j, steps_s = jnp.meshgrid(jnp.arange(group), jnp.arange(planes), indexing="ij")
    sources = (partner_back(plane, steps_s, planes) * group + partner_back(column, steps_j, group)).reshape(-1)
    edge_pairs = jnp.take(later_pairs.reshape(parts, -1, 2), sources, axis=0).reshape(-1, 2)
    operator, edge_operator = setup_track(later_pairs, edge_pairs)
    ids = [(z, c) for z in range(planes) for c in range(group)]
    arrived = [packed[0]]
    for s in range(1, planes):
        far = [(z * group + c, partner(z, s, planes) * group + c) for z, c in ids]
        arrived.append(lax.ppermute(packed[s], "pix", far))
    by_column = regroup(edge_operator, arrived, group)
    pieces = [by_column[0]]
    for j in range(1, group):
        near = [(z * group + c, z * group + partner(c, j, group)) for z, c in ids]
        pieces.append(lax.ppermute(by_column[j], "pix", near))
    later_flags, *_ = lax.optimization_barrier((coherent[0], packed[0], operator))
    inner_stack = lax.all_to_all(
        pack_inner(phases[0], later_flags, parts, tiles), "pix", split_axis=0, concat_axis=0, tiled=True
    )
    north_cells = north.reshape(rows, LANES)
    cells = (
        res_index.reshape(-1, rows, LANES),
        res_weight.reshape(-1, rows, LANES),
        coverage.reshape(rows, 1),
        north_cells,
    )

    def flat(stack):
        return stack.reshape(-1, stack.shape[-1])

    onward = [(i, i + 1) for i in range(parts - 1)]
    back = [(j, i) for i, j in onward]
    seam, own, ends, for_before, for_after = edges([flat(piece) for piece in pieces], edge_operator, cells, tiles)
    before = lax.ppermute(for_after, "pix", onward)
    after = lax.ppermute(for_before, "pix", back)
    vals = inner(los, flat(inner_stack), seam, own, ends, before, after, operator, cells, tiles)
    vals = lax.all_gather(vals, "track", axis=0)
    return tuple(final(los, vals, north_cells, before, after, tiles, tiles // tracks))


def solution(mesh):
    in_specs = (
        P("track", "pix", None),
        P("track", "pix", None),
        P("track", None, None),
        P("track", None, "pix"),
        P("track", None, "pix"),
        P("track", "pix", None),
        P(),
        P("pix", None),
    )
    out_specs = (P(None, "pix", "track"), P(None, "pix", "track"))
    return jax.shard_map(
        per_device, mesh=mesh, in_specs=in_specs, out_specs=out_specs, check_vma=False
    )
```

```python
import functools

import jax
import jax.numpy as jnp
from jax import lax
from jax.experimental import pallas as pl
from jax.experimental.pallas import tpu as pltpu
from jax.sharding import PartitionSpec as P

EPOCHS = 200
EXTRA = 16
HALO = 128
CTILE = 128
MBLK = 128
LANES = 128
TILE = 256
GROUP = 4
EDGE_COST = 54_000_000_000

token = jax.ShapeDtypeStruct((8, LANES), jnp.float32)


prior_var = 0.1
ridge_term = 0.5
medium = 24 * 1024 * 1024


def stay(array):
    return pltpu.with_memory_space_constraint(array, pltpu.HBM)


def expand_masks(flags_ref, stacked_ref, firsts, wanted, tile_out):
    ifgs = flags_ref.shape[0]
    for n, first in enumerate(firsts):
        stacked_ref[n * ifgs : (n + 1) * ifgs, :] = part_flags(flags_ref, first)
    stacked = stacked_ref[...].astype(jnp.bfloat16)
    block = lax.broadcasted_iota(jnp.int32, (LANES, 2 * MBLK), 0)
    right = lax.broadcasted_iota(jnp.int32, (LANES, 2 * MBLK), 1) >= MBLK
    for start in range(0, len(wanted), 2):
        here = jnp.where(right, wanted[start + 1], wanted[start])
        ones = (block == here).astype(jnp.bfloat16)
        keep = jnp.dot(stacked, ones, preferred_element_type=jnp.float32).astype(jnp.bfloat16)
        for n in range(len(firsts)):
            tile_out(n, start * MBLK, keep[n * ifgs : (n + 1) * ifgs])


def part_flags(flags_ref, first):
    lead = pl.multiple_of(first // LANES * LANES, LANES)
    flags = (flags_ref[:, pl.ds(lead, LANES)] == 1).astype(jnp.float32)
    return pltpu.roll(flags, (LANES - (first - lead)) % LANES, 1)


def partner(index, step, size):
    return index ^ step if size & (size - 1) == 0 else (index + step) % size


def partner_back(index, step, size):
    return index ^ step if size & (size - 1) == 0 else (index - step + size) % size


def pack_edges_kernel(tiles, group, flags_hbm, phases_ref, *refs):
    *out_refs, token_ref, flags_ref, stacked_ref, near_ref, flag_sem, in_sem = refs
    token_ref[...] = jnp.zeros_like(token_ref)
    planes = len(out_refs)
    parts = planes * group
    ifgs, blocks = flags_ref.shape
    span = blocks // parts
    reach = tiles + 1
    half = reach * MBLK
    flag_copy = pltpu.make_async_copy(flags_hbm, flags_ref, flag_sem)
    flag_copy.start()
    ends = [
        pltpu.make_async_copy(phases_ref.at[:, pl.ds(0, half)], near_ref.at[0, :, pl.ds(half, half)], in_sem.at[0]),
        pltpu.make_async_copy(
            phases_ref.at[:, pl.ds(blocks * MBLK - half, half)], near_ref.at[parts, :, pl.ds(0, half)], in_sem.at[parts]
        ),
    ]

    def between(b):
        low = pl.multiple_of((span * b - reach) * MBLK, MBLK)
        return pltpu.make_async_copy(phases_ref.at[:, pl.ds(low, 2 * half)], near_ref.at[b], in_sem.at[b])

    ends[0].start()

    @pl.loop(1, parts)
    def _(b):
        between(b).start()

    ends[1].start()
    flag_copy.wait()
    plane = lax.axis_index("pix") // group
    firsts = [(partner(plane, s, planes) * group + g) * span for s in range(planes) for g in range(group)]

    def tile_out(n, start, keep):
        out_refs[n // group][n % group, :, start : start + 2 * MBLK] = keep

    wanted = [k if k < reach else span - 2 * reach + k for k in range(2 * reach)]
    expand_masks(flags_ref, stacked_ref, firsts, wanted, tile_out)
    ends[0].wait()

    @pl.loop(1, parts)
    def _(b):
        between(b).wait()

    ends[1].wait()
    for s in range(planes):
        first_part = partner(plane, s, planes) * group

        @pl.loop(0, group, unroll=2)
        def _(g):
            out_refs[s][g, :, :half] *= near_ref[first_part + g, :, half:]
            out_refs[s][g, :, half:] *= near_ref[first_part + g + 1, :, :half]


def pack_edges(phases, flags, parts, group, tiles):
    ifgs = phases.shape[0]
    planes = parts // group
    hbm = pl.BlockSpec(memory_space=pltpu.HBM)
    width = 2 * (tiles + 1) * MBLK
    return pl.pallas_call(
        functools.partial(pack_edges_kernel, tiles, group),
        in_specs=[hbm, hbm],
        out_specs=[pl.BlockSpec(memory_space=pltpu.VMEM)] * (planes + 1),
        out_shape=[jax.ShapeDtypeStruct((group, ifgs, width), jnp.bfloat16)] * planes + [token],
        scratch_shapes=[
            pltpu.VMEM(flags.shape, jnp.int32),
            pltpu.VMEM((parts * ifgs, LANES), jnp.float32),
            pltpu.VMEM((parts + 1, ifgs, 2 * (tiles + 1) * MBLK), jnp.bfloat16),
            pltpu.SemaphoreType.DMA,
            pltpu.SemaphoreType.DMA((parts + 1,)),
        ],
        compiler_params=pltpu.CompilerParams(vmem_limit_bytes=medium),
        name="pack_edges",
    )(stay(flags), stay(phases))


def regroup_kernel(planes, group, after_ref, *refs):
    in_refs, out_refs = refs[:planes], refs[planes:]
    for j in range(group):
        column = partner(lax.rem(lax.axis_index("pix"), group), j, group)
        for s in range(planes):
            out_refs[j][s] = in_refs[s][column]


def regroup(after, pieces, group):
    planes = len(pieces)
    vmem = pl.BlockSpec(memory_space=pltpu.VMEM)
    shape = (planes, *pieces[0].shape[1:])
    return pl.pallas_call(
        functools.partial(regroup_kernel, planes, group),
        in_specs=[vmem] * (planes + 1),
        out_specs=[vmem] * group,
        out_shape=[jax.ShapeDtypeStruct(shape, jnp.bfloat16)] * group,
        compiler_params=pltpu.CompilerParams(vmem_limit_bytes=medium),
        name="regroup",
    )(after, *pieces)


def pack_inner_kernel(reach, flags_hbm, phases_ref, out_ref, flags_ref, stacked_ref, held_ref, flag_sem, in_sem):
    parts, ifgs, width = out_ref.shape
    span = flags_ref.shape[1] // parts
    flag_copy = pltpu.make_async_copy(flags_hbm, flags_ref, flag_sem)
    flag_copy.start()

    def inward(p):
        low = pl.multiple_of((p * span + reach) * MBLK, MBLK)
        return pltpu.make_async_copy(phases_ref.at[:, pl.ds(low, width)], held_ref.at[p], in_sem.at[p])

    @pl.loop(0, parts)
    def _(p):
        inward(p).start()

    flag_copy.wait()

    def tile_out(n, start, keep):
        out_ref[n, :, start : start + 2 * MBLK] = keep

    wanted = list(range(reach, span - reach))
    expand_masks(flags_ref, stacked_ref, [p * span for p in range(parts)], wanted, tile_out)

    @pl.loop(0, parts)
    def _(p):
        inward(p).wait()
        out_ref[p] *= held_ref[p]


def pack_inner(phases, flags, parts, tiles):
    ifgs = phases.shape[0]
    reach = tiles + 1
    width = (flags.shape[1] // parts - 2 * reach) * MBLK
    hbm = pl.BlockSpec(memory_space=pltpu.HBM)
    return pl.pallas_call(
        functools.partial(pack_inner_kernel, reach),
        in_specs=[hbm, hbm],
        out_specs=pl.BlockSpec(memory_space=pltpu.VMEM),
        out_shape=jax.ShapeDtypeStruct((parts, ifgs, width), jnp.bfloat16),
        scratch_shapes=[
            pltpu.VMEM(flags.shape, jnp.int32),
            pltpu.VMEM((parts * ifgs, LANES), jnp.float32),
            pltpu.VMEM((parts, ifgs, width), jnp.bfloat16),
            pltpu.SemaphoreType.DMA,
            pltpu.SemaphoreType.DMA((parts,)),
        ],
        compiler_params=pltpu.CompilerParams(vmem_limit_bytes=medium),
        name="pack_inner",
    )(stay(flags), stay(phases))


def exact_dot(a, b):
    return jnp.dot(a, b, precision=lax.Precision.HIGHEST, preferred_element_type=jnp.float32)


def operator_kernel(pairs_ref, other_ref, out_ref, other_out_ref, token_ref, normal_ref, inverse_ref):
    token_ref[...] = jnp.zeros_like(token_ref)
    ifgs = pairs_ref.shape[1]
    size = normal_ref.shape[0]
    epoch = lax.broadcasted_iota(jnp.int32, (size, ifgs), 0)

    def ends(ref):
        return (epoch == ref[1:2, :]).astype(jnp.float32) - (epoch == ref[0:1, :]).astype(jnp.float32)

    across = ends(pairs_ref)
    down = across.T
    eye = (
        lax.broadcasted_iota(jnp.int32, (size, size), 0) == lax.broadcasted_iota(jnp.int32, (size, size), 1)
    ).astype(jnp.float32)
    normal = eye + jnp.dot(
        across.astype(jnp.bfloat16), down.astype(jnp.bfloat16), preferred_element_type=jnp.float32
    )
    normal_ref[...] = normal
    inverse_ref[...] = eye / jnp.where(eye == 1.0, normal, 1.0)

    def unfinished(state):
        step, gap = state
        return jnp.logical_and(step < 24, gap > 1e-5)

    def improve(state):
        step, _ = state
        inverse = inverse_ref[...]
        rest = eye - exact_dot(normal_ref[...], inverse)
        inverse_ref[...] = inverse + exact_dot(inverse, rest)
        return step + 1, jnp.max(jnp.abs(rest))

    lax.while_loop(unfinished, improve, (jnp.int32(0), jnp.float32(1.0)))
    place = lax.broadcasted_iota(jnp.int32, (size, ifgs), 0)
    centred = place.astype(jnp.float32) - (EPOCHS - 1) / 2.0
    square = sum((e - (EPOCHS - 1) / 2.0) ** 2 for e in range(EPOCHS))
    slope = jnp.where(place < EPOCHS, centred * (EPOCHS - 1) / square, 0.0)
    same = lax.broadcasted_iota(jnp.int32, (ifgs, ifgs), 0) == lax.broadcasted_iota(jnp.int32, (ifgs, ifgs), 1)
    extra = lax.broadcasted_iota(jnp.int32, (EXTRA, ifgs), 0)
    for ref, to_ref in ((pairs_ref, out_ref), (other_ref, other_out_ref)):
        across = ends(ref)
        pseudo = exact_dot(inverse_ref[...], across).astype(jnp.bfloat16)
        fitted = jnp.dot(across.T.astype(jnp.bfloat16), pseudo, preferred_element_type=jnp.float32)
        to_ref[:ifgs, :] = (same.astype(jnp.float32) - fitted).astype(jnp.bfloat16)
        row = jnp.sum(pseudo.astype(jnp.float32) * slope, axis=0, keepdims=True)
        high = row.astype(jnp.bfloat16).astype(jnp.float32)
        rest = row - high
        middle = rest.astype(jnp.bfloat16).astype(jnp.float32)
        low = rest - middle
        terms = jnp.where(extra == 0, high, jnp.where(extra == 1, middle, jnp.where(extra == 2, low, 0.0)))
        to_ref[ifgs:, :] = terms.astype(jnp.bfloat16)


def setup_track(pair_rows, other_rows):
    ifgs = pair_rows.shape[0]
    size = -(-EPOCHS // LANES) * LANES
    vmem = pl.BlockSpec(memory_space=pltpu.VMEM)
    return pl.pallas_call(
        operator_kernel,
        in_specs=[vmem] * 2,
        out_specs=[vmem] * 3,
        out_shape=[jax.ShapeDtypeStruct((ifgs + EXTRA, ifgs), jnp.bfloat16)] * 2 + [token],
        scratch_shapes=[pltpu.VMEM((size, size), jnp.float32), pltpu.VMEM((size, size), jnp.float32)],
        compiler_params=pltpu.CompilerParams(vmem_limit_bytes=medium),
        name="misfit_operator",
    )(pair_rows.T, other_rows.T)


def invert_tiles(stack_refs, first, width, operator_ref, fields_ref, base):
    ifgs = operator_ref.shape[1]
    for start in range(0, width, TILE):
        here = pl.ds(pl.multiple_of(first + start, LANES), TILE)
        stack = jnp.concatenate([ref[:, here] for ref in stack_refs], axis=0)
        product = jnp.dot(operator_ref[...], stack, preferred_element_type=jnp.float32)
        velocity = jnp.sum(product[ifgs : ifgs + 8], axis=0, keepdims=True)
        variance = jnp.sum(product[:ifgs] * product[:ifgs], axis=0, keepdims=True) / ifgs
        for k in range(TILE // LANES):
            row = pl.ds(base + start // LANES + k, 1)
            fields_ref[0, row, :] = velocity[:, k * LANES : (k + 1) * LANES]
            fields_ref[1, row, :] = variance[:, k * LANES : (k + 1) * LANES]


def pick(source, lane):
    return jnp.take_along_axis(source, lane, axis=1, mode="promise_in_bounds")


def resample(near, cell, index_ref, weight_ref):
    lanes = lax.broadcasted_iota(jnp.int32, (8, LANES), 1)
    here = pl.ds(cell, 8)
    sums = [jnp.zeros((8, LANES), jnp.float32)] * 2
    total = jnp.zeros((8, LANES), jnp.float32)
    for b in range(index_ref.shape[0]):
        weight = weight_ref[b, here, :]
        place = lanes + index_ref[b, here, :] + HALO
        lane = place & (LANES - 1)
        which = place >> 7
        total = total + weight
        for f in range(2):
            low, mid, high = (pick(near[f][k], lane) for k in range(3))
            taken = jnp.where(which == 0, low, jnp.where(which == 1, mid, high))
            sums[f] = sums[f] + taken * weight
    return sums[0] / total, sums[1] / total, total


def boundary(row, offsets, weights, sources, wanted):
    lanes = lax.broadcasted_iota(jnp.int32, (8, LANES), 1)
    rows = lax.broadcasted_iota(jnp.int32, (8, LANES), 0)
    sums = [jnp.zeros((8, LANES), jnp.float32)] * 2
    for offset, weight in zip(offsets, weights):
        place = lanes + offset + HALO
        lane = place & (LANES - 1)
        keep = jnp.where(jnp.logical_and(place >> 7 == wanted, rows == row), weight, 0.0)
        for f in range(2):
            sums[f] = sums[f] + pick(jnp.broadcast_to(sources[f], (8, LANES)), lane) * keep
    return sums


def store_cells(out_ref, at, velocity, variance, cover, north, north_c):
    out_ref[0, at : at + 8, :] = cover / (variance + prior_var)
    out_ref[1, at : at + 8, :] = velocity - north_c * north


def fixed_kernel(tiles, index_ref, weight_ref, cover_ref, north_ref, back_ref, onward_ref):
    taps, rows, _ = index_ref.shape
    place = lax.broadcasted_iota(jnp.int32, (tiles, LANES), 0) == lax.broadcasted_iota(jnp.int32, (tiles, LANES), 1)
    for half, to_ref in enumerate((back_ref, onward_ref)):
        edge = slice(half * (rows - tiles), half * (rows - tiles) + tiles)
        outermost = half * (rows - 1)
        row = slice(outermost, outermost + 1)
        to_ref[:tiles, :] = north_ref[edge, :]
        total = sum(weight_ref[b, row, :] for b in range(taps))
        for b in range(taps):
            to_ref[tiles + b : tiles + b + 1, :] = index_ref[b, row, :].astype(jnp.float32)
            to_ref[tiles + taps + b : tiles + taps + b + 1, :] = weight_ref[b, row, :] / total
        at = tiles + 2 * taps
        cover = jnp.where(place, jnp.broadcast_to(cover_ref[edge, :].astype(jnp.float32), (tiles, LANES)), 0.0)
        to_ref[at : at + 1, :] = jnp.sum(cover, axis=0, keepdims=True)
        to_ref[at + 1 :, :] = jnp.zeros((to_ref.shape[0] - at - 1, LANES), jnp.float32)


def fixed(cells, tiles):
    rows = -(-(tiles + 2 * cells[0].shape[0] + 1) // 8) * 8
    vmem = pl.BlockSpec(memory_space=pltpu.VMEM)
    return pl.pallas_call(
        functools.partial(fixed_kernel, tiles),
        in_specs=[vmem] * 4,
        out_specs=[vmem] * 2,
        out_shape=[jax.ShapeDtypeStruct((rows, LANES), jnp.float32)] * 2,
        compiler_params=pltpu.CompilerParams(vmem_limit_bytes=medium),
        name="edge_inputs",
    )(*cells)


def edges_kernel(tiles, group, los_ref, *refs):
    stack_refs = refs[:group]
    operator_ref, index_ref, weight_ref, *fixed_refs, kept_ref, back_ref, onward_ref, fields_ref = refs[group:]
    width = stack_refs[0].shape[1]
    count = width // LANES
    rows = index_ref.shape[1]
    none = jnp.zeros((2, 1, LANES), jnp.float32)
    fields_ref[:, :1, :] = none
    fields_ref[:, count + 1 : count + 2, :] = none
    invert_tiles(stack_refs, 0, width, operator_ref, fields_ref, 1)
    seam = 2 * tiles
    kept_ref[:, seam : seam + 4, :] = fields_ref[:, tiles : tiles + 4, :]
    kept_ref[:, seam + 4 : seam + 5, :] = fields_ref[:, 1:2, :]
    kept_ref[:, seam + 5 : seam + 6, :] = fields_ref[:, count : count + 1, :]
    kept_ref[:, seam + 6 :, :] = jnp.zeros((2, kept_ref.shape[1] - seam - 6, LANES), jnp.float32)
    tracks = los_ref.shape[0]
    scalars = [los_ref[t, part] for part in (0, 2) for t in range(tracks)] + [los_ref[lax.axis_index("track"), 1]]
    for k, scalar in enumerate(scalars):
        row = seam + 8 + k
        kept_ref[0, row : row + 1, :] = jnp.full((1, LANES), scalar, jnp.float32)
    for half, (fixed_ref, to_ref) in enumerate(zip(fixed_refs, (back_ref, onward_ref))):
        first = half * (rows - tiles)
        after = to_ref.shape[0] - fixed_ref.shape[0]
        to_ref[after:, :] = fixed_ref[...]
        for r in range(0, tiles, 8):
            base = half * (tiles + 2) + r
            near = [[fields_ref[f, base + k : base + k + 8, :] for k in range(3)] for f in range(2)]
            velocity, variance, _ = resample(near, first + r, index_ref, weight_ref)
            for f, values in enumerate((velocity, variance)):
                kept_ref[f, half * tiles + r : half * tiles + r + 8, :] = values
                to_ref[f * tiles + r : f * tiles + r + 8, :] = values
        for f in range(2):
            to_ref[seam + f : seam + f + 1, :] = kept_ref[f, seam + 4 + half : seam + 5 + half, :]
        to_ref[seam + 2 : after, :] = jnp.zeros((after - seam - 2, LANES), jnp.float32)


def edges(los, stacks, operator, cells, both_fixed, tiles):
    rows = 2 * (tiles + 1)
    payload = -(-(2 * tiles + 2) // 8) * 8 + both_fixed[0].shape[0]
    sight = -(-(2 * los.shape[0] + 1) // 8) * 8
    shapes = [(2, 2 * tiles + 8 + sight, LANES), (payload, LANES), (payload, LANES)]
    vmem = pl.BlockSpec(memory_space=pltpu.VMEM)
    return pl.pallas_call(
        functools.partial(edges_kernel, tiles, len(stacks)),
        in_specs=[pl.BlockSpec(memory_space=pltpu.SMEM)] + [vmem] * (len(stacks) + 5),
        out_specs=[vmem] * 3,
        out_shape=[jax.ShapeDtypeStruct(shape, jnp.float32) for shape in shapes],
        scratch_shapes=[pltpu.VMEM((2, -(-(rows + 2) // 8) * 8, LANES), jnp.float32)],
        compiler_params=pltpu.CompilerParams(vmem_limit_bytes=medium),
        cost_estimate=pl.CostEstimate(flops=EDGE_COST, bytes_accessed=0, transcendentals=0),
        name="edge_rows",
    )(los, *stacks, operator, *cells[:2], *both_fixed)


def finish_kernel(
    tiles, tracks, kept_ref, before_ref, after_ref, index_ref, weight_ref, cover_ref, north_ref, out_ref
):
    taps, rows, _ = index_ref.shape
    seam = 2 * tiles
    north_c = kept_ref[0, seam + 8 + 2 * tracks : seam + 9 + 2 * tracks, :]
    place = lax.broadcasted_iota(jnp.int32, (8, LANES), 0) - lax.broadcasted_iota(jnp.int32, (8, LANES), 1)
    for half, from_ref in enumerate((before_ref, after_ref)):
        fixed_ref = from_ref.at[-(-(seam + 2) // 8) * 8 :]
        edge = half * (tiles - 8)
        row = 7 * half
        outermost = half * (rows - 1)
        total = sum(weight_ref[b, outermost : outermost + 1, :] for b in range(taps))
        to_own = boundary(
            row,
            [index_ref[b, outermost : outermost + 1, :] for b in range(taps)],
            [weight_ref[b, outermost : outermost + 1, :] / total for b in range(taps)],
            [from_ref[seam + f : seam + f + 1, :] for f in range(2)],
            2 * half,
        )
        to_other = boundary(
            7 - row,
            [fixed_ref[tiles + b : tiles + b + 1, :].astype(jnp.int32) for b in range(taps)],
            [fixed_ref[tiles + taps + b : tiles + taps + b + 1, :] for b in range(taps)],
            [kept_ref[f, seam + 4 + half : seam + 5 + half, :] for f in range(2)],
            2 - 2 * half,
        )
        covers = fixed_ref[tiles + 2 * taps : tiles + 2 * taps + 1, :]
        for r in range(0, tiles, 8):
            first = half * (rows - tiles) + r
            values = [kept_ref[f, half * tiles + r : half * tiles + r + 8, :] for f in range(2)]
            if r == edge:
                values = [value + more for value, more in zip(values, to_own)]
            cover = cover_ref[first : first + 8, :].astype(jnp.float32)
            store_cells(out_ref, (1 + half) * tiles + r, *values, cover, north_ref[first : first + 8, :], north_c)
            values = [from_ref[f * tiles + r : f * tiles + r + 8, :] for f in range(2)]
            if r == tiles - 8 - edge:
                values = [value + more for value, more in zip(values, to_other)]
            cover = jnp.sum(jnp.where(place == -r, jnp.broadcast_to(covers, (8, LANES)), 0.0), axis=1, keepdims=True)
            store_cells(out_ref, 3 * half * tiles + r, *values, cover, fixed_ref[r : r + 8, :], north_c)
    out_ref[:, 4 * tiles :, :] = kept_ref[:, seam:, :]


def finish(kept, before, after, cells, tiles, tracks):
    vmem = pl.BlockSpec(memory_space=pltpu.VMEM)
    return pl.pallas_call(
        functools.partial(finish_kernel, tiles, tracks),
        in_specs=[vmem] * 7,
        out_specs=vmem,
        out_shape=jax.ShapeDtypeStruct((2, kept.shape[1] + 2 * tiles, LANES), jnp.float32),
        compiler_params=pltpu.CompilerParams(vmem_limit_bytes=medium),
        name="edge_cells",
    )(kept, before, after, *cells)


def inner_kernel(
    tiles, tracks, stack_ref, edge_ref, operator_ref, index_ref, weight_ref, cover_ref, north_ref, out_ref, sight_ref, fields_ref
):
    width = stack_ref.shape[1]
    rows = index_ref.shape[1]
    seam = 4 * tiles
    sight_ref[...] = edge_ref[0, seam + 8 :, :]
    north_c = edge_ref[0, seam + 8 + 2 * tracks : seam + 9 + 2 * tracks, :]
    pixel_rows = width // LANES
    fields_ref[:, 0:2, :] = edge_ref[:, seam : seam + 2, :]
    fields_ref[:, pixel_rows + 2 : pixel_rows + 4, :] = edge_ref[:, seam + 2 : seam + 4, :]
    out_ref[:, : 2 * tiles, :] = edge_ref[:, : 2 * tiles, :]
    out_ref[:, rows:, :] = edge_ref[:, 2 * tiles : 4 * tiles, :]
    invert_tiles([stack_ref], 0, width, operator_ref, fields_ref, 2)
    for r in range(0, rows - 2 * tiles, 8):
        near = [[fields_ref[f, r + k : r + k + 8, :] for k in range(3)] for f in range(2)]
        first = tiles + r
        velocity, variance, _ = resample(near, first, index_ref, weight_ref)
        cover = cover_ref[first : first + 8, :].astype(jnp.float32)
        store_cells(out_ref, tiles + first, velocity, variance, cover, north_ref[first : first + 8, :], north_c)


def inner(stack, edge, operator, cells, tiles, tracks):
    rows = cells[0].shape[1]
    vmem = pl.BlockSpec(memory_space=pltpu.VMEM)
    return pl.pallas_call(
        functools.partial(inner_kernel, tiles, tracks),
        in_specs=[vmem] * 7,
        out_specs=[vmem] * 2,
        out_shape=[
            jax.ShapeDtypeStruct((2, rows + 2 * tiles, LANES), jnp.float32),
            jax.ShapeDtypeStruct((edge.shape[1] - 4 * tiles - 8, LANES), jnp.float32),
        ],
        scratch_shapes=[pltpu.VMEM((2, -(-(rows - 2 * tiles + 2) // 8) * 8, LANES), jnp.float32)],
        compiler_params=pltpu.CompilerParams(vmem_limit_bytes=medium),
        name="inner_rows",
    )(stack, edge, operator, *cells)


def solve_cells(of_tracks, sight_ref, tracks):
    a11 = a12 = a22 = b1 = b2 = 0.0
    for t, values_ref in of_tracks:
        weight, target = values_ref[0], values_ref[1]
        east_c, up_c = sight_ref[pl.ds(t, 1), :], sight_ref[pl.ds(tracks + t, 1), :]
        by_east, by_up = weight * east_c, weight * up_c
        a11 = a11 + by_east * east_c
        a12 = a12 + by_east * up_c
        a22 = a22 + by_up * up_c
        b1 = b1 + by_east * target
        b2 = b2 + by_up * target
    a11 = a11 + ridge_term
    a22 = a22 + ridge_term
    determ = a11 * a22 - a12 * a12
    return (a22 * b1 - a12 * b2) / determ, (a11 * b2 - a12 * b1) / determ


def final_kernel(tiles, own, tracks, sight_ref, own_ref, other_ref, north_ref, before_ref, after_ref, east_up_ref, strain_ref, work_ref):
    rows = north_ref.shape[0]
    lane = lax.broadcasted_iota(jnp.int32, (rows, LANES), 1)
    tile = lax.broadcasted_iota(jnp.int32, (rows, LANES), 0) % tiles

    def across(field):
        right = jnp.where(tile == tiles - 1, 0.0, pltpu.roll(field, rows - 1, 0))
        left = jnp.where(tile == 0, 0.0, pltpu.roll(field, 1, 0))
        following = jnp.where(lane == LANES - 1, pltpu.roll(right, LANES - 1, 1), pltpu.roll(field, LANES - 1, 1))
        previous = jnp.where(lane == 0, pltpu.roll(left, 1, 1), pltpu.roll(field, 1, 1))
        return following - previous

    here = lax.axis_index("track")
    if other_ref.shape[0] == 1:
        of_tracks = [(here, own_ref), (1 - here, other_ref.at[0])]
    else:
        of_tracks = [(t, other_ref.at[t]) for t in range(other_ref.shape[0])]
    wide_east, wide_up = solve_cells(of_tracks, sight_ref, tracks)
    at = -(-(2 * tiles + 2) // 8) * 8
    wide_north = jnp.concatenate([before_ref[at : at + tiles, :], north_ref[...], after_ref[at : at + tiles, :]], axis=0)
    east, north = (wide[tiles : tiles + rows] for wide in (wide_east, wide_north))
    work_ref[0] = east
    work_ref[1] = wide_up[tiles : tiles + rows]
    work_ref[2] = across(east) / 2.0
    work_ref[3] = (wide_north[2 * tiles :] - wide_north[:rows]) / 2.0
    work_ref[4] = (wide_east[2 * tiles :] - wide_east[:rows] + across(north)) / 4.0
    start = here * own
    for field in range(5):
        target, at = (east_up_ref, field) if field < 2 else (strain_ref, field - 2)
        for i in range(rows // tiles):
            for j in range(own):
                target[at, i : i + 1, j * LANES : (j + 1) * LANES] = work_ref[field, pl.ds(i * tiles + start + j, 1), :]


def final(sight, vals, others, north, before, after, tiles, own, tracks):
    rows = north.shape[0]
    shape = (rows // tiles, own * LANES)
    vmem = pl.BlockSpec(memory_space=pltpu.VMEM)
    return pl.pallas_call(
        functools.partial(final_kernel, tiles, own, tracks),
        in_specs=[vmem] * 6,
        out_specs=[vmem] * 2,
        out_shape=[jax.ShapeDtypeStruct((2, *shape), jnp.float32), jax.ShapeDtypeStruct((3, *shape), jnp.float32)],
        scratch_shapes=[pltpu.VMEM((5, rows, LANES), jnp.float32)],
        compiler_params=pltpu.CompilerParams(vmem_limit_bytes=medium),
        name="solve_and_strain",
    )(sight, vals, others, north, before, after)


def per_device(phases, coherent, pairs, res_index, res_weight, coverage, los, north):
    parts = lax.axis_size("pix")
    tracks = lax.axis_size("track")
    grid_rows, columns = north.shape
    tiles = columns // CTILE
    rows = grid_rows * tiles
    group = GROUP if parts % GROUP == 0 else parts
    planes = parts // group
    plane, column = jnp.divmod(lax.axis_index("pix").astype(jnp.int32), group)
    *packed, packed_token = pack_edges(phases[0], coherent[0], parts, group, tiles)
    later_pairs, _ = lax.optimization_barrier((pairs[0], packed_token))
    steps_j, steps_s = jnp.meshgrid(jnp.arange(group), jnp.arange(planes), indexing="ij")
    sources = (partner_back(plane, steps_s, planes) * group + partner_back(column, steps_j, group)).reshape(-1)
    edge_pairs = jnp.take(later_pairs.reshape(parts, -1, 2), sources, axis=0).reshape(-1, 2)
    operator, edge_operator, formed_token = setup_track(later_pairs, edge_pairs)
    ids = [(z, c) for z in range(planes) for c in range(group)]
    arrived = [packed[0]] * planes
    for s in reversed(range(1, planes)):
        far = [(z * group + c, partner(z, s, planes) * group + c) for z, c in ids]
        arrived[s] = lax.ppermute(packed[s], "pix", far)
    by_column = regroup(formed_token, arrived, group)
    pieces = [by_column[0]]
    for j in range(1, group):
        near = [(z * group + c, z * group + partner(c, j, group)) for z, c in ids]
        pieces.append(lax.ppermute(by_column[j], "pix", near))
    later_flags, *_ = lax.optimization_barrier((coherent[0], formed_token))
    inner_stack = lax.all_to_all(
        pack_inner(phases[0], later_flags, parts, tiles), "pix", split_axis=0, concat_axis=0, tiled=True
    )
    north_cells = north.reshape(rows, LANES)
    cells = (
        res_index.reshape(-1, rows, LANES),
        res_weight.reshape(-1, rows, LANES),
        coverage.reshape(rows, 1),
        north_cells,
    )

    def flat(stack):
        return stack.reshape(-1, stack.shape[-1])

    onward = [(i, i + 1) for i in range(parts - 1)]
    back = [(j, i) for i, j in onward]
    kept, for_before, for_after = edges(
        los, [flat(piece) for piece in pieces], edge_operator, cells, fixed(cells, tiles), tiles
    )
    before = lax.ppermute(for_after, "pix", onward)
    after = lax.ppermute(for_before, "pix", back)
    edge_vals = finish(kept, before, after, cells, tiles, tracks)
    vals, sight = inner(flat(inner_stack), edge_vals, operator, cells, tiles, tracks)
    if tracks == 2:
        others = lax.ppermute(vals, "track", [(0, 1), (1, 0)])[None]
    else:
        others = lax.all_gather(vals, "track", axis=0)
    return tuple(final(sight, vals, others, north_cells, before, after, tiles, tiles // tracks, tracks))


def solution(mesh):
    in_specs = (
        P("track", "pix", None),
        P("track", "pix", None),
        P("track", None, None),
        P("track", None, "pix"),
        P("track", None, "pix"),
        P("track", "pix", None),
        P(),
        P("pix", None),
    )
    out_specs = (P(None, "pix", "track"), P(None, "pix", "track"))
    return jax.shard_map(
        per_device, mesh=mesh, in_specs=in_specs, out_specs=out_specs, check_vma=False
    )
```

```python
import functools

import jax
import jax.numpy as jnp
from jax import lax
from jax.experimental import pallas as pl
from jax.experimental.pallas import tpu as pltpu
from jax.sharding import PartitionSpec as P

EPOCHS = 200
EXTRA = 16
HALO = 128
CTILE = 128
MBLK = 128
LANES = 128
TILE = 256
GROUP = 4
EDGE_COST = 54_000_000_000

token = jax.ShapeDtypeStruct((8, LANES), jnp.float32)


prior_var = 0.1
ridge_term = 0.5
medium = 24 * 1024 * 1024


def stay(array):
    return pltpu.with_memory_space_constraint(array, pltpu.HBM)


def expand_masks(flags_ref, stacked_ref, firsts, wanted, tile_out):
    ifgs = flags_ref.shape[0]
    for n, first in enumerate(firsts):
        stacked_ref[n * ifgs : (n + 1) * ifgs, :] = part_flags(flags_ref, first)
    stacked = stacked_ref[...].astype(jnp.bfloat16)
    block = lax.broadcasted_iota(jnp.int32, (LANES, 2 * MBLK), 0)
    right = lax.broadcasted_iota(jnp.int32, (LANES, 2 * MBLK), 1) >= MBLK
    for start in range(0, len(wanted), 2):
        here = jnp.where(right, wanted[start + 1], wanted[start])
        ones = (block == here).astype(jnp.bfloat16)
        keep = jnp.dot(stacked, ones, preferred_element_type=jnp.float32).astype(jnp.bfloat16)
        for n in range(len(firsts)):
            tile_out(n, start * MBLK, keep[n * ifgs : (n + 1) * ifgs])


def part_flags(flags_ref, first):
    lead = pl.multiple_of(first // LANES * LANES, LANES)
    flags = (flags_ref[:, pl.ds(lead, LANES)] == 1).astype(jnp.float32)
    return pltpu.roll(flags, (LANES - (first - lead)) % LANES, 1)


def partner(index, step, size):
    return index ^ step if size & (size - 1) == 0 else (index + step) % size


def partner_back(index, step, size):
    return index ^ step if size & (size - 1) == 0 else (index - step + size) % size


def pack_edges_kernel(tiles, group, flags_hbm, phases_ref, *refs):
    *out_refs, token_ref, flags_ref, stacked_ref, near_ref, flag_sem, in_sem = refs
    token_ref[...] = jnp.zeros_like(token_ref)
    planes = len(out_refs)
    parts = planes * group
    ifgs, blocks = flags_ref.shape
    span = blocks // parts
    reach = tiles + 1
    half = reach * MBLK
    flag_copy = pltpu.make_async_copy(flags_hbm, flags_ref, flag_sem)
    flag_copy.start()
    ends = [
        pltpu.make_async_copy(phases_ref.at[:, pl.ds(0, half)], near_ref.at[0, :, pl.ds(half, half)], in_sem.at[0]),
        pltpu.make_async_copy(
            phases_ref.at[:, pl.ds(blocks * MBLK - half, half)], near_ref.at[parts, :, pl.ds(0, half)], in_sem.at[parts]
        ),
    ]

    def between(b):
        low = pl.multiple_of((span * b - reach) * MBLK, MBLK)
        return pltpu.make_async_copy(phases_ref.at[:, pl.ds(low, 2 * half)], near_ref.at[b], in_sem.at[b])

    ends[0].start()

    @pl.loop(1, parts)
    def _(b):
        between(b).start()

    ends[1].start()
    flag_copy.wait()
    plane = lax.axis_index("pix") // group
    firsts = [(partner(plane, -s % planes, planes) * group + g) * span for s in range(planes) for g in range(group)]

    def tile_out(n, start, keep):
        out_refs[n // group][n % group, :, start : start + 2 * MBLK] = keep

    wanted = [k if k < reach else span - 2 * reach + k for k in range(2 * reach)]
    expand_masks(flags_ref, stacked_ref, firsts, wanted, tile_out)
    ends[0].wait()

    @pl.loop(1, parts)
    def _(b):
        between(b).wait()

    ends[1].wait()
    for s in range(planes):
        first_part = partner(plane, -s % planes, planes) * group

        @pl.loop(0, group, unroll=2)
        def _(g):
            out_refs[s][g, :, :half] *= near_ref[first_part + g, :, half:]
            out_refs[s][g, :, half:] *= near_ref[first_part + g + 1, :, :half]


def pack_edges(phases, flags, parts, group, tiles):
    ifgs = phases.shape[0]
    planes = parts // group
    hbm = pl.BlockSpec(memory_space=pltpu.HBM)
    width = 2 * (tiles + 1) * MBLK
    return pl.pallas_call(
        functools.partial(pack_edges_kernel, tiles, group),
        in_specs=[hbm, hbm],
        out_specs=[pl.BlockSpec(memory_space=pltpu.VMEM)] * (planes + 1),
        out_shape=[jax.ShapeDtypeStruct((group, ifgs, width), jnp.bfloat16)] * planes + [token],
        scratch_shapes=[
            pltpu.VMEM(flags.shape, jnp.int32),
            pltpu.VMEM((parts * ifgs, LANES), jnp.float32),
            pltpu.VMEM((parts + 1, ifgs, 2 * (tiles + 1) * MBLK), jnp.bfloat16),
            pltpu.SemaphoreType.DMA,
            pltpu.SemaphoreType.DMA((parts + 1,)),
        ],
        compiler_params=pltpu.CompilerParams(vmem_limit_bytes=medium),
        name="pack_edges",
    )(stay(flags), stay(phases))


def regroup_kernel(planes, group, after_ref, *refs):
    in_refs, out_refs = refs[:planes], refs[planes:]
    for j in range(group):
        column = partner(lax.rem(lax.axis_index("pix"), group), j, group)
        for s in range(planes):
            out_refs[j][s] = in_refs[s][column]


def regroup(after, pieces, group):
    planes = len(pieces)
    vmem = pl.BlockSpec(memory_space=pltpu.VMEM)
    shape = (planes, *pieces[0].shape[1:])
    return pl.pallas_call(
        functools.partial(regroup_kernel, planes, group),
        in_specs=[vmem] * (planes + 1),
        out_specs=[vmem] * group,
        out_shape=[jax.ShapeDtypeStruct(shape, jnp.bfloat16)] * group,
        compiler_params=pltpu.CompilerParams(vmem_limit_bytes=medium),
        name="regroup",
    )(after, *pieces)


def pack_inner_kernel(reach, flags_hbm, phases_ref, out_ref, flags_ref, stacked_ref, held_ref, flag_sem, in_sem):
    parts, ifgs, width = out_ref.shape
    span = flags_ref.shape[1] // parts
    flag_copy = pltpu.make_async_copy(flags_hbm, flags_ref, flag_sem)
    flag_copy.start()

    def inward(p):
        low = pl.multiple_of((p * span + reach) * MBLK, MBLK)
        return pltpu.make_async_copy(phases_ref.at[:, pl.ds(low, width)], held_ref.at[p], in_sem.at[p])

    @pl.loop(0, parts)
    def _(p):
        inward(p).start()

    flag_copy.wait()

    def tile_out(n, start, keep):
        out_ref[n, :, start : start + 2 * MBLK] = keep

    wanted = list(range(reach, span - reach))
    expand_masks(flags_ref, stacked_ref, [p * span for p in range(parts)], wanted, tile_out)

    @pl.loop(0, parts)
    def _(p):
        inward(p).wait()
        out_ref[p] *= held_ref[p]


def pack_inner(phases, flags, parts, tiles):
    ifgs = phases.shape[0]
    reach = tiles + 1
    width = (flags.shape[1] // parts - 2 * reach) * MBLK
    hbm = pl.BlockSpec(memory_space=pltpu.HBM)
    return pl.pallas_call(
        functools.partial(pack_inner_kernel, reach),
        in_specs=[hbm, hbm],
        out_specs=pl.BlockSpec(memory_space=pltpu.VMEM),
        out_shape=jax.ShapeDtypeStruct((parts, ifgs, width), jnp.bfloat16),
        scratch_shapes=[
            pltpu.VMEM(flags.shape, jnp.int32),
            pltpu.VMEM((parts * ifgs, LANES), jnp.float32),
            pltpu.VMEM((parts, ifgs, width), jnp.bfloat16),
            pltpu.SemaphoreType.DMA,
            pltpu.SemaphoreType.DMA((parts,)),
        ],
        compiler_params=pltpu.CompilerParams(vmem_limit_bytes=medium),
        name="pack_inner",
    )(stay(flags), stay(phases))


def exact_dot(a, b):
    return jnp.dot(a, b, precision=lax.Precision.HIGHEST, preferred_element_type=jnp.float32)


def operator_kernel(pairs_ref, other_ref, out_ref, other_out_ref, token_ref, normal_ref, inverse_ref):
    token_ref[...] = jnp.zeros_like(token_ref)
    ifgs = pairs_ref.shape[1]
    size = normal_ref.shape[0]
    epoch = lax.broadcasted_iota(jnp.int32, (size, ifgs), 0)

    def ends(ref):
        return (epoch == ref[1:2, :]).astype(jnp.float32) - (epoch == ref[0:1, :]).astype(jnp.float32)

    across = ends(pairs_ref)
    down = across.T
    eye = (
        lax.broadcasted_iota(jnp.int32, (size, size), 0) == lax.broadcasted_iota(jnp.int32, (size, size), 1)
    ).astype(jnp.float32)
    normal = eye + jnp.dot(
        across.astype(jnp.bfloat16), down.astype(jnp.bfloat16), preferred_element_type=jnp.float32
    )
    normal_ref[...] = normal
    inverse_ref[...] = eye / jnp.where(eye == 1.0, normal, 1.0)

    def unfinished(state):
        step, gap = state
        return jnp.logical_and(step < 24, gap > 1e-5)

    def improve(state):
        step, _ = state
        inverse = inverse_ref[...]
        rest = eye - exact_dot(normal_ref[...], inverse)
        inverse_ref[...] = inverse + exact_dot(inverse, rest)
        return step + 1, jnp.max(jnp.abs(rest))

    lax.while_loop(unfinished, improve, (jnp.int32(0), jnp.float32(1.0)))
    place = lax.broadcasted_iota(jnp.int32, (size, ifgs), 0)
    centred = place.astype(jnp.float32) - (EPOCHS - 1) / 2.0
    square = sum((e - (EPOCHS - 1) / 2.0) ** 2 for e in range(EPOCHS))
    slope = jnp.where(place < EPOCHS, centred * (EPOCHS - 1) / square, 0.0)
    same = lax.broadcasted_iota(jnp.int32, (ifgs, ifgs), 0) == lax.broadcasted_iota(jnp.int32, (ifgs, ifgs), 1)
    extra = lax.broadcasted_iota(jnp.int32, (EXTRA, ifgs), 0)
    for ref, to_ref in ((pairs_ref, out_ref), (other_ref, other_out_ref)):
        across = ends(ref)
        pseudo = exact_dot(inverse_ref[...], across).astype(jnp.bfloat16)
        fitted = jnp.dot(across.T.astype(jnp.bfloat16), pseudo, preferred_element_type=jnp.float32)
        to_ref[:ifgs, :] = (same.astype(jnp.float32) - fitted).astype(jnp.bfloat16)
        row = jnp.sum(pseudo.astype(jnp.float32) * slope, axis=0, keepdims=True)
        high = row.astype(jnp.bfloat16).astype(jnp.float32)
        rest = row - high
        middle = rest.astype(jnp.bfloat16).astype(jnp.float32)
        low = rest - middle
        terms = jnp.where(extra == 0, high, jnp.where(extra == 1, middle, jnp.where(extra == 2, low, 0.0)))
        to_ref[ifgs:, :] = terms.astype(jnp.bfloat16)


def setup_track(pair_rows, other_rows):
    ifgs = pair_rows.shape[0]
    size = -(-EPOCHS // LANES) * LANES
    vmem = pl.BlockSpec(memory_space=pltpu.VMEM)
    return pl.pallas_call(
        operator_kernel,
        in_specs=[vmem] * 2,
        out_specs=[vmem] * 3,
        out_shape=[jax.ShapeDtypeStruct((ifgs + EXTRA, ifgs), jnp.bfloat16)] * 2 + [token],
        scratch_shapes=[pltpu.VMEM((size, size), jnp.float32), pltpu.VMEM((size, size), jnp.float32)],
        compiler_params=pltpu.CompilerParams(vmem_limit_bytes=medium),
        name="misfit_operator",
    )(pair_rows.T, other_rows.T)


def invert_tiles(stack_refs, first, width, operator_ref, fields_ref, base):
    ifgs = operator_ref.shape[1]
    for start in range(0, width, TILE):
        here = pl.ds(pl.multiple_of(first + start, LANES), TILE)
        stack = jnp.concatenate([ref[:, here] for ref in stack_refs], axis=0)
        product = jnp.dot(operator_ref[...], stack, preferred_element_type=jnp.float32)
        velocity = jnp.sum(product[ifgs : ifgs + 8], axis=0, keepdims=True)
        variance = jnp.sum(product[:ifgs] * product[:ifgs], axis=0, keepdims=True) / ifgs
        for k in range(TILE // LANES):
            row = pl.ds(base + start // LANES + k, 1)
            fields_ref[0, row, :] = velocity[:, k * LANES : (k + 1) * LANES]
            fields_ref[1, row, :] = variance[:, k * LANES : (k + 1) * LANES]


def pick(source, lane):
    return jnp.take_along_axis(source, lane, axis=1, mode="promise_in_bounds")


def resample(near, cell, index_ref, weight_ref):
    lanes = lax.broadcasted_iota(jnp.int32, (8, LANES), 1)
    here = pl.ds(cell, 8)
    sums = [jnp.zeros((8, LANES), jnp.float32)] * 2
    total = jnp.zeros((8, LANES), jnp.float32)
    for b in range(index_ref.shape[0]):
        weight = weight_ref[b, here, :]
        place = lanes + index_ref[b, here, :] + HALO
        lane = place & (LANES - 1)
        which = place >> 7
        total = total + weight
        for f in range(2):
            low, mid, high = (pick(near[f][k], lane) for k in range(3))
            taken = jnp.where(which == 0, low, jnp.where(which == 1, mid, high))
            sums[f] = sums[f] + taken * weight
    return sums[0] / total, sums[1] / total, total


def boundary(row, offsets, weights, sources, wanted):
    lanes = lax.broadcasted_iota(jnp.int32, (8, LANES), 1)
    rows = lax.broadcasted_iota(jnp.int32, (8, LANES), 0)
    sums = [jnp.zeros((8, LANES), jnp.float32)] * 2
    for offset, weight in zip(offsets, weights):
        place = lanes + offset + HALO
        lane = place & (LANES - 1)
        keep = jnp.where(jnp.logical_and(place >> 7 == wanted, rows == row), weight, 0.0)
        for f in range(2):
            sums[f] = sums[f] + pick(jnp.broadcast_to(sources[f], (8, LANES)), lane) * keep
    return sums


def store_cells(out_ref, at, velocity, variance, cover, north, north_c):
    out_ref[0, at : at + 8, :] = cover / (variance + prior_var)
    out_ref[1, at : at + 8, :] = velocity - north_c * north


def fixed_kernel(tiles, index_ref, weight_ref, cover_ref, north_ref, back_ref, onward_ref):
    taps, rows, _ = index_ref.shape
    place = lax.broadcasted_iota(jnp.int32, (tiles, LANES), 0) == lax.broadcasted_iota(jnp.int32, (tiles, LANES), 1)
    for half, to_ref in enumerate((back_ref, onward_ref)):
        edge = slice(half * (rows - tiles), half * (rows - tiles) + tiles)
        outermost = half * (rows - 1)
        row = slice(outermost, outermost + 1)
        to_ref[:tiles, :] = north_ref[edge, :]
        total = sum(weight_ref[b, row, :] for b in range(taps))
        for b in range(taps):
            to_ref[tiles + b : tiles + b + 1, :] = index_ref[b, row, :].astype(jnp.float32)
            to_ref[tiles + taps + b : tiles + taps + b + 1, :] = weight_ref[b, row, :] / total
        at = tiles + 2 * taps
        cover = jnp.where(place, jnp.broadcast_to(cover_ref[edge, :].astype(jnp.float32), (tiles, LANES)), 0.0)
        to_ref[at : at + 1, :] = jnp.sum(cover, axis=0, keepdims=True)
        to_ref[at + 1 :, :] = jnp.zeros((to_ref.shape[0] - at - 1, LANES), jnp.float32)


def fixed(cells, tiles):
    rows = -(-(tiles + 2 * cells[0].shape[0] + 1) // 8) * 8
    vmem = pl.BlockSpec(memory_space=pltpu.VMEM)
    return pl.pallas_call(
        functools.partial(fixed_kernel, tiles),
        in_specs=[vmem] * 4,
        out_specs=[vmem] * 2,
        out_shape=[jax.ShapeDtypeStruct((rows, LANES), jnp.float32)] * 2,
        compiler_params=pltpu.CompilerParams(vmem_limit_bytes=medium),
        name="edge_inputs",
    )(*cells)


def edges_kernel(tiles, group, los_ref, *refs):
    stack_refs = refs[:group]
    operator_ref, index_ref, weight_ref, *fixed_refs, kept_ref, back_ref, onward_ref, fields_ref = refs[group:]
    width = stack_refs[0].shape[1]
    count = width // LANES
    rows = index_ref.shape[1]
    none = jnp.zeros((2, 1, LANES), jnp.float32)
    fields_ref[:, :1, :] = none
    fields_ref[:, count + 1 : count + 2, :] = none
    invert_tiles(stack_refs, 0, width, operator_ref, fields_ref, 1)
    seam = 2 * tiles
    kept_ref[:, seam : seam + 4, :] = fields_ref[:, tiles : tiles + 4, :]
    kept_ref[:, seam + 4 : seam + 5, :] = fields_ref[:, 1:2, :]
    kept_ref[:, seam + 5 : seam + 6, :] = fields_ref[:, count : count + 1, :]
    kept_ref[:, seam + 6 :, :] = jnp.zeros((2, kept_ref.shape[1] - seam - 6, LANES), jnp.float32)
    tracks = los_ref.shape[0]
    scalars = [los_ref[t, part] for part in (0, 2) for t in range(tracks)] + [los_ref[lax.axis_index("track"), 1]]
    for k, scalar in enumerate(scalars):
        row = seam + 8 + k
        kept_ref[0, row : row + 1, :] = jnp.full((1, LANES), scalar, jnp.float32)
    for half, (fixed_ref, to_ref) in enumerate(zip(fixed_refs, (back_ref, onward_ref))):
        first = half * (rows - tiles)
        after = to_ref.shape[0] - fixed_ref.shape[0]
        to_ref[after:, :] = fixed_ref[...]
        for r in range(0, tiles, 8):
            base = half * (tiles + 2) + r
            near = [[fields_ref[f, base + k : base + k + 8, :] for k in range(3)] for f in range(2)]
            velocity, variance, _ = resample(near, first + r, index_ref, weight_ref)
            for f, values in enumerate((velocity, variance)):
                kept_ref[f, half * tiles + r : half * tiles + r + 8, :] = values
                to_ref[f * tiles + r : f * tiles + r + 8, :] = values
        for f in range(2):
            to_ref[seam + f : seam + f + 1, :] = kept_ref[f, seam + 4 + half : seam + 5 + half, :]
        to_ref[seam + 2 : after, :] = jnp.zeros((after - seam - 2, LANES), jnp.float32)


def edges(los, stacks, operator, cells, both_fixed, tiles):
    rows = 2 * (tiles + 1)
    payload = -(-(2 * tiles + 2) // 8) * 8 + both_fixed[0].shape[0]
    sight = -(-(2 * los.shape[0] + 1) // 8) * 8
    shapes = [(2, 2 * tiles + 8 + sight, LANES), (payload, LANES), (payload, LANES)]
    vmem = pl.BlockSpec(memory_space=pltpu.VMEM)
    return pl.pallas_call(
        functools.partial(edges_kernel, tiles, len(stacks)),
        in_specs=[pl.BlockSpec(memory_space=pltpu.SMEM)] + [vmem] * (len(stacks) + 5),
        out_specs=[vmem] * 3,
        out_shape=[jax.ShapeDtypeStruct(shape, jnp.float32) for shape in shapes],
        scratch_shapes=[pltpu.VMEM((2, -(-(rows + 2) // 8) * 8, LANES), jnp.float32)],
        compiler_params=pltpu.CompilerParams(vmem_limit_bytes=medium),
        cost_estimate=pl.CostEstimate(flops=EDGE_COST, bytes_accessed=0, transcendentals=0),
        name="edge_rows",
    )(los, *stacks, operator, *cells[:2], *both_fixed)


def finish_kernel(
    tiles, tracks, kept_ref, before_ref, after_ref, index_ref, weight_ref, cover_ref, north_ref, out_ref
):
    taps, rows, _ = index_ref.shape
    seam = 2 * tiles
    north_c = kept_ref[0, seam + 8 + 2 * tracks : seam + 9 + 2 * tracks, :]
    place = lax.broadcasted_iota(jnp.int32, (8, LANES), 0) - lax.broadcasted_iota(jnp.int32, (8, LANES), 1)
    for half, from_ref in enumerate((before_ref, after_ref)):
        fixed_ref = from_ref.at[-(-(seam + 2) // 8) * 8 :]
        edge = half * (tiles - 8)
        row = 7 * half
        outermost = half * (rows - 1)
        total = sum(weight_ref[b, outermost : outermost + 1, :] for b in range(taps))
        to_own = boundary(
            row,
            [index_ref[b, outermost : outermost + 1, :] for b in range(taps)],
            [weight_ref[b, outermost : outermost + 1, :] / total for b in range(taps)],
            [from_ref[seam + f : seam + f + 1, :] for f in range(2)],
            2 * half,
        )
        to_other = boundary(
            7 - row,
            [fixed_ref[tiles + b : tiles + b + 1, :].astype(jnp.int32) for b in range(taps)],
            [fixed_ref[tiles + taps + b : tiles + taps + b + 1, :] for b in range(taps)],
            [kept_ref[f, seam + 4 + half : seam + 5 + half, :] for f in range(2)],
            2 - 2 * half,
        )
        covers = fixed_ref[tiles + 2 * taps : tiles + 2 * taps + 1, :]
        for r in range(0, tiles, 8):
            first = half * (rows - tiles) + r
            values = [kept_ref[f, half * tiles + r : half * tiles + r + 8, :] for f in range(2)]
            if r == edge:
                values = [value + more for value, more in zip(values, to_own)]
            cover = cover_ref[first : first + 8, :].astype(jnp.float32)
            store_cells(out_ref, (1 + half) * tiles + r, *values, cover, north_ref[first : first + 8, :], north_c)
            values = [from_ref[f * tiles + r : f * tiles + r + 8, :] for f in range(2)]
            if r == tiles - 8 - edge:
                values = [value + more for value, more in zip(values, to_other)]
            cover = jnp.sum(jnp.where(place == -r, jnp.broadcast_to(covers, (8, LANES)), 0.0), axis=1, keepdims=True)
            store_cells(out_ref, 3 * half * tiles + r, *values, cover, fixed_ref[r : r + 8, :], north_c)
    out_ref[:, 4 * tiles :, :] = kept_ref[:, seam:, :]


def finish(kept, before, after, cells, tiles, tracks):
    vmem = pl.BlockSpec(memory_space=pltpu.VMEM)
    return pl.pallas_call(
        functools.partial(finish_kernel, tiles, tracks),
        in_specs=[vmem] * 7,
        out_specs=vmem,
        out_shape=jax.ShapeDtypeStruct((2, kept.shape[1] + 2 * tiles, LANES), jnp.float32),
        compiler_params=pltpu.CompilerParams(vmem_limit_bytes=medium),
        name="edge_cells",
    )(kept, before, after, *cells)


def inner_kernel(
    tiles, tracks, span, stack_ref, edge_ref, operator_ref, index_ref, weight_ref, cover_ref, north_ref, *refs
):
    *to_refs, sight_ref, fields_ref, out_ref = refs
    width = stack_ref.shape[1]
    rows = index_ref.shape[1]
    seam = 4 * tiles
    sight_ref[...] = edge_ref[0, seam + 8 :, :]
    north_c = edge_ref[0, seam + 8 + 2 * tracks : seam + 9 + 2 * tracks, :]
    pixel_rows = width // LANES
    fields_ref[:, 0:2, :] = edge_ref[:, seam : seam + 2, :]
    fields_ref[:, pixel_rows + 2 : pixel_rows + 4, :] = edge_ref[:, seam + 2 : seam + 4, :]
    out_ref[:, : 2 * tiles, :] = edge_ref[:, : 2 * tiles, :]
    out_ref[:, rows:, :] = edge_ref[:, 2 * tiles : 4 * tiles, :]
    invert_tiles([stack_ref], 0, width, operator_ref, fields_ref, 2)
    for r in range(0, rows - 2 * tiles, 8):
        near = [[fields_ref[f, r + k : r + k + 8, :] for k in range(3)] for f in range(2)]
        first = tiles + r
        velocity, variance, _ = resample(near, first, index_ref, weight_ref)
        cover = cover_ref[first : first + 8, :].astype(jnp.float32)
        store_cells(out_ref, tiles + first, velocity, variance, cover, north_ref[first : first + 8, :], north_c)


    here = lax.axis_index("track")
    lines = rows // tiles + 2
    for half, to_ref in zip((here, 1 - here), to_refs):
        start = half * (tiles - span)
        for i in range(lines):
            to_ref[:, i * span : (i + 1) * span, :] = out_ref[:, pl.ds(i * tiles + start, span), :]
        left = to_ref.shape[1] - lines * span
        if left:
            to_ref[:, lines * span :, :] = jnp.zeros((2, left, LANES), jnp.float32)


def inner(stack, edge, operator, cells, tiles, tracks, span, copies):
    rows = cells[0].shape[1]
    compact = -(-(rows // tiles + 2) * span // 8) * 8
    vmem = pl.BlockSpec(memory_space=pltpu.VMEM)
    return pl.pallas_call(
        functools.partial(inner_kernel, tiles, tracks, span),
        in_specs=[vmem] * 7,
        out_specs=[vmem] * (copies + 1),
        out_shape=[jax.ShapeDtypeStruct((2, compact, LANES), jnp.float32)] * copies
        + [jax.ShapeDtypeStruct((edge.shape[1] - 4 * tiles - 8, LANES), jnp.float32)],
        scratch_shapes=[
            pltpu.VMEM((2, -(-(rows - 2 * tiles + 2) // 8) * 8, LANES), jnp.float32),
            pltpu.VMEM((2, rows + 2 * tiles, LANES), jnp.float32),
        ],
        compiler_params=pltpu.CompilerParams(vmem_limit_bytes=medium),
        name="inner_rows",
    )(stack, edge, operator, *cells)


def solve_cells(of_tracks, sight_ref, tracks):
    a11 = a12 = a22 = b1 = b2 = 0.0
    for t, values_ref in of_tracks:
        weight, target = values_ref[0], values_ref[1]
        east_c, up_c = sight_ref[pl.ds(t, 1), :], sight_ref[pl.ds(tracks + t, 1), :]
        by_east, by_up = weight * east_c, weight * up_c
        a11 = a11 + by_east * east_c
        a12 = a12 + by_east * up_c
        a22 = a22 + by_up * up_c
        b1 = b1 + by_east * target
        b2 = b2 + by_up * target
    a11 = a11 + ridge_term
    a22 = a22 + ridge_term
    determ = a11 * a22 - a12 * a12
    return (a22 * b1 - a12 * b2) / determ, (a11 * b2 - a12 * b1) / determ


def final_kernel(
    tiles, span, own, tracks, sight_ref, own_ref, other_ref, north_ref, before_ref, after_ref, east_up_ref, strain_ref, work_ref, line_ref
):
    lines = north_ref.shape[0] // tiles
    rows = lines * span
    here = lax.axis_index("track")
    start = here * (tiles - span)
    at = -(-(2 * tiles + 2) // 8) * 8 + start
    line_ref[:span, :] = before_ref[pl.ds(at, span), :]
    for i in range(lines):
        line_ref[(i + 1) * span : (i + 2) * span, :] = north_ref[pl.ds(i * tiles + start, span), :]
    line_ref[rows + span : rows + 2 * span, :] = after_ref[pl.ds(at, span), :]
    lane = lax.broadcasted_iota(jnp.int32, (rows, LANES), 1)
    tile = lax.broadcasted_iota(jnp.int32, (rows, LANES), 0) % span

    def across(field):
        right = jnp.where(tile == span - 1, 0.0, pltpu.roll(field, rows - 1, 0))
        left = jnp.where(tile == 0, 0.0, pltpu.roll(field, 1, 0))
        following = jnp.where(lane == LANES - 1, pltpu.roll(right, LANES - 1, 1), pltpu.roll(field, LANES - 1, 1))
        previous = jnp.where(lane == 0, pltpu.roll(left, 1, 1), pltpu.roll(field, 1, 1))
        return following - previous

    if other_ref.shape[0] == 1:
        of_tracks = [(here, own_ref), (1 - here, other_ref.at[0])]
    else:
        of_tracks = [(t, other_ref.at[t]) for t in range(other_ref.shape[0])]
    wide_east, wide_up = solve_cells(of_tracks, sight_ref, tracks)
    wide_north = line_ref[...]
    east, up, north = (wide[span : span + rows] for wide in (wide_east, wide_up, wide_north))
    work_ref[0] = east
    work_ref[1] = up
    work_ref[2] = across(east) / 2.0
    work_ref[3] = (wide_north[2 * span : 2 * span + rows] - wide_north[:rows]) / 2.0
    work_ref[4] = (wide_east[2 * span : 2 * span + rows] - wide_east[:rows] + across(north)) / 4.0
    first = here * own - start
    for field in range(5):
        target, at = (east_up_ref, field) if field < 2 else (strain_ref, field - 2)
        for i in range(lines):
            for j in range(own):
                target[at, i : i + 1, j * LANES : (j + 1) * LANES] = work_ref[field, pl.ds(i * span + first + j, 1), :]


def final(sight, vals, others, north, before, after, tiles, span, own, tracks):
    lines = north.shape[0] // tiles
    shape = (lines, own * LANES)
    vmem = pl.BlockSpec(memory_space=pltpu.VMEM)
    return pl.pallas_call(
        functools.partial(final_kernel, tiles, span, own, tracks),
        in_specs=[vmem] * 6,
        out_specs=[vmem] * 2,
        out_shape=[jax.ShapeDtypeStruct((2, *shape), jnp.float32), jax.ShapeDtypeStruct((3, *shape), jnp.float32)],
        scratch_shapes=[pltpu.VMEM((5, lines * span, LANES), jnp.float32), pltpu.VMEM(vals.shape[1:], jnp.float32)],
        compiler_params=pltpu.CompilerParams(vmem_limit_bytes=medium),
        name="solve_and_strain",
    )(sight, vals, others, north, before, after)


def per_device(phases, coherent, pairs, res_index, res_weight, coverage, los, north):
    parts = lax.axis_size("pix")
    tracks = lax.axis_size("track")
    grid_rows, columns = north.shape
    tiles = columns // CTILE
    rows = grid_rows * tiles
    group = GROUP if parts % GROUP == 0 else parts
    planes = parts // group
    plane, column = jnp.divmod(lax.axis_index("pix").astype(jnp.int32), group)
    *packed, packed_token = pack_edges(phases[0], coherent[0], parts, group, tiles)
    later_pairs, _ = lax.optimization_barrier((pairs[0], packed_token))
    steps_j, steps_s = jnp.meshgrid(jnp.arange(group), jnp.arange(planes), indexing="ij")
    sources = (partner_back(plane, -steps_s % planes, planes) * group + partner_back(column, steps_j, group)).reshape(-1)
    edge_pairs = jnp.take(later_pairs.reshape(parts, -1, 2), sources, axis=0).reshape(-1, 2)
    operator, edge_operator, formed_token = setup_track(later_pairs, edge_pairs)
    ids = [(z, c) for z in range(planes) for c in range(group)]
    arrived = [packed[0]] * planes
    for s in range(1, planes):
        far = [(z * group + c, partner(z, planes - s, planes) * group + c) for z, c in ids]
        arrived[s] = lax.ppermute(packed[s], "pix", far)
    by_column = regroup(formed_token, arrived, group)
    pieces = [by_column[0]]
    for j in range(1, group):
        near = [(z * group + c, z * group + partner(c, j, group)) for z, c in ids]
        pieces.append(lax.ppermute(by_column[j], "pix", near))
    later_flags, *_ = lax.optimization_barrier((coherent[0], formed_token))
    inner_stack = lax.all_to_all(
        pack_inner(phases[0], later_flags, parts, tiles), "pix", split_axis=0, concat_axis=0, tiled=True
    )
    north_cells = north.reshape(rows, LANES)
    cells = (
        res_index.reshape(-1, rows, LANES),
        res_weight.reshape(-1, rows, LANES),
        coverage.reshape(rows, 1),
        north_cells,
    )

    def flat(stack):
        return stack.reshape(-1, stack.shape[-1])

    onward = [(i, i + 1) for i in range(parts - 1)]
    back = [(j, i) for i, j in onward]
    kept, for_before, for_after = edges(
        los, [flat(piece) for piece in pieces], edge_operator, cells, fixed(cells, tiles), tiles
    )
    before = lax.ppermute(for_after, "pix", onward)
    after = lax.ppermute(for_before, "pix", back)
    edge_vals = finish(kept, before, after, cells, tiles, tracks)
    own_tiles = tiles // tracks
    if tracks == 2:
        span = own_tiles + 1
        vals, for_other, sight = inner(flat(inner_stack), edge_vals, operator, cells, tiles, tracks, span, 2)
        others = lax.ppermute(for_other, "track", [(0, 1), (1, 0)])[None]
    else:
        span = tiles
        vals, sight = inner(flat(inner_stack), edge_vals, operator, cells, tiles, tracks, span, 1)
        others = lax.all_gather(vals, "track", axis=0)
    return tuple(final(sight, vals, others, north_cells, before, after, tiles, span, own_tiles, tracks))


def solution(mesh):
    in_specs = (
        P("track", "pix", None),
        P("track", "pix", None),
        P("track", None, None),
        P("track", None, "pix"),
        P("track", None, "pix"),
        P("track", "pix", None),
        P(),
        P("pix", None),
    )
    out_specs = (P(None, "pix", "track"), P(None, "pix", "track"))
    return jax.shard_map(
        per_device, mesh=mesh, in_specs=in_specs, out_specs=out_specs, check_vma=False
    )
```

```python
import functools

import jax
import jax.numpy as jnp
from jax import lax
from jax.experimental import pallas as pl
from jax.experimental.pallas import tpu as pltpu
from jax.sharding import PartitionSpec as P

EPOCHS = 200
EXTRA = 16
HALO = 128
CTILE = 128
MBLK = 128
LANES = 128
TILE = 256
GROUP = 4
EDGE_COST = 54_000_000_000

token = jax.ShapeDtypeStruct((8, LANES), jnp.float32)


prior_var = 0.1
ridge_term = 0.5
medium = 24 * 1024 * 1024


def stay(array):
    return pltpu.with_memory_space_constraint(array, pltpu.HBM)


def expand_masks(flags_ref, stacked_ref, firsts, wanted, tile_out):
    ifgs = flags_ref.shape[0]
    for n, first in enumerate(firsts):
        stacked_ref[n * ifgs : (n + 1) * ifgs, :] = part_flags(flags_ref, first)
    stacked = stacked_ref[...].astype(jnp.bfloat16)
    block = lax.broadcasted_iota(jnp.int32, (LANES, 2 * MBLK), 0)
    right = lax.broadcasted_iota(jnp.int32, (LANES, 2 * MBLK), 1) >= MBLK
    for start in range(0, len(wanted), 2):
        here = jnp.where(right, wanted[start + 1], wanted[start])
        ones = (block == here).astype(jnp.bfloat16)
        keep = jnp.dot(stacked, ones, preferred_element_type=jnp.float32).astype(jnp.bfloat16)
        for n in range(len(firsts)):
            tile_out(n, start * MBLK, keep[n * ifgs : (n + 1) * ifgs])


def part_flags(flags_ref, first):
    lead = pl.multiple_of(first // LANES * LANES, LANES)
    flags = (flags_ref[:, pl.ds(lead, LANES)] == 1).astype(jnp.float32)
    return pltpu.roll(flags, (LANES - (first - lead)) % LANES, 1)


def partner(index, step, size):
    return index ^ step if size & (size - 1) == 0 else (index + step) % size


def partner_back(index, step, size):
    return index ^ step if size & (size - 1) == 0 else (index - step + size) % size


def pack_edges_kernel(tiles, group, flags_hbm, phases_ref, *refs):
    *out_refs, token_ref, flags_ref, stacked_ref, near_ref, flag_sem, in_sem = refs
    token_ref[...] = jnp.zeros_like(token_ref)
    planes = len(out_refs)
    parts = planes * group
    ifgs, blocks = flags_ref.shape
    span = blocks // parts
    reach = tiles + 1
    half = reach * MBLK
    flag_copy = pltpu.make_async_copy(flags_hbm, flags_ref, flag_sem)
    flag_copy.start()
    ends = [
        pltpu.make_async_copy(phases_ref.at[:, pl.ds(0, half)], near_ref.at[0, :, pl.ds(half, half)], in_sem.at[0]),
        pltpu.make_async_copy(
            phases_ref.at[:, pl.ds(blocks * MBLK - half, half)], near_ref.at[parts, :, pl.ds(0, half)], in_sem.at[parts]
        ),
    ]

    def between(b):
        low = pl.multiple_of((span * b - reach) * MBLK, MBLK)
        return pltpu.make_async_copy(phases_ref.at[:, pl.ds(low, 2 * half)], near_ref.at[b], in_sem.at[b])

    ends[0].start()

    @pl.loop(1, parts)
    def _(b):
        between(b).start()

    ends[1].start()
    flag_copy.wait()
    plane = lax.axis_index("pix") // group
    firsts = [(partner(plane, -s % planes, planes) * group + g) * span for s in range(planes) for g in range(group)]

    def tile_out(n, start, keep):
        out_refs[n // group][n % group, :, start : start + 2 * MBLK] = keep

    wanted = [k if k < reach else span - 2 * reach + k for k in range(2 * reach)]
    expand_masks(flags_ref, stacked_ref, firsts, wanted, tile_out)
    ends[0].wait()

    @pl.loop(1, parts)
    def _(b):
        between(b).wait()

    ends[1].wait()
    for s in range(planes):
        first_part = partner(plane, -s % planes, planes) * group

        @pl.loop(0, group, unroll=2)
        def _(g):
            out_refs[s][g, :, :half] *= near_ref[first_part + g, :, half:]
            out_refs[s][g, :, half:] *= near_ref[first_part + g + 1, :, :half]


def pack_edges(phases, flags, parts, group, tiles):
    ifgs = phases.shape[0]
    planes = parts // group
    hbm = pl.BlockSpec(memory_space=pltpu.HBM)
    width = 2 * (tiles + 1) * MBLK
    return pl.pallas_call(
        functools.partial(pack_edges_kernel, tiles, group),
        in_specs=[hbm, hbm],
        out_specs=[pl.BlockSpec(memory_space=pltpu.VMEM)] * (planes + 1),
        out_shape=[jax.ShapeDtypeStruct((group, ifgs, width), jnp.bfloat16)] * planes + [token],
        scratch_shapes=[
            pltpu.VMEM(flags.shape, jnp.int32),
            pltpu.VMEM((parts * ifgs, LANES), jnp.float32),
            pltpu.VMEM((parts + 1, ifgs, 2 * (tiles + 1) * MBLK), jnp.bfloat16),
            pltpu.SemaphoreType.DMA,
            pltpu.SemaphoreType.DMA((parts + 1,)),
        ],
        compiler_params=pltpu.CompilerParams(vmem_limit_bytes=medium),
        name="pack_edges",
    )(stay(flags), stay(phases))


def regroup_kernel(planes, group, after_ref, *refs):
    in_refs, out_refs = refs[:planes], refs[planes:]
    for j in range(group):
        column = partner(lax.rem(lax.axis_index("pix"), group), j, group)
        for s in range(planes):
            out_refs[j][s] = in_refs[s][column]


def regroup(after, pieces, group):
    planes = len(pieces)
    vmem = pl.BlockSpec(memory_space=pltpu.VMEM)
    shape = (planes, *pieces[0].shape[1:])
    return pl.pallas_call(
        functools.partial(regroup_kernel, planes, group),
        in_specs=[vmem] * (planes + 1),
        out_specs=[vmem] * group,
        out_shape=[jax.ShapeDtypeStruct(shape, jnp.bfloat16)] * group,
        compiler_params=pltpu.CompilerParams(vmem_limit_bytes=medium),
        name="regroup",
    )(after, *pieces)


def pack_inner_kernel(reach, flags_hbm, phases_ref, out_ref, flags_ref, stacked_ref, held_ref, flag_sem, in_sem):
    parts, ifgs, width = out_ref.shape
    span = flags_ref.shape[1] // parts
    flag_copy = pltpu.make_async_copy(flags_hbm, flags_ref, flag_sem)
    flag_copy.start()

    def inward(p):
        low = pl.multiple_of((p * span + reach) * MBLK, MBLK)
        return pltpu.make_async_copy(phases_ref.at[:, pl.ds(low, width)], held_ref.at[p], in_sem.at[p])

    @pl.loop(0, parts)
    def _(p):
        inward(p).start()

    flag_copy.wait()

    def tile_out(n, start, keep):
        out_ref[n, :, start : start + 2 * MBLK] = keep

    wanted = list(range(reach, span - reach))
    expand_masks(flags_ref, stacked_ref, [p * span for p in range(parts)], wanted, tile_out)

    @pl.loop(0, parts)
    def _(p):
        inward(p).wait()
        out_ref[p] *= held_ref[p]


def pack_inner(phases, flags, parts, tiles):
    ifgs = phases.shape[0]
    reach = tiles + 1
    width = (flags.shape[1] // parts - 2 * reach) * MBLK
    hbm = pl.BlockSpec(memory_space=pltpu.HBM)
    return pl.pallas_call(
        functools.partial(pack_inner_kernel, reach),
        in_specs=[hbm, hbm],
        out_specs=pl.BlockSpec(memory_space=pltpu.VMEM),
        out_shape=jax.ShapeDtypeStruct((parts, ifgs, width), jnp.bfloat16),
        scratch_shapes=[
            pltpu.VMEM(flags.shape, jnp.int32),
            pltpu.VMEM((parts * ifgs, LANES), jnp.float32),
            pltpu.VMEM((parts, ifgs, width), jnp.bfloat16),
            pltpu.SemaphoreType.DMA,
            pltpu.SemaphoreType.DMA((parts,)),
        ],
        compiler_params=pltpu.CompilerParams(vmem_limit_bytes=medium),
        name="pack_inner",
    )(stay(flags), stay(phases))


def split(a, terms):
    parts = []
    for _ in range(terms):
        parts.append(a.astype(jnp.bfloat16))
        a = a - parts[-1].astype(jnp.float32)
    return parts


def sum_dots(pairs):
    return sum(jnp.dot(a, b, preferred_element_type=jnp.float32) for a, b in pairs)


def operator_kernel(pairs_ref, other_ref, out_ref, other_out_ref, token_ref, laplacian_ref, inverse_ref):
    token_ref[...] = jnp.zeros_like(token_ref)
    ifgs = pairs_ref.shape[1]
    size = inverse_ref.shape[0]
    epoch = lax.broadcasted_iota(jnp.int32, (size, ifgs), 0)

    def ends(ref):
        return (epoch == ref[1:2, :]).astype(jnp.float32) - (epoch == ref[0:1, :]).astype(jnp.float32)

    across = ends(pairs_ref)
    down = across.T
    eye = (
        lax.broadcasted_iota(jnp.int32, (size, size), 0) == lax.broadcasted_iota(jnp.int32, (size, size), 1)
    ).astype(jnp.float32)
    laplacian = jnp.dot(across.astype(jnp.bfloat16), down.astype(jnp.bfloat16), preferred_element_type=jnp.float32)
    normal = eye + laplacian
    laplacian_ref[...] = laplacian.astype(jnp.bfloat16)
    first = eye / jnp.where(eye == 1.0, normal, 1.0)
    scaled = jnp.sum(first, axis=1, keepdims=True) * normal * jnp.sum(first, axis=0, keepdims=True)
    inverse_ref[...] = 2.0 * first - scaled

    def unfinished(state):
        step, gap = state
        return jnp.logical_and(step < 24, gap > 1e-5)

    def improve(state):
        step, _ = state
        inverse = inverse_ref[...]
        parts = split(inverse, 3)
        rest = eye - inverse - sum_dots((laplacian_ref[...], part) for part in parts)
        high, low = split(rest, 2)
        inverse_ref[...] = inverse + sum_dots(((parts[0], low), (parts[1], high), (parts[0], high)))
        return step + 1, jnp.max(jnp.abs(rest))

    lax.while_loop(unfinished, improve, (jnp.int32(0), jnp.float32(1.0)))
    place = lax.broadcasted_iota(jnp.int32, (size, ifgs), 0)
    centred = place.astype(jnp.float32) - (EPOCHS - 1) / 2.0
    square = sum((e - (EPOCHS - 1) / 2.0) ** 2 for e in range(EPOCHS))
    slope = jnp.where(place < EPOCHS, centred * (EPOCHS - 1) / square, 0.0)
    same = lax.broadcasted_iota(jnp.int32, (ifgs, ifgs), 0) == lax.broadcasted_iota(jnp.int32, (ifgs, ifgs), 1)
    extra = lax.broadcasted_iota(jnp.int32, (EXTRA, ifgs), 0)
    for ref, to_ref in ((pairs_ref, out_ref), (other_ref, other_out_ref)):
        across = ends(ref)
        ones = across.astype(jnp.bfloat16)
        pseudo = sum_dots((part, ones) for part in split(inverse_ref[...], 3)).astype(jnp.bfloat16)
        fitted = jnp.dot(across.T.astype(jnp.bfloat16), pseudo, preferred_element_type=jnp.float32)
        to_ref[:ifgs, :] = (same.astype(jnp.float32) - fitted).astype(jnp.bfloat16)
        row = jnp.sum(pseudo.astype(jnp.float32) * slope, axis=0, keepdims=True)
        high = row.astype(jnp.bfloat16).astype(jnp.float32)
        rest = row - high
        middle = rest.astype(jnp.bfloat16).astype(jnp.float32)
        low = rest - middle
        terms = jnp.where(extra == 0, high, jnp.where(extra == 1, middle, jnp.where(extra == 2, low, 0.0)))
        to_ref[ifgs:, :] = terms.astype(jnp.bfloat16)


def setup_track(pair_rows, other_rows):
    ifgs = pair_rows.shape[0]
    size = -(-EPOCHS // LANES) * LANES
    vmem = pl.BlockSpec(memory_space=pltpu.VMEM)
    return pl.pallas_call(
        operator_kernel,
        in_specs=[vmem] * 2,
        out_specs=[vmem] * 3,
        out_shape=[jax.ShapeDtypeStruct((ifgs + EXTRA, ifgs), jnp.bfloat16)] * 2 + [token],
        scratch_shapes=[pltpu.VMEM((size, size), jnp.bfloat16), pltpu.VMEM((size, size), jnp.float32)],
        compiler_params=pltpu.CompilerParams(vmem_limit_bytes=medium),
        name="misfit_operator",
    )(pair_rows.T, other_rows.T)


def invert_tiles(stack_refs, first, width, operator_ref, fields_ref, base):
    ifgs = operator_ref.shape[1]
    for start in range(0, width, TILE):
        here = pl.ds(pl.multiple_of(first + start, LANES), TILE)
        stack = jnp.concatenate([ref[:, here] for ref in stack_refs], axis=0)
        product = jnp.dot(operator_ref[...], stack, preferred_element_type=jnp.float32)
        velocity = jnp.sum(product[ifgs : ifgs + 8], axis=0, keepdims=True)
        variance = jnp.sum(product[:ifgs] * product[:ifgs], axis=0, keepdims=True) / ifgs
        for k in range(TILE // LANES):
            row = pl.ds(base + start // LANES + k, 1)
            fields_ref[0, row, :] = velocity[:, k * LANES : (k + 1) * LANES]
            fields_ref[1, row, :] = variance[:, k * LANES : (k + 1) * LANES]


def pick(source, lane):
    return jnp.take_along_axis(source, lane, axis=1, mode="promise_in_bounds")


def resample(near, cell, index_ref, weight_ref):
    lanes = lax.broadcasted_iota(jnp.int32, (8, LANES), 1)
    here = pl.ds(cell, 8)
    sums = [jnp.zeros((8, LANES), jnp.float32)] * 2
    total = jnp.zeros((8, LANES), jnp.float32)
    for b in range(index_ref.shape[0]):
        weight = weight_ref[b, here, :]
        place = lanes + index_ref[b, here, :] + HALO
        lane = place & (LANES - 1)
        which = place >> 7
        total = total + weight
        for f in range(2):
            low, mid, high = (pick(near[f][k], lane) for k in range(3))
            taken = jnp.where(which == 0, low, jnp.where(which == 1, mid, high))
            sums[f] = sums[f] + taken * weight
    return sums[0] / total, sums[1] / total, total


def boundary(row, offsets, weights, sources, wanted):
    lanes = lax.broadcasted_iota(jnp.int32, (8, LANES), 1)
    rows = lax.broadcasted_iota(jnp.int32, (8, LANES), 0)
    sums = [jnp.zeros((8, LANES), jnp.float32)] * 2
    for offset, weight in zip(offsets, weights):
        place = lanes + offset + HALO
        lane = place & (LANES - 1)
        keep = jnp.where(jnp.logical_and(place >> 7 == wanted, rows == row), weight, 0.0)
        for f in range(2):
            sums[f] = sums[f] + pick(jnp.broadcast_to(sources[f], (8, LANES)), lane) * keep
    return sums


def store_cells(out_ref, at, velocity, variance, cover, north, north_c):
    out_ref[0, at : at + 8, :] = cover / (variance + prior_var)
    out_ref[1, at : at + 8, :] = velocity - north_c * north


def fixed_kernel(tiles, index_ref, weight_ref, cover_ref, north_ref, back_ref, onward_ref):
    taps, rows, _ = index_ref.shape
    place = lax.broadcasted_iota(jnp.int32, (tiles, LANES), 0) == lax.broadcasted_iota(jnp.int32, (tiles, LANES), 1)
    for half, to_ref in enumerate((back_ref, onward_ref)):
        edge = slice(half * (rows - tiles), half * (rows - tiles) + tiles)
        outermost = half * (rows - 1)
        row = slice(outermost, outermost + 1)
        to_ref[:tiles, :] = north_ref[edge, :]
        total = sum(weight_ref[b, row, :] for b in range(taps))
        for b in range(taps):
            to_ref[tiles + b : tiles + b + 1, :] = index_ref[b, row, :].astype(jnp.float32)
            to_ref[tiles + taps + b : tiles + taps + b + 1, :] = weight_ref[b, row, :] / total
        at = tiles + 2 * taps
        cover = jnp.where(place, jnp.broadcast_to(cover_ref[edge, :].astype(jnp.float32), (tiles, LANES)), 0.0)
        to_ref[at : at + 1, :] = jnp.sum(cover, axis=0, keepdims=True)
        to_ref[at + 1 :, :] = jnp.zeros((to_ref.shape[0] - at - 1, LANES), jnp.float32)


def fixed(cells, tiles):
    rows = -(-(tiles + 2 * cells[0].shape[0] + 1) // 8) * 8
    vmem = pl.BlockSpec(memory_space=pltpu.VMEM)
    return pl.pallas_call(
        functools.partial(fixed_kernel, tiles),
        in_specs=[vmem] * 4,
        out_specs=[vmem] * 2,
        out_shape=[jax.ShapeDtypeStruct((rows, LANES), jnp.float32)] * 2,
        compiler_params=pltpu.CompilerParams(vmem_limit_bytes=medium),
        name="edge_inputs",
    )(*cells)


def edges_kernel(tiles, group, los_ref, *refs):
    stack_refs = refs[:group]
    operator_ref, index_ref, weight_ref, *fixed_refs, kept_ref, back_ref, onward_ref, fields_ref = refs[group:]
    width = stack_refs[0].shape[1]
    count = width // LANES
    rows = index_ref.shape[1]
    none = jnp.zeros((2, 1, LANES), jnp.float32)
    fields_ref[:, :1, :] = none
    fields_ref[:, count + 1 : count + 2, :] = none
    invert_tiles(stack_refs, 0, width, operator_ref, fields_ref, 1)
    seam = 2 * tiles
    kept_ref[:, seam : seam + 4, :] = fields_ref[:, tiles : tiles + 4, :]
    kept_ref[:, seam + 4 : seam + 5, :] = fields_ref[:, 1:2, :]
    kept_ref[:, seam + 5 : seam + 6, :] = fields_ref[:, count : count + 1, :]
    kept_ref[:, seam + 6 :, :] = jnp.zeros((2, kept_ref.shape[1] - seam - 6, LANES), jnp.float32)
    tracks = los_ref.shape[0]
    scalars = [los_ref[t, part] for part in (0, 2) for t in range(tracks)] + [los_ref[lax.axis_index("track"), 1]]
    for k, scalar in enumerate(scalars):
        row = seam + 8 + k
        kept_ref[0, row : row + 1, :] = jnp.full((1, LANES), scalar, jnp.float32)
    for half, (fixed_ref, to_ref) in enumerate(zip(fixed_refs, (back_ref, onward_ref))):
        first = half * (rows - tiles)
        after = to_ref.shape[0] - fixed_ref.shape[0]
        to_ref[after:, :] = fixed_ref[...]
        for r in range(0, tiles, 8):
            base = half * (tiles + 2) + r
            near = [[fields_ref[f, base + k : base + k + 8, :] for k in range(3)] for f in range(2)]
            velocity, variance, _ = resample(near, first + r, index_ref, weight_ref)
            for f, values in enumerate((velocity, variance)):
                kept_ref[f, half * tiles + r : half * tiles + r + 8, :] = values
                to_ref[f * tiles + r : f * tiles + r + 8, :] = values
        for f in range(2):
            to_ref[seam + f : seam + f + 1, :] = kept_ref[f, seam + 4 + half : seam + 5 + half, :]
        to_ref[seam + 2 : after, :] = jnp.zeros((after - seam - 2, LANES), jnp.float32)


def edges(los, stacks, operator, cells, both_fixed, tiles):
    rows = 2 * (tiles + 1)
    payload = -(-(2 * tiles + 2) // 8) * 8 + both_fixed[0].shape[0]
    sight = -(-(2 * los.shape[0] + 1) // 8) * 8
    shapes = [(2, 2 * tiles + 8 + sight, LANES), (payload, LANES), (payload, LANES)]
    vmem = pl.BlockSpec(memory_space=pltpu.VMEM)
    return pl.pallas_call(
        functools.partial(edges_kernel, tiles, len(stacks)),
        in_specs=[pl.BlockSpec(memory_space=pltpu.SMEM)] + [vmem] * (len(stacks) + 5),
        out_specs=[vmem] * 3,
        out_shape=[jax.ShapeDtypeStruct(shape, jnp.float32) for shape in shapes],
        scratch_shapes=[pltpu.VMEM((2, -(-(rows + 2) // 8) * 8, LANES), jnp.float32)],
        compiler_params=pltpu.CompilerParams(vmem_limit_bytes=medium),
        cost_estimate=pl.CostEstimate(flops=EDGE_COST, bytes_accessed=0, transcendentals=0),
        name="edge_rows",
    )(los, *stacks, operator, *cells[:2], *both_fixed)


def finish_kernel(
    tiles, tracks, kept_ref, before_ref, after_ref, index_ref, weight_ref, cover_ref, north_ref, out_ref
):
    taps, rows, _ = index_ref.shape
    seam = 2 * tiles
    north_c = kept_ref[0, seam + 8 + 2 * tracks : seam + 9 + 2 * tracks, :]
    place = lax.broadcasted_iota(jnp.int32, (8, LANES), 0) - lax.broadcasted_iota(jnp.int32, (8, LANES), 1)
    for half, from_ref in enumerate((before_ref, after_ref)):
        fixed_ref = from_ref.at[-(-(seam + 2) // 8) * 8 :]
        edge = half * (tiles - 8)
        row = 7 * half
        outermost = half * (rows - 1)
        total = sum(weight_ref[b, outermost : outermost + 1, :] for b in range(taps))
        to_own = boundary(
            row,
            [index_ref[b, outermost : outermost + 1, :] for b in range(taps)],
            [weight_ref[b, outermost : outermost + 1, :] / total for b in range(taps)],
            [from_ref[seam + f : seam + f + 1, :] for f in range(2)],
            2 * half,
        )
        to_other = boundary(
            7 - row,
            [fixed_ref[tiles + b : tiles + b + 1, :].astype(jnp.int32) for b in range(taps)],
            [fixed_ref[tiles + taps + b : tiles + taps + b + 1, :] for b in range(taps)],
            [kept_ref[f, seam + 4 + half : seam + 5 + half, :] for f in range(2)],
            2 - 2 * half,
        )
        covers = fixed_ref[tiles + 2 * taps : tiles + 2 * taps + 1, :]
        for r in range(0, tiles, 8):
            first = half * (rows - tiles) + r
            values = [kept_ref[f, half * tiles + r : half * tiles + r + 8, :] for f in range(2)]
            if r == edge:
                values = [value + more for value, more in zip(values, to_own)]
            cover = cover_ref[first : first + 8, :].astype(jnp.float32)
            store_cells(out_ref, (1 + half) * tiles + r, *values, cover, north_ref[first : first + 8, :], north_c)
            values = [from_ref[f * tiles + r : f * tiles + r + 8, :] for f in range(2)]
            if r == tiles - 8 - edge:
                values = [value + more for value, more in zip(values, to_other)]
            cover = jnp.sum(jnp.where(place == -r, jnp.broadcast_to(covers, (8, LANES)), 0.0), axis=1, keepdims=True)
            store_cells(out_ref, 3 * half * tiles + r, *values, cover, fixed_ref[r : r + 8, :], north_c)
    out_ref[:, 4 * tiles :, :] = kept_ref[:, seam:, :]


def finish(kept, before, after, cells, tiles, tracks):
    vmem = pl.BlockSpec(memory_space=pltpu.VMEM)
    return pl.pallas_call(
        functools.partial(finish_kernel, tiles, tracks),
        in_specs=[vmem] * 7,
        out_specs=vmem,
        out_shape=jax.ShapeDtypeStruct((2, kept.shape[1] + 2 * tiles, LANES), jnp.float32),
        compiler_params=pltpu.CompilerParams(vmem_limit_bytes=medium),
        name="edge_cells",
    )(kept, before, after, *cells)


def inner_kernel(
    tiles, tracks, span, stack_ref, edge_ref, operator_ref, index_ref, weight_ref, cover_ref, north_ref, *refs
):
    *to_refs, sight_ref, fields_ref, out_ref = refs
    width = stack_ref.shape[1]
    rows = index_ref.shape[1]
    seam = 4 * tiles
    sight_ref[...] = edge_ref[0, seam + 8 :, :]
    north_c = edge_ref[0, seam + 8 + 2 * tracks : seam + 9 + 2 * tracks, :]
    pixel_rows = width // LANES
    fields_ref[:, 0:2, :] = edge_ref[:, seam : seam + 2, :]
    fields_ref[:, pixel_rows + 2 : pixel_rows + 4, :] = edge_ref[:, seam + 2 : seam + 4, :]
    out_ref[:, : 2 * tiles, :] = edge_ref[:, : 2 * tiles, :]
    out_ref[:, rows:, :] = edge_ref[:, 2 * tiles : 4 * tiles, :]
    invert_tiles([stack_ref], 0, width, operator_ref, fields_ref, 2)
    for r in range(0, rows - 2 * tiles, 8):
        near = [[fields_ref[f, r + k : r + k + 8, :] for k in range(3)] for f in range(2)]
        first = tiles + r
        velocity, variance, _ = resample(near, first, index_ref, weight_ref)
        cover = cover_ref[first : first + 8, :].astype(jnp.float32)
        store_cells(out_ref, tiles + first, velocity, variance, cover, north_ref[first : first + 8, :], north_c)


    here = lax.axis_index("track")
    lines = rows // tiles + 2
    for half, to_ref in zip((here, 1 - here), to_refs):
        start = half * (tiles - span)
        for i in range(lines):
            to_ref[:, i * span : (i + 1) * span, :] = out_ref[:, pl.ds(i * tiles + start, span), :]
        left = to_ref.shape[1] - lines * span
        if left:
            to_ref[:, lines * span :, :] = jnp.zeros((2, left, LANES), jnp.float32)


def inner(stack, edge, operator, cells, tiles, tracks, span, copies):
    rows = cells[0].shape[1]
    compact = -(-(rows // tiles + 2) * span // 8) * 8
    vmem = pl.BlockSpec(memory_space=pltpu.VMEM)
    return pl.pallas_call(
        functools.partial(inner_kernel, tiles, tracks, span),
        in_specs=[vmem] * 7,
        out_specs=[vmem] * (copies + 1),
        out_shape=[jax.ShapeDtypeStruct((2, compact, LANES), jnp.float32)] * copies
        + [jax.ShapeDtypeStruct((edge.shape[1] - 4 * tiles - 8, LANES), jnp.float32)],
        scratch_shapes=[
            pltpu.VMEM((2, -(-(rows - 2 * tiles + 2) // 8) * 8, LANES), jnp.float32),
            pltpu.VMEM((2, rows + 2 * tiles, LANES), jnp.float32),
        ],
        compiler_params=pltpu.CompilerParams(vmem_limit_bytes=medium),
        name="inner_rows",
    )(stack, edge, operator, *cells)


def solve_cells(of_tracks, sight_ref, tracks):
    a11 = a12 = a22 = b1 = b2 = 0.0
    for t, values_ref in of_tracks:
        weight, target = values_ref[0], values_ref[1]
        east_c, up_c = sight_ref[pl.ds(t, 1), :], sight_ref[pl.ds(tracks + t, 1), :]
        by_east, by_up = weight * east_c, weight * up_c
        a11 = a11 + by_east * east_c
        a12 = a12 + by_east * up_c
        a22 = a22 + by_up * up_c
        b1 = b1 + by_east * target
        b2 = b2 + by_up * target
    a11 = a11 + ridge_term
    a22 = a22 + ridge_term
    determ = a11 * a22 - a12 * a12
    return (a22 * b1 - a12 * b2) / determ, (a11 * b2 - a12 * b1) / determ


def final_kernel(
    tiles, span, own, tracks, sight_ref, own_ref, other_ref, north_ref, before_ref, after_ref, east_up_ref, strain_ref, work_ref, line_ref
):
    lines = north_ref.shape[0] // tiles
    rows = lines * span
    here = lax.axis_index("track")
    start = here * (tiles - span)
    at = -(-(2 * tiles + 2) // 8) * 8 + start
    line_ref[:span, :] = before_ref[pl.ds(at, span), :]
    for i in range(lines):
        line_ref[(i + 1) * span : (i + 2) * span, :] = north_ref[pl.ds(i * tiles + start, span), :]
    line_ref[rows + span : rows + 2 * span, :] = after_ref[pl.ds(at, span), :]
    lane = lax.broadcasted_iota(jnp.int32, (rows, LANES), 1)
    tile = lax.broadcasted_iota(jnp.int32, (rows, LANES), 0) % span

    def across(field):
        right = jnp.where(tile == span - 1, 0.0, pltpu.roll(field, rows - 1, 0))
        left = jnp.where(tile == 0, 0.0, pltpu.roll(field, 1, 0))
        following = jnp.where(lane == LANES - 1, pltpu.roll(right, LANES - 1, 1), pltpu.roll(field, LANES - 1, 1))
        previous = jnp.where(lane == 0, pltpu.roll(left, 1, 1), pltpu.roll(field, 1, 1))
        return following - previous

    if other_ref.shape[0] == 1:
        of_tracks = [(here, own_ref), (1 - here, other_ref.at[0])]
    else:
        of_tracks = [(t, other_ref.at[t]) for t in range(other_ref.shape[0])]
    wide_east, wide_up = solve_cells(of_tracks, sight_ref, tracks)
    wide_north = line_ref[...]
    east, up, north = (wide[span : span + rows] for wide in (wide_east, wide_up, wide_north))
    work_ref[0] = east
    work_ref[1] = up
    work_ref[2] = across(east) / 2.0
    work_ref[3] = (wide_north[2 * span : 2 * span + rows] - wide_north[:rows]) / 2.0
    work_ref[4] = (wide_east[2 * span : 2 * span + rows] - wide_east[:rows] + across(north)) / 4.0
    first = here * own - start
    for field in range(5):
        target, at = (east_up_ref, field) if field < 2 else (strain_ref, field - 2)
        for i in range(lines):
            for j in range(own):
                target[at, i : i + 1, j * LANES : (j + 1) * LANES] = work_ref[field, pl.ds(i * span + first + j, 1), :]


def final(sight, vals, others, north, before, after, tiles, span, own, tracks):
    lines = north.shape[0] // tiles
    shape = (lines, own * LANES)
    vmem = pl.BlockSpec(memory_space=pltpu.VMEM)
    return pl.pallas_call(
        functools.partial(final_kernel, tiles, span, own, tracks),
        in_specs=[vmem] * 6,
        out_specs=[vmem] * 2,
        out_shape=[jax.ShapeDtypeStruct((2, *shape), jnp.float32), jax.ShapeDtypeStruct((3, *shape), jnp.float32)],
        scratch_shapes=[pltpu.VMEM((5, lines * span, LANES), jnp.float32), pltpu.VMEM(vals.shape[1:], jnp.float32)],
        compiler_params=pltpu.CompilerParams(vmem_limit_bytes=medium),
        name="solve_and_strain",
    )(sight, vals, others, north, before, after)


def per_device(phases, coherent, pairs, res_index, res_weight, coverage, los, north):
    parts = lax.axis_size("pix")
    tracks = lax.axis_size("track")
    grid_rows, columns = north.shape
    tiles = columns // CTILE
    rows = grid_rows * tiles
    group = GROUP if parts % GROUP == 0 else parts
    planes = parts // group
    plane, column = jnp.divmod(lax.axis_index("pix").astype(jnp.int32), group)
    *packed, packed_token = pack_edges(phases[0], coherent[0], parts, group, tiles)
    later_pairs, _ = lax.optimization_barrier((pairs[0], packed_token))
    steps_j, steps_s = jnp.meshgrid(jnp.arange(group), jnp.arange(planes), indexing="ij")
    sources = (partner_back(plane, -steps_s % planes, planes) * group + partner_back(column, steps_j, group)).reshape(-1)
    edge_pairs = jnp.take(later_pairs.reshape(parts, -1, 2), sources, axis=0).reshape(-1, 2)
    operator, edge_operator, formed_token = setup_track(later_pairs, edge_pairs)
    ids = [(z, c) for z in range(planes) for c in range(group)]
    arrived = [packed[0]] * planes
    for s in range(1, planes):
        far = [(z * group + c, partner(z, planes - s, planes) * group + c) for z, c in ids]
        arrived[s] = lax.ppermute(packed[s], "pix", far)
    by_column = regroup(formed_token, arrived, group)
    pieces = [by_column[0]]
    for j in range(1, group):
        near = [(z * group + c, z * group + partner(c, j, group)) for z, c in ids]
        pieces.append(lax.ppermute(by_column[j], "pix", near))
    later_flags, *_ = lax.optimization_barrier((coherent[0], formed_token))
    inner_stack = lax.all_to_all(
        pack_inner(phases[0], later_flags, parts, tiles), "pix", split_axis=0, concat_axis=0, tiled=True
    )
    north_cells = north.reshape(rows, LANES)
    cells = (
        res_index.reshape(-1, rows, LANES),
        res_weight.reshape(-1, rows, LANES),
        coverage.reshape(rows, 1),
        north_cells,
    )

    def flat(stack):
        return stack.reshape(-1, stack.shape[-1])

    onward = [(i, i + 1) for i in range(parts - 1)]
    back = [(j, i) for i, j in onward]
    kept, for_before, for_after = edges(
        los, [flat(piece) for piece in pieces], edge_operator, cells, fixed(cells, tiles), tiles
    )
    before = lax.ppermute(for_after, "pix", onward)
    after = lax.ppermute(for_before, "pix", back)
    edge_vals = finish(kept, before, after, cells, tiles, tracks)
    own_tiles = tiles // tracks
    if tracks == 2:
        span = own_tiles + 1
        vals, for_other, sight = inner(flat(inner_stack), edge_vals, operator, cells, tiles, tracks, span, 2)
        others = lax.ppermute(for_other, "track", [(0, 1), (1, 0)])[None]
    else:
        span = tiles
        vals, sight = inner(flat(inner_stack), edge_vals, operator, cells, tiles, tracks, span, 1)
        others = lax.all_gather(vals, "track", axis=0)
    return tuple(final(sight, vals, others, north_cells, before, after, tiles, span, own_tiles, tracks))


def solution(mesh):
    in_specs = (
        P("track", "pix", None),
        P("track", "pix", None),
        P("track", None, None),
        P("track", None, "pix"),
        P("track", None, "pix"),
        P("track", "pix", None),
        P(),
        P("pix", None),
    )
    out_specs = (P(None, "pix", "track"), P(None, "pix", "track"))
    return jax.shard_map(
        per_device, mesh=mesh, in_specs=in_specs, out_specs=out_specs, check_vma=False
    )
```

```python
import functools

import jax
import jax.numpy as jnp
from jax import lax
from jax.experimental import pallas as pl
from jax.experimental.pallas import tpu as pltpu
from jax.sharding import PartitionSpec as P

EPOCHS = 200
EXTRA = 16
HALO = 128
CTILE = 128
MBLK = 128
LANES = 128
TILE = 256
GROUP = 4
EDGE_COST = 54_000_000_000

token = jax.ShapeDtypeStruct((8, LANES), jnp.float32)


prior_var = 0.1
ridge_term = 0.5
medium = 24 * 1024 * 1024


def stay(array):
    return pltpu.with_memory_space_constraint(array, pltpu.HBM)


def expand_masks(flags_ref, stacked_ref, firsts, wanted, tile_out):
    ifgs = flags_ref.shape[0]
    for n, first in enumerate(firsts):
        stacked_ref[n * ifgs : (n + 1) * ifgs, :] = part_flags(flags_ref, first)
    stacked = stacked_ref[...].astype(jnp.bfloat16)
    block = lax.broadcasted_iota(jnp.int32, (LANES, 2 * MBLK), 0)
    right = lax.broadcasted_iota(jnp.int32, (LANES, 2 * MBLK), 1) >= MBLK
    for start in range(0, len(wanted), 2):
        here = jnp.where(right, wanted[start + 1], wanted[start])
        ones = (block == here).astype(jnp.bfloat16)
        keep = jnp.dot(stacked, ones, preferred_element_type=jnp.float32).astype(jnp.bfloat16)
        for n in range(len(firsts)):
            tile_out(n, start * MBLK, keep[n * ifgs : (n + 1) * ifgs])


def part_flags(flags_ref, first):
    lead = pl.multiple_of(first // LANES * LANES, LANES)
    flags = (flags_ref[:, pl.ds(lead, LANES)] == 1).astype(jnp.float32)
    return pltpu.roll(flags, (LANES - (first - lead)) % LANES, 1)


def partner(index, step, size):
    return index ^ step if size & (size - 1) == 0 else (index + step) % size


def partner_back(index, step, size):
    return index ^ step if size & (size - 1) == 0 else (index - step + size) % size


def pack_edges_kernel(tiles, group, steps, flags_hbm, phases_ref, *refs):
    *out_refs, token_ref, flags_ref, stacked_ref, near_ref, flag_sem, in_sem = refs
    token_ref[...] = jnp.zeros_like(token_ref)
    ifgs, blocks = flags_ref.shape
    reach = tiles + 1
    half = reach * MBLK
    parts = lax.axis_size("pix")
    planes = parts // group
    span = blocks // parts
    flag_copy = pltpu.make_async_copy(flags_hbm, flags_ref, flag_sem)
    flag_copy.start()
    plane = lax.axis_index("pix") // group
    first_parts = [partner(plane, step, planes) * group for step in steps]

    def regions(act):
        for n, first_part in enumerate(first_parts):
            for g in range(group + 1):
                b = first_part + g
                to_ref, sem = near_ref.at[n, g], in_sem.at[n, g]

                @pl.when(b == 0)
                def _():
                    act(pltpu.make_async_copy(phases_ref.at[:, pl.ds(0, half)], to_ref.at[:, pl.ds(half, half)], sem))

                @pl.when(b == parts)
                def _():
                    low = blocks * MBLK - half
                    act(pltpu.make_async_copy(phases_ref.at[:, pl.ds(low, half)], to_ref.at[:, pl.ds(0, half)], sem))

                @pl.when(jnp.logical_and(b > 0, b < parts))
                def _():
                    low = pl.multiple_of((span * jnp.clip(b, 1, parts - 1) - reach) * MBLK, MBLK)
                    act(pltpu.make_async_copy(phases_ref.at[:, pl.ds(low, 2 * half)], to_ref, sem))

    regions(lambda copy: copy.start())
    flag_copy.wait()
    firsts = [(first_part + g) * span for first_part in first_parts for g in range(group)]

    def tile_out(n, start, keep):
        out_refs[n // group][n % group, :, start : start + 2 * MBLK] = keep

    wanted = [k if k < reach else span - 2 * reach + k for k in range(2 * reach)]
    expand_masks(flags_ref, stacked_ref, firsts, wanted, tile_out)
    regions(lambda copy: copy.wait())
    for n, out_ref in enumerate(out_refs):
        for g in range(group):
            out_ref[g, :, :half] *= near_ref[n, g, :, half:]
            out_ref[g, :, half:] *= near_ref[n, g + 1, :, :half]


def pack_edges(phases, flags, group, tiles, steps):
    ifgs = phases.shape[0]
    hbm = pl.BlockSpec(memory_space=pltpu.HBM)
    width = 2 * (tiles + 1) * MBLK
    count = len(steps)
    return pl.pallas_call(
        functools.partial(pack_edges_kernel, tiles, group, steps),
        in_specs=[hbm, hbm],
        out_specs=[pl.BlockSpec(memory_space=pltpu.VMEM)] * (count + 1),
        out_shape=[jax.ShapeDtypeStruct((group, ifgs, width), jnp.bfloat16)] * count + [token],
        scratch_shapes=[
            pltpu.VMEM(flags.shape, jnp.int32),
            pltpu.VMEM((count * group * ifgs, LANES), jnp.float32),
            pltpu.VMEM((count, group + 1, ifgs, width), jnp.bfloat16),
            pltpu.SemaphoreType.DMA,
            pltpu.SemaphoreType.DMA((count, group + 1)),
        ],
        compiler_params=pltpu.CompilerParams(vmem_limit_bytes=medium),
        name="pack_edges",
    )(stay(flags), stay(phases))


def regroup_kernel(planes, group, after_ref, *refs):
    in_refs, out_refs = refs[:planes], refs[planes:]
    for j in range(group):
        column = partner(lax.rem(lax.axis_index("pix"), group), j, group)
        for s in range(planes):
            out_refs[j][s] = in_refs[s][column]


def regroup(after, pieces, group):
    planes = len(pieces)
    vmem = pl.BlockSpec(memory_space=pltpu.VMEM)
    shape = (planes, *pieces[0].shape[1:])
    return pl.pallas_call(
        functools.partial(regroup_kernel, planes, group),
        in_specs=[vmem] * (planes + 1),
        out_specs=[vmem] * group,
        out_shape=[jax.ShapeDtypeStruct(shape, jnp.bfloat16)] * group,
        compiler_params=pltpu.CompilerParams(vmem_limit_bytes=medium),
        name="regroup",
    )(after, *pieces)


def pack_inner_kernel(reach, flags_hbm, phases_ref, out_ref, flags_ref, stacked_ref, held_ref, flag_sem, in_sem):
    parts, ifgs, width = out_ref.shape
    span = flags_ref.shape[1] // parts
    flag_copy = pltpu.make_async_copy(flags_hbm, flags_ref, flag_sem)
    flag_copy.start()

    def inward(p):
        low = pl.multiple_of((p * span + reach) * MBLK, MBLK)
        return pltpu.make_async_copy(phases_ref.at[:, pl.ds(low, width)], held_ref.at[p], in_sem.at[p])

    @pl.loop(0, parts)
    def _(p):
        inward(p).start()

    flag_copy.wait()

    def tile_out(n, start, keep):
        out_ref[n, :, start : start + 2 * MBLK] = keep

    wanted = list(range(reach, span - reach))
    expand_masks(flags_ref, stacked_ref, [p * span for p in range(parts)], wanted, tile_out)

    @pl.loop(0, parts)
    def _(p):
        inward(p).wait()
        out_ref[p] *= held_ref[p]


def pack_inner(phases, flags, parts, tiles):
    ifgs = phases.shape[0]
    reach = tiles + 1
    width = (flags.shape[1] // parts - 2 * reach) * MBLK
    hbm = pl.BlockSpec(memory_space=pltpu.HBM)
    return pl.pallas_call(
        functools.partial(pack_inner_kernel, reach),
        in_specs=[hbm, hbm],
        out_specs=pl.BlockSpec(memory_space=pltpu.VMEM),
        out_shape=jax.ShapeDtypeStruct((parts, ifgs, width), jnp.bfloat16),
        scratch_shapes=[
            pltpu.VMEM(flags.shape, jnp.int32),
            pltpu.VMEM((parts * ifgs, LANES), jnp.float32),
            pltpu.VMEM((parts, ifgs, width), jnp.bfloat16),
            pltpu.SemaphoreType.DMA,
            pltpu.SemaphoreType.DMA((parts,)),
        ],
        compiler_params=pltpu.CompilerParams(vmem_limit_bytes=medium),
        name="pack_inner",
    )(stay(flags), stay(phases))


def split(a, terms):
    parts = []
    for _ in range(terms):
        parts.append(a.astype(jnp.bfloat16))
        a = a - parts[-1].astype(jnp.float32)
    return parts


def sum_dots(pairs):
    return sum(jnp.dot(a, b, preferred_element_type=jnp.float32) for a, b in pairs)


def operator_kernel(pairs_ref, other_ref, out_ref, other_out_ref, token_ref, laplacian_ref, inverse_ref):
    token_ref[...] = jnp.zeros_like(token_ref)
    ifgs = pairs_ref.shape[1]
    size = inverse_ref.shape[0]
    epoch = lax.broadcasted_iota(jnp.int32, (size, ifgs), 0)

    def ends(ref):
        return (epoch == ref[1:2, :]).astype(jnp.float32) - (epoch == ref[0:1, :]).astype(jnp.float32)

    across = ends(pairs_ref)
    down = across.T
    eye = (
        lax.broadcasted_iota(jnp.int32, (size, size), 0) == lax.broadcasted_iota(jnp.int32, (size, size), 1)
    ).astype(jnp.float32)
    laplacian = jnp.dot(across.astype(jnp.bfloat16), down.astype(jnp.bfloat16), preferred_element_type=jnp.float32)
    normal = eye + laplacian
    laplacian_ref[...] = laplacian.astype(jnp.bfloat16)
    first = eye / jnp.where(eye == 1.0, normal, 1.0)
    scaled = jnp.sum(first, axis=1, keepdims=True) * normal * jnp.sum(first, axis=0, keepdims=True)
    inverse_ref[...] = 2.0 * first - scaled

    def unfinished(state):
        step, gap = state
        return jnp.logical_and(step < 24, gap > 1e-5)

    def improve(state):
        step, _ = state
        inverse = inverse_ref[...]
        parts = split(inverse, 3)
        rest = eye - inverse - sum_dots((laplacian_ref[...], part) for part in parts)
        high, low = split(rest, 2)
        inverse_ref[...] = inverse + sum_dots(((parts[0], low), (parts[1], high), (parts[0], high)))
        return step + 1, jnp.max(jnp.abs(rest))

    lax.while_loop(unfinished, improve, (jnp.int32(0), jnp.float32(1.0)))
    place = lax.broadcasted_iota(jnp.int32, (size, ifgs), 0)
    centred = place.astype(jnp.float32) - (EPOCHS - 1) / 2.0
    square = sum((e - (EPOCHS - 1) / 2.0) ** 2 for e in range(EPOCHS))
    slope = jnp.where(place < EPOCHS, centred * (EPOCHS - 1) / square, 0.0)
    same = lax.broadcasted_iota(jnp.int32, (ifgs, ifgs), 0) == lax.broadcasted_iota(jnp.int32, (ifgs, ifgs), 1)
    extra = lax.broadcasted_iota(jnp.int32, (EXTRA, ifgs), 0)
    for ref, to_ref in ((pairs_ref, out_ref), (other_ref, other_out_ref)):
        across = ends(ref)
        ones = across.astype(jnp.bfloat16)
        pseudo = sum_dots((part, ones) for part in split(inverse_ref[...], 3)).astype(jnp.bfloat16)
        fitted = jnp.dot(across.T.astype(jnp.bfloat16), pseudo, preferred_element_type=jnp.float32)
        to_ref[:ifgs, :] = (same.astype(jnp.float32) - fitted).astype(jnp.bfloat16)
        row = jnp.sum(pseudo.astype(jnp.float32) * slope, axis=0, keepdims=True)
        high = row.astype(jnp.bfloat16).astype(jnp.float32)
        rest = row - high
        middle = rest.astype(jnp.bfloat16).astype(jnp.float32)
        low = rest - middle
        terms = jnp.where(extra == 0, high, jnp.where(extra == 1, middle, jnp.where(extra == 2, low, 0.0)))
        to_ref[ifgs:, :] = terms.astype(jnp.bfloat16)


def setup_track(pair_rows, other_rows):
    ifgs = pair_rows.shape[0]
    size = -(-EPOCHS // LANES) * LANES
    vmem = pl.BlockSpec(memory_space=pltpu.VMEM)
    return pl.pallas_call(
        operator_kernel,
        in_specs=[vmem] * 2,
        out_specs=[vmem] * 3,
        out_shape=[jax.ShapeDtypeStruct((ifgs + EXTRA, ifgs), jnp.bfloat16)] * 2 + [token],
        scratch_shapes=[pltpu.VMEM((size, size), jnp.bfloat16), pltpu.VMEM((size, size), jnp.float32)],
        compiler_params=pltpu.CompilerParams(vmem_limit_bytes=medium),
        name="misfit_operator",
    )(pair_rows.T, other_rows.T)


def invert_tiles(stack_refs, first, width, operator_ref, fields_ref, base):
    ifgs = operator_ref.shape[1]
    for start in range(0, width, TILE):
        here = pl.ds(pl.multiple_of(first + start, LANES), TILE)
        stack = jnp.concatenate([ref[:, here] for ref in stack_refs], axis=0)
        product = jnp.dot(operator_ref[...], stack, preferred_element_type=jnp.float32)
        velocity = jnp.sum(product[ifgs : ifgs + 8], axis=0, keepdims=True)
        variance = jnp.sum(product[:ifgs] * product[:ifgs], axis=0, keepdims=True) / ifgs
        for k in range(TILE // LANES):
            row = pl.ds(base + start // LANES + k, 1)
            fields_ref[0, row, :] = velocity[:, k * LANES : (k + 1) * LANES]
            fields_ref[1, row, :] = variance[:, k * LANES : (k + 1) * LANES]


def pick(source, lane):
    return jnp.take_along_axis(source, lane, axis=1, mode="promise_in_bounds")


def resample(near, cell, index_ref, weight_ref):
    lanes = lax.broadcasted_iota(jnp.int32, (8, LANES), 1)
    here = pl.ds(cell, 8)
    sums = [jnp.zeros((8, LANES), jnp.float32)] * 2
    total = jnp.zeros((8, LANES), jnp.float32)
    for b in range(index_ref.shape[0]):
        weight = weight_ref[b, here, :]
        place = lanes + index_ref[b, here, :] + HALO
        lane = place & (LANES - 1)
        which = place >> 7
        total = total + weight
        for f in range(2):
            low, mid, high = (pick(near[f][k], lane) for k in range(3))
            taken = jnp.where(which == 0, low, jnp.where(which == 1, mid, high))
            sums[f] = sums[f] + taken * weight
    return sums[0] / total, sums[1] / total, total


def boundary(row, offsets, weights, sources, wanted):
    lanes = lax.broadcasted_iota(jnp.int32, (8, LANES), 1)
    rows = lax.broadcasted_iota(jnp.int32, (8, LANES), 0)
    sums = [jnp.zeros((8, LANES), jnp.float32)] * 2
    for offset, weight in zip(offsets, weights):
        place = lanes + offset + HALO
        lane = place & (LANES - 1)
        keep = jnp.where(jnp.logical_and(place >> 7 == wanted, rows == row), weight, 0.0)
        for f in range(2):
            sums[f] = sums[f] + pick(jnp.broadcast_to(sources[f], (8, LANES)), lane) * keep
    return sums


def store_cells(out_ref, at, velocity, variance, cover, north, north_c):
    out_ref[0, at : at + 8, :] = cover / (variance + prior_var)
    out_ref[1, at : at + 8, :] = velocity - north_c * north


def fixed_kernel(tiles, index_ref, weight_ref, cover_ref, north_ref, back_ref, onward_ref):
    taps, rows, _ = index_ref.shape
    place = lax.broadcasted_iota(jnp.int32, (tiles, LANES), 0) == lax.broadcasted_iota(jnp.int32, (tiles, LANES), 1)
    for half, to_ref in enumerate((back_ref, onward_ref)):
        edge = slice(half * (rows - tiles), half * (rows - tiles) + tiles)
        outermost = half * (rows - 1)
        row = slice(outermost, outermost + 1)
        to_ref[:tiles, :] = north_ref[edge, :]
        total = sum(weight_ref[b, row, :] for b in range(taps))
        for b in range(taps):
            to_ref[tiles + b : tiles + b + 1, :] = index_ref[b, row, :].astype(jnp.float32)
            to_ref[tiles + taps + b : tiles + taps + b + 1, :] = weight_ref[b, row, :] / total
        at = tiles + 2 * taps
        cover = jnp.where(place, jnp.broadcast_to(cover_ref[edge, :].astype(jnp.float32), (tiles, LANES)), 0.0)
        to_ref[at : at + 1, :] = jnp.sum(cover, axis=0, keepdims=True)
        to_ref[at + 1 :, :] = jnp.zeros((to_ref.shape[0] - at - 1, LANES), jnp.float32)


def fixed(cells, tiles):
    rows = -(-(tiles + 2 * cells[0].shape[0] + 1) // 8) * 8
    vmem = pl.BlockSpec(memory_space=pltpu.VMEM)
    return pl.pallas_call(
        functools.partial(fixed_kernel, tiles),
        in_specs=[vmem] * 4,
        out_specs=[vmem] * 2,
        out_shape=[jax.ShapeDtypeStruct((rows, LANES), jnp.float32)] * 2,
        compiler_params=pltpu.CompilerParams(vmem_limit_bytes=medium),
        name="edge_inputs",
    )(*cells)


def edges_kernel(tiles, group, los_ref, *refs):
    stack_refs = refs[:group]
    operator_ref, index_ref, weight_ref, *fixed_refs, kept_ref, back_ref, onward_ref, fields_ref = refs[group:]
    width = stack_refs[0].shape[1]
    count = width // LANES
    rows = index_ref.shape[1]
    none = jnp.zeros((2, 1, LANES), jnp.float32)
    fields_ref[:, :1, :] = none
    fields_ref[:, count + 1 : count + 2, :] = none
    invert_tiles(stack_refs, 0, width, operator_ref, fields_ref, 1)
    seam = 2 * tiles
    kept_ref[:, seam : seam + 4, :] = fields_ref[:, tiles : tiles + 4, :]
    kept_ref[:, seam + 4 : seam + 5, :] = fields_ref[:, 1:2, :]
    kept_ref[:, seam + 5 : seam + 6, :] = fields_ref[:, count : count + 1, :]
    kept_ref[:, seam + 6 :, :] = jnp.zeros((2, kept_ref.shape[1] - seam - 6, LANES), jnp.float32)
    tracks = los_ref.shape[0]
    scalars = [los_ref[t, part] for part in (0, 2) for t in range(tracks)] + [los_ref[lax.axis_index("track"), 1]]
    for k, scalar in enumerate(scalars):
        row = seam + 8 + k
        kept_ref[0, row : row + 1, :] = jnp.full((1, LANES), scalar, jnp.float32)
    for half, (fixed_ref, to_ref) in enumerate(zip(fixed_refs, (back_ref, onward_ref))):
        first = half * (rows - tiles)
        after = to_ref.shape[0] - fixed_ref.shape[0]
        to_ref[after:, :] = fixed_ref[...]
        for r in range(0, tiles, 8):
            base = half * (tiles + 2) + r
            near = [[fields_ref[f, base + k : base + k + 8, :] for k in range(3)] for f in range(2)]
            velocity, variance, _ = resample(near, first + r, index_ref, weight_ref)
            for f, values in enumerate((velocity, variance)):
                kept_ref[f, half * tiles + r : half * tiles + r + 8, :] = values
                to_ref[f * tiles + r : f * tiles + r + 8, :] = values
        for f in range(2):
            to_ref[seam + f : seam + f + 1, :] = kept_ref[f, seam + 4 + half : seam + 5 + half, :]
        to_ref[seam + 2 : after, :] = jnp.zeros((after - seam - 2, LANES), jnp.float32)


def edges(los, stacks, operator, cells, both_fixed, tiles):
    rows = 2 * (tiles + 1)
    payload = -(-(2 * tiles + 2) // 8) * 8 + both_fixed[0].shape[0]
    sight = -(-(2 * los.shape[0] + 1) // 8) * 8
    shapes = [(2, 2 * tiles + 8 + sight, LANES), (payload, LANES), (payload, LANES)]
    vmem = pl.BlockSpec(memory_space=pltpu.VMEM)
    return pl.pallas_call(
        functools.partial(edges_kernel, tiles, len(stacks)),
        in_specs=[pl.BlockSpec(memory_space=pltpu.SMEM)] + [vmem] * (len(stacks) + 5),
        out_specs=[vmem] * 3,
        out_shape=[jax.ShapeDtypeStruct(shape, jnp.float32) for shape in shapes],
        scratch_shapes=[pltpu.VMEM((2, -(-(rows + 2) // 8) * 8, LANES), jnp.float32)],
        compiler_params=pltpu.CompilerParams(vmem_limit_bytes=medium),
        cost_estimate=pl.CostEstimate(flops=EDGE_COST, bytes_accessed=0, transcendentals=0),
        name="edge_rows",
    )(los, *stacks, operator, *cells[:2], *both_fixed)


def finish_kernel(
    tiles, tracks, kept_ref, before_ref, after_ref, index_ref, weight_ref, cover_ref, north_ref, out_ref
):
    taps, rows, _ = index_ref.shape
    seam = 2 * tiles
    north_c = kept_ref[0, seam + 8 + 2 * tracks : seam + 9 + 2 * tracks, :]
    place = lax.broadcasted_iota(jnp.int32, (8, LANES), 0) - lax.broadcasted_iota(jnp.int32, (8, LANES), 1)
    for half, from_ref in enumerate((before_ref, after_ref)):
        fixed_ref = from_ref.at[-(-(seam + 2) // 8) * 8 :]
        edge = half * (tiles - 8)
        row = 7 * half
        outermost = half * (rows - 1)
        total = sum(weight_ref[b, outermost : outermost + 1, :] for b in range(taps))
        to_own = boundary(
            row,
            [index_ref[b, outermost : outermost + 1, :] for b in range(taps)],
            [weight_ref[b, outermost : outermost + 1, :] / total for b in range(taps)],
            [from_ref[seam + f : seam + f + 1, :] for f in range(2)],
            2 * half,
        )
        to_other = boundary(
            7 - row,
            [fixed_ref[tiles + b : tiles + b + 1, :].astype(jnp.int32) for b in range(taps)],
            [fixed_ref[tiles + taps + b : tiles + taps + b + 1, :] for b in range(taps)],
            [kept_ref[f, seam + 4 + half : seam + 5 + half, :] for f in range(2)],
            2 - 2 * half,
        )
        covers = fixed_ref[tiles + 2 * taps : tiles + 2 * taps + 1, :]
        for r in range(0, tiles, 8):
            first = half * (rows - tiles) + r
            values = [kept_ref[f, half * tiles + r : half * tiles + r + 8, :] for f in range(2)]
            if r == edge:
                values = [value + more for value, more in zip(values, to_own)]
            cover = cover_ref[first : first + 8, :].astype(jnp.float32)
            store_cells(out_ref, (1 + half) * tiles + r, *values, cover, north_ref[first : first + 8, :], north_c)
            values = [from_ref[f * tiles + r : f * tiles + r + 8, :] for f in range(2)]
            if r == tiles - 8 - edge:
                values = [value + more for value, more in zip(values, to_other)]
            cover = jnp.sum(jnp.where(place == -r, jnp.broadcast_to(covers, (8, LANES)), 0.0), axis=1, keepdims=True)
            store_cells(out_ref, 3 * half * tiles + r, *values, cover, fixed_ref[r : r + 8, :], north_c)
    out_ref[:, 4 * tiles :, :] = kept_ref[:, seam:, :]


def finish(kept, before, after, cells, tiles, tracks):
    vmem = pl.BlockSpec(memory_space=pltpu.VMEM)
    return pl.pallas_call(
        functools.partial(finish_kernel, tiles, tracks),
        in_specs=[vmem] * 7,
        out_specs=vmem,
        out_shape=jax.ShapeDtypeStruct((2, kept.shape[1] + 2 * tiles, LANES), jnp.float32),
        compiler_params=pltpu.CompilerParams(vmem_limit_bytes=medium),
        name="edge_cells",
    )(kept, before, after, *cells)


def inner_kernel(
    tiles, tracks, span, stack_ref, edge_ref, operator_ref, index_ref, weight_ref, cover_ref, north_ref, *refs
):
    *to_refs, sight_ref, fields_ref, out_ref = refs
    width = stack_ref.shape[1]
    rows = index_ref.shape[1]
    seam = 4 * tiles
    sight_ref[...] = edge_ref[0, seam + 8 :, :]
    north_c = edge_ref[0, seam + 8 + 2 * tracks : seam + 9 + 2 * tracks, :]
    pixel_rows = width // LANES
    fields_ref[:, 0:2, :] = edge_ref[:, seam : seam + 2, :]
    fields_ref[:, pixel_rows + 2 : pixel_rows + 4, :] = edge_ref[:, seam + 2 : seam + 4, :]
    out_ref[:, : 2 * tiles, :] = edge_ref[:, : 2 * tiles, :]
    out_ref[:, rows:, :] = edge_ref[:, 2 * tiles : 4 * tiles, :]
    invert_tiles([stack_ref], 0, width, operator_ref, fields_ref, 2)
    for r in range(0, rows - 2 * tiles, 8):
        near = [[fields_ref[f, r + k : r + k + 8, :] for k in range(3)] for f in range(2)]
        first = tiles + r
        velocity, variance, _ = resample(near, first, index_ref, weight_ref)
        cover = cover_ref[first : first + 8, :].astype(jnp.float32)
        store_cells(out_ref, tiles + first, velocity, variance, cover, north_ref[first : first + 8, :], north_c)


    here = lax.axis_index("track")
    lines = rows // tiles + 2
    for half, to_ref in zip((here, 1 - here), to_refs):
        start = half * (tiles - span)
        for i in range(lines):
            to_ref[:, i * span : (i + 1) * span, :] = out_ref[:, pl.ds(i * tiles + start, span), :]
        left = to_ref.shape[1] - lines * span
        if left:
            to_ref[:, lines * span :, :] = jnp.zeros((2, left, LANES), jnp.float32)


def inner(stack, edge, operator, cells, tiles, tracks, span, copies):
    rows = cells[0].shape[1]
    compact = -(-(rows // tiles + 2) * span // 8) * 8
    vmem = pl.BlockSpec(memory_space=pltpu.VMEM)
    return pl.pallas_call(
        functools.partial(inner_kernel, tiles, tracks, span),
        in_specs=[vmem] * 7,
        out_specs=[vmem] * (copies + 1),
        out_shape=[jax.ShapeDtypeStruct((2, compact, LANES), jnp.float32)] * copies
        + [jax.ShapeDtypeStruct((edge.shape[1] - 4 * tiles - 8, LANES), jnp.float32)],
        scratch_shapes=[
            pltpu.VMEM((2, -(-(rows - 2 * tiles + 2) // 8) * 8, LANES), jnp.float32),
            pltpu.VMEM((2, rows + 2 * tiles, LANES), jnp.float32),
        ],
        compiler_params=pltpu.CompilerParams(vmem_limit_bytes=medium),
        name="inner_rows",
    )(stack, edge, operator, *cells)


def solve_cells(of_tracks, sight_ref, tracks):
    a11 = a12 = a22 = b1 = b2 = 0.0
    for t, values_ref in of_tracks:
        weight, target = values_ref[0], values_ref[1]
        east_c, up_c = sight_ref[pl.ds(t, 1), :], sight_ref[pl.ds(tracks + t, 1), :]
        by_east, by_up = weight * east_c, weight * up_c
        a11 = a11 + by_east * east_c
        a12 = a12 + by_east * up_c
        a22 = a22 + by_up * up_c
        b1 = b1 + by_east * target
        b2 = b2 + by_up * target
    a11 = a11 + ridge_term
    a22 = a22 + ridge_term
    determ = a11 * a22 - a12 * a12
    return (a22 * b1 - a12 * b2) / determ, (a11 * b2 - a12 * b1) / determ


def final_kernel(
    tiles, span, own, tracks, sight_ref, own_ref, other_ref, north_ref, before_ref, after_ref, east_up_ref, strain_ref, work_ref, line_ref
):
    lines = north_ref.shape[0] // tiles
    rows = lines * span
    here = lax.axis_index("track")
    start = here * (tiles - span)
    at = -(-(2 * tiles + 2) // 8) * 8 + start
    line_ref[:span, :] = before_ref[pl.ds(at, span), :]
    for i in range(lines):
        line_ref[(i + 1) * span : (i + 2) * span, :] = north_ref[pl.ds(i * tiles + start, span), :]
    line_ref[rows + span : rows + 2 * span, :] = after_ref[pl.ds(at, span), :]
    lane = lax.broadcasted_iota(jnp.int32, (rows, LANES), 1)
    tile = lax.broadcasted_iota(jnp.int32, (rows, LANES), 0) % span

    def across(field):
        right = jnp.where(tile == span - 1, 0.0, pltpu.roll(field, rows - 1, 0))
        left = jnp.where(tile == 0, 0.0, pltpu.roll(field, 1, 0))
        following = jnp.where(lane == LANES - 1, pltpu.roll(right, LANES - 1, 1), pltpu.roll(field, LANES - 1, 1))
        previous = jnp.where(lane == 0, pltpu.roll(left, 1, 1), pltpu.roll(field, 1, 1))
        return following - previous

    if other_ref.shape[0] == 1:
        of_tracks = [(here, own_ref), (1 - here, other_ref.at[0])]
    else:
        of_tracks = [(t, other_ref.at[t]) for t in range(other_ref.shape[0])]
    wide_east, wide_up = solve_cells(of_tracks, sight_ref, tracks)
    wide_north = line_ref[...]
    east, up, north = (wide[span : span + rows] for wide in (wide_east, wide_up, wide_north))
    work_ref[0] = east
    work_ref[1] = up
    work_ref[2] = across(east) / 2.0
    work_ref[3] = (wide_north[2 * span : 2 * span + rows] - wide_north[:rows]) / 2.0
    work_ref[4] = (wide_east[2 * span : 2 * span + rows] - wide_east[:rows] + across(north)) / 4.0
    first = here * own - start
    for field in range(5):
        target, at = (east_up_ref, field) if field < 2 else (strain_ref, field - 2)
        for i in range(lines):
            for j in range(own):
                target[at, i : i + 1, j * LANES : (j + 1) * LANES] = work_ref[field, pl.ds(i * span + first + j, 1), :]


def final(sight, vals, others, north, before, after, tiles, span, own, tracks):
    lines = north.shape[0] // tiles
    shape = (lines, own * LANES)
    vmem = pl.BlockSpec(memory_space=pltpu.VMEM)
    return pl.pallas_call(
        functools.partial(final_kernel, tiles, span, own, tracks),
        in_specs=[vmem] * 6,
        out_specs=[vmem] * 2,
        out_shape=[jax.ShapeDtypeStruct((2, *shape), jnp.float32), jax.ShapeDtypeStruct((3, *shape), jnp.float32)],
        scratch_shapes=[pltpu.VMEM((5, lines * span, LANES), jnp.float32), pltpu.VMEM(vals.shape[1:], jnp.float32)],
        compiler_params=pltpu.CompilerParams(vmem_limit_bytes=medium),
        name="solve_and_strain",
    )(sight, vals, others, north, before, after)


def per_device(phases, coherent, pairs, res_index, res_weight, coverage, los, north):
    parts = lax.axis_size("pix")
    tracks = lax.axis_size("track")
    grid_rows, columns = north.shape
    tiles = columns // CTILE
    rows = grid_rows * tiles
    group = GROUP if parts % GROUP == 0 else parts
    planes = parts // group
    plane, column = jnp.divmod(lax.axis_index("pix").astype(jnp.int32), group)
    steps = [-s % planes for s in range(planes)]
    first_piece, first_token = pack_edges(phases[0], coherent[0], group, tiles, steps[1:2])
    rest_flags, _ = lax.optimization_barrier((coherent[0], first_token))
    own_piece, *others, packed_token = pack_edges(phases[0], rest_flags, group, tiles, steps[:1] + steps[2:])
    packed = [own_piece, first_piece, *others]
    later_pairs, _ = lax.optimization_barrier((pairs[0], packed_token))
    steps_j, steps_s = jnp.meshgrid(jnp.arange(group), jnp.arange(planes), indexing="ij")
    sources = (partner_back(plane, -steps_s % planes, planes) * group + partner_back(column, steps_j, group)).reshape(-1)
    edge_pairs = jnp.take(later_pairs.reshape(parts, -1, 2), sources, axis=0).reshape(-1, 2)
    operator, edge_operator, formed_token = setup_track(later_pairs, edge_pairs)
    ids = [(z, c) for z in range(planes) for c in range(group)]
    arrived = [packed[0]] * planes
    for s in range(1, planes):
        far = [(z * group + c, partner(z, planes - s, planes) * group + c) for z, c in ids]
        arrived[s] = lax.ppermute(packed[s], "pix", far)
    by_column = regroup(formed_token, arrived, group)
    pieces = [by_column[0]]
    for j in range(1, group):
        near = [(z * group + c, z * group + partner(c, j, group)) for z, c in ids]
        pieces.append(lax.ppermute(by_column[j], "pix", near))
    later_flags, *_ = lax.optimization_barrier((coherent[0], packed_token))
    inner_stack = lax.all_to_all(
        pack_inner(phases[0], later_flags, parts, tiles), "pix", split_axis=0, concat_axis=0, tiled=True
    )
    north_cells = north.reshape(rows, LANES)
    cells = (
        res_index.reshape(-1, rows, LANES),
        res_weight.reshape(-1, rows, LANES),
        coverage.reshape(rows, 1),
        north_cells,
    )

    def flat(stack):
        return stack.reshape(-1, stack.shape[-1])

    onward = [(i, i + 1) for i in range(parts - 1)]
    back = [(j, i) for i, j in onward]
    kept, for_before, for_after = edges(
        los, [flat(piece) for piece in pieces], edge_operator, cells, fixed(cells, tiles), tiles
    )
    before = lax.ppermute(for_after, "pix", onward)
    after = lax.ppermute(for_before, "pix", back)
    edge_vals = finish(kept, before, after, cells, tiles, tracks)
    own_tiles = tiles // tracks
    if tracks == 2:
        span = own_tiles + 1
        vals, for_other, sight = inner(flat(inner_stack), edge_vals, operator, cells, tiles, tracks, span, 2)
        others = lax.ppermute(for_other, "track", [(0, 1), (1, 0)])[None]
    else:
        span = tiles
        vals, sight = inner(flat(inner_stack), edge_vals, operator, cells, tiles, tracks, span, 1)
        others = lax.all_gather(vals, "track", axis=0)
    return tuple(final(sight, vals, others, north_cells, before, after, tiles, span, own_tiles, tracks))


def solution(mesh):
    in_specs = (
        P("track", "pix", None),
        P("track", "pix", None),
        P("track", None, None),
        P("track", None, "pix"),
        P("track", None, "pix"),
        P("track", "pix", None),
        P(),
        P("pix", None),
    )
    out_specs = (P(None, "pix", "track"), P(None, "pix", "track"))
    return jax.shard_map(
        per_device, mesh=mesh, in_specs=in_specs, out_specs=out_specs, check_vma=False
    )
```

```python
import functools

import jax
import jax.numpy as jnp
from jax import lax
from jax.experimental import pallas as pl
from jax.experimental.pallas import tpu as pltpu
from jax.sharding import PartitionSpec as P

EPOCHS = 200
EXTRA = 16
HALO = 128
CTILE = 128
MBLK = 128
LANES = 128
TILE = 256
GROUP = 4
EDGE_COST = 54_000_000_000

token = jax.ShapeDtypeStruct((8, LANES), jnp.float32)


prior_var = 0.1
ridge_term = 0.5
medium = 24 * 1024 * 1024


def stay(array):
    return pltpu.with_memory_space_constraint(array, pltpu.HBM)


def expand_masks(flags_ref, stacked_ref, firsts, wanted, tile_out):
    ifgs = flags_ref.shape[0]
    for n, first in enumerate(firsts):
        stacked_ref[n * ifgs : (n + 1) * ifgs, :] = part_flags(flags_ref, first)
    stacked = stacked_ref[...].astype(jnp.bfloat16)
    block = lax.broadcasted_iota(jnp.int32, (LANES, 2 * MBLK), 0)
    right = lax.broadcasted_iota(jnp.int32, (LANES, 2 * MBLK), 1) >= MBLK
    for start in range(0, len(wanted), 2):
        here = jnp.where(right, wanted[start + 1], wanted[start])
        ones = (block == here).astype(jnp.bfloat16)
        keep = jnp.dot(stacked, ones, preferred_element_type=jnp.float32).astype(jnp.bfloat16)
        for n in range(len(firsts)):
            tile_out(n, start * MBLK, keep[n * ifgs : (n + 1) * ifgs])


def part_flags(flags_ref, first):
    lead = pl.multiple_of(first // LANES * LANES, LANES)
    flags = (flags_ref[:, pl.ds(lead, LANES)] == 1).astype(jnp.float32)
    return pltpu.roll(flags, (LANES - (first - lead)) % LANES, 1)


def partner(index, step, size):
    return index ^ step if size & (size - 1) == 0 else (index + step) % size


def partner_back(index, step, size):
    return index ^ step if size & (size - 1) == 0 else (index - step + size) % size


def pack_edges_kernel(tiles, group, steps, flags_hbm, phases_ref, *refs):
    *out_refs, token_ref, flags_ref, stacked_ref, near_ref, flag_sem, in_sem = refs
    token_ref[...] = jnp.zeros_like(token_ref)
    ifgs, blocks = flags_ref.shape
    reach = tiles + 1
    half = reach * MBLK
    parts = lax.axis_size("pix")
    planes = parts // group
    span = blocks // parts
    flag_copy = pltpu.make_async_copy(flags_hbm, flags_ref, flag_sem)
    flag_copy.start()
    plane = lax.axis_index("pix") // group
    first_parts = [partner(plane, step, planes) * group for step in steps]

    def regions(act):
        for n, first_part in enumerate(first_parts):
            for g in range(group + 1):
                b = first_part + g
                to_ref, sem = near_ref.at[n, g], in_sem.at[n, g]

                @pl.when(b == 0)
                def _():
                    act(pltpu.make_async_copy(phases_ref.at[:, pl.ds(0, half)], to_ref.at[:, pl.ds(half, half)], sem))

                @pl.when(b == parts)
                def _():
                    low = blocks * MBLK - half
                    act(pltpu.make_async_copy(phases_ref.at[:, pl.ds(low, half)], to_ref.at[:, pl.ds(0, half)], sem))

                @pl.when(jnp.logical_and(b > 0, b < parts))
                def _():
                    low = pl.multiple_of((span * jnp.clip(b, 1, parts - 1) - reach) * MBLK, MBLK)
                    act(pltpu.make_async_copy(phases_ref.at[:, pl.ds(low, 2 * half)], to_ref, sem))

    regions(lambda copy: copy.start())
    flag_copy.wait()
    firsts = [(first_part + g) * span for first_part in first_parts for g in range(group)]

    def tile_out(n, start, keep):
        out_refs[n // group][n % group, :, start : start + 2 * MBLK] = keep

    wanted = [k if k < reach else span - 2 * reach + k for k in range(2 * reach)]
    expand_masks(flags_ref, stacked_ref, firsts, wanted, tile_out)
    regions(lambda copy: copy.wait())
    for n, out_ref in enumerate(out_refs):
        for g in range(group):
            out_ref[g, :, :half] *= near_ref[n, g, :, half:]
            out_ref[g, :, half:] *= near_ref[n, g + 1, :, :half]


def pack_edges(phases, flags, group, tiles, steps):
    ifgs = phases.shape[0]
    hbm = pl.BlockSpec(memory_space=pltpu.HBM)
    width = 2 * (tiles + 1) * MBLK
    count = len(steps)
    return pl.pallas_call(
        functools.partial(pack_edges_kernel, tiles, group, steps),
        in_specs=[hbm, hbm],
        out_specs=[pl.BlockSpec(memory_space=pltpu.VMEM)] * (count + 1),
        out_shape=[jax.ShapeDtypeStruct((group, ifgs, width), jnp.bfloat16)] * count + [token],
        scratch_shapes=[
            pltpu.VMEM(flags.shape, jnp.int32),
            pltpu.VMEM((count * group * ifgs, LANES), jnp.float32),
            pltpu.VMEM((count, group + 1, ifgs, width), jnp.bfloat16),
            pltpu.SemaphoreType.DMA,
            pltpu.SemaphoreType.DMA((count, group + 1)),
        ],
        compiler_params=pltpu.CompilerParams(vmem_limit_bytes=medium),
        name="pack_edges",
    )(stay(flags), stay(phases))


def regroup_kernel(planes, group, after_ref, *refs):
    in_refs, out_refs = refs[:planes], refs[planes:]
    for j in range(group):
        column = partner(lax.rem(lax.axis_index("pix"), group), j, group)
        for s in range(planes):
            out_refs[j][s] = in_refs[s][column]


def regroup(after, pieces, group):
    planes = len(pieces)
    vmem = pl.BlockSpec(memory_space=pltpu.VMEM)
    shape = (planes, *pieces[0].shape[1:])
    return pl.pallas_call(
        functools.partial(regroup_kernel, planes, group),
        in_specs=[vmem] * (planes + 1),
        out_specs=[vmem] * group,
        out_shape=[jax.ShapeDtypeStruct(shape, jnp.bfloat16)] * group,
        compiler_params=pltpu.CompilerParams(vmem_limit_bytes=medium),
        name="regroup",
    )(after, *pieces)


def snake(n, group):
    plane, column = n // group, n % group
    return n + plane % 2 * (group - 1 - 2 * column)


def pack_inner_kernel(reach, group, flags_hbm, phases_ref, out_ref, flags_ref, stacked_ref, held_ref, flag_sem, in_sem):
    parts, ifgs, width = out_ref.shape
    span = flags_ref.shape[1] // parts
    flag_copy = pltpu.make_async_copy(flags_hbm, flags_ref, flag_sem)
    flag_copy.start()

    def inward(n):
        low = pl.multiple_of((snake(n, group) * span + reach) * MBLK, MBLK)
        return pltpu.make_async_copy(phases_ref.at[:, pl.ds(low, width)], held_ref.at[n], in_sem.at[n])

    @pl.loop(0, parts)
    def _(p):
        inward(p).start()

    flag_copy.wait()

    def tile_out(n, start, keep):
        out_ref[n, :, start : start + 2 * MBLK] = keep

    wanted = list(range(reach, span - reach))
    expand_masks(flags_ref, stacked_ref, [snake(n, group) * span for n in range(parts)], wanted, tile_out)

    @pl.loop(0, parts)
    def _(p):
        inward(p).wait()
        out_ref[p] *= held_ref[p]


def pack_inner(phases, flags, parts, group, tiles):
    ifgs = phases.shape[0]
    reach = tiles + 1
    width = (flags.shape[1] // parts - 2 * reach) * MBLK
    hbm = pl.BlockSpec(memory_space=pltpu.HBM)
    return pl.pallas_call(
        functools.partial(pack_inner_kernel, reach, group),
        in_specs=[hbm, hbm],
        out_specs=pl.BlockSpec(memory_space=pltpu.VMEM),
        out_shape=jax.ShapeDtypeStruct((parts, ifgs, width), jnp.bfloat16),
        scratch_shapes=[
            pltpu.VMEM(flags.shape, jnp.int32),
            pltpu.VMEM((parts * ifgs, LANES), jnp.float32),
            pltpu.VMEM((parts, ifgs, width), jnp.bfloat16),
            pltpu.SemaphoreType.DMA,
            pltpu.SemaphoreType.DMA((parts,)),
        ],
        compiler_params=pltpu.CompilerParams(vmem_limit_bytes=medium),
        name="pack_inner",
    )(stay(flags), stay(phases))


def split(a, terms):
    parts = []
    for _ in range(terms):
        parts.append(a.astype(jnp.bfloat16))
        a = a - parts[-1].astype(jnp.float32)
    return parts


def sum_dots(pairs):
    return sum(jnp.dot(a, b, preferred_element_type=jnp.float32) for a, b in pairs)


def operator_kernel(pairs_ref, other_ref, out_ref, other_out_ref, token_ref, laplacian_ref, inverse_ref):
    token_ref[...] = jnp.zeros_like(token_ref)
    ifgs = pairs_ref.shape[1]
    size = inverse_ref.shape[0]
    epoch = lax.broadcasted_iota(jnp.int32, (size, ifgs), 0)

    def ends(ref):
        return (epoch == ref[1:2, :]).astype(jnp.float32) - (epoch == ref[0:1, :]).astype(jnp.float32)

    across = ends(pairs_ref)
    down = across.T
    eye = (
        lax.broadcasted_iota(jnp.int32, (size, size), 0) == lax.broadcasted_iota(jnp.int32, (size, size), 1)
    ).astype(jnp.float32)
    laplacian = jnp.dot(across.astype(jnp.bfloat16), down.astype(jnp.bfloat16), preferred_element_type=jnp.float32)
    normal = eye + laplacian
    laplacian_ref[...] = laplacian.astype(jnp.bfloat16)
    first = eye / jnp.where(eye == 1.0, normal, 1.0)
    scaled = jnp.sum(first, axis=1, keepdims=True) * normal * jnp.sum(first, axis=0, keepdims=True)
    inverse_ref[...] = 2.0 * first - scaled

    def unfinished(state):
        step, gap = state
        return jnp.logical_and(step < 24, gap > 1e-5)

    def improve(state):
        step, _ = state
        inverse = inverse_ref[...]
        parts = split(inverse, 3)
        rest = eye - inverse - sum_dots((laplacian_ref[...], part) for part in parts)
        high, low = split(rest, 2)
        inverse_ref[...] = inverse + sum_dots(((parts[0], low), (parts[1], high), (parts[0], high)))
        return step + 1, jnp.max(jnp.abs(rest))

    lax.while_loop(unfinished, improve, (jnp.int32(0), jnp.float32(1.0)))
    place = lax.broadcasted_iota(jnp.int32, (size, ifgs), 0)
    centred = place.astype(jnp.float32) - (EPOCHS - 1) / 2.0
    square = sum((e - (EPOCHS - 1) / 2.0) ** 2 for e in range(EPOCHS))
    slope = jnp.where(place < EPOCHS, centred * (EPOCHS - 1) / square, 0.0)
    same = lax.broadcasted_iota(jnp.int32, (ifgs, ifgs), 0) == lax.broadcasted_iota(jnp.int32, (ifgs, ifgs), 1)
    extra = lax.broadcasted_iota(jnp.int32, (EXTRA, ifgs), 0)
    for ref, to_ref in ((pairs_ref, out_ref), (other_ref, other_out_ref)):
        across = ends(ref)
        ones = across.astype(jnp.bfloat16)
        pseudo = sum_dots((part, ones) for part in split(inverse_ref[...], 3)).astype(jnp.bfloat16)
        fitted = jnp.dot(across.T.astype(jnp.bfloat16), pseudo, preferred_element_type=jnp.float32)
        to_ref[:ifgs, :] = (same.astype(jnp.float32) - fitted).astype(jnp.bfloat16)
        row = jnp.sum(pseudo.astype(jnp.float32) * slope, axis=0, keepdims=True)
        high = row.astype(jnp.bfloat16).astype(jnp.float32)
        rest = row - high
        middle = rest.astype(jnp.bfloat16).astype(jnp.float32)
        low = rest - middle
        terms = jnp.where(extra == 0, high, jnp.where(extra == 1, middle, jnp.where(extra == 2, low, 0.0)))
        to_ref[ifgs:, :] = terms.astype(jnp.bfloat16)


def setup_track(pair_rows, other_rows):
    ifgs = pair_rows.shape[0]
    size = -(-EPOCHS // LANES) * LANES
    vmem = pl.BlockSpec(memory_space=pltpu.VMEM)
    return pl.pallas_call(
        operator_kernel,
        in_specs=[vmem] * 2,
        out_specs=[vmem] * 3,
        out_shape=[jax.ShapeDtypeStruct((ifgs + EXTRA, ifgs), jnp.bfloat16)] * 2 + [token],
        scratch_shapes=[pltpu.VMEM((size, size), jnp.bfloat16), pltpu.VMEM((size, size), jnp.float32)],
        compiler_params=pltpu.CompilerParams(vmem_limit_bytes=medium),
        name="misfit_operator",
    )(pair_rows.T, other_rows.T)


def invert_tiles(stack_refs, first, width, operator_ref, fields_ref, base):
    ifgs = operator_ref.shape[1]
    for start in range(0, width, TILE):
        here = pl.ds(pl.multiple_of(first + start, LANES), TILE)
        stack = jnp.concatenate([ref[:, here] for ref in stack_refs], axis=0)
        product = jnp.dot(operator_ref[...], stack, preferred_element_type=jnp.float32)
        velocity = jnp.sum(product[ifgs : ifgs + 8], axis=0, keepdims=True)
        variance = jnp.sum(product[:ifgs] * product[:ifgs], axis=0, keepdims=True) / ifgs
        for k in range(TILE // LANES):
            row = pl.ds(base + start // LANES + k, 1)
            fields_ref[0, row, :] = velocity[:, k * LANES : (k + 1) * LANES]
            fields_ref[1, row, :] = variance[:, k * LANES : (k + 1) * LANES]


def pick(source, lane):
    return jnp.take_along_axis(source, lane, axis=1, mode="promise_in_bounds")


def resample(near, cell, index_ref, weight_ref):
    lanes = lax.broadcasted_iota(jnp.int32, (8, LANES), 1)
    here = pl.ds(cell, 8)
    sums = [jnp.zeros((8, LANES), jnp.float32)] * 2
    total = jnp.zeros((8, LANES), jnp.float32)
    for b in range(index_ref.shape[0]):
        weight = weight_ref[b, here, :]
        place = lanes + index_ref[b, here, :] + HALO
        lane = place & (LANES - 1)
        which = place >> 7
        total = total + weight
        for f in range(2):
            low, mid, high = (pick(near[f][k], lane) for k in range(3))
            taken = jnp.where(which == 0, low, jnp.where(which == 1, mid, high))
            sums[f] = sums[f] + taken * weight
    return sums[0] / total, sums[1] / total, total


def boundary(row, offsets, weights, sources, wanted):
    lanes = lax.broadcasted_iota(jnp.int32, (8, LANES), 1)
    rows = lax.broadcasted_iota(jnp.int32, (8, LANES), 0)
    sums = [jnp.zeros((8, LANES), jnp.float32)] * 2
    for offset, weight in zip(offsets, weights):
        place = lanes + offset + HALO
        lane = place & (LANES - 1)
        keep = jnp.where(jnp.logical_and(place >> 7 == wanted, rows == row), weight, 0.0)
        for f in range(2):
            sums[f] = sums[f] + pick(jnp.broadcast_to(sources[f], (8, LANES)), lane) * keep
    return sums


def store_cells(out_ref, at, velocity, variance, cover, north, north_c):
    out_ref[0, at : at + 8, :] = cover / (variance + prior_var)
    out_ref[1, at : at + 8, :] = velocity - north_c * north


def fixed_kernel(tiles, index_ref, weight_ref, cover_ref, north_ref, back_ref, onward_ref):
    taps, rows, _ = index_ref.shape
    place = lax.broadcasted_iota(jnp.int32, (tiles, LANES), 0) == lax.broadcasted_iota(jnp.int32, (tiles, LANES), 1)
    for half, to_ref in enumerate((back_ref, onward_ref)):
        edge = slice(half * (rows - tiles), half * (rows - tiles) + tiles)
        outermost = half * (rows - 1)
        row = slice(outermost, outermost + 1)
        to_ref[:tiles, :] = north_ref[edge, :]
        total = sum(weight_ref[b, row, :] for b in range(taps))
        for b in range(taps):
            to_ref[tiles + b : tiles + b + 1, :] = index_ref[b, row, :].astype(jnp.float32)
            to_ref[tiles + taps + b : tiles + taps + b + 1, :] = weight_ref[b, row, :] / total
        at = tiles + 2 * taps
        cover = jnp.where(place, jnp.broadcast_to(cover_ref[edge, :].astype(jnp.float32), (tiles, LANES)), 0.0)
        to_ref[at : at + 1, :] = jnp.sum(cover, axis=0, keepdims=True)
        to_ref[at + 1 :, :] = jnp.zeros((to_ref.shape[0] - at - 1, LANES), jnp.float32)


def fixed(cells, tiles):
    rows = -(-(tiles + 2 * cells[0].shape[0] + 1) // 8) * 8
    vmem = pl.BlockSpec(memory_space=pltpu.VMEM)
    return pl.pallas_call(
        functools.partial(fixed_kernel, tiles),
        in_specs=[vmem] * 4,
        out_specs=[vmem] * 2,
        out_shape=[jax.ShapeDtypeStruct((rows, LANES), jnp.float32)] * 2,
        compiler_params=pltpu.CompilerParams(vmem_limit_bytes=medium),
        name="edge_inputs",
    )(*cells)


def edges_kernel(tiles, group, los_ref, *refs):
    stack_refs = refs[:group]
    operator_ref, index_ref, weight_ref, *fixed_refs, kept_ref, back_ref, onward_ref, fields_ref = refs[group:]
    width = stack_refs[0].shape[1]
    count = width // LANES
    rows = index_ref.shape[1]
    none = jnp.zeros((2, 1, LANES), jnp.float32)
    fields_ref[:, :1, :] = none
    fields_ref[:, count + 1 : count + 2, :] = none
    invert_tiles(stack_refs, 0, width, operator_ref, fields_ref, 1)
    seam = 2 * tiles
    kept_ref[:, seam : seam + 4, :] = fields_ref[:, tiles : tiles + 4, :]
    kept_ref[:, seam + 4 : seam + 5, :] = fields_ref[:, 1:2, :]
    kept_ref[:, seam + 5 : seam + 6, :] = fields_ref[:, count : count + 1, :]
    kept_ref[:, seam + 6 :, :] = jnp.zeros((2, kept_ref.shape[1] - seam - 6, LANES), jnp.float32)
    tracks = los_ref.shape[0]
    scalars = [los_ref[t, part] for part in (0, 2) for t in range(tracks)] + [los_ref[lax.axis_index("track"), 1]]
    for k, scalar in enumerate(scalars):
        row = seam + 8 + k
        kept_ref[0, row : row + 1, :] = jnp.full((1, LANES), scalar, jnp.float32)
    for half, (fixed_ref, to_ref) in enumerate(zip(fixed_refs, (back_ref, onward_ref))):
        first = half * (rows - tiles)
        after = to_ref.shape[0] - fixed_ref.shape[0]
        to_ref[after:, :] = fixed_ref[...]
        for r in range(0, tiles, 8):
            base = half * (tiles + 2) + r
            near = [[fields_ref[f, base + k : base + k + 8, :] for k in range(3)] for f in range(2)]
            velocity, variance, _ = resample(near, first + r, index_ref, weight_ref)
            for f, values in enumerate((velocity, variance)):
                kept_ref[f, half * tiles + r : half * tiles + r + 8, :] = values
                to_ref[f * tiles + r : f * tiles + r + 8, :] = values
        for f in range(2):
            to_ref[seam + f : seam + f + 1, :] = kept_ref[f, seam + 4 + half : seam + 5 + half, :]
        to_ref[seam + 2 : after, :] = jnp.zeros((after - seam - 2, LANES), jnp.float32)


def edges(los, stacks, operator, cells, both_fixed, tiles):
    rows = 2 * (tiles + 1)
    payload = -(-(2 * tiles + 2) // 8) * 8 + both_fixed[0].shape[0]
    sight = -(-(2 * los.shape[0] + 1) // 8) * 8
    shapes = [(2, 2 * tiles + 8 + sight, LANES), (payload, LANES), (payload, LANES)]
    vmem = pl.BlockSpec(memory_space=pltpu.VMEM)
    return pl.pallas_call(
        functools.partial(edges_kernel, tiles, len(stacks)),
        in_specs=[pl.BlockSpec(memory_space=pltpu.SMEM)] + [vmem] * (len(stacks) + 5),
        out_specs=[vmem] * 3,
        out_shape=[jax.ShapeDtypeStruct(shape, jnp.float32) for shape in shapes],
        scratch_shapes=[pltpu.VMEM((2, -(-(rows + 2) // 8) * 8, LANES), jnp.float32)],
        compiler_params=pltpu.CompilerParams(vmem_limit_bytes=medium),
        cost_estimate=pl.CostEstimate(flops=EDGE_COST, bytes_accessed=0, transcendentals=0),
        name="edge_rows",
    )(los, *stacks, operator, *cells[:2], *both_fixed)


def finish_kernel(
    tiles, tracks, kept_ref, before_ref, after_ref, index_ref, weight_ref, cover_ref, north_ref, out_ref
):
    taps, rows, _ = index_ref.shape
    seam = 2 * tiles
    north_c = kept_ref[0, seam + 8 + 2 * tracks : seam + 9 + 2 * tracks, :]
    place = lax.broadcasted_iota(jnp.int32, (8, LANES), 0) - lax.broadcasted_iota(jnp.int32, (8, LANES), 1)
    for half, from_ref in enumerate((before_ref, after_ref)):
        fixed_ref = from_ref.at[-(-(seam + 2) // 8) * 8 :]
        edge = half * (tiles - 8)
        row = 7 * half
        outermost = half * (rows - 1)
        total = sum(weight_ref[b, outermost : outermost + 1, :] for b in range(taps))
        to_own = boundary(
            row,
            [index_ref[b, outermost : outermost + 1, :] for b in range(taps)],
            [weight_ref[b, outermost : outermost + 1, :] / total for b in range(taps)],
            [from_ref[seam + f : seam + f + 1, :] for f in range(2)],
            2 * half,
        )
        to_other = boundary(
            7 - row,
            [fixed_ref[tiles + b : tiles + b + 1, :].astype(jnp.int32) for b in range(taps)],
            [fixed_ref[tiles + taps + b : tiles + taps + b + 1, :] for b in range(taps)],
            [kept_ref[f, seam + 4 + half : seam + 5 + half, :] for f in range(2)],
            2 - 2 * half,
        )
        covers = fixed_ref[tiles + 2 * taps : tiles + 2 * taps + 1, :]
        for r in range(0, tiles, 8):
            first = half * (rows - tiles) + r
            values = [kept_ref[f, half * tiles + r : half * tiles + r + 8, :] for f in range(2)]
            if r == edge:
                values = [value + more for value, more in zip(values, to_own)]
            cover = cover_ref[first : first + 8, :].astype(jnp.float32)
            store_cells(out_ref, (1 + half) * tiles + r, *values, cover, north_ref[first : first + 8, :], north_c)
            values = [from_ref[f * tiles + r : f * tiles + r + 8, :] for f in range(2)]
            if r == tiles - 8 - edge:
                values = [value + more for value, more in zip(values, to_other)]
            cover = jnp.sum(jnp.where(place == -r, jnp.broadcast_to(covers, (8, LANES)), 0.0), axis=1, keepdims=True)
            store_cells(out_ref, 3 * half * tiles + r, *values, cover, fixed_ref[r : r + 8, :], north_c)
    rest = 4 * tiles + kept_ref.shape[1] - seam
    out_ref[:, 4 * tiles : rest, :] = kept_ref[:, seam:, :]
    at = -(-(seam + 2) // 8) * 8
    for half, from_ref in enumerate((before_ref, after_ref)):
        here = slice(rest + half * tiles, rest + (half + 1) * tiles)
        out_ref[0, here, :] = from_ref[at : at + tiles, :]
        out_ref[1, here, :] = jnp.zeros((tiles, LANES), jnp.float32)


def finish(kept, before, after, cells, tiles, tracks):
    vmem = pl.BlockSpec(memory_space=pltpu.VMEM)
    return pl.pallas_call(
        functools.partial(finish_kernel, tiles, tracks),
        in_specs=[vmem] * 7,
        out_specs=vmem,
        out_shape=pltpu.VMEM((2, kept.shape[1] + 4 * tiles, LANES), jnp.float32),
        compiler_params=pltpu.CompilerParams(vmem_limit_bytes=medium),
        name="edge_cells",
    )(kept, before, after, *cells)


def inner_kernel(
    tiles, tracks, span, stack_ref, edge_ref, operator_ref, index_ref, weight_ref, cover_ref, north_ref, *refs
):
    *to_refs, sight_ref, fields_ref, out_ref = refs
    width = stack_ref.shape[1]
    rows = index_ref.shape[1]
    seam = 4 * tiles
    sight_ref[...] = edge_ref[0, seam + 8 :, :]
    north_c = edge_ref[0, seam + 8 + 2 * tracks : seam + 9 + 2 * tracks, :]
    pixel_rows = width // LANES
    fields_ref[:, 0:2, :] = edge_ref[:, seam : seam + 2, :]
    fields_ref[:, pixel_rows + 2 : pixel_rows + 4, :] = edge_ref[:, seam + 2 : seam + 4, :]
    out_ref[:, : 2 * tiles, :] = edge_ref[:, : 2 * tiles, :]
    out_ref[:, rows:, :] = edge_ref[:, 2 * tiles : 4 * tiles, :]
    invert_tiles([stack_ref], 0, width, operator_ref, fields_ref, 2)
    for r in range(0, rows - 2 * tiles, 8):
        near = [[fields_ref[f, r + k : r + k + 8, :] for k in range(3)] for f in range(2)]
        first = tiles + r
        velocity, variance, _ = resample(near, first, index_ref, weight_ref)
        cover = cover_ref[first : first + 8, :].astype(jnp.float32)
        store_cells(out_ref, tiles + first, velocity, variance, cover, north_ref[first : first + 8, :], north_c)


    here = lax.axis_index("track")
    lines = rows // tiles + 2
    for half, to_ref in zip((here, 1 - here), to_refs):
        start = half * (tiles - span)
        for i in range(lines):
            to_ref[:, i * span : (i + 1) * span, :] = out_ref[:, pl.ds(i * tiles + start, span), :]
        left = to_ref.shape[1] - lines * span
        if left:
            to_ref[:, lines * span :, :] = jnp.zeros((2, left, LANES), jnp.float32)


def inner(stack, edge, operator, cells, tiles, tracks, span, copies):
    rows = cells[0].shape[1]
    compact = -(-(rows // tiles + 2) * span // 8) * 8
    vmem = pl.BlockSpec(memory_space=pltpu.VMEM)
    return pl.pallas_call(
        functools.partial(inner_kernel, tiles, tracks, span),
        in_specs=[vmem] * 7,
        out_specs=[vmem] * (copies + 1),
        out_shape=[jax.ShapeDtypeStruct((2, compact, LANES), jnp.float32)] * copies
        + [jax.ShapeDtypeStruct((edge.shape[1] - 4 * tiles - 8, LANES), jnp.float32)],
        scratch_shapes=[
            pltpu.VMEM((2, -(-(rows - 2 * tiles + 2) // 8) * 8, LANES), jnp.float32),
            pltpu.VMEM((2, rows + 2 * tiles, LANES), jnp.float32),
        ],
        compiler_params=pltpu.CompilerParams(vmem_limit_bytes=medium),
        name="inner_rows",
    )(stack, *(pltpu.with_memory_space_constraint(a, pltpu.VMEM) for a in (edge, operator, *cells)))


def solve_cells(of_tracks, sight_ref, tracks):
    a11 = a12 = a22 = b1 = b2 = 0.0
    for t, values_ref in of_tracks:
        weight, target = values_ref[0], values_ref[1]
        east_c, up_c = sight_ref[pl.ds(t, 1), :], sight_ref[pl.ds(tracks + t, 1), :]
        by_east, by_up = weight * east_c, weight * up_c
        a11 = a11 + by_east * east_c
        a12 = a12 + by_east * up_c
        a22 = a22 + by_up * up_c
        b1 = b1 + by_east * target
        b2 = b2 + by_up * target
    a11 = a11 + ridge_term
    a22 = a22 + ridge_term
    determ = a11 * a22 - a12 * a12
    return (a22 * b1 - a12 * b2) / determ, (a11 * b2 - a12 * b1) / determ


def final_kernel(
    tiles, span, own, tracks, sight_ref, own_ref, other_ref, north_ref, east_up_ref, strain_ref, work_ref, line_ref
):
    lines = north_ref.shape[0] // tiles
    rows = lines * span
    here = lax.axis_index("track")
    start = here * (tiles - span)
    at = sight_ref.shape[0] - 2 * tiles + start
    line_ref[:span, :] = sight_ref[pl.ds(at, span), :]
    for i in range(lines):
        line_ref[(i + 1) * span : (i + 2) * span, :] = north_ref[pl.ds(i * tiles + start, span), :]
    line_ref[rows + span : rows + 2 * span, :] = sight_ref[pl.ds(at + tiles, span), :]
    lane = lax.broadcasted_iota(jnp.int32, (rows, LANES), 1)
    tile = lax.broadcasted_iota(jnp.int32, (rows, LANES), 0) % span

    def across(field):
        right = jnp.where(tile == span - 1, 0.0, pltpu.roll(field, rows - 1, 0))
        left = jnp.where(tile == 0, 0.0, pltpu.roll(field, 1, 0))
        following = jnp.where(lane == LANES - 1, pltpu.roll(right, LANES - 1, 1), pltpu.roll(field, LANES - 1, 1))
        previous = jnp.where(lane == 0, pltpu.roll(left, 1, 1), pltpu.roll(field, 1, 1))
        return following - previous

    if other_ref.shape[0] == 1:
        of_tracks = [(here, own_ref), (1 - here, other_ref.at[0])]
    else:
        of_tracks = [(t, other_ref.at[t]) for t in range(other_ref.shape[0])]
    wide_east, wide_up = solve_cells(of_tracks, sight_ref, tracks)
    wide_north = line_ref[...]
    east, up, north = (wide[span : span + rows] for wide in (wide_east, wide_up, wide_north))
    work_ref[0] = east
    work_ref[1] = up
    work_ref[2] = across(east) / 2.0
    work_ref[3] = (wide_north[2 * span : 2 * span + rows] - wide_north[:rows]) / 2.0
    work_ref[4] = (wide_east[2 * span : 2 * span + rows] - wide_east[:rows] + across(north)) / 4.0
    first = here * own - start
    for field in range(5):
        target, at = (east_up_ref, field) if field < 2 else (strain_ref, field - 2)
        for i in range(lines):
            for j in range(own):
                target[at, i : i + 1, j * LANES : (j + 1) * LANES] = work_ref[field, pl.ds(i * span + first + j, 1), :]


def final(sight, vals, others, north, tiles, span, own, tracks):
    lines = north.shape[0] // tiles
    shape = (lines, own * LANES)
    vmem = pl.BlockSpec(memory_space=pltpu.VMEM)
    return pl.pallas_call(
        functools.partial(final_kernel, tiles, span, own, tracks),
        in_specs=[vmem] * 4,
        out_specs=[vmem] * 2,
        out_shape=[jax.ShapeDtypeStruct((2, *shape), jnp.float32), jax.ShapeDtypeStruct((3, *shape), jnp.float32)],
        scratch_shapes=[pltpu.VMEM((5, lines * span, LANES), jnp.float32), pltpu.VMEM(vals.shape[1:], jnp.float32)],
        compiler_params=pltpu.CompilerParams(vmem_limit_bytes=medium),
        name="solve_and_strain",
    )(sight, vals, others, north)


def per_device(phases, coherent, pairs, res_index, res_weight, coverage, los, north):
    parts = lax.axis_size("pix")
    tracks = lax.axis_size("track")
    grid_rows, columns = north.shape
    tiles = columns // CTILE
    rows = grid_rows * tiles
    group = GROUP if parts % GROUP == 0 else parts
    planes = parts // group
    plane, column = jnp.divmod(lax.axis_index("pix").astype(jnp.int32), group)
    steps = [-s % planes for s in range(planes)]
    first_piece, first_token = pack_edges(phases[0], coherent[0], group, tiles, steps[1:2])
    rest_flags, _ = lax.optimization_barrier((coherent[0], first_token))
    own_piece, *others, packed_token = pack_edges(phases[0], rest_flags, group, tiles, steps[:1] + steps[2:])
    packed = [own_piece, first_piece, *others]
    later_pairs, _ = lax.optimization_barrier((pairs[0], packed_token))
    steps_j, steps_s = jnp.meshgrid(jnp.arange(group), jnp.arange(planes), indexing="ij")
    sources = (partner_back(plane, -steps_s % planes, planes) * group + partner_back(column, steps_j, group)).reshape(-1)
    by_part = later_pairs.reshape(parts, -1, 2)
    edge_pairs = jnp.take(by_part, sources, axis=0).reshape(-1, 2)
    order = [snake(n, group) for n in range(parts)]
    inner_pairs = jnp.concatenate([by_part[p] for p in order], axis=0)
    operator, edge_operator, formed_token = setup_track(inner_pairs, edge_pairs)
    ids = [(z, c) for z in range(planes) for c in range(group)]
    arrived = [packed[0]] * planes
    for s in range(1, planes):
        far = [(z * group + c, partner(z, planes - s, planes) * group + c) for z, c in ids]
        arrived[s] = lax.ppermute(packed[s], "pix", far)
    by_column = regroup(formed_token, arrived, group)
    pieces = [by_column[0]]
    for j in range(1, group):
        near = [(z * group + c, z * group + partner(c, j, group)) for z, c in ids]
        pieces.append(lax.ppermute(by_column[j], "pix", near))
    later_flags, *_ = lax.optimization_barrier((coherent[0], packed_token))
    inner_stack = lax.all_to_all(
        pack_inner(phases[0], later_flags, parts, group, tiles),
        "pix",
        split_axis=0,
        concat_axis=0,
        tiled=True,
        axis_index_groups=[order],
    )
    north_cells = north.reshape(rows, LANES)
    cells = (
        res_index.reshape(-1, rows, LANES),
        res_weight.reshape(-1, rows, LANES),
        coverage.reshape(rows, 1),
        north_cells,
    )

    def flat(stack):
        return stack.reshape(-1, stack.shape[-1])

    onward = [(i, i + 1) for i in range(parts - 1)]
    back = [(j, i) for i, j in onward]
    kept, for_before, for_after = edges(
        los, [flat(piece) for piece in pieces], edge_operator, cells, fixed(cells, tiles), tiles
    )
    before = lax.ppermute(for_after, "pix", onward)
    after = lax.ppermute(for_before, "pix", back)
    edge_vals = finish(kept, before, after, cells, tiles, tracks)
    own_tiles = tiles // tracks
    if tracks == 2:
        span = own_tiles + 1
        vals, for_other, sight = inner(flat(inner_stack), edge_vals, operator, cells, tiles, tracks, span, 2)
        others = lax.ppermute(for_other, "track", [(0, 1), (1, 0)])[None]
    else:
        span = tiles
        vals, sight = inner(flat(inner_stack), edge_vals, operator, cells, tiles, tracks, span, 1)
        others = lax.all_gather(vals, "track", axis=0)
    return tuple(final(sight, vals, others, north_cells, tiles, span, own_tiles, tracks))


def solution(mesh):
    in_specs = (
        P("track", "pix", None),
        P("track", "pix", None),
        P("track", None, None),
        P("track", None, "pix"),
        P("track", None, "pix"),
        P("track", "pix", None),
        P(),
        P("pix", None),
    )
    out_specs = (P(None, "pix", "track"), P(None, "pix", "track"))
    return jax.shard_map(
        per_device, mesh=mesh, in_specs=in_specs, out_specs=out_specs, check_vma=False
    )
```

```python
import functools

import jax
import jax.numpy as jnp
from jax import lax
from jax.experimental import pallas as pl
from jax.experimental.pallas import tpu as pltpu
from jax.sharding import PartitionSpec as P

EPOCHS = 200
EXTRA = 16
HALO = 128
CTILE = 128
MBLK = 128
LANES = 128
TILE = 256
GROUP = 4
EDGE_COST = 54_000_000_000

token = jax.ShapeDtypeStruct((8, LANES), jnp.float32)


prior_var = 0.1
ridge_term = 0.5
medium = 24 * 1024 * 1024


def stay(array):
    return pltpu.with_memory_space_constraint(array, pltpu.HBM)


def expand_masks(flags_ref, stacked_ref, firsts, wanted, tile_out):
    ifgs = flags_ref.shape[0]
    for n, first in enumerate(firsts):
        stacked_ref[n * ifgs : (n + 1) * ifgs, :] = part_flags(flags_ref, first)
    stacked = stacked_ref[...].astype(jnp.bfloat16)
    block = lax.broadcasted_iota(jnp.int32, (LANES, 2 * MBLK), 0)
    right = lax.broadcasted_iota(jnp.int32, (LANES, 2 * MBLK), 1) >= MBLK
    for start in range(0, len(wanted), 2):
        here = jnp.where(right, wanted[start + 1], wanted[start])
        ones = (block == here).astype(jnp.bfloat16)
        keep = jnp.dot(stacked, ones, preferred_element_type=jnp.float32).astype(jnp.bfloat16)
        for n in range(len(firsts)):
            tile_out(n, start * MBLK, keep[n * ifgs : (n + 1) * ifgs])


def part_flags(flags_ref, first):
    lead = pl.multiple_of(first // LANES * LANES, LANES)
    flags = (flags_ref[:, pl.ds(lead, LANES)] == 1).astype(jnp.float32)
    return pltpu.roll(flags, (LANES - (first - lead)) % LANES, 1)


def partner(index, step, size):
    return index ^ step if size & (size - 1) == 0 else (index + step) % size


def partner_back(index, step, size):
    return index ^ step if size & (size - 1) == 0 else (index - step + size) % size


def pack_edges_kernel(tiles, group, steps, flags_hbm, phases_ref, *refs):
    *out_refs, token_ref, flags_ref, stacked_ref, near_ref, flag_sem, in_sem = refs
    token_ref[...] = jnp.zeros_like(token_ref)
    ifgs, blocks = flags_ref.shape
    reach = tiles + 1
    half = reach * MBLK
    parts = lax.axis_size("pix")
    planes = parts // group
    span = blocks // parts
    flag_copy = pltpu.make_async_copy(flags_hbm, flags_ref, flag_sem)
    flag_copy.start()
    plane = lax.axis_index("pix") // group
    first_parts = [partner(plane, step, planes) * group for step in steps]

    def regions(act):
        for n, first_part in enumerate(first_parts):
            for g in range(group + 1):
                b = first_part + g
                to_ref, sem = near_ref.at[n, g], in_sem.at[n, g]

                @pl.when(b == 0)
                def _():
                    act(pltpu.make_async_copy(phases_ref.at[:, pl.ds(0, half)], to_ref.at[:, pl.ds(half, half)], sem))

                @pl.when(b == parts)
                def _():
                    low = blocks * MBLK - half
                    act(pltpu.make_async_copy(phases_ref.at[:, pl.ds(low, half)], to_ref.at[:, pl.ds(0, half)], sem))

                @pl.when(jnp.logical_and(b > 0, b < parts))
                def _():
                    low = pl.multiple_of((span * jnp.clip(b, 1, parts - 1) - reach) * MBLK, MBLK)
                    act(pltpu.make_async_copy(phases_ref.at[:, pl.ds(low, 2 * half)], to_ref, sem))

    regions(lambda copy: copy.start())
    flag_copy.wait()
    firsts = [(first_part + g) * span for first_part in first_parts for g in range(group)]

    def tile_out(n, start, keep):
        out_refs[n // group][n % group, :, start : start + 2 * MBLK] = keep

    wanted = [k if k < reach else span - 2 * reach + k for k in range(2 * reach)]
    expand_masks(flags_ref, stacked_ref, firsts, wanted, tile_out)
    regions(lambda copy: copy.wait())
    for n, out_ref in enumerate(out_refs):
        for g in range(group):
            out_ref[g, :, :half] *= near_ref[n, g, :, half:]
            out_ref[g, :, half:] *= near_ref[n, g + 1, :, :half]


def pack_edges(phases, flags, group, tiles, steps):
    ifgs = phases.shape[0]
    hbm = pl.BlockSpec(memory_space=pltpu.HBM)
    width = 2 * (tiles + 1) * MBLK
    count = len(steps)
    return pl.pallas_call(
        functools.partial(pack_edges_kernel, tiles, group, steps),
        in_specs=[hbm, hbm],
        out_specs=[pl.BlockSpec(memory_space=pltpu.VMEM)] * (count + 1),
        out_shape=[jax.ShapeDtypeStruct((group, ifgs, width), jnp.bfloat16)] * count + [token],
        scratch_shapes=[
            pltpu.VMEM(flags.shape, jnp.int32),
            pltpu.VMEM((count * group * ifgs, LANES), jnp.float32),
            pltpu.VMEM((count, group + 1, ifgs, width), jnp.bfloat16),
            pltpu.SemaphoreType.DMA,
            pltpu.SemaphoreType.DMA((count, group + 1)),
        ],
        compiler_params=pltpu.CompilerParams(vmem_limit_bytes=medium),
        name="pack_edges",
    )(stay(flags), stay(phases))


def regroup_kernel(planes, group, after_ref, *refs):
    in_refs, out_refs = refs[:planes], refs[planes:]
    for j in range(group):
        column = partner(lax.rem(lax.axis_index("pix"), group), j, group)
        for s in range(planes):
            out_refs[j][s] = in_refs[s][column]


def regroup(after, pieces, group):
    planes = len(pieces)
    vmem = pl.BlockSpec(memory_space=pltpu.VMEM)
    shape = (planes, *pieces[0].shape[1:])
    return pl.pallas_call(
        functools.partial(regroup_kernel, planes, group),
        in_specs=[vmem] * (planes + 1),
        out_specs=[vmem] * group,
        out_shape=[jax.ShapeDtypeStruct(shape, jnp.bfloat16)] * group,
        compiler_params=pltpu.CompilerParams(vmem_limit_bytes=medium),
        name="regroup",
    )(after, *pieces)


def snake(n, group):
    plane, column = n // group, n % group
    return n + (plane + 1) % 2 * (group - 1 - 2 * column)


def pack_inner_kernel(reach, group, flags_hbm, phases_ref, out_ref, flags_ref, stacked_ref, held_ref, flag_sem, in_sem):
    parts, ifgs, width = out_ref.shape
    span = flags_ref.shape[1] // parts
    flag_copy = pltpu.make_async_copy(flags_hbm, flags_ref, flag_sem)
    flag_copy.start()

    def inward(n):
        low = pl.multiple_of((snake(n, group) * span + reach) * MBLK, MBLK)
        return pltpu.make_async_copy(phases_ref.at[:, pl.ds(low, width)], held_ref.at[n], in_sem.at[n])

    @pl.loop(0, parts)
    def _(p):
        inward(p).start()

    flag_copy.wait()

    def tile_out(n, start, keep):
        out_ref[n, :, start : start + 2 * MBLK] = keep

    wanted = list(range(reach, span - reach))
    expand_masks(flags_ref, stacked_ref, [snake(n, group) * span for n in range(parts)], wanted, tile_out)

    @pl.loop(0, parts)
    def _(p):
        inward(p).wait()
        out_ref[p] *= held_ref[p]


def pack_inner(phases, flags, parts, group, tiles):
    ifgs = phases.shape[0]
    reach = tiles + 1
    width = (flags.shape[1] // parts - 2 * reach) * MBLK
    hbm = pl.BlockSpec(memory_space=pltpu.HBM)
    return pl.pallas_call(
        functools.partial(pack_inner_kernel, reach, group),
        in_specs=[hbm, hbm],
        out_specs=pl.BlockSpec(memory_space=pltpu.VMEM),
        out_shape=jax.ShapeDtypeStruct((parts, ifgs, width), jnp.bfloat16),
        scratch_shapes=[
            pltpu.VMEM(flags.shape, jnp.int32),
            pltpu.VMEM((parts * ifgs, LANES), jnp.float32),
            pltpu.VMEM((parts, ifgs, width), jnp.bfloat16),
            pltpu.SemaphoreType.DMA,
            pltpu.SemaphoreType.DMA((parts,)),
        ],
        compiler_params=pltpu.CompilerParams(vmem_limit_bytes=medium),
        name="pack_inner",
    )(stay(flags), stay(phases))


def split(a, terms):
    parts = []
    for _ in range(terms):
        parts.append(a.astype(jnp.bfloat16))
        a = a - parts[-1].astype(jnp.float32)
    return parts


def sum_dots(pairs):
    return sum(jnp.dot(a, b, preferred_element_type=jnp.float32) for a, b in pairs)


def operator_kernel(pairs_ref, other_ref, out_ref, other_out_ref, token_ref, laplacian_ref, inverse_ref):
    token_ref[...] = jnp.zeros_like(token_ref)
    ifgs = pairs_ref.shape[1]
    size = inverse_ref.shape[0]
    epoch = lax.broadcasted_iota(jnp.int32, (size, ifgs), 0)

    def ends(ref):
        return (epoch == ref[1:2, :]).astype(jnp.float32) - (epoch == ref[0:1, :]).astype(jnp.float32)

    across = ends(pairs_ref)
    down = across.T
    eye = (
        lax.broadcasted_iota(jnp.int32, (size, size), 0) == lax.broadcasted_iota(jnp.int32, (size, size), 1)
    ).astype(jnp.float32)
    laplacian = jnp.dot(across.astype(jnp.bfloat16), down.astype(jnp.bfloat16), preferred_element_type=jnp.float32)
    normal = eye + laplacian
    laplacian_ref[...] = laplacian.astype(jnp.bfloat16)
    first = eye / jnp.where(eye == 1.0, normal, 1.0)
    scaled = jnp.sum(first, axis=1, keepdims=True) * normal * jnp.sum(first, axis=0, keepdims=True)
    inverse_ref[...] = 2.0 * first - scaled

    def unfinished(state):
        step, gap = state
        return jnp.logical_and(step < 24, gap > 1e-5)

    def improve(state):
        step, _ = state
        inverse = inverse_ref[...]
        parts = split(inverse, 3)
        rest = eye - inverse - sum_dots((laplacian_ref[...], part) for part in parts)
        high, low = split(rest, 2)
        inverse_ref[...] = inverse + sum_dots(((parts[0], low), (parts[1], high), (parts[0], high)))
        return step + 1, jnp.max(jnp.abs(rest))

    lax.while_loop(unfinished, improve, (jnp.int32(0), jnp.float32(1.0)))
    place = lax.broadcasted_iota(jnp.int32, (size, ifgs), 0)
    centred = place.astype(jnp.float32) - (EPOCHS - 1) / 2.0
    square = sum((e - (EPOCHS - 1) / 2.0) ** 2 for e in range(EPOCHS))
    slope = jnp.where(place < EPOCHS, centred * (EPOCHS - 1) / square, 0.0)
    same = lax.broadcasted_iota(jnp.int32, (ifgs, ifgs), 0) == lax.broadcasted_iota(jnp.int32, (ifgs, ifgs), 1)
    extra = lax.broadcasted_iota(jnp.int32, (EXTRA, ifgs), 0)
    for ref, to_ref in ((pairs_ref, out_ref), (other_ref, other_out_ref)):
        across = ends(ref)
        ones = across.astype(jnp.bfloat16)
        pseudo = sum_dots((part, ones) for part in split(inverse_ref[...], 3)).astype(jnp.bfloat16)
        fitted = jnp.dot(across.T.astype(jnp.bfloat16), pseudo, preferred_element_type=jnp.float32)
        to_ref[:ifgs, :] = (same.astype(jnp.float32) - fitted).astype(jnp.bfloat16)
        row = jnp.sum(pseudo.astype(jnp.float32) * slope, axis=0, keepdims=True)
        high = row.astype(jnp.bfloat16).astype(jnp.float32)
        rest = row - high
        middle = rest.astype(jnp.bfloat16).astype(jnp.float32)
        low = rest - middle
        terms = jnp.where(extra == 0, high, jnp.where(extra == 1, middle, jnp.where(extra == 2, low, 0.0)))
        to_ref[ifgs:, :] = terms.astype(jnp.bfloat16)


def setup_track(pair_rows, other_rows):
    ifgs = pair_rows.shape[0]
    size = -(-EPOCHS // LANES) * LANES
    vmem = pl.BlockSpec(memory_space=pltpu.VMEM)
    return pl.pallas_call(
        operator_kernel,
        in_specs=[vmem] * 2,
        out_specs=[vmem] * 3,
        out_shape=[jax.ShapeDtypeStruct((ifgs + EXTRA, ifgs), jnp.bfloat16)] * 2 + [token],
        scratch_shapes=[pltpu.VMEM((size, size), jnp.bfloat16), pltpu.VMEM((size, size), jnp.float32)],
        compiler_params=pltpu.CompilerParams(vmem_limit_bytes=medium),
        name="misfit_operator",
    )(pair_rows.T, other_rows.T)


def invert_tiles(stack_refs, first, width, operator_ref, fields_ref, base):
    ifgs = operator_ref.shape[1]
    for start in range(0, width, TILE):
        here = pl.ds(pl.multiple_of(first + start, LANES), TILE)
        stack = jnp.concatenate([ref[:, here] for ref in stack_refs], axis=0)
        product = jnp.dot(operator_ref[...], stack, preferred_element_type=jnp.float32)
        velocity = jnp.sum(product[ifgs : ifgs + 8], axis=0, keepdims=True)
        variance = jnp.sum(product[:ifgs] * product[:ifgs], axis=0, keepdims=True) / ifgs
        for k in range(TILE // LANES):
            row = pl.ds(base + start // LANES + k, 1)
            fields_ref[0, row, :] = velocity[:, k * LANES : (k + 1) * LANES]
            fields_ref[1, row, :] = variance[:, k * LANES : (k + 1) * LANES]


def pick(source, lane):
    return jnp.take_along_axis(source, lane, axis=1, mode="promise_in_bounds")


def resample(near, cell, index_ref, weight_ref):
    lanes = lax.broadcasted_iota(jnp.int32, (8, LANES), 1)
    here = pl.ds(cell, 8)
    sums = [jnp.zeros((8, LANES), jnp.float32)] * 2
    total = jnp.zeros((8, LANES), jnp.float32)
    for b in range(index_ref.shape[0]):
        weight = weight_ref[b, here, :]
        place = lanes + index_ref[b, here, :] + HALO
        lane = place & (LANES - 1)
        which = place >> 7
        total = total + weight
        for f in range(2):
            low, mid, high = (pick(near[f][k], lane) for k in range(3))
            taken = jnp.where(which == 0, low, jnp.where(which == 1, mid, high))
            sums[f] = sums[f] + taken * weight
    return sums[0] / total, sums[1] / total, total


def boundary(row, offsets, weights, sources, wanted):
    lanes = lax.broadcasted_iota(jnp.int32, (8, LANES), 1)
    rows = lax.broadcasted_iota(jnp.int32, (8, LANES), 0)
    sums = [jnp.zeros((8, LANES), jnp.float32)] * 2
    for offset, weight in zip(offsets, weights):
        place = lanes + offset + HALO
        lane = place & (LANES - 1)
        keep = jnp.where(jnp.logical_and(place >> 7 == wanted, rows == row), weight, 0.0)
        for f in range(2):
            sums[f] = sums[f] + pick(jnp.broadcast_to(sources[f], (8, LANES)), lane) * keep
    return sums


def store_cells(out_ref, at, velocity, variance, cover, north, north_c):
    out_ref[0, at : at + 8, :] = cover / (variance + prior_var)
    out_ref[1, at : at + 8, :] = velocity - north_c * north


def fixed_kernel(tiles, index_ref, weight_ref, cover_ref, north_ref, back_ref, onward_ref):
    taps, rows, _ = index_ref.shape
    place = lax.broadcasted_iota(jnp.int32, (tiles, LANES), 0) == lax.broadcasted_iota(jnp.int32, (tiles, LANES), 1)
    for half, to_ref in enumerate((back_ref, onward_ref)):
        edge = slice(half * (rows - tiles), half * (rows - tiles) + tiles)
        outermost = half * (rows - 1)
        row = slice(outermost, outermost + 1)
        to_ref[:tiles, :] = north_ref[edge, :]
        total = sum(weight_ref[b, row, :] for b in range(taps))
        for b in range(taps):
            to_ref[tiles + b : tiles + b + 1, :] = index_ref[b, row, :].astype(jnp.float32)
            to_ref[tiles + taps + b : tiles + taps + b + 1, :] = weight_ref[b, row, :] / total
        at = tiles + 2 * taps
        cover = jnp.where(place, jnp.broadcast_to(cover_ref[edge, :].astype(jnp.float32), (tiles, LANES)), 0.0)
        to_ref[at : at + 1, :] = jnp.sum(cover, axis=0, keepdims=True)
        to_ref[at + 1 :, :] = jnp.zeros((to_ref.shape[0] - at - 1, LANES), jnp.float32)


def fixed(cells, tiles):
    rows = -(-(tiles + 2 * cells[0].shape[0] + 1) // 8) * 8
    vmem = pl.BlockSpec(memory_space=pltpu.VMEM)
    return pl.pallas_call(
        functools.partial(fixed_kernel, tiles),
        in_specs=[vmem] * 4,
        out_specs=[vmem] * 2,
        out_shape=[jax.ShapeDtypeStruct((rows, LANES), jnp.float32)] * 2,
        compiler_params=pltpu.CompilerParams(vmem_limit_bytes=medium),
        name="edge_inputs",
    )(*cells)


def edges_kernel(tiles, group, los_ref, *refs):
    stack_refs = refs[:group]
    operator_ref, index_ref, weight_ref, *fixed_refs, kept_ref, back_ref, onward_ref, fields_ref = refs[group:]
    width = stack_refs[0].shape[1]
    count = width // LANES
    rows = index_ref.shape[1]
    none = jnp.zeros((2, 1, LANES), jnp.float32)
    fields_ref[:, :1, :] = none
    fields_ref[:, count + 1 : count + 2, :] = none
    invert_tiles(stack_refs, 0, width, operator_ref, fields_ref, 1)
    seam = 2 * tiles
    kept_ref[:, seam : seam + 4, :] = fields_ref[:, tiles : tiles + 4, :]
    kept_ref[:, seam + 4 : seam + 5, :] = fields_ref[:, 1:2, :]
    kept_ref[:, seam + 5 : seam + 6, :] = fields_ref[:, count : count + 1, :]
    kept_ref[:, seam + 6 :, :] = jnp.zeros((2, kept_ref.shape[1] - seam - 6, LANES), jnp.float32)
    tracks = los_ref.shape[0]
    scalars = [los_ref[t, part] for part in (0, 2) for t in range(tracks)] + [los_ref[lax.axis_index("track"), 1]]
    for k, scalar in enumerate(scalars):
        row = seam + 8 + k
        kept_ref[0, row : row + 1, :] = jnp.full((1, LANES), scalar, jnp.float32)
    for half, (fixed_ref, to_ref) in enumerate(zip(fixed_refs, (back_ref, onward_ref))):
        first = half * (rows - tiles)
        after = to_ref.shape[0] - fixed_ref.shape[0]
        to_ref[after:, :] = fixed_ref[...]
        for r in range(0, tiles, 8):
            base = half * (tiles + 2) + r
            near = [[fields_ref[f, base + k : base + k + 8, :] for k in range(3)] for f in range(2)]
            velocity, variance, _ = resample(near, first + r, index_ref, weight_ref)
            for f, values in enumerate((velocity, variance)):
                kept_ref[f, half * tiles + r : half * tiles + r + 8, :] = values
                to_ref[f * tiles + r : f * tiles + r + 8, :] = values
        for f in range(2):
            to_ref[seam + f : seam + f + 1, :] = kept_ref[f, seam + 4 + half : seam + 5 + half, :]
        to_ref[seam + 2 : after, :] = jnp.zeros((after - seam - 2, LANES), jnp.float32)


def edges(los, stacks, operator, cells, both_fixed, tiles):
    rows = 2 * (tiles + 1)
    payload = -(-(2 * tiles + 2) // 8) * 8 + both_fixed[0].shape[0]
    sight = -(-(2 * los.shape[0] + 1) // 8) * 8
    shapes = [(2, 2 * tiles + 8 + sight, LANES), (payload, LANES), (payload, LANES)]
    vmem = pl.BlockSpec(memory_space=pltpu.VMEM)
    return pl.pallas_call(
        functools.partial(edges_kernel, tiles, len(stacks)),
        in_specs=[pl.BlockSpec(memory_space=pltpu.SMEM)] + [vmem] * (len(stacks) + 5),
        out_specs=[vmem] * 3,
        out_shape=[jax.ShapeDtypeStruct(shape, jnp.float32) for shape in shapes],
        scratch_shapes=[pltpu.VMEM((2, -(-(rows + 2) // 8) * 8, LANES), jnp.float32)],
        compiler_params=pltpu.CompilerParams(vmem_limit_bytes=medium),
        cost_estimate=pl.CostEstimate(flops=EDGE_COST, bytes_accessed=0, transcendentals=0),
        name="edge_rows",
    )(los, *stacks, operator, *cells[:2], *both_fixed)


def finish_kernel(
    tiles, tracks, kept_ref, before_ref, after_ref, index_ref, weight_ref, cover_ref, north_ref, out_ref
):
    taps, rows, _ = index_ref.shape
    seam = 2 * tiles
    north_c = kept_ref[0, seam + 8 + 2 * tracks : seam + 9 + 2 * tracks, :]
    place = lax.broadcasted_iota(jnp.int32, (8, LANES), 0) - lax.broadcasted_iota(jnp.int32, (8, LANES), 1)
    for half, from_ref in enumerate((before_ref, after_ref)):
        fixed_ref = from_ref.at[-(-(seam + 2) // 8) * 8 :]
        edge = half * (tiles - 8)
        row = 7 * half
        outermost = half * (rows - 1)
        total = sum(weight_ref[b, outermost : outermost + 1, :] for b in range(taps))
        to_own = boundary(
            row,
            [index_ref[b, outermost : outermost + 1, :] for b in range(taps)],
            [weight_ref[b, outermost : outermost + 1, :] / total for b in range(taps)],
            [from_ref[seam + f : seam + f + 1, :] for f in range(2)],
            2 * half,
        )
        to_other = boundary(
            7 - row,
            [fixed_ref[tiles + b : tiles + b + 1, :].astype(jnp.int32) for b in range(taps)],
            [fixed_ref[tiles + taps + b : tiles + taps + b + 1, :] for b in range(taps)],
            [kept_ref[f, seam + 4 + half : seam + 5 + half, :] for f in range(2)],
            2 - 2 * half,
        )
        covers = fixed_ref[tiles + 2 * taps : tiles + 2 * taps + 1, :]
        for r in range(0, tiles, 8):
            first = half * (rows - tiles) + r
            values = [kept_ref[f, half * tiles + r : half * tiles + r + 8, :] for f in range(2)]
            if r == edge:
                values = [value + more for value, more in zip(values, to_own)]
            cover = cover_ref[first : first + 8, :].astype(jnp.float32)
            store_cells(out_ref, (1 + half) * tiles + r, *values, cover, north_ref[first : first + 8, :], north_c)
            values = [from_ref[f * tiles + r : f * tiles + r + 8, :] for f in range(2)]
            if r == tiles - 8 - edge:
                values = [value + more for value, more in zip(values, to_other)]
            cover = jnp.sum(jnp.where(place == -r, jnp.broadcast_to(covers, (8, LANES)), 0.0), axis=1, keepdims=True)
            store_cells(out_ref, 3 * half * tiles + r, *values, cover, fixed_ref[r : r + 8, :], north_c)
    rest = 4 * tiles + kept_ref.shape[1] - seam
    out_ref[:, 4 * tiles : rest, :] = kept_ref[:, seam:, :]
    at = -(-(seam + 2) // 8) * 8
    for half, from_ref in enumerate((before_ref, after_ref)):
        here = slice(rest + half * tiles, rest + (half + 1) * tiles)
        out_ref[0, here, :] = from_ref[at : at + tiles, :]
        out_ref[1, here, :] = jnp.zeros((tiles, LANES), jnp.float32)


def finish(kept, before, after, cells, tiles, tracks):
    vmem = pl.BlockSpec(memory_space=pltpu.VMEM)
    return pl.pallas_call(
        functools.partial(finish_kernel, tiles, tracks),
        in_specs=[vmem] * 7,
        out_specs=vmem,
        out_shape=pltpu.VMEM((2, kept.shape[1] + 4 * tiles, LANES), jnp.float32),
        compiler_params=pltpu.CompilerParams(vmem_limit_bytes=medium),
        name="edge_cells",
    )(kept, before, after, *cells)


def inner_kernel(
    tiles, tracks, span, stack_ref, edge_ref, operator_ref, index_ref, weight_ref, cover_ref, north_ref, *refs
):
    *to_refs, sight_ref, fields_ref, out_ref = refs
    width = stack_ref.shape[1]
    rows = index_ref.shape[1]
    seam = 4 * tiles
    sight_ref[...] = edge_ref[0, seam + 8 :, :]
    north_c = edge_ref[0, seam + 8 + 2 * tracks : seam + 9 + 2 * tracks, :]
    pixel_rows = width // LANES
    fields_ref[:, 0:2, :] = edge_ref[:, seam : seam + 2, :]
    fields_ref[:, pixel_rows + 2 : pixel_rows + 4, :] = edge_ref[:, seam + 2 : seam + 4, :]
    out_ref[:, : 2 * tiles, :] = edge_ref[:, : 2 * tiles, :]
    out_ref[:, rows:, :] = edge_ref[:, 2 * tiles : 4 * tiles, :]
    invert_tiles([stack_ref], 0, width, operator_ref, fields_ref, 2)
    for r in range(0, rows - 2 * tiles, 8):
        near = [[fields_ref[f, r + k : r + k + 8, :] for k in range(3)] for f in range(2)]
        first = tiles + r
        velocity, variance, _ = resample(near, first, index_ref, weight_ref)
        cover = cover_ref[first : first + 8, :].astype(jnp.float32)
        store_cells(out_ref, tiles + first, velocity, variance, cover, north_ref[first : first + 8, :], north_c)


    here = lax.axis_index("track")
    lines = rows // tiles + 2
    for half, to_ref in zip((here, 1 - here), to_refs):
        start = half * (tiles - span)
        for i in range(lines):
            to_ref[:, i * span : (i + 1) * span, :] = out_ref[:, pl.ds(i * tiles + start, span), :]
        left = to_ref.shape[1] - lines * span
        if left:
            to_ref[:, lines * span :, :] = jnp.zeros((2, left, LANES), jnp.float32)


def inner(stack, edge, operator, cells, tiles, tracks, span, copies):
    rows = cells[0].shape[1]
    compact = -(-(rows // tiles + 2) * span // 8) * 8
    vmem = pl.BlockSpec(memory_space=pltpu.VMEM)
    return pl.pallas_call(
        functools.partial(inner_kernel, tiles, tracks, span),
        in_specs=[vmem] * 7,
        out_specs=[vmem] * (copies + 1),
        out_shape=[jax.ShapeDtypeStruct((2, compact, LANES), jnp.float32)] * copies
        + [jax.ShapeDtypeStruct((edge.shape[1] - 4 * tiles - 8, LANES), jnp.float32)],
        scratch_shapes=[
            pltpu.VMEM((2, -(-(rows - 2 * tiles + 2) // 8) * 8, LANES), jnp.float32),
            pltpu.VMEM((2, rows + 2 * tiles, LANES), jnp.float32),
        ],
        compiler_params=pltpu.CompilerParams(vmem_limit_bytes=medium),
        name="inner_rows",
    )(stack, *(pltpu.with_memory_space_constraint(a, pltpu.VMEM) for a in (edge, operator, *cells)))


def solve_cells(of_tracks, sight_ref, tracks):
    a11 = a12 = a22 = b1 = b2 = 0.0
    for t, values_ref in of_tracks:
        weight, target = values_ref[0], values_ref[1]
        east_c, up_c = sight_ref[pl.ds(t, 1), :], sight_ref[pl.ds(tracks + t, 1), :]
        by_east, by_up = weight * east_c, weight * up_c
        a11 = a11 + by_east * east_c
        a12 = a12 + by_east * up_c
        a22 = a22 + by_up * up_c
        b1 = b1 + by_east * target
        b2 = b2 + by_up * target
    a11 = a11 + ridge_term
    a22 = a22 + ridge_term
    determ = a11 * a22 - a12 * a12
    return (a22 * b1 - a12 * b2) / determ, (a11 * b2 - a12 * b1) / determ


def final_kernel(
    tiles, span, own, tracks, sight_ref, own_ref, other_ref, north_ref, east_up_ref, strain_ref, work_ref, line_ref
):
    lines = north_ref.shape[0] // tiles
    rows = lines * span
    here = lax.axis_index("track")
    start = here * (tiles - span)
    at = sight_ref.shape[0] - 2 * tiles + start
    line_ref[:span, :] = sight_ref[pl.ds(at, span), :]
    for i in range(lines):
        line_ref[(i + 1) * span : (i + 2) * span, :] = north_ref[pl.ds(i * tiles + start, span), :]
    line_ref[rows + span : rows + 2 * span, :] = sight_ref[pl.ds(at + tiles, span), :]
    lane = lax.broadcasted_iota(jnp.int32, (rows, LANES), 1)
    tile = lax.broadcasted_iota(jnp.int32, (rows, LANES), 0) % span

    def across(field):
        right = jnp.where(tile == span - 1, 0.0, pltpu.roll(field, rows - 1, 0))
        left = jnp.where(tile == 0, 0.0, pltpu.roll(field, 1, 0))
        following = jnp.where(lane == LANES - 1, pltpu.roll(right, LANES - 1, 1), pltpu.roll(field, LANES - 1, 1))
        previous = jnp.where(lane == 0, pltpu.roll(left, 1, 1), pltpu.roll(field, 1, 1))
        return following - previous

    if other_ref.shape[0] == 1:
        of_tracks = [(here, own_ref), (1 - here, other_ref.at[0])]
    else:
        of_tracks = [(t, other_ref.at[t]) for t in range(other_ref.shape[0])]
    wide_east, wide_up = solve_cells(of_tracks, sight_ref, tracks)
    wide_north = line_ref[...]
    east, up, north = (wide[span : span + rows] for wide in (wide_east, wide_up, wide_north))
    work_ref[0] = east
    work_ref[1] = up
    work_ref[2] = across(east) / 2.0
    work_ref[3] = (wide_north[2 * span : 2 * span + rows] - wide_north[:rows]) / 2.0
    work_ref[4] = (wide_east[2 * span : 2 * span + rows] - wide_east[:rows] + across(north)) / 4.0
    first = here * own - start
    for field in range(5):
        target, at = (east_up_ref, field) if field < 2 else (strain_ref, field - 2)
        for j in range(own):
            target[at, :, j * LANES : (j + 1) * LANES] = work_ref[field, pl.ds(first + j, lines, stride=span), :]


def final(sight, vals, others, north, tiles, span, own, tracks):
    lines = north.shape[0] // tiles
    shape = (lines, own * LANES)
    vmem = pl.BlockSpec(memory_space=pltpu.VMEM)
    return pl.pallas_call(
        functools.partial(final_kernel, tiles, span, own, tracks),
        in_specs=[vmem] * 4,
        out_specs=[vmem] * 2,
        out_shape=[jax.ShapeDtypeStruct((2, *shape), jnp.float32), jax.ShapeDtypeStruct((3, *shape), jnp.float32)],
        scratch_shapes=[pltpu.VMEM((5, lines * span, LANES), jnp.float32), pltpu.VMEM(vals.shape[1:], jnp.float32)],
        compiler_params=pltpu.CompilerParams(vmem_limit_bytes=medium),
        name="solve_and_strain",
    )(sight, vals, others, north)


def per_device(phases, coherent, pairs, res_index, res_weight, coverage, los, north):
    parts = lax.axis_size("pix")
    tracks = lax.axis_size("track")
    grid_rows, columns = north.shape
    tiles = columns // CTILE
    rows = grid_rows * tiles
    group = GROUP if parts % GROUP == 0 else parts
    planes = parts // group
    plane, column = jnp.divmod(lax.axis_index("pix").astype(jnp.int32), group)
    steps = [-s % planes for s in range(planes)]
    first_piece, first_token = pack_edges(phases[0], coherent[0], group, tiles, steps[1:2])
    rest_flags, _ = lax.optimization_barrier((coherent[0], first_token))
    own_piece, *others, packed_token = pack_edges(phases[0], rest_flags, group, tiles, steps[:1] + steps[2:])
    packed = [own_piece, first_piece, *others]
    later_pairs, _ = lax.optimization_barrier((pairs[0], packed_token))
    steps_j, steps_s = jnp.meshgrid(jnp.arange(group), jnp.arange(planes), indexing="ij")
    sources = (partner_back(plane, -steps_s % planes, planes) * group + partner_back(column, steps_j, group)).reshape(-1)
    by_part = later_pairs.reshape(parts, -1, 2)
    edge_pairs = jnp.take(by_part, sources, axis=0).reshape(-1, 2)
    order = [snake(n, group) for n in range(parts)]
    inner_pairs = jnp.concatenate([by_part[p] for p in order], axis=0)
    operator, edge_operator, formed_token = setup_track(inner_pairs, edge_pairs)
    ids = [(z, c) for z in range(planes) for c in range(group)]
    arrived = [packed[0]] * planes
    for s in range(1, planes):
        far = [(z * group + c, partner(z, planes - s, planes) * group + c) for z, c in ids]
        arrived[s] = lax.ppermute(packed[s], "pix", far)
    by_column = regroup(formed_token, arrived, group)
    pieces = [by_column[0]]
    for j in range(1, group):
        near = [(z * group + c, z * group + partner(c, j, group)) for z, c in ids]
        pieces.append(lax.ppermute(by_column[j], "pix", near))
    later_flags, *_ = lax.optimization_barrier((coherent[0], packed_token))
    inner_stack = lax.all_to_all(
        pack_inner(phases[0], later_flags, parts, group, tiles),
        "pix",
        split_axis=0,
        concat_axis=0,
        tiled=True,
        axis_index_groups=[order],
    )
    north_cells = north.reshape(rows, LANES)
    cells = (
        res_index.reshape(-1, rows, LANES),
        res_weight.reshape(-1, rows, LANES),
        coverage.reshape(rows, 1),
        north_cells,
    )

    def flat(stack):
        return stack.reshape(-1, stack.shape[-1])

    onward = [(i, i + 1) for i in range(parts - 1)]
    back = [(j, i) for i, j in onward]
    kept, for_before, for_after = edges(
        los, [flat(piece) for piece in pieces], edge_operator, cells, fixed(cells, tiles), tiles
    )
    before = lax.ppermute(for_after, "pix", onward)
    after = lax.ppermute(for_before, "pix", back)
    edge_vals = finish(kept, before, after, cells, tiles, tracks)
    own_tiles = tiles // tracks
    if tracks == 2:
        span = own_tiles + 1
        vals, for_other, sight = inner(flat(inner_stack), edge_vals, operator, cells, tiles, tracks, span, 2)
        others = lax.ppermute(for_other, "track", [(0, 1), (1, 0)])[None]
    else:
        span = tiles
        vals, sight = inner(flat(inner_stack), edge_vals, operator, cells, tiles, tracks, span, 1)
        others = lax.all_gather(vals, "track", axis=0)
    return tuple(final(sight, vals, others, north_cells, tiles, span, own_tiles, tracks))


def solution(mesh):
    in_specs = (
        P("track", "pix", None),
        P("track", "pix", None),
        P("track", None, None),
        P("track", None, "pix"),
        P("track", None, "pix"),
        P("track", "pix", None),
        P(),
        P("pix", None),
    )
    out_specs = (P(None, "pix", "track"), P(None, "pix", "track"))
    return jax.shard_map(
        per_device, mesh=mesh, in_specs=in_specs, out_specs=out_specs, check_vma=False
    )
```

```python
import functools

import jax
import jax.numpy as jnp
from jax import lax
from jax.experimental import pallas as pl
from jax.experimental.pallas import tpu as pltpu
from jax.sharding import PartitionSpec as P

EPOCHS = 200
EXTRA = 16
HALO = 128
CTILE = 128
MBLK = 128
LANES = 128
TILE = 256
GROUP = 4
EDGE_COST = 54_000_000_000

token = jax.ShapeDtypeStruct((8, LANES), jnp.float32)


prior_var = 0.1
ridge_term = 0.5
medium = 24 * 1024 * 1024


def stay(array):
    return pltpu.with_memory_space_constraint(array, pltpu.HBM)


def expand_masks(flags_ref, stacked_ref, firsts, wanted, tile_out):
    ifgs = flags_ref.shape[0]
    for n, first in enumerate(firsts):
        stacked_ref[n * ifgs : (n + 1) * ifgs, :] = part_flags(flags_ref, first)
    stacked = stacked_ref[...].astype(jnp.bfloat16)
    block = lax.broadcasted_iota(jnp.int32, (LANES, 2 * MBLK), 0)
    right = lax.broadcasted_iota(jnp.int32, (LANES, 2 * MBLK), 1) >= MBLK
    for start in range(0, len(wanted), 2):
        here = jnp.where(right, wanted[start + 1], wanted[start])
        ones = (block == here).astype(jnp.bfloat16)
        keep = jnp.dot(stacked, ones, preferred_element_type=jnp.float32).astype(jnp.bfloat16)
        for n in range(len(firsts)):
            tile_out(n, start * MBLK, keep[n * ifgs : (n + 1) * ifgs])


def part_flags(flags_ref, first):
    lead = pl.multiple_of(first // LANES * LANES, LANES)
    flags = (flags_ref[:, pl.ds(lead, LANES)] == 1).astype(jnp.float32)
    return pltpu.roll(flags, (LANES - (first - lead)) % LANES, 1)


def partner(index, step, size):
    return index ^ step if size & (size - 1) == 0 else (index + step) % size


def partner_back(index, step, size):
    return index ^ step if size & (size - 1) == 0 else (index - step + size) % size


def pack_edges_kernel(tiles, group, steps, flags_hbm, phases_ref, *refs):
    *out_refs, token_ref, flags_ref, stacked_ref, near_ref, flag_sem, in_sem = refs
    token_ref[...] = jnp.zeros_like(token_ref)
    ifgs, blocks = flags_ref.shape
    reach = tiles + 1
    half = reach * MBLK
    parts = lax.axis_size("pix")
    planes = parts // group
    span = blocks // parts
    flag_copy = pltpu.make_async_copy(flags_hbm, flags_ref, flag_sem)
    flag_copy.start()
    plane = lax.axis_index("pix") // group
    first_parts = [partner(plane, step, planes) * group for step in steps]

    def regions(act):
        for n, first_part in enumerate(first_parts):
            for g in range(group + 1):
                b = first_part + g
                to_ref, sem = near_ref.at[n, g], in_sem.at[n, g]

                @pl.when(b == 0)
                def _():
                    act(pltpu.make_async_copy(phases_ref.at[:, pl.ds(0, half)], to_ref.at[:, pl.ds(half, half)], sem))

                @pl.when(b == parts)
                def _():
                    low = blocks * MBLK - half
                    act(pltpu.make_async_copy(phases_ref.at[:, pl.ds(low, half)], to_ref.at[:, pl.ds(0, half)], sem))

                @pl.when(jnp.logical_and(b > 0, b < parts))
                def _():
                    low = pl.multiple_of((span * jnp.clip(b, 1, parts - 1) - reach) * MBLK, MBLK)
                    act(pltpu.make_async_copy(phases_ref.at[:, pl.ds(low, 2 * half)], to_ref, sem))

    regions(lambda copy: copy.start())
    flag_copy.wait()
    firsts = [(first_part + g) * span for first_part in first_parts for g in range(group)]

    def tile_out(n, start, keep):
        out_refs[n // group][n % group, :, start : start + 2 * MBLK] = keep

    wanted = [k if k < reach else span - 2 * reach + k for k in range(2 * reach)]
    expand_masks(flags_ref, stacked_ref, firsts, wanted, tile_out)
    regions(lambda copy: copy.wait())
    for n, out_ref in enumerate(out_refs):
        for g in range(group):
            out_ref[g, :, :half] *= near_ref[n, g, :, half:]
            out_ref[g, :, half:] *= near_ref[n, g + 1, :, :half]


def pack_edges(phases, flags, group, tiles, steps):
    ifgs = phases.shape[0]
    hbm = pl.BlockSpec(memory_space=pltpu.HBM)
    width = 2 * (tiles + 1) * MBLK
    count = len(steps)
    return pl.pallas_call(
        functools.partial(pack_edges_kernel, tiles, group, steps),
        in_specs=[hbm, hbm],
        out_specs=[pl.BlockSpec(memory_space=pltpu.VMEM)] * (count + 1),
        out_shape=[jax.ShapeDtypeStruct((group, ifgs, width), jnp.bfloat16)] * count + [token],
        scratch_shapes=[
            pltpu.VMEM(flags.shape, jnp.int32),
            pltpu.VMEM((count * group * ifgs, LANES), jnp.float32),
            pltpu.VMEM((count, group + 1, ifgs, width), jnp.bfloat16),
            pltpu.SemaphoreType.DMA,
            pltpu.SemaphoreType.DMA((count, group + 1)),
        ],
        compiler_params=pltpu.CompilerParams(vmem_limit_bytes=medium),
        name="pack_edges",
    )(stay(flags), stay(phases))


def regroup_kernel(planes, group, after_ref, *refs):
    in_refs, out_refs = refs[:planes], refs[planes:]
    for j in range(group):
        column = partner(lax.rem(lax.axis_index("pix"), group), j, group)
        for s in range(planes):
            out_refs[j][s] = in_refs[s][column]


def regroup(after, pieces, group):
    planes = len(pieces)
    vmem = pl.BlockSpec(memory_space=pltpu.VMEM)
    shape = (planes, *pieces[0].shape[1:])
    return pl.pallas_call(
        functools.partial(regroup_kernel, planes, group),
        in_specs=[vmem] * (planes + 1),
        out_specs=[vmem] * group,
        out_shape=[jax.ShapeDtypeStruct(shape, jnp.bfloat16)] * group,
        compiler_params=pltpu.CompilerParams(vmem_limit_bytes=medium),
        name="regroup",
    )(after, *pieces)


def snake(n, group):
    plane, column = n // group, n % group
    return n + (plane + 1) % 2 * (group - 1 - 2 * column)


def pack_inner_kernel(reach, group, flags_hbm, phases_ref, out_ref, flags_ref, stacked_ref, held_ref, flag_sem, in_sem):
    parts, ifgs, width = out_ref.shape
    span = flags_ref.shape[1] // parts
    flag_copy = pltpu.make_async_copy(flags_hbm, flags_ref, flag_sem)
    flag_copy.start()

    def inward(n):
        low = pl.multiple_of((snake(n, group) * span + reach) * MBLK, MBLK)
        return pltpu.make_async_copy(phases_ref.at[:, pl.ds(low, width)], held_ref.at[n], in_sem.at[n])

    @pl.loop(0, parts)
    def _(p):
        inward(p).start()

    flag_copy.wait()

    def tile_out(n, start, keep):
        out_ref[n, :, start : start + 2 * MBLK] = keep

    wanted = list(range(reach, span - reach))
    expand_masks(flags_ref, stacked_ref, [snake(n, group) * span for n in range(parts)], wanted, tile_out)

    @pl.loop(0, parts)
    def _(p):
        inward(p).wait()
        out_ref[p] *= held_ref[p]


def pack_inner(phases, flags, parts, group, tiles):
    ifgs = phases.shape[0]
    reach = tiles + 1
    width = (flags.shape[1] // parts - 2 * reach) * MBLK
    hbm = pl.BlockSpec(memory_space=pltpu.HBM)
    return pl.pallas_call(
        functools.partial(pack_inner_kernel, reach, group),
        in_specs=[hbm, hbm],
        out_specs=pl.BlockSpec(memory_space=pltpu.VMEM),
        out_shape=jax.ShapeDtypeStruct((parts, ifgs, width), jnp.bfloat16),
        scratch_shapes=[
            pltpu.VMEM(flags.shape, jnp.int32),
            pltpu.VMEM((parts * ifgs, LANES), jnp.float32),
            pltpu.VMEM((parts, ifgs, width), jnp.bfloat16),
            pltpu.SemaphoreType.DMA,
            pltpu.SemaphoreType.DMA((parts,)),
        ],
        compiler_params=pltpu.CompilerParams(vmem_limit_bytes=medium),
        name="pack_inner",
    )(stay(flags), stay(phases))


def split(a, terms):
    parts = []
    for _ in range(terms):
        parts.append(a.astype(jnp.bfloat16))
        a = a - parts[-1].astype(jnp.float32)
    return parts


def sum_dots(pairs):
    return sum(jnp.dot(a, b, preferred_element_type=jnp.float32) for a, b in pairs)


def operator_kernel(pairs_ref, other_ref, out_ref, other_out_ref, token_ref, laplacian_ref, inverse_ref):
    token_ref[...] = jnp.zeros_like(token_ref)
    ifgs = pairs_ref.shape[1]
    size = inverse_ref.shape[0]
    epoch = lax.broadcasted_iota(jnp.int32, (size, ifgs), 0)

    def ends(ref):
        return (epoch == ref[1:2, :]).astype(jnp.float32) - (epoch == ref[0:1, :]).astype(jnp.float32)

    across = ends(pairs_ref)
    down = across.T
    eye = (
        lax.broadcasted_iota(jnp.int32, (size, size), 0) == lax.broadcasted_iota(jnp.int32, (size, size), 1)
    ).astype(jnp.float32)
    laplacian = jnp.dot(across.astype(jnp.bfloat16), down.astype(jnp.bfloat16), preferred_element_type=jnp.float32)
    normal = eye + laplacian
    laplacian_ref[...] = laplacian.astype(jnp.bfloat16)
    first = eye / jnp.where(eye == 1.0, normal, 1.0)
    scaled = jnp.sum(first, axis=1, keepdims=True) * normal * jnp.sum(first, axis=0, keepdims=True)
    inverse_ref[...] = 2.0 * first - scaled

    def unfinished(state):
        step, gap = state
        return jnp.logical_and(step < 24, gap > 1e-5)

    def improve(state):
        step, _ = state
        inverse = inverse_ref[...]
        parts = split(inverse, 3)
        rest = eye - inverse - sum_dots((laplacian_ref[...], part) for part in parts)
        high, low = split(rest, 2)
        inverse_ref[...] = inverse + sum_dots(((parts[0], low), (parts[1], high), (parts[0], high)))
        return step + 1, jnp.max(jnp.abs(rest))

    lax.while_loop(unfinished, improve, (jnp.int32(0), jnp.float32(1.0)))
    place = lax.broadcasted_iota(jnp.int32, (size, ifgs), 0)
    centred = place.astype(jnp.float32) - (EPOCHS - 1) / 2.0
    square = sum((e - (EPOCHS - 1) / 2.0) ** 2 for e in range(EPOCHS))
    slope = jnp.where(place < EPOCHS, centred * (EPOCHS - 1) / square, 0.0)
    same = lax.broadcasted_iota(jnp.int32, (ifgs, ifgs), 0) == lax.broadcasted_iota(jnp.int32, (ifgs, ifgs), 1)
    extra = lax.broadcasted_iota(jnp.int32, (EXTRA, ifgs), 0)
    for ref, to_ref in ((pairs_ref, out_ref), (other_ref, other_out_ref)):
        across = ends(ref)
        ones = across.astype(jnp.bfloat16)
        pseudo = sum_dots((part, ones) for part in split(inverse_ref[...], 3)).astype(jnp.bfloat16)
        fitted = jnp.dot(across.T.astype(jnp.bfloat16), pseudo, preferred_element_type=jnp.float32)
        to_ref[:ifgs, :] = (same.astype(jnp.float32) - fitted).astype(jnp.bfloat16)
        row = jnp.sum(pseudo.astype(jnp.float32) * slope, axis=0, keepdims=True)
        high = row.astype(jnp.bfloat16).astype(jnp.float32)
        rest = row - high
        middle = rest.astype(jnp.bfloat16).astype(jnp.float32)
        low = rest - middle
        terms = jnp.where(extra == 0, high, jnp.where(extra == 1, middle, jnp.where(extra == 2, low, 0.0)))
        to_ref[ifgs:, :] = terms.astype(jnp.bfloat16)


def setup_track(pair_rows, other_rows):
    ifgs = pair_rows.shape[0]
    size = -(-EPOCHS // LANES) * LANES
    vmem = pl.BlockSpec(memory_space=pltpu.VMEM)
    return pl.pallas_call(
        operator_kernel,
        in_specs=[vmem] * 2,
        out_specs=[vmem] * 3,
        out_shape=[jax.ShapeDtypeStruct((ifgs + EXTRA, ifgs), jnp.bfloat16)] * 2 + [token],
        scratch_shapes=[pltpu.VMEM((size, size), jnp.bfloat16), pltpu.VMEM((size, size), jnp.float32)],
        compiler_params=pltpu.CompilerParams(vmem_limit_bytes=medium),
        name="misfit_operator",
    )(pair_rows.T, other_rows.T)


def invert_tiles(stack_refs, first, width, operator_ref, fields_ref, base):
    ifgs = operator_ref.shape[1]
    for start in range(0, width, TILE):
        here = pl.ds(pl.multiple_of(first + start, LANES), TILE)
        stack = jnp.concatenate([ref[:, here] for ref in stack_refs], axis=0)
        product = jnp.dot(operator_ref[...], stack, preferred_element_type=jnp.float32)
        velocity = jnp.sum(product[ifgs : ifgs + 8], axis=0, keepdims=True)
        variance = jnp.sum(product[:ifgs] * product[:ifgs], axis=0, keepdims=True) / ifgs
        for k in range(TILE // LANES):
            row = pl.ds(base + start // LANES + k, 1)
            fields_ref[0, row, :] = velocity[:, k * LANES : (k + 1) * LANES]
            fields_ref[1, row, :] = variance[:, k * LANES : (k + 1) * LANES]


def pick(source, lane):
    return jnp.take_along_axis(source, lane, axis=1, mode="promise_in_bounds")


def resample(near, cell, index_ref, weight_ref):
    lanes = lax.broadcasted_iota(jnp.int32, (8, LANES), 1)
    here = pl.ds(cell, 8)
    sums = [jnp.zeros((8, LANES), jnp.float32)] * 2
    for b in range(index_ref.shape[0]):
        weight = weight_ref[b, here, :]
        place = lanes + index_ref[b, here, :] + HALO
        lane = place & (LANES - 1)
        which = place >> 7
        for f in range(2):
            low, mid, high = (pick(near[f][k], lane) for k in range(3))
            taken = jnp.where(which == 0, low, jnp.where(which == 1, mid, high))
            sums[f] = sums[f] + taken * weight
    return sums


def boundary(row, offsets, weights, sources, wanted):
    lanes = lax.broadcasted_iota(jnp.int32, (8, LANES), 1)
    rows = lax.broadcasted_iota(jnp.int32, (8, LANES), 0)
    sums = [jnp.zeros((8, LANES), jnp.float32)] * 2
    for offset, weight in zip(offsets, weights):
        place = lanes + offset + HALO
        lane = place & (LANES - 1)
        keep = jnp.where(jnp.logical_and(place >> 7 == wanted, rows == row), weight, 0.0)
        for f in range(2):
            sums[f] = sums[f] + pick(jnp.broadcast_to(sources[f], (8, LANES)), lane) * keep
    return sums


def store_cells(out_ref, at, velocity, variance, cover, north, north_c):
    out_ref[0, at : at + 8, :] = cover / (variance + prior_var)
    out_ref[1, at : at + 8, :] = velocity - north_c * north


def fixed_kernel(tiles, index_ref, weight_ref, cover_ref, north_ref, back_ref, onward_ref):
    taps, rows, _ = index_ref.shape
    place = lax.broadcasted_iota(jnp.int32, (tiles, LANES), 0) == lax.broadcasted_iota(jnp.int32, (tiles, LANES), 1)
    for half, to_ref in enumerate((back_ref, onward_ref)):
        edge = slice(half * (rows - tiles), half * (rows - tiles) + tiles)
        outermost = half * (rows - 1)
        row = slice(outermost, outermost + 1)
        to_ref[:tiles, :] = north_ref[edge, :]
        total = sum(weight_ref[b, row, :] for b in range(taps))
        for b in range(taps):
            to_ref[tiles + b : tiles + b + 1, :] = index_ref[b, row, :].astype(jnp.float32)
            to_ref[tiles + taps + b : tiles + taps + b + 1, :] = weight_ref[b, row, :] / total
        at = tiles + 2 * taps
        cover = jnp.where(place, jnp.broadcast_to(cover_ref[edge, :].astype(jnp.float32), (tiles, LANES)), 0.0)
        to_ref[at : at + 1, :] = jnp.sum(cover, axis=0, keepdims=True)
        to_ref[at + 1 :, :] = jnp.zeros((to_ref.shape[0] - at - 1, LANES), jnp.float32)


def fixed(cells, tiles):
    rows = -(-(tiles + 2 * cells[0].shape[0] + 1) // 8) * 8
    vmem = pl.BlockSpec(memory_space=pltpu.VMEM)
    return pl.pallas_call(
        functools.partial(fixed_kernel, tiles),
        in_specs=[vmem] * 4,
        out_specs=[vmem] * 2,
        out_shape=[jax.ShapeDtypeStruct((rows, LANES), jnp.float32)] * 2,
        compiler_params=pltpu.CompilerParams(vmem_limit_bytes=medium),
        name="edge_inputs",
    )(*cells)


def edges_kernel(tiles, group, los_ref, *refs):
    stack_refs = refs[:group]
    operator_ref, index_ref, weight_ref, *fixed_refs, kept_ref, back_ref, onward_ref, fields_ref = refs[group:]
    width = stack_refs[0].shape[1]
    count = width // LANES
    rows = index_ref.shape[1]
    none = jnp.zeros((2, 1, LANES), jnp.float32)
    fields_ref[:, :1, :] = none
    fields_ref[:, count + 1 : count + 2, :] = none
    invert_tiles(stack_refs, 0, width, operator_ref, fields_ref, 1)
    seam = 2 * tiles
    kept_ref[:, seam : seam + 4, :] = fields_ref[:, tiles : tiles + 4, :]
    kept_ref[:, seam + 4 : seam + 5, :] = fields_ref[:, 1:2, :]
    kept_ref[:, seam + 5 : seam + 6, :] = fields_ref[:, count : count + 1, :]
    kept_ref[:, seam + 6 :, :] = jnp.zeros((2, kept_ref.shape[1] - seam - 6, LANES), jnp.float32)
    tracks = los_ref.shape[0]
    scalars = [los_ref[t, part] for part in (0, 2) for t in range(tracks)] + [los_ref[lax.axis_index("track"), 1]]
    for k, scalar in enumerate(scalars):
        row = seam + 8 + k
        kept_ref[0, row : row + 1, :] = jnp.full((1, LANES), scalar, jnp.float32)
    for half, (fixed_ref, to_ref) in enumerate(zip(fixed_refs, (back_ref, onward_ref))):
        first = half * (rows - tiles)
        after = to_ref.shape[0] - fixed_ref.shape[0]
        to_ref[after:, :] = fixed_ref[...]
        for r in range(0, tiles, 8):
            base = half * (tiles + 2) + r
            near = [[fields_ref[f, base + k : base + k + 8, :] for k in range(3)] for f in range(2)]
            velocity, variance = resample(near, first + r, index_ref, weight_ref)
            for f, values in enumerate((velocity, variance)):
                kept_ref[f, half * tiles + r : half * tiles + r + 8, :] = values
                to_ref[f * tiles + r : f * tiles + r + 8, :] = values
        for f in range(2):
            to_ref[seam + f : seam + f + 1, :] = kept_ref[f, seam + 4 + half : seam + 5 + half, :]
        to_ref[seam + 2 : after, :] = jnp.zeros((after - seam - 2, LANES), jnp.float32)


def edges(los, stacks, operator, cells, both_fixed, tiles):
    rows = 2 * (tiles + 1)
    payload = -(-(2 * tiles + 2) // 8) * 8 + both_fixed[0].shape[0]
    sight = -(-(2 * los.shape[0] + 1) // 8) * 8
    shapes = [(2, 2 * tiles + 8 + sight, LANES), (payload, LANES), (payload, LANES)]
    vmem = pl.BlockSpec(memory_space=pltpu.VMEM)
    return pl.pallas_call(
        functools.partial(edges_kernel, tiles, len(stacks)),
        in_specs=[pl.BlockSpec(memory_space=pltpu.SMEM)] + [vmem] * (len(stacks) + 5),
        out_specs=[vmem] * 3,
        out_shape=[jax.ShapeDtypeStruct(shape, jnp.float32) for shape in shapes],
        scratch_shapes=[pltpu.VMEM((2, -(-(rows + 2) // 8) * 8, LANES), jnp.float32)],
        compiler_params=pltpu.CompilerParams(vmem_limit_bytes=medium),
        cost_estimate=pl.CostEstimate(flops=EDGE_COST, bytes_accessed=0, transcendentals=0),
        name="edge_rows",
    )(los, *stacks, operator, *cells[:2], *both_fixed)


def finish_kernel(
    tiles, tracks, kept_ref, before_ref, after_ref, index_ref, weight_ref, cover_ref, north_ref, out_ref
):
    taps, rows, _ = index_ref.shape
    seam = 2 * tiles
    north_c = kept_ref[0, seam + 8 + 2 * tracks : seam + 9 + 2 * tracks, :]
    place = lax.broadcasted_iota(jnp.int32, (8, LANES), 0) - lax.broadcasted_iota(jnp.int32, (8, LANES), 1)
    for half, from_ref in enumerate((before_ref, after_ref)):
        fixed_ref = from_ref.at[-(-(seam + 2) // 8) * 8 :]
        edge = half * (tiles - 8)
        row = 7 * half
        outermost = half * (rows - 1)
        total = sum(weight_ref[b, outermost : outermost + 1, :] for b in range(taps))
        to_own = boundary(
            row,
            [index_ref[b, outermost : outermost + 1, :] for b in range(taps)],
            [weight_ref[b, outermost : outermost + 1, :] / total for b in range(taps)],
            [from_ref[seam + f : seam + f + 1, :] for f in range(2)],
            2 * half,
        )
        to_other = boundary(
            7 - row,
            [fixed_ref[tiles + b : tiles + b + 1, :].astype(jnp.int32) for b in range(taps)],
            [fixed_ref[tiles + taps + b : tiles + taps + b + 1, :] for b in range(taps)],
            [kept_ref[f, seam + 4 + half : seam + 5 + half, :] for f in range(2)],
            2 - 2 * half,
        )
        covers = fixed_ref[tiles + 2 * taps : tiles + 2 * taps + 1, :]
        for r in range(0, tiles, 8):
            first = half * (rows - tiles) + r
            values = [kept_ref[f, half * tiles + r : half * tiles + r + 8, :] for f in range(2)]
            if r == edge:
                values = [value + more for value, more in zip(values, to_own)]
            cover = cover_ref[first : first + 8, :].astype(jnp.float32)
            store_cells(out_ref, (1 + half) * tiles + r, *values, cover, north_ref[first : first + 8, :], north_c)
            values = [from_ref[f * tiles + r : f * tiles + r + 8, :] for f in range(2)]
            if r == tiles - 8 - edge:
                values = [value + more for value, more in zip(values, to_other)]
            cover = jnp.sum(jnp.where(place == -r, jnp.broadcast_to(covers, (8, LANES)), 0.0), axis=1, keepdims=True)
            store_cells(out_ref, 3 * half * tiles + r, *values, cover, fixed_ref[r : r + 8, :], north_c)
    rest = 4 * tiles + kept_ref.shape[1] - seam
    out_ref[:, 4 * tiles : rest, :] = kept_ref[:, seam:, :]
    at = -(-(seam + 2) // 8) * 8
    for half, from_ref in enumerate((before_ref, after_ref)):
        here = slice(rest + half * tiles, rest + (half + 1) * tiles)
        out_ref[0, here, :] = from_ref[at : at + tiles, :]
        out_ref[1, here, :] = jnp.zeros((tiles, LANES), jnp.float32)


def finish(kept, before, after, cells, tiles, tracks):
    vmem = pl.BlockSpec(memory_space=pltpu.VMEM)
    return pl.pallas_call(
        functools.partial(finish_kernel, tiles, tracks),
        in_specs=[vmem] * 7,
        out_specs=vmem,
        out_shape=pltpu.VMEM((2, kept.shape[1] + 4 * tiles, LANES), jnp.float32),
        compiler_params=pltpu.CompilerParams(vmem_limit_bytes=medium),
        name="edge_cells",
    )(kept, before, after, *cells)


def inner_kernel(
    tiles, tracks, span, stack_ref, edge_ref, operator_ref, index_ref, weight_ref, cover_ref, north_ref, *refs
):
    *to_refs, sight_ref, fields_ref, out_ref = refs
    width = stack_ref.shape[1]
    rows = index_ref.shape[1]
    seam = 4 * tiles
    sight_ref[...] = edge_ref[0, seam + 8 :, :]
    north_c = edge_ref[0, seam + 8 + 2 * tracks : seam + 9 + 2 * tracks, :]
    pixel_rows = width // LANES
    fields_ref[:, 0:2, :] = edge_ref[:, seam : seam + 2, :]
    fields_ref[:, pixel_rows + 2 : pixel_rows + 4, :] = edge_ref[:, seam + 2 : seam + 4, :]
    out_ref[:, : 2 * tiles, :] = edge_ref[:, : 2 * tiles, :]
    out_ref[:, rows:, :] = edge_ref[:, 2 * tiles : 4 * tiles, :]
    invert_tiles([stack_ref], 0, width, operator_ref, fields_ref, 2)
    for r in range(0, rows - 2 * tiles, 8):
        near = [[fields_ref[f, r + k : r + k + 8, :] for k in range(3)] for f in range(2)]
        first = tiles + r
        velocity, variance = resample(near, first, index_ref, weight_ref)
        cover = cover_ref[first : first + 8, :].astype(jnp.float32)
        store_cells(out_ref, tiles + first, velocity, variance, cover, north_ref[first : first + 8, :], north_c)


    here = lax.axis_index("track")
    lines = rows // tiles + 2
    for half, to_ref in zip((here, 1 - here), to_refs):
        start = half * (tiles - span)
        for i in range(lines):
            to_ref[:, i * span : (i + 1) * span, :] = out_ref[:, pl.ds(i * tiles + start, span), :]
        left = to_ref.shape[1] - lines * span
        if left:
            to_ref[:, lines * span :, :] = jnp.zeros((2, left, LANES), jnp.float32)


def inner(stack, edge, operator, cells, tiles, tracks, span, copies):
    rows = cells[0].shape[1]
    compact = -(-(rows // tiles + 2) * span // 8) * 8
    vmem = pl.BlockSpec(memory_space=pltpu.VMEM)
    return pl.pallas_call(
        functools.partial(inner_kernel, tiles, tracks, span),
        in_specs=[vmem] * 7,
        out_specs=[vmem] * (copies + 1),
        out_shape=[jax.ShapeDtypeStruct((2, compact, LANES), jnp.float32)] * copies
        + [jax.ShapeDtypeStruct((edge.shape[1] - 4 * tiles - 8, LANES), jnp.float32)],
        scratch_shapes=[
            pltpu.VMEM((2, -(-(rows - 2 * tiles + 2) // 8) * 8, LANES), jnp.float32),
            pltpu.VMEM((2, rows + 2 * tiles, LANES), jnp.float32),
        ],
        compiler_params=pltpu.CompilerParams(vmem_limit_bytes=medium),
        name="inner_rows",
    )(stack, *(pltpu.with_memory_space_constraint(a, pltpu.VMEM) for a in (edge, operator, *cells)))


def solve_cells(of_tracks, sight_ref, tracks):
    a11 = a12 = a22 = b1 = b2 = 0.0
    for t, values_ref in of_tracks:
        weight, target = values_ref[0], values_ref[1]
        east_c, up_c = sight_ref[pl.ds(t, 1), :], sight_ref[pl.ds(tracks + t, 1), :]
        by_east, by_up = weight * east_c, weight * up_c
        a11 = a11 + by_east * east_c
        a12 = a12 + by_east * up_c
        a22 = a22 + by_up * up_c
        b1 = b1 + by_east * target
        b2 = b2 + by_up * target
    a11 = a11 + ridge_term
    a22 = a22 + ridge_term
    determ = a11 * a22 - a12 * a12
    return (a22 * b1 - a12 * b2) / determ, (a11 * b2 - a12 * b1) / determ


def final_kernel(
    tiles, span, own, tracks, sight_ref, own_ref, other_ref, north_ref, east_up_ref, strain_ref, work_ref, line_ref
):
    lines = north_ref.shape[0] // tiles
    rows = lines * span
    here = lax.axis_index("track")
    start = here * (tiles - span)
    at = sight_ref.shape[0] - 2 * tiles + start
    line_ref[:span, :] = sight_ref[pl.ds(at, span), :]
    for i in range(lines):
        line_ref[(i + 1) * span : (i + 2) * span, :] = north_ref[pl.ds(i * tiles + start, span), :]
    line_ref[rows + span : rows + 2 * span, :] = sight_ref[pl.ds(at + tiles, span), :]
    lane = lax.broadcasted_iota(jnp.int32, (rows, LANES), 1)
    tile = lax.broadcasted_iota(jnp.int32, (rows, LANES), 0) % span

    def across(field):
        right = jnp.where(tile == span - 1, 0.0, pltpu.roll(field, rows - 1, 0))
        left = jnp.where(tile == 0, 0.0, pltpu.roll(field, 1, 0))
        following = jnp.where(lane == LANES - 1, pltpu.roll(right, LANES - 1, 1), pltpu.roll(field, LANES - 1, 1))
        previous = jnp.where(lane == 0, pltpu.roll(left, 1, 1), pltpu.roll(field, 1, 1))
        return following - previous

    if other_ref.shape[0] == 1:
        of_tracks = [(here, own_ref), (1 - here, other_ref.at[0])]
    else:
        of_tracks = [(t, other_ref.at[t]) for t in range(other_ref.shape[0])]
    wide_east, wide_up = solve_cells(of_tracks, sight_ref, tracks)
    wide_north = line_ref[...]
    east, up, north = (wide[span : span + rows] for wide in (wide_east, wide_up, wide_north))
    work_ref[0] = east
    work_ref[1] = up
    work_ref[2] = across(east) / 2.0
    work_ref[3] = (wide_north[2 * span : 2 * span + rows] - wide_north[:rows]) / 2.0
    work_ref[4] = (wide_east[2 * span : 2 * span + rows] - wide_east[:rows] + across(north)) / 4.0
    first = here * own - start
    for field in range(5):
        target, at = (east_up_ref, field) if field < 2 else (strain_ref, field - 2)
        for j in range(own):
            target[at, :, j * LANES : (j + 1) * LANES] = work_ref[field, pl.ds(first + j, lines, stride=span), :]


def final(sight, vals, others, north, tiles, span, own, tracks):
    lines = north.shape[0] // tiles
    shape = (lines, own * LANES)
    vmem = pl.BlockSpec(memory_space=pltpu.VMEM)
    return pl.pallas_call(
        functools.partial(final_kernel, tiles, span, own, tracks),
        in_specs=[vmem] * 4,
        out_specs=[vmem] * 2,
        out_shape=[jax.ShapeDtypeStruct((2, *shape), jnp.float32), jax.ShapeDtypeStruct((3, *shape), jnp.float32)],
        scratch_shapes=[pltpu.VMEM((5, lines * span, LANES), jnp.float32), pltpu.VMEM(vals.shape[1:], jnp.float32)],
        compiler_params=pltpu.CompilerParams(vmem_limit_bytes=medium),
        name="solve_and_strain",
    )(sight, vals, others, north)


def per_device(phases, coherent, pairs, res_index, res_weight, coverage, los, north):
    parts = lax.axis_size("pix")
    tracks = lax.axis_size("track")
    grid_rows, columns = north.shape
    tiles = columns // CTILE
    rows = grid_rows * tiles
    group = GROUP if parts % GROUP == 0 else parts
    planes = parts // group
    plane, column = jnp.divmod(lax.axis_index("pix").astype(jnp.int32), group)
    steps = [-s % planes for s in range(planes)]
    first_piece, first_token = pack_edges(phases[0], coherent[0], group, tiles, steps[1:2])
    rest_flags, _ = lax.optimization_barrier((coherent[0], first_token))
    own_piece, *others, packed_token = pack_edges(phases[0], rest_flags, group, tiles, steps[:1] + steps[2:])
    packed = [own_piece, first_piece, *others]
    later_pairs, _ = lax.optimization_barrier((pairs[0], packed_token))
    steps_j, steps_s = jnp.meshgrid(jnp.arange(group), jnp.arange(planes), indexing="ij")
    sources = (partner_back(plane, -steps_s % planes, planes) * group + partner_back(column, steps_j, group)).reshape(-1)
    by_part = later_pairs.reshape(parts, -1, 2)
    edge_pairs = jnp.take(by_part, sources, axis=0).reshape(-1, 2)
    order = [snake(n, group) for n in range(parts)]
    inner_pairs = jnp.concatenate([by_part[p] for p in order], axis=0)
    operator, edge_operator, formed_token = setup_track(inner_pairs, edge_pairs)
    ids = [(z, c) for z in range(planes) for c in range(group)]
    arrived = [packed[0]] * planes
    for s in range(1, planes):
        far = [(z * group + c, partner(z, planes - s, planes) * group + c) for z, c in ids]
        arrived[s] = lax.ppermute(packed[s], "pix", far)
    by_column = regroup(formed_token, arrived, group)
    pieces = [by_column[0]]
    for j in range(1, group):
        near = [(z * group + c, z * group + partner(c, j, group)) for z, c in ids]
        pieces.append(lax.ppermute(by_column[j], "pix", near))
    later_flags, *_ = lax.optimization_barrier((coherent[0], packed_token))
    inner_stack = lax.all_to_all(
        pack_inner(phases[0], later_flags, parts, group, tiles),
        "pix",
        split_axis=0,
        concat_axis=0,
        tiled=True,
        axis_index_groups=[order],
    )
    north_cells = north.reshape(rows, LANES)
    weights = res_weight.reshape(-1, rows, LANES)
    cells = (
        res_index.reshape(-1, rows, LANES),
        weights / jnp.sum(weights, axis=0, keepdims=True),
        coverage.reshape(rows, 1),
        north_cells,
    )

    def flat(stack):
        return stack.reshape(-1, stack.shape[-1])

    onward = [(i, i + 1) for i in range(parts - 1)]
    back = [(j, i) for i, j in onward]
    kept, for_before, for_after = edges(
        los, [flat(piece) for piece in pieces], edge_operator, cells, fixed(cells, tiles), tiles
    )
    before = lax.ppermute(for_after, "pix", onward)
    after = lax.ppermute(for_before, "pix", back)
    edge_vals = finish(kept, before, after, cells, tiles, tracks)
    own_tiles = tiles // tracks
    if tracks == 2:
        span = own_tiles + 1
        vals, for_other, sight = inner(flat(inner_stack), edge_vals, operator, cells, tiles, tracks, span, 2)
        others = lax.ppermute(for_other, "track", [(0, 1), (1, 0)])[None]
    else:
        span = tiles
        vals, sight = inner(flat(inner_stack), edge_vals, operator, cells, tiles, tracks, span, 1)
        others = lax.all_gather(vals, "track", axis=0)
    return tuple(final(sight, vals, others, north_cells, tiles, span, own_tiles, tracks))


def solution(mesh):
    in_specs = (
        P("track", "pix", None),
        P("track", "pix", None),
        P("track", None, None),
        P("track", None, "pix"),
        P("track", None, "pix"),
        P("track", "pix", None),
        P(),
        P("pix", None),
    )
    out_specs = (P(None, "pix", "track"), P(None, "pix", "track"))
    return jax.shard_map(
        per_device, mesh=mesh, in_specs=in_specs, out_specs=out_specs, check_vma=False
    )
```

```python
import functools

import jax
import jax.numpy as jnp
from jax import lax
from jax.experimental import pallas as pl
from jax.experimental.pallas import tpu as pltpu
from jax.sharding import PartitionSpec as P

EPOCHS = 200
EXTRA = 16
HALO = 128
CTILE = 128
MBLK = 128
LANES = 128
TILE = 256
GROUP = 4
EDGE_COST = 54_000_000_000

token = jax.ShapeDtypeStruct((8, LANES), jnp.float32)


prior_var = 0.1
ridge_term = 0.5
medium = 24 * 1024 * 1024


def stay(array):
    return pltpu.with_memory_space_constraint(array, pltpu.HBM)


def expand_masks(flags_ref, stacked_ref, firsts, wanted, tile_out):
    ifgs = flags_ref.shape[0]
    for n, first in enumerate(firsts):
        stacked_ref[n * ifgs : (n + 1) * ifgs, :] = part_flags(flags_ref, first)
    stacked = stacked_ref[...].astype(jnp.bfloat16)
    block = lax.broadcasted_iota(jnp.int32, (LANES, 2 * MBLK), 0)
    right = lax.broadcasted_iota(jnp.int32, (LANES, 2 * MBLK), 1) >= MBLK
    for start in range(0, len(wanted), 2):
        here = jnp.where(right, wanted[start + 1], wanted[start])
        ones = (block == here).astype(jnp.bfloat16)
        keep = jnp.dot(stacked, ones, preferred_element_type=jnp.float32).astype(jnp.bfloat16)
        for n in range(len(firsts)):
            tile_out(n, start * MBLK, keep[n * ifgs : (n + 1) * ifgs])


def part_flags(flags_ref, first):
    lead = pl.multiple_of(first // LANES * LANES, LANES)
    flags = (flags_ref[:, pl.ds(lead, LANES)] == 1).astype(jnp.float32)
    return pltpu.roll(flags, (LANES - (first - lead)) % LANES, 1)


def partner(index, step, size):
    return index ^ step if size & (size - 1) == 0 else (index + step) % size


def partner_back(index, step, size):
    return index ^ step if size & (size - 1) == 0 else (index - step + size) % size


def pack_edges_kernel(tiles, group, steps, flags_hbm, phases_ref, *refs):
    *out_refs, token_ref, flags_ref, stacked_ref, near_ref, flag_sem, in_sem = refs
    token_ref[...] = jnp.zeros_like(token_ref)
    ifgs, blocks = flags_ref.shape
    reach = tiles + 1
    half = reach * MBLK
    parts = lax.axis_size("pix")
    planes = parts // group
    span = blocks // parts
    flag_copy = pltpu.make_async_copy(flags_hbm, flags_ref, flag_sem)
    flag_copy.start()
    plane = lax.axis_index("pix") // group
    first_parts = [partner(plane, step, planes) * group for step in steps]

    def regions(act):
        for n, first_part in enumerate(first_parts):
            for g in range(group + 1):
                b = first_part + g
                to_ref, sem = near_ref.at[n, g], in_sem.at[n, g]

                @pl.when(b == 0)
                def _():
                    act(pltpu.make_async_copy(phases_ref.at[:, pl.ds(0, half)], to_ref.at[:, pl.ds(half, half)], sem))

                @pl.when(b == parts)
                def _():
                    low = blocks * MBLK - half
                    act(pltpu.make_async_copy(phases_ref.at[:, pl.ds(low, half)], to_ref.at[:, pl.ds(0, half)], sem))

                @pl.when(jnp.logical_and(b > 0, b < parts))
                def _():
                    low = pl.multiple_of((span * jnp.clip(b, 1, parts - 1) - reach) * MBLK, MBLK)
                    act(pltpu.make_async_copy(phases_ref.at[:, pl.ds(low, 2 * half)], to_ref, sem))

    regions(lambda copy: copy.start())
    flag_copy.wait()
    firsts = [(first_part + g) * span for first_part in first_parts for g in range(group)]

    def tile_out(n, start, keep):
        out_refs[n // group][n % group, :, start : start + 2 * MBLK] = keep

    wanted = [k if k < reach else span - 2 * reach + k for k in range(2 * reach)]
    expand_masks(flags_ref, stacked_ref, firsts, wanted, tile_out)
    regions(lambda copy: copy.wait())
    for n, out_ref in enumerate(out_refs):
        for g in range(group):
            out_ref[g, :, :half] *= near_ref[n, g, :, half:]
            out_ref[g, :, half:] *= near_ref[n, g + 1, :, :half]


def pack_edges(phases, flags, group, tiles, steps):
    ifgs = phases.shape[0]
    hbm = pl.BlockSpec(memory_space=pltpu.HBM)
    width = 2 * (tiles + 1) * MBLK
    count = len(steps)
    return pl.pallas_call(
        functools.partial(pack_edges_kernel, tiles, group, steps),
        in_specs=[hbm, hbm],
        out_specs=[pl.BlockSpec(memory_space=pltpu.VMEM)] * (count + 1),
        out_shape=[jax.ShapeDtypeStruct((group, ifgs, width), jnp.bfloat16)] * count + [token],
        scratch_shapes=[
            pltpu.VMEM(flags.shape, jnp.int32),
            pltpu.VMEM((count * group * ifgs, LANES), jnp.float32),
            pltpu.VMEM((count, group + 1, ifgs, width), jnp.bfloat16),
            pltpu.SemaphoreType.DMA,
            pltpu.SemaphoreType.DMA((count, group + 1)),
        ],
        compiler_params=pltpu.CompilerParams(vmem_limit_bytes=medium),
        name="pack_edges",
    )(stay(flags), stay(phases))


def regroup_kernel(planes, group, after_ref, *refs):
    in_refs, out_refs = refs[:planes], refs[planes:]
    for j in range(group):
        column = partner(lax.rem(lax.axis_index("pix"), group), j, group)
        for s in range(planes):
            out_refs[j][s] = in_refs[s][column]


def regroup(after, pieces, group):
    planes = len(pieces)
    vmem = pl.BlockSpec(memory_space=pltpu.VMEM)
    shape = (planes, *pieces[0].shape[1:])
    return pl.pallas_call(
        functools.partial(regroup_kernel, planes, group),
        in_specs=[vmem] * (planes + 1),
        out_specs=[vmem] * group,
        out_shape=[jax.ShapeDtypeStruct(shape, jnp.bfloat16)] * group,
        compiler_params=pltpu.CompilerParams(vmem_limit_bytes=medium),
        name="regroup",
    )(after, *pieces)


def snake(n, group):
    plane, column = n // group, n % group
    return n + (plane + 1) % 2 * (group - 1 - 2 * column)


def pack_inner_kernel(reach, group, flags_hbm, phases_ref, out_ref, flags_ref, stacked_ref, held_ref, flag_sem, in_sem):
    parts, ifgs, width = out_ref.shape
    span = flags_ref.shape[1] // parts
    flag_copy = pltpu.make_async_copy(flags_hbm, flags_ref, flag_sem)
    flag_copy.start()

    def inward(n):
        low = pl.multiple_of((snake(n, group) * span + reach) * MBLK, MBLK)
        return pltpu.make_async_copy(phases_ref.at[:, pl.ds(low, width)], held_ref.at[n], in_sem.at[n])

    @pl.loop(0, parts)
    def _(p):
        inward(p).start()

    flag_copy.wait()

    def tile_out(n, start, keep):
        out_ref[n, :, start : start + 2 * MBLK] = keep

    wanted = list(range(reach, span - reach))
    expand_masks(flags_ref, stacked_ref, [snake(n, group) * span for n in range(parts)], wanted, tile_out)

    @pl.loop(0, parts)
    def _(p):
        inward(p).wait()
        out_ref[p] *= held_ref[p]


def pack_inner(phases, flags, parts, group, tiles):
    ifgs = phases.shape[0]
    reach = tiles + 1
    width = (flags.shape[1] // parts - 2 * reach) * MBLK
    hbm = pl.BlockSpec(memory_space=pltpu.HBM)
    return pl.pallas_call(
        functools.partial(pack_inner_kernel, reach, group),
        in_specs=[hbm, hbm],
        out_specs=pl.BlockSpec(memory_space=pltpu.VMEM),
        out_shape=jax.ShapeDtypeStruct((parts, ifgs, width), jnp.bfloat16),
        scratch_shapes=[
            pltpu.VMEM(flags.shape, jnp.int32),
            pltpu.VMEM((parts * ifgs, LANES), jnp.float32),
            pltpu.VMEM((parts, ifgs, width), jnp.bfloat16),
            pltpu.SemaphoreType.DMA,
            pltpu.SemaphoreType.DMA((parts,)),
        ],
        compiler_params=pltpu.CompilerParams(vmem_limit_bytes=medium),
        name="pack_inner",
    )(stay(flags), stay(phases))


def split(a, terms):
    parts = []
    for _ in range(terms):
        parts.append(a.astype(jnp.bfloat16))
        a = a - parts[-1].astype(jnp.float32)
    return parts


def sum_dots(pairs):
    return sum(jnp.dot(a, b, preferred_element_type=jnp.float32) for a, b in pairs)


def operator_kernel(pairs_ref, other_ref, out_ref, other_out_ref, token_ref, laplacian_ref, inverse_ref):
    token_ref[...] = jnp.zeros_like(token_ref)
    ifgs = pairs_ref.shape[1]
    size = inverse_ref.shape[0]
    epoch = lax.broadcasted_iota(jnp.int32, (size, ifgs), 0)

    def ends(ref):
        return (epoch == ref[1:2, :]).astype(jnp.float32) - (epoch == ref[0:1, :]).astype(jnp.float32)

    across = ends(pairs_ref)
    down = across.T
    eye = (
        lax.broadcasted_iota(jnp.int32, (size, size), 0) == lax.broadcasted_iota(jnp.int32, (size, size), 1)
    ).astype(jnp.float32)
    laplacian = jnp.dot(across.astype(jnp.bfloat16), down.astype(jnp.bfloat16), preferred_element_type=jnp.float32)
    normal = eye + laplacian
    laplacian_ref[...] = laplacian.astype(jnp.bfloat16)
    first = eye / jnp.where(eye == 1.0, normal, 1.0)
    scaled = jnp.sum(first, axis=1, keepdims=True) * normal * jnp.sum(first, axis=0, keepdims=True)
    inverse_ref[...] = 2.0 * first - scaled

    def unfinished(state):
        step, gap = state
        return jnp.logical_and(step < 24, gap > 1e-5)

    def improve(state):
        step, _ = state
        inverse = inverse_ref[...]
        parts = split(inverse, 3)
        rest = eye - inverse - sum_dots((laplacian_ref[...], part) for part in parts)
        high, low = split(rest, 2)
        inverse_ref[...] = inverse + sum_dots(((parts[0], low), (parts[1], high), (parts[0], high)))
        return step + 1, jnp.max(jnp.abs(rest))

    lax.while_loop(unfinished, improve, (jnp.int32(0), jnp.float32(1.0)))
    place = lax.broadcasted_iota(jnp.int32, (size, ifgs), 0)
    centred = place.astype(jnp.float32) - (EPOCHS - 1) / 2.0
    square = sum((e - (EPOCHS - 1) / 2.0) ** 2 for e in range(EPOCHS))
    slope = jnp.where(place < EPOCHS, centred * (EPOCHS - 1) / square, 0.0)
    same = lax.broadcasted_iota(jnp.int32, (ifgs, ifgs), 0) == lax.broadcasted_iota(jnp.int32, (ifgs, ifgs), 1)
    extra = lax.broadcasted_iota(jnp.int32, (EXTRA, ifgs), 0)
    for ref, to_ref in ((pairs_ref, out_ref), (other_ref, other_out_ref)):
        across = ends(ref)
        ones = across.astype(jnp.bfloat16)
        pseudo = sum_dots((part, ones) for part in split(inverse_ref[...], 3)).astype(jnp.bfloat16)
        fitted = jnp.dot(across.T.astype(jnp.bfloat16), pseudo, preferred_element_type=jnp.float32)
        to_ref[:ifgs, :] = (same.astype(jnp.float32) - fitted).astype(jnp.bfloat16)
        row = jnp.sum(pseudo.astype(jnp.float32) * slope, axis=0, keepdims=True)
        high = row.astype(jnp.bfloat16).astype(jnp.float32)
        rest = row - high
        middle = rest.astype(jnp.bfloat16).astype(jnp.float32)
        low = rest - middle
        terms = jnp.where(extra == 0, high, jnp.where(extra == 1, middle, jnp.where(extra == 2, low, 0.0)))
        to_ref[ifgs:, :] = terms.astype(jnp.bfloat16)


def setup_track(pair_rows, other_rows):
    ifgs = pair_rows.shape[0]
    size = -(-EPOCHS // LANES) * LANES
    vmem = pl.BlockSpec(memory_space=pltpu.VMEM)
    return pl.pallas_call(
        operator_kernel,
        in_specs=[vmem] * 2,
        out_specs=[vmem] * 3,
        out_shape=[jax.ShapeDtypeStruct((ifgs + EXTRA, ifgs), jnp.bfloat16)] * 2 + [token],
        scratch_shapes=[pltpu.VMEM((size, size), jnp.bfloat16), pltpu.VMEM((size, size), jnp.float32)],
        compiler_params=pltpu.CompilerParams(vmem_limit_bytes=medium),
        name="misfit_operator",
    )(pair_rows.T, other_rows.T)


def invert_tiles(stack_refs, first, width, operator_ref, fields_ref, base):
    ifgs = operator_ref.shape[1]
    for start in range(0, width, TILE):
        here = pl.ds(pl.multiple_of(first + start, LANES), TILE)
        stack = jnp.concatenate([ref[:, here] for ref in stack_refs], axis=0)
        product = jnp.dot(operator_ref[...], stack, preferred_element_type=jnp.float32)
        velocity = jnp.sum(product[ifgs : ifgs + 8], axis=0, keepdims=True)
        variance = jnp.sum(product[:ifgs] * product[:ifgs], axis=0, keepdims=True) / ifgs
        for k in range(TILE // LANES):
            row = pl.ds(base + start // LANES + k, 1)
            fields_ref[0, row, :] = velocity[:, k * LANES : (k + 1) * LANES]
            fields_ref[1, row, :] = variance[:, k * LANES : (k + 1) * LANES]


def pick(source, lane):
    return jnp.take_along_axis(source, lane, axis=1, mode="promise_in_bounds")


def resample(near, cell, index_ref, weight_ref):
    lanes = lax.broadcasted_iota(jnp.int32, (8, LANES), 1)
    here = pl.ds(cell, 8)
    sums = [jnp.zeros((8, LANES), jnp.float32)] * 2
    total = jnp.zeros((8, LANES), jnp.float32)
    for b in range(index_ref.shape[0]):
        weight = weight_ref[b, here, :]
        place = lanes + index_ref[b, here, :] + HALO
        lane = place & (LANES - 1)
        which = place >> 7
        total = total + weight
        for f in range(2):
            low, mid, high = (pick(near[f][k], lane) for k in range(3))
            taken = jnp.where(which == 0, low, jnp.where(which == 1, mid, high))
            sums[f] = sums[f] + taken * weight
    return sums[0] / total, sums[1] / total, total


def boundary(row, offsets, weights, sources, wanted):
    lanes = lax.broadcasted_iota(jnp.int32, (8, LANES), 1)
    rows = lax.broadcasted_iota(jnp.int32, (8, LANES), 0)
    sums = [jnp.zeros((8, LANES), jnp.float32)] * 2
    for offset, weight in zip(offsets, weights):
        place = lanes + offset + HALO
        lane = place & (LANES - 1)
        keep = jnp.where(jnp.logical_and(place >> 7 == wanted, rows == row), weight, 0.0)
        for f in range(2):
            sums[f] = sums[f] + pick(jnp.broadcast_to(sources[f], (8, LANES)), lane) * keep
    return sums


def store_cells(out_ref, at, velocity, variance, cover, north, north_c):
    out_ref[0, at : at + 8, :] = cover / (variance + prior_var)
    out_ref[1, at : at + 8, :] = velocity - north_c * north


def fixed_kernel(tiles, index_ref, weight_ref, cover_ref, north_ref, back_ref, onward_ref):
    taps, rows, _ = index_ref.shape
    place = lax.broadcasted_iota(jnp.int32, (tiles, LANES), 0) == lax.broadcasted_iota(jnp.int32, (tiles, LANES), 1)
    for half, to_ref in enumerate((back_ref, onward_ref)):
        edge = slice(half * (rows - tiles), half * (rows - tiles) + tiles)
        outermost = half * (rows - 1)
        row = slice(outermost, outermost + 1)
        to_ref[:tiles, :] = north_ref[edge, :]
        total = sum(weight_ref[b, row, :] for b in range(taps))
        for b in range(taps):
            to_ref[tiles + b : tiles + b + 1, :] = index_ref[b, row, :].astype(jnp.float32)
            to_ref[tiles + taps + b : tiles + taps + b + 1, :] = weight_ref[b, row, :] / total
        at = tiles + 2 * taps
        cover = jnp.where(place, jnp.broadcast_to(cover_ref[edge, :].astype(jnp.float32), (tiles, LANES)), 0.0)
        to_ref[at : at + 1, :] = jnp.sum(cover, axis=0, keepdims=True)
        to_ref[at + 1 :, :] = jnp.zeros((to_ref.shape[0] - at - 1, LANES), jnp.float32)


def fixed(cells, tiles):
    rows = -(-(tiles + 2 * cells[0].shape[0] + 1) // 8) * 8
    vmem = pl.BlockSpec(memory_space=pltpu.VMEM)
    return pl.pallas_call(
        functools.partial(fixed_kernel, tiles),
        in_specs=[vmem] * 4,
        out_specs=[vmem] * 2,
        out_shape=[jax.ShapeDtypeStruct((rows, LANES), jnp.float32)] * 2,
        compiler_params=pltpu.CompilerParams(vmem_limit_bytes=medium),
        name="edge_inputs",
    )(*cells)


def edges_kernel(tiles, group, los_ref, *refs):
    stack_refs = refs[:group]
    operator_ref, index_ref, weight_ref, *fixed_refs, kept_ref, back_ref, onward_ref, fields_ref = refs[group:]
    width = stack_refs[0].shape[1]
    count = width // LANES
    rows = index_ref.shape[1]
    none = jnp.zeros((2, 1, LANES), jnp.float32)
    fields_ref[:, :1, :] = none
    fields_ref[:, count + 1 : count + 2, :] = none
    invert_tiles(stack_refs, 0, width, operator_ref, fields_ref, 1)
    seam = 2 * tiles
    kept_ref[:, seam : seam + 4, :] = fields_ref[:, tiles : tiles + 4, :]
    kept_ref[:, seam + 4 : seam + 5, :] = fields_ref[:, 1:2, :]
    kept_ref[:, seam + 5 : seam + 6, :] = fields_ref[:, count : count + 1, :]
    kept_ref[:, seam + 6 :, :] = jnp.zeros((2, kept_ref.shape[1] - seam - 6, LANES), jnp.float32)
    tracks = los_ref.shape[0]
    scalars = [los_ref[t, part] for part in (0, 2) for t in range(tracks)] + [los_ref[lax.axis_index("track"), 1]]
    for k, scalar in enumerate(scalars):
        row = seam + 8 + k
        kept_ref[0, row : row + 1, :] = jnp.full((1, LANES), scalar, jnp.float32)
    for half, (fixed_ref, to_ref) in enumerate(zip(fixed_refs, (back_ref, onward_ref))):
        first = half * (rows - tiles)
        after = to_ref.shape[0] - fixed_ref.shape[0]
        to_ref[after:, :] = fixed_ref[...]
        for r in range(0, tiles, 8):
            base = half * (tiles + 2) + r
            near = [[fields_ref[f, base + k : base + k + 8, :] for k in range(3)] for f in range(2)]
            velocity, variance, _ = resample(near, first + r, index_ref, weight_ref)
            for f, values in enumerate((velocity, variance)):
                kept_ref[f, half * tiles + r : half * tiles + r + 8, :] = values
                to_ref[f * tiles + r : f * tiles + r + 8, :] = values
        for f in range(2):
            to_ref[seam + f : seam + f + 1, :] = kept_ref[f, seam + 4 + half : seam + 5 + half, :]
        to_ref[seam + 2 : after, :] = jnp.zeros((after - seam - 2, LANES), jnp.float32)


def edges(los, stacks, operator, cells, both_fixed, tiles):
    rows = 2 * (tiles + 1)
    payload = -(-(2 * tiles + 2) // 8) * 8 + both_fixed[0].shape[0]
    sight = -(-(2 * los.shape[0] + 1) // 8) * 8
    shapes = [(2, 2 * tiles + 8 + sight, LANES), (payload, LANES), (payload, LANES)]
    vmem = pl.BlockSpec(memory_space=pltpu.VMEM)
    return pl.pallas_call(
        functools.partial(edges_kernel, tiles, len(stacks)),
        in_specs=[pl.BlockSpec(memory_space=pltpu.SMEM)] + [vmem] * (len(stacks) + 5),
        out_specs=[vmem] * 3,
        out_shape=[jax.ShapeDtypeStruct(shape, jnp.float32) for shape in shapes],
        scratch_shapes=[pltpu.VMEM((2, -(-(rows + 2) // 8) * 8, LANES), jnp.float32)],
        compiler_params=pltpu.CompilerParams(vmem_limit_bytes=medium),
        cost_estimate=pl.CostEstimate(flops=EDGE_COST, bytes_accessed=0, transcendentals=0),
        name="edge_rows",
    )(los, *stacks, operator, *cells[:2], *both_fixed)


def finish_kernel(
    tiles, tracks, kept_ref, before_ref, after_ref, index_ref, weight_ref, cover_ref, north_ref, out_ref
):
    taps, rows, _ = index_ref.shape
    seam = 2 * tiles
    north_c = kept_ref[0, seam + 8 + 2 * tracks : seam + 9 + 2 * tracks, :]
    place = lax.broadcasted_iota(jnp.int32, (8, LANES), 0) - lax.broadcasted_iota(jnp.int32, (8, LANES), 1)
    for half, from_ref in enumerate((before_ref, after_ref)):
        fixed_ref = from_ref.at[-(-(seam + 2) // 8) * 8 :]
        edge = half * (tiles - 8)
        row = 7 * half
        outermost = half * (rows - 1)
        total = sum(weight_ref[b, outermost : outermost + 1, :] for b in range(taps))
        to_own = boundary(
            row,
            [index_ref[b, outermost : outermost + 1, :] for b in range(taps)],
            [weight_ref[b, outermost : outermost + 1, :] / total for b in range(taps)],
            [from_ref[seam + f : seam + f + 1, :] for f in range(2)],
            2 * half,
        )
        to_other = boundary(
            7 - row,
            [fixed_ref[tiles + b : tiles + b + 1, :].astype(jnp.int32) for b in range(taps)],
            [fixed_ref[tiles + taps + b : tiles + taps + b + 1, :] for b in range(taps)],
            [kept_ref[f, seam + 4 + half : seam + 5 + half, :] for f in range(2)],
            2 - 2 * half,
        )
        covers = fixed_ref[tiles + 2 * taps : tiles + 2 * taps + 1, :]
        for r in range(0, tiles, 8):
            first = half * (rows - tiles) + r
            values = [kept_ref[f, half * tiles + r : half * tiles + r + 8, :] for f in range(2)]
            if r == edge:
                values = [value + more for value, more in zip(values, to_own)]
            cover = cover_ref[first : first + 8, :].astype(jnp.float32)
            store_cells(out_ref, (1 + half) * tiles + r, *values, cover, north_ref[first : first + 8, :], north_c)
            values = [from_ref[f * tiles + r : f * tiles + r + 8, :] for f in range(2)]
            if r == tiles - 8 - edge:
                values = [value + more for value, more in zip(values, to_other)]
            cover = jnp.sum(jnp.where(place == -r, jnp.broadcast_to(covers, (8, LANES)), 0.0), axis=1, keepdims=True)
            store_cells(out_ref, 3 * half * tiles + r, *values, cover, fixed_ref[r : r + 8, :], north_c)
    rest = 4 * tiles + kept_ref.shape[1] - seam
    out_ref[:, 4 * tiles : rest, :] = kept_ref[:, seam:, :]
    at = -(-(seam + 2) // 8) * 8
    for half, from_ref in enumerate((before_ref, after_ref)):
        here = slice(rest + half * tiles, rest + (half + 1) * tiles)
        out_ref[0, here, :] = from_ref[at : at + tiles, :]
        out_ref[1, here, :] = jnp.zeros((tiles, LANES), jnp.float32)


def finish(kept, before, after, cells, tiles, tracks):
    vmem = pl.BlockSpec(memory_space=pltpu.VMEM)
    return pl.pallas_call(
        functools.partial(finish_kernel, tiles, tracks),
        in_specs=[vmem] * 7,
        out_specs=vmem,
        out_shape=pltpu.VMEM((2, kept.shape[1] + 4 * tiles, LANES), jnp.float32),
        compiler_params=pltpu.CompilerParams(vmem_limit_bytes=medium),
        name="edge_cells",
    )(kept, before, after, *cells)


def inner_kernel(
    tiles, tracks, span, stack_ref, edge_ref, operator_ref, index_ref, weight_ref, cover_ref, north_ref, *refs
):
    *to_refs, sight_ref, fields_ref, out_ref = refs
    width = stack_ref.shape[1]
    rows = index_ref.shape[1]
    seam = 4 * tiles
    sight_ref[...] = edge_ref[0, seam + 8 :, :]
    north_c = edge_ref[0, seam + 8 + 2 * tracks : seam + 9 + 2 * tracks, :]
    pixel_rows = width // LANES
    fields_ref[:, 0:2, :] = edge_ref[:, seam : seam + 2, :]
    fields_ref[:, pixel_rows + 2 : pixel_rows + 4, :] = edge_ref[:, seam + 2 : seam + 4, :]
    out_ref[:, : 2 * tiles, :] = edge_ref[:, : 2 * tiles, :]
    out_ref[:, rows:, :] = edge_ref[:, 2 * tiles : 4 * tiles, :]
    invert_tiles([stack_ref], 0, width, operator_ref, fields_ref, 2)
    for r in range(0, rows - 2 * tiles, 8):
        near = [[fields_ref[f, r + k : r + k + 8, :] for k in range(3)] for f in range(2)]
        first = tiles + r
        velocity, variance, _ = resample(near, first, index_ref, weight_ref)
        cover = cover_ref[first : first + 8, :].astype(jnp.float32)
        store_cells(out_ref, tiles + first, velocity, variance, cover, north_ref[first : first + 8, :], north_c)


    here = lax.axis_index("track")
    lines = rows // tiles + 2
    for half, to_ref in zip((here, 1 - here), to_refs):
        start = half * (tiles - span)
        for field in range(2):
            for j in range(span):
                to_ref[field, pl.ds(j, lines, stride=span), :] = out_ref[field, pl.ds(start + j, lines, stride=tiles), :]
        left = to_ref.shape[1] - lines * span
        if left:
            to_ref[:, lines * span :, :] = jnp.zeros((2, left, LANES), jnp.float32)


def inner(stack, edge, operator, cells, tiles, tracks, span, copies):
    rows = cells[0].shape[1]
    compact = -(-(rows // tiles + 2) * span // 8) * 8
    vmem = pl.BlockSpec(memory_space=pltpu.VMEM)
    return pl.pallas_call(
        functools.partial(inner_kernel, tiles, tracks, span),
        in_specs=[vmem] * 7,
        out_specs=[vmem] * (copies + 1),
        out_shape=[jax.ShapeDtypeStruct((2, compact, LANES), jnp.float32)] * copies
        + [jax.ShapeDtypeStruct((edge.shape[1] - 4 * tiles - 8, LANES), jnp.float32)],
        scratch_shapes=[
            pltpu.VMEM((2, -(-(rows - 2 * tiles + 2) // 8) * 8, LANES), jnp.float32),
            pltpu.VMEM((2, rows + 2 * tiles, LANES), jnp.float32),
        ],
        compiler_params=pltpu.CompilerParams(vmem_limit_bytes=medium),
        name="inner_rows",
    )(stack, *(pltpu.with_memory_space_constraint(a, pltpu.VMEM) for a in (edge, operator, *cells)))


def solve_cells(of_tracks, sight_ref, tracks):
    a11 = a12 = a22 = b1 = b2 = 0.0
    for t, values_ref in of_tracks:
        weight, target = values_ref[0], values_ref[1]
        east_c, up_c = sight_ref[pl.ds(t, 1), :], sight_ref[pl.ds(tracks + t, 1), :]
        by_east, by_up = weight * east_c, weight * up_c
        a11 = a11 + by_east * east_c
        a12 = a12 + by_east * up_c
        a22 = a22 + by_up * up_c
        b1 = b1 + by_east * target
        b2 = b2 + by_up * target
    a11 = a11 + ridge_term
    a22 = a22 + ridge_term
    determ = a11 * a22 - a12 * a12
    return (a22 * b1 - a12 * b2) / determ, (a11 * b2 - a12 * b1) / determ


def final_kernel(
    tiles, span, own, tracks, sight_ref, own_ref, other_ref, north_ref, east_up_ref, strain_ref, work_ref, line_ref
):
    lines = north_ref.shape[0] // tiles
    rows = lines * span
    here = lax.axis_index("track")
    start = here * (tiles - span)
    at = sight_ref.shape[0] - 2 * tiles + start
    line_ref[:span, :] = sight_ref[pl.ds(at, span), :]
    for i in range(lines):
        line_ref[(i + 1) * span : (i + 2) * span, :] = north_ref[pl.ds(i * tiles + start, span), :]
    line_ref[rows + span : rows + 2 * span, :] = sight_ref[pl.ds(at + tiles, span), :]
    lane = lax.broadcasted_iota(jnp.int32, (rows, LANES), 1)
    tile = lax.broadcasted_iota(jnp.int32, (rows, LANES), 0) % span

    def across(field):
        right = jnp.where(tile == span - 1, 0.0, pltpu.roll(field, rows - 1, 0))
        left = jnp.where(tile == 0, 0.0, pltpu.roll(field, 1, 0))
        following = jnp.where(lane == LANES - 1, pltpu.roll(right, LANES - 1, 1), pltpu.roll(field, LANES - 1, 1))
        previous = jnp.where(lane == 0, pltpu.roll(left, 1, 1), pltpu.roll(field, 1, 1))
        return following - previous

    if other_ref.shape[0] == 1:
        of_tracks = [(here, own_ref), (1 - here, other_ref.at[0])]
    else:
        of_tracks = [(t, other_ref.at[t]) for t in range(other_ref.shape[0])]
    wide_east, wide_up = solve_cells(of_tracks, sight_ref, tracks)
    wide_north = line_ref[...]
    east, up, north = (wide[span : span + rows] for wide in (wide_east, wide_up, wide_north))
    work_ref[0] = east
    work_ref[1] = up
    work_ref[2] = across(east) / 2.0
    work_ref[3] = (wide_north[2 * span : 2 * span + rows] - wide_north[:rows]) / 2.0
    work_ref[4] = (wide_east[2 * span : 2 * span + rows] - wide_east[:rows] + across(north)) / 4.0
    first = here * own - start
    for field in range(5):
        target, at = (east_up_ref, field) if field < 2 else (strain_ref, field - 2)
        for j in range(own):
            target[at, :, j * LANES : (j + 1) * LANES] = work_ref[field, pl.ds(first + j, lines, stride=span), :]


def final(sight, vals, others, north, tiles, span, own, tracks):
    lines = north.shape[0] // tiles
    shape = (lines, own * LANES)
    vmem = pl.BlockSpec(memory_space=pltpu.VMEM)
    return pl.pallas_call(
        functools.partial(final_kernel, tiles, span, own, tracks),
        in_specs=[vmem] * 4,
        out_specs=[vmem] * 2,
        out_shape=[jax.ShapeDtypeStruct((2, *shape), jnp.float32), jax.ShapeDtypeStruct((3, *shape), jnp.float32)],
        scratch_shapes=[pltpu.VMEM((5, lines * span, LANES), jnp.float32), pltpu.VMEM(vals.shape[1:], jnp.float32)],
        compiler_params=pltpu.CompilerParams(vmem_limit_bytes=medium),
        name="solve_and_strain",
    )(sight, vals, others, north)


def per_device(phases, coherent, pairs, res_index, res_weight, coverage, los, north):
    parts = lax.axis_size("pix")
    tracks = lax.axis_size("track")
    grid_rows, columns = north.shape
    tiles = columns // CTILE
    rows = grid_rows * tiles
    group = GROUP if parts % GROUP == 0 else parts
    planes = parts // group
    plane, column = jnp.divmod(lax.axis_index("pix").astype(jnp.int32), group)
    steps = [-s % planes for s in range(planes)]
    first_piece, first_token = pack_edges(phases[0], coherent[0], group, tiles, steps[1:2])
    rest_flags, _ = lax.optimization_barrier((coherent[0], first_token))
    own_piece, *others, packed_token = pack_edges(phases[0], rest_flags, group, tiles, steps[:1] + steps[2:])
    packed = [own_piece, first_piece, *others]
    later_pairs, _ = lax.optimization_barrier((pairs[0], packed_token))
    steps_j, steps_s = jnp.meshgrid(jnp.arange(group), jnp.arange(planes), indexing="ij")
    sources = (partner_back(plane, -steps_s % planes, planes) * group + partner_back(column, steps_j, group)).reshape(-1)
    by_part = later_pairs.reshape(parts, -1, 2)
    edge_pairs = jnp.take(by_part, sources, axis=0).reshape(-1, 2)
    order = [snake(n, group) for n in range(parts)]
    inner_pairs = jnp.concatenate([by_part[p] for p in order], axis=0)
    operator, edge_operator, formed_token = setup_track(inner_pairs, edge_pairs)
    ids = [(z, c) for z in range(planes) for c in range(group)]
    arrived = [packed[0]] * planes
    for s in range(1, planes):
        far = [(z * group + c, partner(z, planes - s, planes) * group + c) for z, c in ids]
        arrived[s] = lax.ppermute(packed[s], "pix", far)
    by_column = regroup(formed_token, arrived, group)
    pieces = [by_column[0]]
    for j in range(1, group):
        near = [(z * group + c, z * group + partner(c, j, group)) for z, c in ids]
        pieces.append(lax.ppermute(by_column[j], "pix", near))
    later_flags, *_ = lax.optimization_barrier((coherent[0], packed_token))
    inner_stack = lax.all_to_all(
        pack_inner(phases[0], later_flags, parts, group, tiles),
        "pix",
        split_axis=0,
        concat_axis=0,
        tiled=True,
        axis_index_groups=[order],
    )
    north_cells = north.reshape(rows, LANES)
    cells = (
        res_index.reshape(-1, rows, LANES),
        res_weight.reshape(-1, rows, LANES),
        coverage.reshape(rows, 1),
        north_cells,
    )

    def flat(stack):
        return stack.reshape(-1, stack.shape[-1])

    onward = [(i, i + 1) for i in range(parts - 1)]
    back = [(j, i) for i, j in onward]
    kept, for_before, for_after = edges(
        los, [flat(piece) for piece in pieces], edge_operator, cells, fixed(cells, tiles), tiles
    )
    before = lax.ppermute(for_after, "pix", onward)
    after = lax.ppermute(for_before, "pix", back)
    edge_vals = finish(kept, before, after, cells, tiles, tracks)
    own_tiles = tiles // tracks
    if tracks == 2:
        span = own_tiles + 1
        vals, for_other, sight = inner(flat(inner_stack), edge_vals, operator, cells, tiles, tracks, span, 2)
        others = lax.ppermute(for_other, "track", [(0, 1), (1, 0)])[None]
    else:
        span = tiles
        vals, sight = inner(flat(inner_stack), edge_vals, operator, cells, tiles, tracks, span, 1)
        others = lax.all_gather(vals, "track", axis=0)
    return tuple(final(sight, vals, others, north_cells, tiles, span, own_tiles, tracks))


def solution(mesh):
    in_specs = (
        P("track", "pix", None),
        P("track", "pix", None),
        P("track", None, None),
        P("track", None, "pix"),
        P("track", None, "pix"),
        P("track", "pix", None),
        P(),
        P("pix", None),
    )
    out_specs = (P(None, "pix", "track"), P(None, "pix", "track"))
    return jax.shard_map(
        per_device, mesh=mesh, in_specs=in_specs, out_specs=out_specs, check_vma=False
    )
```
